32 devices in a mesh: curve: 8 (over z, y), cross: 4 (over x, core).
Axes of the slice: x: 2, y: 2, z: 4, core: 2. Of those that a mesh axis runs over, the one named last changes fastest.
Arguments:
- populations: float32 [96, 19, 4096], P(('curve', 'cross')), may hold values from 0 to 3, as said below
- site_flags: int32 [96, 5832], P(('curve', 'cross')), may hold values from 0 to 1, as said below
- neighbours: int32 [96, 18], P(('curve', 'cross')), may hold values from -1 to 95, as said below
- migrations: int32 [32, 3], replicated, may hold values from -1 to 31, as said below
- counts: int32 [32], P(('curve', 'cross')), may hold values from 1 to 3, as said below
Outputs:
- advanced: float32 [96, 19, 4096], P(('curve', 'cross'))
The draws below stay inside these ranges and needn't reach their ends.
Inputs may be any that keep to these rules, and one draw needn't show every extreme that they name: Weighted populations of a flow of density near one and small velocity; every entry is positive. `site_flags`: the padding sites carry the flags of the neighbouring block's sites there, 0 where no block lies; corner padding sites and all sites of empty slots are 0. `neighbours`: A block named in direction c_j lies on the device whose curve index exceeds the block's own by the first component of c_j and whose cross index exceeds it by the second; a block in direction c_j names the first block in direction -c_j. Empty slots name none. `migrations`: at most one block leaves a device, to the device one step lower or higher along curve with the same cross index; -1 in all three columns where none leaves. Destination slots lie below the receiver's count and no two moves share one. `counts`: the live blocks of a device fill its slots 0 to count - 1; in every draw some device holds 3.
All inputs are finite; a program needn't handle non-finite values.
Results may differ from the reference program's by a relative error of at most 0.0003.
Values sent between devices are 32-bit elements; how exact they have to be, the bound alone decides.
No kernel may reach another device: no remote copies, remote signals or barrier semaphores. Data moves between devices by JAX's collectives and lax.ppermute only.
A program may use at most 128 MiB of HBM per device.

```python
import jax
import jax.numpy as jnp
import numpy as np
from jax import lax

EDGE = 16
SLOTS = 3
STEPS = 3
N_CURVE = 8
N_CROSS = 4


VELOCITY = [(0, 0, 0), (1, 0, 0), (-1, 0, 0), (0, 1, 0), (0, -1, 0), (0, 0, 1), (0, 0, -1), (1, 1, 0), (-1, -1, 0), (1, -1, 0), (-1, 1, 0), (1, 0, 1), (-1, 0, -1), (1, 0, -1), (-1, 0, 1), (0, 1, 1), (0, -1, -1), (0, 1, -1), (0, -1, 1)]


def region_codes():
    span = EDGE + 2
    flat = np.arange(span * span * span, dtype=np.int32)
    grid = np.stack([flat // (span * span), flat // span % span, flat % span])
    sides = np.where(grid == 0, -1, np.where(grid == span - 1, 1, 0))
    codes = np.zeros(grid.shape[1], dtype=np.int32)
    for position in range(grid.shape[1]):
        offset = (int(sides[0, position]), int(sides[1, position]), int(sides[2, position]))
        if offset in VELOCITY:
            codes[position] = VELOCITY.index(offset)
        else:
            codes[position] = 19
    return (codes, grid - 1)


def plan_layout(key):
    curve_len = N_CURVE
    cross_len = N_CROSS
    rank_total = curve_len * cross_len
    levels = 2 * SLOTS
    keys = jax.random.split(key, 6)
    curve_pos = jnp.arange(curve_len, dtype=jnp.int32)[:, None]
    cross_pos = jnp.arange(cross_len, dtype=jnp.int32)[None, :]
    kept = jax.random.randint(keys[0], (curve_len, cross_len), 1, SLOTS - 1, dtype=jnp.int32)
    heading = jax.random.randint(keys[1], (curve_len, cross_len), -1, 2, dtype=jnp.int32)
    heading = jnp.where((curve_pos == 0) & (heading < 0), 1, heading)
    heading = jnp.where((curve_pos == curve_len - 1) & (heading > 0), -1, heading)
    centre = jax.random.randint(keys[2], (), 1, curve_len - 1, dtype=jnp.int32)
    column = jax.random.randint(keys[3], (), 0, cross_len, dtype=jnp.int32)
    chosen = cross_pos == column
    heading = jnp.where(chosen & (curve_pos == centre - 1), 1, heading)
    heading = jnp.where(chosen & (curve_pos == centre + 1), -1, heading)
    kept = jnp.where(chosen & (curve_pos == centre), SLOTS - 2, kept)
    no_row = jnp.zeros((1, cross_len), jnp.int32)
    from_lower = jnp.concatenate([no_row, (heading[:-1] > 0).astype(jnp.int32)], axis=0)
    from_upper = jnp.concatenate([(heading[1:] < 0).astype(jnp.int32), no_row], axis=0)
    count_grid = kept + from_lower + from_upper
    kept_above = jnp.concatenate([kept[1:], kept[-1:]], axis=0)
    kept_below = jnp.concatenate([kept[:1], kept[:-1]], axis=0)
    lower_below = jnp.concatenate([from_lower[:1], from_lower[:-1]], axis=0)
    sending = heading != 0
    dest_slot = jnp.where(heading > 0, kept_above, kept_below + lower_below)
    rank_grid = curve_pos * cross_len + cross_pos
    migrations = jnp.stack([jnp.where(sending, kept, -1), jnp.where(sending, rank_grid + heading * cross_len, -1), jnp.where(sending, dest_slot, -1)], axis=-1).reshape(rank_total, 3)
    counts = count_grid.reshape(rank_total)
    scores = jax.random.randint(keys[4], (rank_total, levels), 0, 1 << 20, dtype=jnp.int32) * levels + jnp.arange(levels, dtype=jnp.int32)[None, :]
    order = jnp.argsort(scores, axis=1).astype(jnp.int32)[:, :SLOTS]
    live_slot = jnp.arange(SLOTS, dtype=jnp.int32)[None, :] < counts[:, None]
    level = jnp.where(live_slot, order, -1)
    lookup = jnp.sum((level[:, :, None] == jnp.arange(levels, dtype=jnp.int32)[None, None, :]).astype(jnp.int32) * (jnp.arange(SLOTS, dtype=jnp.int32)[None, :, None] + 1), axis=1) - 1
    rank_curve = (jnp.arange(rank_total, dtype=jnp.int32) // cross_len)[:, None]
    rank_cross = (jnp.arange(rank_total, dtype=jnp.int32) % cross_len)[:, None]
    columns = []
    for direction in range(1, 19):
        offset = VELOCITY[direction]
        other_curve = rank_curve + offset[0]
        other_cross = rank_cross + offset[1]
        other_level = level + offset[2]
        inside = (other_curve >= 0) & (other_curve < curve_len) & (other_cross >= 0) & (other_cross < cross_len)
        inside = inside & (level >= 0) & (other_level >= 0) & (other_level < levels)
        other_rank = jnp.clip(other_curve, 0, curve_len - 1) * cross_len + jnp.clip(other_cross, 0, cross_len - 1)
        slot_there = lookup[other_rank, jnp.clip(other_level, 0, levels - 1)]
        found = inside & (slot_there >= 0)
        columns.append(jnp.where(found, other_rank * SLOTS + slot_there, -1))
    neighbours = jnp.stack(columns, axis=-1).reshape(rank_total * SLOTS, 18)
    codes, places = region_codes()
    live_flat = live_slot.reshape(rank_total * SLOTS, 1)
    present = jnp.concatenate([live_flat, neighbours >= 0, jnp.zeros_like(live_flat)], axis=1)
    region_ok = present[:, jnp.asarray(codes)]
    block_curve = jnp.repeat(rank_curve, SLOTS, axis=0)
    block_cross = jnp.repeat(rank_cross, SLOTS, axis=0)
    block_level = level.reshape(rank_total * SLOTS, 1)
    global_x = block_curve * EDGE + jnp.asarray(places[0], jnp.int32)[None, :]
    global_y = block_cross * EDGE + jnp.asarray(places[1], jnp.int32)[None, :]
    global_z = block_level * EDGE + jnp.asarray(places[2], jnp.int32)[None, :]
    factors = jax.random.randint(keys[5], (3,), 1, 1 << 20, dtype=jnp.int32)
    mixed = global_x * factors[0] + global_y * factors[1] + global_z * factors[2]
    mixed = mixed ^ mixed >> 13
    mixed = mixed * 1540483477
    mixed = mixed ^ mixed >> 15
    open_site = mixed & 7 != 0
    site_flags = (region_ok & open_site).astype(jnp.int32)
    return (counts, migrations, neighbours, site_flags)


def draw_counts(key, part):
    shared = plan_layout(key)
    key = jax.random.fold_in(key, 21)
    return shared[0]


def draw_migrations(key, part):
    shared = plan_layout(key)
    key = jax.random.fold_in(key, 22)
    return shared[1]


def draw_neighbours(key, part):
    shared = plan_layout(key)
    key = jax.random.fold_in(key, 23)
    return shared[2]


def draw_site_flags(key, part):
    shared = plan_layout(key)
    key = jax.random.fold_in(key, 24)
    return shared[3]


def draw_populations(key, part):
    key = jax.random.fold_in(key, 11)
    block_total = SLOTS * N_CURVE * N_CROSS
    sites = EDGE ** 3
    keys = jax.random.split(key, 4)
    density = jax.random.uniform(keys[0], (block_total, 1, sites), jnp.float32, 0.9, 1.1)
    velocity = jax.random.uniform(keys[1], (block_total, 3, sites), jnp.float32, -0.05, 0.05)
    spread = 0.25
    noise = jax.random.uniform(keys[2], (block_total, 19, sites), jnp.float32, -spread, spread)
    along = jnp.stack([VELOCITY[pop_index][0] * velocity[:, 0] + VELOCITY[pop_index][1] * velocity[:, 1] + VELOCITY[pop_index][2] * velocity[:, 2] for pop_index in range(19)], axis=1)
    square_speed = jnp.sum(velocity * velocity, axis=1)
    return density * (1.0 + 3.0 * along + 4.5 * along * along - 1.5 * square_speed[:, None, :]) + noise


def setup_inputs(seed: int = 0) -> dict:
    splits = jax.random.split(jax.random.key(seed), 6)
    populations = draw_populations(jax.random.fold_in(splits[5], 71), 0)
    site_flags = draw_site_flags(jax.random.fold_in(splits[5], 71), 0)
    neighbours = draw_neighbours(jax.random.fold_in(splits[5], 71), 0)
    migrations = draw_migrations(jax.random.fold_in(splits[5], 71), 0)
    counts = draw_counts(jax.random.fold_in(splits[5], 71), 0)
    return {"populations": populations, "site_flags": site_flags, "neighbours": neighbours, "migrations": migrations, "counts": counts}


VELOCITY = [(0, 0, 0), (1, 0, 0), (-1, 0, 0), (0, 1, 0), (0, -1, 0), (0, 0, 1), (0, 0, -1), (1, 1, 0), (-1, -1, 0), (1, -1, 0), (-1, 1, 0), (1, 0, 1), (-1, 0, -1), (1, 0, -1), (-1, 0, 1), (0, 1, 1), (0, -1, -1), (0, 1, -1), (0, -1, 1)]
OPPOSITE = [0, 2, 1, 4, 3, 6, 5, 8, 7, 10, 9, 12, 11, 14, 13, 16, 15, 18, 17]
WEIGHTS = [1.0 / 3.0] + [1.0 / 18.0] * 6 + [1.0 / 36.0] * 12


def relaxation_table():
    velocity_f = np.array(VELOCITY, dtype=np.float32)
    comp_x = velocity_f[:, 0]
    comp_y = velocity_f[:, 1]
    comp_z = velocity_f[:, 2]
    squared = comp_x * comp_x + comp_y * comp_y + comp_z * comp_z
    moment_rows = [np.ones(19, dtype=np.float32), 19.0 * squared - 30.0, (21.0 * squared * squared - 53.0 * squared + 24.0) / 2.0,
                   comp_x, (5.0 * squared - 9.0) * comp_x, comp_y, (5.0 * squared - 9.0) * comp_y,
                   comp_z, (5.0 * squared - 9.0) * comp_z, 3.0 * comp_x * comp_x - squared,
                   (3.0 * squared - 5.0) * (3.0 * comp_x * comp_x - squared), comp_y * comp_y - comp_z * comp_z,
                   (3.0 * squared - 5.0) * (comp_y * comp_y - comp_z * comp_z), comp_x * comp_y, comp_y * comp_z,
                   comp_x * comp_z, (comp_y * comp_y - comp_z * comp_z) * comp_x,
                   (comp_z * comp_z - comp_x * comp_x) * comp_y, (comp_x * comp_x - comp_y * comp_y) * comp_z]
    moments = np.stack(moment_rows).astype(np.float32)
    shear_rate = 1.0 / 0.6
    relax_rates = np.array([0.0, 1.19, 1.4, 0.0, 1.2, 0.0, 1.2, 0.0, 1.2, shear_rate, 1.4, shear_rate, 1.4,
                            shear_rate, shear_rate, shear_rate, 1.98, 1.98, 1.98], dtype=np.float32)
    row_norms = np.sum(moments * moments, axis=1)
    scaled = (relax_rates / row_norms)[:, None] * moments
    plain = moments.T @ scaled
    weights_f = np.array(WEIGHTS, dtype=np.float32)
    return (plain * (weights_f[None, :] / weights_f[:, None])).astype(np.float32)


def collide_sites(current, fluid_flat, relax_table):
    highest = lax.Precision.HIGHEST
    velocity_f = jnp.asarray(np.array(VELOCITY, dtype=np.float32))
    weighted_velocity = jnp.asarray(np.array(VELOCITY, dtype=np.float32) * np.array(WEIGHTS, dtype=np.float32)[:, None])
    weight_row = jnp.asarray(np.array(WEIGHTS, dtype=np.float32))
    density = jnp.einsum("i,bis->bs", weight_row, current, precision=highest)
    safe_density = jnp.where(fluid_flat, density, 1.0)
    momentum = jnp.einsum("iq,bis->bqs", weighted_velocity, current, precision=highest)
    speed = momentum / safe_density[:, None, :]
    along = jnp.einsum("iq,bqs->bis", velocity_f, speed, precision=highest)
    square_speed = jnp.sum(speed * speed, axis=1)
    balance = density[:, None, :] * (1.0 + 3.0 * along + 4.5 * along * along - 1.5 * square_speed[:, None, :])
    relaxed = current - jnp.einsum("ij,bjs->bis", relax_table, current - balance, precision=highest)
    return jnp.where(fluid_flat[:, None, :], relaxed, 0.0)


def leading_axis(direction):
    offset = VELOCITY[direction]
    for axis_index in range(3):
        if offset[axis_index] != 0:
            return axis_index, offset[axis_index]
    return 0, 0


def source_face(direction):
    axis_index, sign_value = leading_axis(direction)
    return 2 * axis_index + (1 if sign_value > 0 else 0)


def face_exports(cube_data):
    faces_out = []
    for face_index in range(6):
        axis_index = face_index // 2
        side = 1 - 2 * (face_index % 2)
        chosen_pops = [pop_index for pop_index in range(19) if VELOCITY[pop_index][axis_index] == side]
        boundary = EDGE - 1 if side > 0 else 0
        picked = jnp.stack([cube_data[:, pop_index] for pop_index in chosen_pops], axis=1)
        faces_out.append(jnp.take(picked, boundary, axis=2 + axis_index))
    return jnp.stack(faces_out, axis=1)


def edge_line(exported, direction):
    offset = VELOCITY[direction]
    nonzero = [axis_index for axis_index in range(3) if offset[axis_index] != 0]
    first_axis = nonzero[0]
    second_axis = nonzero[1]
    chosen_pops = [pop_index for pop_index in range(19) if VELOCITY[pop_index][first_axis] == -offset[first_axis]]
    position = chosen_pops.index(OPPOSITE[direction])
    boundary = 0 if offset[second_axis] > 0 else EDGE - 1
    remaining = [axis_index for axis_index in range(3) if axis_index != first_axis]
    if remaining[0] == second_axis:
        return exported[..., position, boundary, :]
    return exported[..., position, :, boundary]


def fill_and_stream(cube_data, ghost_faces, ghost_lines, padded_fluid, live_fluid):
    padded = jnp.pad(cube_data, ((0, 0), (0, 0), (1, 1), (1, 1), (1, 1)))
    inner = slice(1, EDGE + 1)
    for direction in range(1, 7):
        offset = VELOCITY[direction]
        axis_index = (direction - 1) // 2
        chosen_pops = [pop_index for pop_index in range(19) if VELOCITY[pop_index][axis_index] == -offset[axis_index]]
        for position, pop_index in enumerate(chosen_pops):
            spot = [inner, inner, inner]
            spot[axis_index] = EDGE + 1 if offset[axis_index] > 0 else 0
            padded = padded.at[(slice(None), pop_index) + tuple(spot)].set(ghost_faces[:, direction - 1, position])
    for direction in range(7, 19):
        offset = VELOCITY[direction]
        spot = [inner, inner, inner]
        for axis_index in range(3):
            if offset[axis_index] != 0:
                spot[axis_index] = EDGE + 1 if offset[axis_index] > 0 else 0
        padded = padded.at[(slice(None), OPPOSITE[direction]) + tuple(spot)].set(ghost_lines[:, direction - 7])
    read = []
    for pop_index in range(19):
        offset = VELOCITY[pop_index]
        window = tuple(slice(1 - offset[axis_index], 1 - offset[axis_index] + EDGE) for axis_index in range(3))
        arriving = padded[(slice(None), pop_index) + window]
        blocked = jnp.logical_not(padded_fluid[(slice(None),) + window])
        read.append(jnp.where(blocked, cube_data[:, OPPOSITE[pop_index]], arriving))
    result = jnp.stack(read, axis=1)
    return jnp.where(live_fluid[:, None], result, 0.0)


def reference(populations, site_flags, neighbours, migrations, counts):
    block_total = populations.shape[0]
    rank_total = migrations.shape[0]
    slot_count = block_total // rank_total
    relax_table = jnp.asarray(relaxation_table())
    send_slot = migrations[:, 0]
    sending = send_slot >= 0
    anchor = jnp.arange(rank_total, dtype=jnp.int32) * slot_count + jnp.maximum(send_slot, 0)
    target = jnp.where(sending, migrations[:, 1] * slot_count + migrations[:, 2], block_total)
    current = populations.at[target].set(populations[anchor], mode="drop")
    live_slot = (jnp.arange(block_total, dtype=jnp.int32) % slot_count) < jnp.repeat(counts, slot_count)
    padded_fluid = site_flags.reshape(block_total, EDGE + 2, EDGE + 2, EDGE + 2) > 0
    live_fluid = padded_fluid[:, 1:-1, 1:-1, 1:-1] & live_slot[:, None, None, None]
    fluid_flat = live_fluid.reshape(block_total, EDGE ** 3)
    for step_number in range(STEPS):
        relaxed = collide_sites(current, fluid_flat, relax_table)
        cube_all = relaxed.reshape(block_total, 19, EDGE, EDGE, EDGE)

        def one_block(block_item):
            block_index, neighbour_row, fluid_padded, fluid_live = block_item
            face_list = []
            line_list = []
            for direction in range(1, 19):
                named = neighbour_row[direction - 1]
                neighbour_cube = cube_all[jnp.maximum(named, 0)]
                neighbour_cube = jnp.where(named >= 0, neighbour_cube, 0.0)
                exported = face_exports(neighbour_cube[None])[0, source_face(direction)]
                if direction <= 6:
                    face_list.append(exported)
                else:
                    line_list.append(edge_line(exported, direction))
            own_cube = lax.dynamic_index_in_dim(cube_all, block_index, 0, keepdims=True)
            ghost_faces = jnp.stack(face_list, axis=0)[None]
            ghost_lines = jnp.stack(line_list, axis=0)[None]
            return fill_and_stream(own_cube, ghost_faces, ghost_lines, fluid_padded[None], fluid_live[None])[0]

        stepped = lax.map(one_block, (jnp.arange(block_total, dtype=jnp.int32), neighbours, padded_fluid, live_fluid))
        current = stepped.reshape(block_total, 19, EDGE ** 3)
    return current
```

```python
import functools

import jax
import jax.numpy as jnp
import numpy as np
from jax import lax
from jax.experimental import pallas as pl
from jax.experimental.pallas import tpu as pltpu
from jax.sharding import PartitionSpec as P

EDGE = 16
STEPS = 3
SLOTS = 3
POPS = 19
PLANES = SLOTS * POPS + SLOTS
FLAG0 = SLOTS * POPS
GROUP = 24
PLANE = 4 * GROUP
SLOT = POPS * PLANE
STRIP = 6 * PLANES
HALF = POPS * EDGE
PAIRS = PLANES // 2
LIMIT = 48 * 1024 * 1024

VELOCITY = [
    (0, 0, 0),
    (1, 0, 0),
    (-1, 0, 0),
    (0, 1, 0),
    (0, -1, 0),
    (0, 0, 1),
    (0, 0, -1),
    (1, 1, 0),
    (-1, -1, 0),
    (1, -1, 0),
    (-1, 1, 0),
    (1, 0, 1),
    (-1, 0, -1),
    (1, 0, -1),
    (-1, 0, 1),
    (0, 1, 1),
    (0, -1, -1),
    (0, 1, -1),
    (0, -1, 1),
]
OPPOSITE = [0, 2, 1, 4, 3, 6, 5, 8, 7, 10, 9, 12, 11, 14, 13, 16, 15, 18, 17]


def lanes_iota():
    return lax.broadcasted_iota(jnp.int32, (8, 128), 1)


def rows_iota():
    return lax.broadcasted_iota(jnp.int32, (8, 128), 0)


def aligned(start, size=8):
    return pl.ds(pl.multiple_of(start, 8), size)


def move_slots(moves, where, curve_size, cross_size):
    curve, cross = where[0], where[1]

    def landed(source, target):
        inside = (source >= 0) & (source < curve_size) & (target >= 0) & (target < curve_size)
        row = jnp.clip(source, 0, curve_size - 1) * cross_size + cross
        rank = target * cross_size + cross
        hit = inside & (moves[row * 3] >= 0) & (moves[row * 3 + 1] == rank)
        return jnp.where(hit, moves[row * 3 + 2], -1)

    here = curve * cross_size + cross
    return (
        landed(curve - 1, curve),
        landed(curve + 1, curve),
        landed(curve - 2, curve - 1),
        landed(curve, curve - 1),
        landed(curve + 2, curve + 1),
        landed(curve, curve + 1),
        jnp.maximum(moves[here * 3], 0),
    )


def pack_kernel(
    curve_size,
    cross_size,
    moves,
    where,
    counts,
    pops,
    flags,
    cells,
    up_msg,
    down_msg,
    up2_msg,
    down2_msg,
    inner_msg,
    wide_flags,
    plane_flags,
    site_flags,
):
    wide_flags[...] = jnp.zeros_like(wide_flags)
    wide_flags[0:SLOTS, 0 : flags.shape[1]] = flags[...].astype(jnp.float32)
    span = EDGE + 2
    for x in range(EDGE):
        start = (x + 1) * span * span
        base = start // 128 * 128
        window = wide_flags[:, base : base + 512]
        window = pltpu.roll(window, (512 - (start - base)) % 512, axis=1)
        plane_flags[8 * x : 8 * x + 8, :] = window[:, :384].astype(jnp.bfloat16)
    lane_in = lax.broadcasted_iota(jnp.int32, (384, 256), 0)
    site = lax.broadcasted_iota(jnp.int32, (384, 256), 1)
    chosen = lane_in == (site // EDGE + 1) * span + site % EDGE + 1
    product = jnp.dot(
        plane_flags[...],
        jnp.where(chosen, 1.0, 0.0).astype(jnp.bfloat16),
        preferred_element_type=jnp.float32,
    )
    site_flags[0:128, :] = product[:, :128]
    site_flags[128:256, :] = product[:, 128:]
    for s in range(SLOTS):
        live = s < counts[0]
        for y in range(2):
            piece = site_flags[pl.ds(128 * y + s, EDGE, stride=8), :]
            is_fluid = (piece == 1.0) & live
            row = (FLAG0 + s) * 32 + y * EDGE
            cells[row : row + EDGE, :] = jnp.where(is_fluid, 1.0, 0.0)

    for s in range(SLOTS):
        for x in range(EDGE):
            for y in range(2):
                tile = 2 * x + y
                for p, size in ((0, 8), (8, 8), (16, 3)):
                    row = (s * POPS + p) * 32 + y * EDGE + x
                    cells[pl.ds(row, size, stride=32), :] = pops[
                        s, p : p + size, 128 * tile : 128 * tile + 128
                    ]

    for y in range(2):
        for k in range(3):
            out = (y * 3 + k) * PLANES
            up_msg[out : out + PLANES, :] = cells[pl.ds(y * EDGE + 13 + k, PLANES, stride=32), :]
            down_msg[out : out + PLANES, :] = cells[pl.ds(y * EDGE + k, PLANES, stride=32), :]

    curve, cross = where[0], where[1]
    leaving = jnp.maximum(moves[(curve * cross_size + cross) * 3], 0)
    low = lanes_iota() < 64
    for p in range(POPS):
        for v in range(2):
            base = leaving * (POPS * 32) + p * 32 + v * 8
            first = cells[aligned(base), :]
            second = cells[aligned(base + EDGE), :]
            outer = jnp.where(low, first, second)
            row = p * EDGE + v * 8
            up_msg[STRIP + row : STRIP + row + 8, :] = outer
            down_msg[STRIP + row : STRIP + row + 8, :] = outer
            inner_msg[row : row + 8, :] = jnp.where(low, second, first)
    for s in range(SLOTS):

        @pl.when(leaving == s)
        def _():
            for y in range(2):
                for k in range(3):
                    out = (y * 3 + k) * GROUP
                    row = s * POPS * 32 + y * EDGE + k
                    up2_msg[out : out + POPS, :] = cells[pl.ds(row + 13, POPS, stride=32), :]
                    down2_msg[out : out + POPS, :] = cells[pl.ds(row, POPS, stride=32), :]


def own_strip(cells, slot, y, x):
    return cells[pl.ds(slot * POPS * 32 + y * EDGE + x, POPS, stride=32), :]


def edge_kernel(
    curve_size,
    cross_size,
    moves,
    where,
    cells,
    low_msg,
    high_msg,
    low2_msg,
    high2_msg,
    north_msg,
    south_msg,
    outer,
):
    from_low, from_high, low_low, low_me, high_high, high_me, leaving = move_slots(
        moves, where, curve_size, cross_size
    )
    low = lanes_iota() < 64
    for q in range(PLANES):
        for v in range(2):
            first = cells[q * 32 + v * 8 : q * 32 + v * 8 + 8, :]
            second = cells[q * 32 + EDGE + v * 8 : q * 32 + EDGE + v * 8 + 8, :]
            outer[q * GROUP + v * 8 : q * GROUP + v * 8 + 8, :] = jnp.where(low, first, second)

    def both(first, second):
        lane = lax.broadcasted_iota(jnp.int32, first.shape, 1)
        return jnp.where(lane < 64, first, second)

    for msg, row0 in ((high_msg, 16), (low_msg, 21)):
        for k in range(3):
            outer[pl.ds(row0 + k, PLANES, stride=GROUP), :] = both(
                msg[k * PLANES : (k + 1) * PLANES, :],
                msg[(3 + k) * PLANES : (4 + k) * PLANES, :],
            )
    for slot, msg in ((from_low, low_msg), (from_high, high_msg)):

        @pl.when(slot >= 0)
        def _():
            for p in range(POPS):
                for v in range(2):
                    row = STRIP + p * EDGE + v * 8
                    base = slot * (POPS * GROUP) + p * GROUP + v * 8
                    outer[aligned(base), :] = msg[row : row + 8, :]

    for s in range(SLOTS):
        for slot, msg, row0 in ((low_low, low2_msg, 21), (high_high, high2_msg, 16)):

            @pl.when(slot == s)
            def _():
                for k in range(3):
                    outer[pl.ds(s * POPS * GROUP + row0 + k, POPS, stride=GROUP), :] = both(
                        msg[k * GROUP : k * GROUP + POPS, :],
                        msg[(3 + k) * GROUP : (3 + k) * GROUP + POPS, :],
                    )

        for mine in range(SLOTS):
            for slot, x0, row0 in ((low_me, 13, 21), (high_me, 0, 16)):

                @pl.when((slot == s) & (leaving == mine))
                def _():
                    for k in range(3):
                        outer[pl.ds(s * POPS * GROUP + row0 + k, POPS, stride=GROUP), :] = both(
                            own_strip(cells, mine, 0, x0 + k), own_strip(cells, mine, 1, x0 + k)
                        )

    for pair in range(PAIRS):
        for v in range(3):
            row = 2 * pair * GROUP + v * 8
            first = outer[row : row + 8, :]
            second = pltpu.roll(outer[row + GROUP : row + GROUP + 8, :], 64, axis=1)
            out = pair * GROUP + v * 8
            north_msg[out : out + 8, :] = jnp.where(low, second, first)
            south_msg[out : out + 8, :] = jnp.where(low, first, second)


def collided(h, is_fluid):
    shear = 1.0 / 0.6
    rest = h[0]
    sx, dx = h[1] + h[2], h[1] - h[2]
    sy, dy = h[3] + h[4], h[3] - h[4]
    sz, dz = h[5] + h[6], h[5] - h[6]
    s7, d7 = h[7] + h[8], h[7] - h[8]
    s9, d9 = h[9] + h[10], h[9] - h[10]
    s11, d11 = h[11] + h[12], h[11] - h[12]
    s13, d13 = h[13] + h[14], h[13] - h[14]
    s15, d15 = h[15] + h[16], h[15] - h[16]
    s17, d17 = h[17] + h[18], h[17] - h[18]
    txy, txz, tyz = s7 + s9, s11 + s13, s15 + s17
    pxy, pxz, pyz = s7 - s9, s11 - s13, s15 - s17
    ax, bx = d7 + d9, d11 + d13
    ay, by = d7 - d9, d15 + d17
    az, bz = d11 - d13, d15 - d17
    axes = sx + sy + sz
    diags = txy + txz + tyz
    rho = rest * (1.0 / 3.0) + axes * (1.0 / 18.0) + diags * (1.0 / 36.0)
    fx, fy, fz = ax + bx, ay + by, az + bz
    jx = dx * (1.0 / 18.0) + fx * (1.0 / 36.0)
    jy = dy * (1.0 / 18.0) + fy * (1.0 / 36.0)
    jz = dz * (1.0 / 18.0) + fz * (1.0 / 36.0)
    inverse = 1.0 / jnp.where(is_fluid, rho, 1.0)
    ux, uy, uz = jx * inverse, jy * inverse, jz * inverse
    qxx, qyy, qzz = jx * ux, jy * uy, jz * uz
    total = qxx + qyy + qzz

    energy = -10.0 * rest - axes * (11.0 / 18.0) + diags * (8.0 / 36.0)
    energy = (energy + 11.0 * rho - 19.0 * total) * (1.19 / 2394.0)
    square = 4.0 * rest - axes * (4.0 / 18.0) + diags * (1.0 / 36.0)
    square = (square - 3.0 * rho + 5.5 * total) * (1.4 / 252.0)
    axis_x = (3.0 * sx - axes) * (1.0 / 18.0)
    diag_x = (diags - 3.0 * tyz) * (1.0 / 36.0)
    want_x = 3.0 * qxx - total
    stress_x = (axis_x + diag_x - want_x) * (shear / 36.0)
    third_x = (diag_x - 2.0 * axis_x + 0.5 * want_x) * (1.4 / 72.0)
    axis_w = (sy - sz) * (1.0 / 18.0)
    diag_w = (txy - txz) * (1.0 / 36.0)
    want_w = qyy - qzz
    stress_w = (axis_w + diag_w - want_w) * (shear / 12.0)
    third_w = (diag_w - 2.0 * axis_w + 0.5 * want_w) * (1.4 / 24.0)

    rest_out = rest - 3.0 * (12.0 * square - 30.0 * energy)
    common = -18.0 * (11.0 * energy + 4.0 * square)
    along_x = 18.0 * (stress_x - 2.0 * third_x)
    along_w = 18.0 * (stress_w - 2.0 * third_w)
    ex = common + 2.0 * along_x
    ey = common - along_x + along_w
    ez = common - along_x - along_w
    common = 36.0 * (8.0 * energy + square)
    across_x = 36.0 * (stress_x + third_x)
    across_w = 36.0 * (stress_w + third_w)
    exy = common + across_x + across_w
    exz = common + across_x - across_w
    eyz = common - 2.0 * across_x
    cxy = shear * (0.25 * pxy - 9.0 * jx * uy)
    cxz = shear * (0.25 * pxz - 9.0 * jx * uz)
    cyz = shear * (0.25 * pyz - 9.0 * jy * uz)

    def flux(d, f, j):
        return (f * (1.0 / 36.0) - d * (4.0 / 18.0) + j * (2.0 / 3.0)) * (1.2 / 40.0)

    hx, hy, hz = flux(dx, fx, jx), flux(dy, fy, jy), flux(dz, fz, jz)
    mx = (ax - bx) * (1.98 / 8.0)
    my = (by - ay) * (1.98 / 8.0)
    mz = (az - bz) * (1.98 / 8.0)
    hx36, hy36, hz36 = 36.0 * hx, 36.0 * hy, 36.0 * hz
    xy_x, xz_x = hx36 + mx, hx36 - mx
    yz_y, xy_y = hy36 + my, hy36 - my
    xz_z, yz_z = hz36 + mz, hz36 - mz
    ox, oy, oz = -2.0 * hx36, -2.0 * hy36, -2.0 * hz36

    out = [rest_out]

    def pair(i, even, odd):
        out.append(h[i] - (even + odd))
        out.append(h[i + 1] - (even - odd))

    pair(1, ex, ox)
    pair(3, ey, oy)
    pair(5, ez, oz)
    pair(7, exy + cxy, xy_x + xy_y)
    pair(9, exy - cxy, xy_x - xy_y)
    pair(11, exz + cxz, xz_x + xz_z)
    pair(13, exz - cxz, xz_x - xz_z)
    pair(15, eyz + cyz, yz_y + yz_z)
    pair(17, eyz - cyz, yz_y - yz_z)
    return out


def collide_all(h_ref, post_ref, fluid):
    def chunk(s, c):
        base = s * SLOT + c * 8
        is_fluid = fluid[aligned(s * PLANE + c * 8), :] > 0.0
        h = [h_ref[aligned(base + p * PLANE), :] for p in range(POPS)]
        for p, value in enumerate(collided(h, is_fluid)):
            post_ref[aligned(base + p * PLANE), :] = jnp.where(is_fluid, value, jnp.nan)

    @pl.loop(0, SLOTS)
    def _(s):
        @pl.loop(0, PLANE // 8)
        def _(c):
            chunk(s, c)


def stream_all(post_ref, h_ref, fluid, table, groups, vregs):
    lane = lanes_iota()
    row = rows_iota()
    side = {0: -1, 1: 0, 2: 0, 3: 1}

    def one_slot(s):
        own = s * SLOT

        def look(i, j, offset):
            if offset == (0, 0, 0):
                return own
            region = (i + 1) * 3 + j + 1
            return table[(region * SLOTS + s) * 18 + VELOCITY.index(offset) - 1]

        def shifted(pop, group, j, dy, dz):
            cx = VELOCITY[pop][0]

            def rows(start, v):
                return post_ref[aligned(start + pop * PLANE + group * GROUP + v * 8), :]

            inner = look(0, j, (0, dy, dz))
            need_last = vregs == 3
            values = [rows(inner, 0), rows(inner, 1)]
            if need_last:
                if dy == 0 and dz == 0:
                    values.append(rows(inner, 2))
                else:
                    values.append(
                        jnp.where(
                            row < 4,
                            rows(look(1, j, (0, dy, dz)), 2),
                            rows(look(-1, j, (0, dy, dz)), 2),
                        )
                    )
            if cx == 0:
                return values
            turn = 1 if cx > 0 else 7
            rolled = [pltpu.roll(value, turn, axis=0) for value in values]
            if cx > 0:
                before = pltpu.roll(rows(look(0, j, (-1, dy, dz)), 2), 1, axis=0)
                result = [
                    jnp.where(row == 0, before, rolled[0]),
                    jnp.where(row == 0, rolled[0], rolled[1]),
                ]
                if need_last:
                    edge = pltpu.roll(rows(look(1, j, (-1, dy, dz)), 1), 1, axis=0)
                    result.append(jnp.where(row == 0, edge, rolled[2]))
                return result
            after = pltpu.roll(rows(look(0, j, (1, dy, dz)), 2), 7, axis=0)
            result = [
                jnp.where(row == 7, rolled[1], rolled[0]),
                jnp.where(row == 7, after, rolled[1]),
            ]
            if need_last:
                edge = pltpu.roll(rows(look(-1, j, (1, dy, dz)), 0), 7, axis=0)
                result.append(jnp.where(row == 7, edge, rolled[2]))
            return result

        for pop in range(POPS):
            cx, cy, cz = VELOCITY[pop]
            kept = {}

            def source(group, j, dy, dz):
                key = (group, j, dy, dz)
                if key not in kept:
                    kept[key] = shifted(pop, group, j, dy, dz)
                return kept[key]

            def along_y(group, dz):
                j = side[group]
                values = source(group, j, 0, dz)
                other = group - cy
                if cy == 0 or other < 0 or other > 3:
                    return values
                dy = 0 if side[other] == j else -cy
                carried = source(other, j, dy, dz)
                mask = lane >= 112 if cy > 0 else lane < 16
                return [jnp.where(mask, b, a) for a, b in zip(values, carried)]

            for group in groups:
                values = along_y(group, 0)
                turn = (16 * cy + cz) % 128
                if turn:
                    values = [pltpu.roll(value, turn, axis=1) for value in values]
                if cz:
                    turn = (16 * cy - 15 * cz) % 128
                    wrapped = [pltpu.roll(value, turn, axis=1) for value in along_y(group, -cz)]
                    mask = lane % 16 == (0 if cz > 0 else 15)
                    values = [jnp.where(mask, b, a) for a, b in zip(values, wrapped)]
                for v, value in enumerate(values[:vregs]):
                    place = group * GROUP + v * 8
                    if pop:
                        back = post_ref[aligned(own + OPPOSITE[pop] * PLANE + place), :]
                        value = jnp.where(value != value, back, value)
                    is_fluid = fluid[aligned(s * PLANE + place), :] > 0.0
                    h_ref[aligned(own + pop * PLANE + place), :] = jnp.where(is_fluid, value, 0.0)

    @pl.loop(0, SLOTS)
    def _(s):
        one_slot(s)


def steps_kernel(
    curve_size,
    cross_size,
    moves,
    where,
    table,
    cells,
    low_msg,
    high_msg,
    low2_msg,
    high2_msg,
    low_inner,
    high_inner,
    south_msg,
    north_msg,
    out,
    h_ref,
    post_ref,
    fluid,
):
    from_low, from_high, low_low, low_me, high_high, high_me, leaving = move_slots(
        moves, where, curve_size, cross_size
    )
    low = lanes_iota() < 64
    fluid[...] = jnp.zeros_like(fluid)
    post_ref[SLOTS * SLOT :, :] = jnp.full((SLOT, 128), jnp.nan, jnp.float32)

    def home(q):
        if q < FLAG0:
            return h_ref, q * PLANE
        return fluid, (q - FLAG0) * PLANE

    for q in range(PLANES):
        ref, base = home(q)
        for y in range(2):
            start = base + (1 + y) * GROUP
            ref[start : start + EDGE, :] = cells[q * 32 + y * EDGE : q * 32 + (y + 1) * EDGE, :]
    for slot, msg, inner in (
        (from_low, low_msg, low_inner),
        (from_high, high_msg, high_inner),
    ):

        @pl.when(slot >= 0)
        def _():
            for p in range(POPS):
                for v in range(2):
                    row = p * EDGE + v * 8
                    outside = msg[STRIP + row : STRIP + row + 8, :]
                    inside = inner[row : row + 8, :]
                    start = slot * SLOT + p * PLANE + GROUP + v * 8
                    h_ref[aligned(start), :] = jnp.where(low, outside, inside)
                    h_ref[aligned(start + GROUP), :] = jnp.where(low, inside, outside)

    for msg, row0 in ((high_msg, 16), (low_msg, 21)):
        for y in range(2):
            for k in range(3):
                row = (1 + y) * GROUP + row0 + k
                source = (y * 3 + k) * PLANES
                h_ref[pl.ds(row, FLAG0, stride=PLANE), :] = msg[source : source + FLAG0, :]
                fluid[pl.ds(row, SLOTS, stride=PLANE), :] = msg[source + FLAG0 : source + PLANES, :]
    for s in range(SLOTS):
        for slot, msg, row0 in ((low_low, low2_msg, 21), (high_high, high2_msg, 16)):

            @pl.when(slot == s)
            def _():
                for y in range(2):
                    for k in range(3):
                        row = s * SLOT + (1 + y) * GROUP + row0 + k
                        source = (y * 3 + k) * GROUP
                        h_ref[pl.ds(row, POPS, stride=PLANE), :] = msg[source : source + POPS, :]

        for mine in range(SLOTS):
            for slot, x0, row0 in ((low_me, 13, 21), (high_me, 0, 16)):

                @pl.when((slot == s) & (leaving == mine))
                def _():
                    for y in range(2):
                        for k in range(3):
                            row = s * SLOT + (1 + y) * GROUP + row0 + k
                            h_ref[pl.ds(row, POPS, stride=PLANE), :] = own_strip(
                                cells, mine, y, x0 + k
                            )

    for msg, group in ((south_msg, 0), (north_msg, 3)):
        for pair in range(PAIRS):
            for v in range(3):
                value = msg[pair * GROUP + v * 8 : pair * GROUP + v * 8 + 8, :]
                ref, base = home(2 * pair)
                row = base + group * GROUP + v * 8
                ref[row : row + 8, :] = value
                ref, base = home(2 * pair + 1)
                row = base + group * GROUP + v * 8
                ref[row : row + 8, :] = pltpu.roll(value, 64, axis=1)

    for step in range(STEPS):
        collide_all(h_ref, post_ref, fluid)
        if step < STEPS - 1:
            stream_all(post_ref, h_ref, fluid, table, (0, 1, 2, 3), 3)
        else:
            stream_all(post_ref, h_ref, fluid, table, (1, 2), 2)

    for s in range(SLOTS):
        for x in range(EDGE):
            for y in range(2):
                tile = 2 * x + y
                for p, size in ((0, 8), (8, 8), (16, 3)):
                    row = s * SLOT + p * PLANE + (1 + y) * GROUP + x
                    out[s, p : p + size, 128 * tile : 128 * tile + 128] = h_ref[
                        pl.ds(row, size, stride=PLANE), :
                    ]


def shifted_from(value, axis, step):
    count = lax.axis_size(axis)
    pairs = [(i, i + step) for i in range(count) if 0 <= i + step < count]
    return lax.ppermute(value, axis, pairs)


def rows128(count):
    return jax.ShapeDtypeStruct((count, 128), jnp.float32)


def call(kernel, outs, ins, scratch):
    smem = pl.BlockSpec(memory_space=pltpu.SMEM)
    vmem = pl.BlockSpec(memory_space=pltpu.VMEM)
    return pl.pallas_call(
        kernel,
        out_shape=outs,
        in_specs=[smem if x.ndim == 1 else vmem for x in ins],
        out_specs=jax.tree.map(lambda _: vmem, outs),
        scratch_shapes=scratch,
        compiler_params=pltpu.CompilerParams(vmem_limit_bytes=LIMIT),
    )(*ins)


def per_device(populations, site_flags, neighbours, migrations, counts):
    curve_size = lax.axis_size("curve")
    cross_size = lax.axis_size("cross")
    curve = lax.axis_index("curve")
    cross = lax.axis_index("cross")
    where = jnp.stack([curve, cross]).astype(jnp.int32)
    moves = migrations.reshape(-1)

    everyone = lax.all_gather(neighbours, ("curve", "cross"), tiled=True)
    ranks = [
        jnp.clip(curve + i, 0, curve_size - 1) * cross_size + jnp.clip(cross + j, 0, cross_size - 1)
        for i in (-1, 0, 1)
        for j in (-1, 0, 1)
    ]
    near = jnp.concatenate(
        [lax.dynamic_slice_in_dim(everyone, rank * SLOTS, SLOTS, axis=0) for rank in ranks]
    )
    table = (jnp.where(near >= 0, near % SLOTS, SLOTS) * SLOT).reshape(-1)

    sizes = (curve_size, cross_size)
    cells, up_msg, down_msg, up2_msg, down2_msg, inner_msg = call(
        functools.partial(pack_kernel, *sizes),
        [
            rows128(PLANES * 32),
            rows128(STRIP + HALF),
            rows128(STRIP + HALF),
            rows128(6 * GROUP),
            rows128(6 * GROUP),
            rows128(HALF),
        ],
        (moves, where, counts, populations, site_flags),
        [
            pltpu.VMEM((8, 5888), jnp.float32),
            pltpu.VMEM((128, 384), jnp.bfloat16),
            pltpu.VMEM((256, 128), jnp.float32),
        ],
    )
    low_msg = shifted_from(up_msg, "curve", 1)
    high_msg = shifted_from(down_msg, "curve", -1)
    low2_msg = shifted_from(up2_msg, "curve", 2)
    high2_msg = shifted_from(down2_msg, "curve", -2)
    low_inner = shifted_from(inner_msg, "curve", 1)
    high_inner = shifted_from(inner_msg, "curve", -1)
    north_msg, south_msg = call(
        functools.partial(edge_kernel, *sizes),
        [rows128(PAIRS * GROUP), rows128(PAIRS * GROUP)],
        (moves, where, cells, low_msg, high_msg, low2_msg, high2_msg),
        [pltpu.VMEM((PLANES * GROUP, 128), jnp.float32)],
    )
    from_south = shifted_from(north_msg, "cross", 1)
    from_north = shifted_from(south_msg, "cross", -1)
    return call(
        functools.partial(steps_kernel, *sizes),
        jax.ShapeDtypeStruct(populations.shape, jnp.float32),
        (
            moves,
            where,
            table,
            cells,
            low_msg,
            high_msg,
            low2_msg,
            high2_msg,
            low_inner,
            high_inner,
            from_south,
            from_north,
        ),
        [
            pltpu.VMEM((SLOTS * SLOT, 128), jnp.float32),
            pltpu.VMEM(((SLOTS + 1) * SLOT, 128), jnp.float32),
            pltpu.VMEM((SLOTS * PLANE, 128), jnp.float32),
        ],
    )


def solution(mesh):
    return jax.shard_map(
        per_device,
        mesh=mesh,
        in_specs=(
            P(("curve", "cross"), None, None),
            P(("curve", "cross"), None),
            P(("curve", "cross"), None),
            P(),
            P(("curve", "cross")),
        ),
        out_specs=P(("curve", "cross"), None, None),
        check_vma=False,
    )
```

```python
import functools

import jax
import jax.numpy as jnp
import numpy as np
from jax import lax
from jax.experimental import pallas as pl
from jax.experimental.pallas import tpu as pltpu
from jax.sharding import PartitionSpec as P

EDGE = 16
STEPS = 3
SLOTS = 3
POPS = 19
PLANES = SLOTS * POPS + SLOTS
FLAG0 = SLOTS * POPS
GROUP = 24
PLANE = 4 * GROUP
SLOT = POPS * PLANE
STRIP = 6 * PLANES
HALF = POPS * EDGE
PAIRS = PLANES // 2
TABLE = STRIP + HALF
EDGE_TABLE = PAIRS * GROUP
LIMIT = 48 * 1024 * 1024

VELOCITY = [
    (0, 0, 0),
    (1, 0, 0),
    (-1, 0, 0),
    (0, 1, 0),
    (0, -1, 0),
    (0, 0, 1),
    (0, 0, -1),
    (1, 1, 0),
    (-1, -1, 0),
    (1, -1, 0),
    (-1, 1, 0),
    (1, 0, 1),
    (-1, 0, -1),
    (1, 0, -1),
    (-1, 0, 1),
    (0, 1, 1),
    (0, -1, -1),
    (0, 1, -1),
    (0, -1, 1),
]
OPPOSITE = [0, 2, 1, 4, 3, 6, 5, 8, 7, 10, 9, 12, 11, 14, 13, 16, 15, 18, 17]


def lanes_iota():
    return lax.broadcasted_iota(jnp.int32, (8, 128), 1)


def rows_iota():
    return lax.broadcasted_iota(jnp.int32, (8, 128), 0)


def aligned(start, size=8):
    return pl.ds(pl.multiple_of(start, 8), size)


def move_slots(moves, where, curve_size, cross_size):
    curve, cross = where[0], where[1]

    def landed(source, target):
        inside = (source >= 0) & (source < curve_size) & (target >= 0) & (target < curve_size)
        row = jnp.clip(source, 0, curve_size - 1) * cross_size + cross
        rank = target * cross_size + cross
        hit = inside & (moves[0, row] >= 0) & (moves[1, row] == rank)
        return jnp.where(hit, moves[2, row], -1)

    here = curve * cross_size + cross
    return (
        landed(curve - 1, curve),
        landed(curve + 1, curve),
        landed(curve - 2, curve - 1),
        landed(curve, curve - 1),
        landed(curve + 2, curve + 1),
        landed(curve, curve + 1),
        jnp.maximum(moves[0, here], 0),
    )


def pack_kernel(
    curve_size,
    cross_size,
    moves,
    where,
    counts,
    pops_hbm,
    flags_hbm,
    neighbours,
    cells,
    up_msg,
    down_msg,
    up2_msg,
    down2_msg,
    inner_msg,
    pops,
    flags,
    wide_flags,
    plane_flags,
    site_flags,
    near,
    sems,
):
    flags_copy = pltpu.make_async_copy(flags_hbm, flags, sems.at[SLOTS])
    flags_copy.start()
    copies = [
        pltpu.make_async_copy(pops_hbm.at[s], pops.at[s], sems.at[s]) for s in range(SLOTS)
    ]
    for copy in copies:
        copy.start()

    near[...] = jnp.zeros_like(near)
    named = neighbours[...]
    slot = jnp.where(named >= 0, lax.rem(jnp.maximum(named, 0), SLOTS), SLOTS)
    near[0:SLOTS, 0 : named.shape[1]] = slot.astype(jnp.float32)
    for ref, row in ((cells, PLANES * 32), (up_msg, TABLE), (down_msg, TABLE)):
        ref[row : row + 8, :] = near[...]

    wide_flags[...] = jnp.zeros_like(wide_flags)
    flags_copy.wait()
    wide_flags[0:SLOTS, 0 : flags.shape[1]] = flags[...].astype(jnp.float32)
    span = EDGE + 2
    for x in range(EDGE):
        start = (x + 1) * span * span
        base = start // 128 * 128
        window = wide_flags[:, base : base + 512]
        window = pltpu.roll(window, (512 - (start - base)) % 512, axis=1)
        plane_flags[8 * x : 8 * x + 8, :] = window[:, :384].astype(jnp.bfloat16)
    lane_in = lax.broadcasted_iota(jnp.int32, (384, 256), 0)
    site = lax.broadcasted_iota(jnp.int32, (384, 256), 1)
    chosen = lane_in == (site // EDGE + 1) * span + site % EDGE + 1
    product = jnp.dot(
        plane_flags[...],
        jnp.where(chosen, 1.0, 0.0).astype(jnp.bfloat16),
        preferred_element_type=jnp.float32,
    )
    site_flags[0:128, :] = product[:, :128]
    site_flags[128:256, :] = product[:, 128:]
    for s in range(SLOTS):
        live = s < counts[0]
        for y in range(2):
            piece = site_flags[pl.ds(128 * y + s, EDGE, stride=8), :]
            is_fluid = (piece == 1.0) & live
            row = (FLAG0 + s) * 32 + y * EDGE
            cells[row : row + EDGE, :] = jnp.where(is_fluid, 1.0, 0.0)

    for s in range(SLOTS):
        copies[s].wait()
        for x in range(EDGE):
            for y in range(2):
                tile = 2 * x + y
                for p, size in ((0, 8), (8, 8), (16, 3)):
                    row = (s * POPS + p) * 32 + y * EDGE + x
                    cells[pl.ds(row, size, stride=32), :] = pops[
                        s, p : p + size, 128 * tile : 128 * tile + 128
                    ]

    for y in range(2):
        for k in range(3):
            out = (y * 3 + k) * PLANES
            up_msg[out : out + PLANES, :] = cells[pl.ds(y * EDGE + 13 + k, PLANES, stride=32), :]
            down_msg[out : out + PLANES, :] = cells[pl.ds(y * EDGE + k, PLANES, stride=32), :]

    curve, cross = where[0], where[1]
    leaving = jnp.maximum(moves[0, curve * cross_size + cross], 0)
    low = lanes_iota() < 64
    for p in range(POPS):
        for v in range(2):
            base = leaving * (POPS * 32) + p * 32 + v * 8
            first = cells[aligned(base), :]
            second = cells[aligned(base + EDGE), :]
            outer = jnp.where(low, first, second)
            row = p * EDGE + v * 8
            up_msg[STRIP + row : STRIP + row + 8, :] = outer
            down_msg[STRIP + row : STRIP + row + 8, :] = outer
            inner_msg[row : row + 8, :] = jnp.where(low, second, first)
    for s in range(SLOTS):

        @pl.when(leaving == s)
        def _():
            for y in range(2):
                for k in range(3):
                    out = (y * 3 + k) * GROUP
                    row = s * POPS * 32 + y * EDGE + k
                    up2_msg[out : out + POPS, :] = cells[pl.ds(row + 13, POPS, stride=32), :]
                    down2_msg[out : out + POPS, :] = cells[pl.ds(row, POPS, stride=32), :]


def own_strip(cells, slot, y, x):
    return cells[pl.ds(slot * POPS * 32 + y * EDGE + x, POPS, stride=32), :]


def edge_kernel(
    curve_size,
    cross_size,
    moves,
    where,
    cells,
    low_msg,
    high_msg,
    low2_msg,
    high2_msg,
    north_msg,
    south_msg,
    outer,
):
    from_low, from_high, low_low, low_me, high_high, high_me, leaving = move_slots(
        moves, where, curve_size, cross_size
    )
    low = lanes_iota() < 64
    for q in range(PLANES):
        for v in range(2):
            first = cells[q * 32 + v * 8 : q * 32 + v * 8 + 8, :]
            second = cells[q * 32 + EDGE + v * 8 : q * 32 + EDGE + v * 8 + 8, :]
            outer[q * GROUP + v * 8 : q * GROUP + v * 8 + 8, :] = jnp.where(low, first, second)

    def both(first, second):
        lane = lax.broadcasted_iota(jnp.int32, first.shape, 1)
        return jnp.where(lane < 64, first, second)

    for msg, row0 in ((high_msg, 16), (low_msg, 21)):
        for k in range(3):
            outer[pl.ds(row0 + k, PLANES, stride=GROUP), :] = both(
                msg[k * PLANES : (k + 1) * PLANES, :],
                msg[(3 + k) * PLANES : (4 + k) * PLANES, :],
            )
    for slot, msg in ((from_low, low_msg), (from_high, high_msg)):

        @pl.when(slot >= 0)
        def _():
            for p in range(POPS):
                for v in range(2):
                    row = STRIP + p * EDGE + v * 8
                    base = slot * (POPS * GROUP) + p * GROUP + v * 8
                    outer[aligned(base), :] = msg[row : row + 8, :]

    for s in range(SLOTS):
        for slot, msg, row0 in ((low_low, low2_msg, 21), (high_high, high2_msg, 16)):

            @pl.when(slot == s)
            def _():
                for k in range(3):
                    outer[pl.ds(s * POPS * GROUP + row0 + k, POPS, stride=GROUP), :] = both(
                        msg[k * GROUP : k * GROUP + POPS, :],
                        msg[(3 + k) * GROUP : (3 + k) * GROUP + POPS, :],
                    )

        for mine in range(SLOTS):
            for slot, x0, row0 in ((low_me, 13, 21), (high_me, 0, 16)):

                @pl.when((slot == s) & (leaving == mine))
                def _():
                    for k in range(3):
                        outer[pl.ds(s * POPS * GROUP + row0 + k, POPS, stride=GROUP), :] = both(
                            own_strip(cells, mine, 0, x0 + k), own_strip(cells, mine, 1, x0 + k)
                        )

    for pair in range(PAIRS):
        for v in range(3):
            row = 2 * pair * GROUP + v * 8
            first = outer[row : row + 8, :]
            second = pltpu.roll(outer[row + GROUP : row + GROUP + 8, :], 64, axis=1)
            out = pair * GROUP + v * 8
            north_msg[out : out + 8, :] = jnp.where(low, second, first)
            south_msg[out : out + 8, :] = jnp.where(low, first, second)
    tables = (low_msg, TABLE), (cells, PLANES * 32), (high_msg, TABLE)
    for i, (ref, row) in enumerate(tables):
        out = EDGE_TABLE + 8 * i
        north_msg[out : out + 8, :] = ref[row : row + 8, :]
        south_msg[out : out + 8, :] = ref[row : row + 8, :]


def collided(h, is_fluid):
    shear = 1.0 / 0.6
    rest = h[0]
    sx, dx = h[1] + h[2], h[1] - h[2]
    sy, dy = h[3] + h[4], h[3] - h[4]
    sz, dz = h[5] + h[6], h[5] - h[6]
    s7, d7 = h[7] + h[8], h[7] - h[8]
    s9, d9 = h[9] + h[10], h[9] - h[10]
    s11, d11 = h[11] + h[12], h[11] - h[12]
    s13, d13 = h[13] + h[14], h[13] - h[14]
    s15, d15 = h[15] + h[16], h[15] - h[16]
    s17, d17 = h[17] + h[18], h[17] - h[18]
    txy, txz, tyz = s7 + s9, s11 + s13, s15 + s17
    pxy, pxz, pyz = s7 - s9, s11 - s13, s15 - s17
    ax, bx = d7 + d9, d11 + d13
    ay, by = d7 - d9, d15 + d17
    az, bz = d11 - d13, d15 - d17
    axes = sx + sy + sz
    diags = txy + txz + tyz
    rho = rest * (1.0 / 3.0) + axes * (1.0 / 18.0) + diags * (1.0 / 36.0)
    fx, fy, fz = ax + bx, ay + by, az + bz
    jx = dx * (1.0 / 18.0) + fx * (1.0 / 36.0)
    jy = dy * (1.0 / 18.0) + fy * (1.0 / 36.0)
    jz = dz * (1.0 / 18.0) + fz * (1.0 / 36.0)
    inverse = 1.0 / jnp.where(is_fluid, rho, 1.0)
    ux, uy, uz = jx * inverse, jy * inverse, jz * inverse
    qxx, qyy, qzz = jx * ux, jy * uy, jz * uz
    total = qxx + qyy + qzz

    energy = -10.0 * rest - axes * (11.0 / 18.0) + diags * (8.0 / 36.0)
    energy = (energy + 11.0 * rho - 19.0 * total) * (1.19 / 2394.0)
    square = 4.0 * rest - axes * (4.0 / 18.0) + diags * (1.0 / 36.0)
    square = (square - 3.0 * rho + 5.5 * total) * (1.4 / 252.0)
    axis_x = (3.0 * sx - axes) * (1.0 / 18.0)
    diag_x = (diags - 3.0 * tyz) * (1.0 / 36.0)
    want_x = 3.0 * qxx - total
    stress_x = (axis_x + diag_x - want_x) * (shear / 36.0)
    third_x = (diag_x - 2.0 * axis_x + 0.5 * want_x) * (1.4 / 72.0)
    axis_w = (sy - sz) * (1.0 / 18.0)
    diag_w = (txy - txz) * (1.0 / 36.0)
    want_w = qyy - qzz
    stress_w = (axis_w + diag_w - want_w) * (shear / 12.0)
    third_w = (diag_w - 2.0 * axis_w + 0.5 * want_w) * (1.4 / 24.0)

    rest_out = rest - 3.0 * (12.0 * square - 30.0 * energy)
    common = -18.0 * (11.0 * energy + 4.0 * square)
    along_x = 18.0 * (stress_x - 2.0 * third_x)
    along_w = 18.0 * (stress_w - 2.0 * third_w)
    ex = common + 2.0 * along_x
    ey = common - along_x + along_w
    ez = common - along_x - along_w
    common = 36.0 * (8.0 * energy + square)
    across_x = 36.0 * (stress_x + third_x)
    across_w = 36.0 * (stress_w + third_w)
    exy = common + across_x + across_w
    exz = common + across_x - across_w
    eyz = common - 2.0 * across_x
    cxy = shear * (0.25 * pxy - 9.0 * jx * uy)
    cxz = shear * (0.25 * pxz - 9.0 * jx * uz)
    cyz = shear * (0.25 * pyz - 9.0 * jy * uz)

    def flux(d, f, j):
        return (f * (1.0 / 36.0) - d * (4.0 / 18.0) + j * (2.0 / 3.0)) * (1.2 / 40.0)

    hx, hy, hz = flux(dx, fx, jx), flux(dy, fy, jy), flux(dz, fz, jz)
    mx = (ax - bx) * (1.98 / 8.0)
    my = (by - ay) * (1.98 / 8.0)
    mz = (az - bz) * (1.98 / 8.0)
    hx36, hy36, hz36 = 36.0 * hx, 36.0 * hy, 36.0 * hz
    xy_x, xz_x = hx36 + mx, hx36 - mx
    yz_y, xy_y = hy36 + my, hy36 - my
    xz_z, yz_z = hz36 + mz, hz36 - mz
    ox, oy, oz = -2.0 * hx36, -2.0 * hy36, -2.0 * hz36

    out = [rest_out]

    def pair(i, even, odd):
        out.append(h[i] - (even + odd))
        out.append(h[i + 1] - (even - odd))

    pair(1, ex, ox)
    pair(3, ey, oy)
    pair(5, ez, oz)
    pair(7, exy + cxy, xy_x + xy_y)
    pair(9, exy - cxy, xy_x - xy_y)
    pair(11, exz + cxz, xz_x + xz_z)
    pair(13, exz - cxz, xz_x - xz_z)
    pair(15, eyz + cyz, yz_y + yz_z)
    pair(17, eyz - cyz, yz_y - yz_z)
    return out


def collide_all(h_ref, post_ref, fluid):
    def chunk(s, c):
        base = s * SLOT + c * 8
        is_fluid = fluid[aligned(s * PLANE + c * 8), :] > 0.0
        h = [h_ref[aligned(base + p * PLANE), :] for p in range(POPS)]
        for p, value in enumerate(collided(h, is_fluid)):
            post_ref[aligned(base + p * PLANE), :] = jnp.where(is_fluid, value, jnp.nan)

    @pl.loop(0, SLOTS)
    def _(s):
        @pl.loop(0, PLANE // 8)
        def _(c):
            chunk(s, c)


def stream_all(post_ref, h_ref, fluid, table, groups, vregs, finish=None):
    lane = lanes_iota()
    row = rows_iota()
    side = {0: -1, 1: 0, 2: 0, 3: 1}

    def one_slot(s):
        own = s * SLOT

        def look(i, j, offset):
            if offset == (0, 0, 0):
                return own
            region = (i + 1) * 3 + j + 1
            return table[region * 8 + s, VELOCITY.index(offset) - 1]

        def shifted(pop, group, j, dy, dz):
            cx = VELOCITY[pop][0]

            def rows(start, v):
                return post_ref[aligned(start + pop * PLANE + group * GROUP + v * 8), :]

            inner = look(0, j, (0, dy, dz))
            need_last = vregs == 3
            values = [rows(inner, 0), rows(inner, 1)]
            if need_last:
                if dy == 0 and dz == 0:
                    values.append(rows(inner, 2))
                else:
                    values.append(
                        jnp.where(
                            row < 4,
                            rows(look(1, j, (0, dy, dz)), 2),
                            rows(look(-1, j, (0, dy, dz)), 2),
                        )
                    )
            if cx == 0:
                return values
            turn = 1 if cx > 0 else 7
            rolled = [pltpu.roll(value, turn, axis=0) for value in values]
            if cx > 0:
                before = pltpu.roll(rows(look(0, j, (-1, dy, dz)), 2), 1, axis=0)
                result = [
                    jnp.where(row == 0, before, rolled[0]),
                    jnp.where(row == 0, rolled[0], rolled[1]),
                ]
                if need_last:
                    edge = pltpu.roll(rows(look(1, j, (-1, dy, dz)), 1), 1, axis=0)
                    result.append(jnp.where(row == 0, edge, rolled[2]))
                return result
            after = pltpu.roll(rows(look(0, j, (1, dy, dz)), 2), 7, axis=0)
            result = [
                jnp.where(row == 7, rolled[1], rolled[0]),
                jnp.where(row == 7, after, rolled[1]),
            ]
            if need_last:
                edge = pltpu.roll(rows(look(-1, j, (1, dy, dz)), 0), 7, axis=0)
                result.append(jnp.where(row == 7, edge, rolled[2]))
            return result

        for pop in range(POPS):
            cx, cy, cz = VELOCITY[pop]
            kept = {}

            def source(group, j, dy, dz):
                key = (group, j, dy, dz)
                if key not in kept:
                    kept[key] = shifted(pop, group, j, dy, dz)
                return kept[key]

            def along_y(group, dz):
                j = side[group]
                values = source(group, j, 0, dz)
                other = group - cy
                if cy == 0 or other < 0 or other > 3:
                    return values
                dy = 0 if side[other] == j else -cy
                carried = source(other, j, dy, dz)
                mask = lane >= 112 if cy > 0 else lane < 16
                return [jnp.where(mask, b, a) for a, b in zip(values, carried)]

            for group in groups:
                values = along_y(group, 0)
                turn = (16 * cy + cz) % 128
                if turn:
                    values = [pltpu.roll(value, turn, axis=1) for value in values]
                if cz:
                    turn = (16 * cy - 15 * cz) % 128
                    wrapped = [pltpu.roll(value, turn, axis=1) for value in along_y(group, -cz)]
                    mask = lane % 16 == (0 if cz > 0 else 15)
                    values = [jnp.where(mask, b, a) for a, b in zip(values, wrapped)]
                for v, value in enumerate(values[:vregs]):
                    place = group * GROUP + v * 8
                    if pop:
                        back = post_ref[aligned(own + OPPOSITE[pop] * PLANE + place), :]
                        value = jnp.where(value != value, back, value)
                    is_fluid = fluid[aligned(s * PLANE + place), :] > 0.0
                    h_ref[aligned(own + pop * PLANE + place), :] = jnp.where(is_fluid, value, 0.0)

    @pl.loop(0, SLOTS)
    def _(s):
        one_slot(s)
        if finish is not None:
            finish(s)


def steps_kernel(
    curve_size,
    cross_size,
    moves,
    where,
    cells,
    low_msg,
    high_msg,
    low2_msg,
    high2_msg,
    low_inner,
    high_inner,
    south_msg,
    north_msg,
    out_hbm,
    h_ref,
    post_ref,
    fluid,
    out,
    slots,
    table,
    sems,
):
    for i in range(3):
        for j, (ref, row) in enumerate(
            (
                (south_msg, EDGE_TABLE + 8 * i),
                ((low_msg, TABLE), (cells, PLANES * 32), (high_msg, TABLE))[i],
                (north_msg, EDGE_TABLE + 8 * i),
            )
        ):
            first = ref[row : row + 8, :].astype(jnp.int32) * SLOT
            region = 8 * (3 * i + j)
            slots[region : region + 8, :] = first
    table_copy = pltpu.make_async_copy(slots, table, sems.at[SLOTS])
    table_copy.start()

    from_low, from_high, low_low, low_me, high_high, high_me, leaving = move_slots(
        moves, where, curve_size, cross_size
    )
    low = lanes_iota() < 64
    fluid[...] = jnp.zeros_like(fluid)
    post_ref[SLOTS * SLOT :, :] = jnp.full((SLOT, 128), jnp.nan, jnp.float32)

    def home(q):
        if q < FLAG0:
            return h_ref, q * PLANE
        return fluid, (q - FLAG0) * PLANE

    for q in range(PLANES):
        ref, base = home(q)
        for y in range(2):
            start = base + (1 + y) * GROUP
            ref[start : start + EDGE, :] = cells[q * 32 + y * EDGE : q * 32 + (y + 1) * EDGE, :]
    for slot, msg, inner in (
        (from_low, low_msg, low_inner),
        (from_high, high_msg, high_inner),
    ):

        @pl.when(slot >= 0)
        def _():
            for p in range(POPS):
                for v in range(2):
                    row = p * EDGE + v * 8
                    outside = msg[STRIP + row : STRIP + row + 8, :]
                    inside = inner[row : row + 8, :]
                    start = slot * SLOT + p * PLANE + GROUP + v * 8
                    h_ref[aligned(start), :] = jnp.where(low, outside, inside)
                    h_ref[aligned(start + GROUP), :] = jnp.where(low, inside, outside)

    for msg, row0 in ((high_msg, 16), (low_msg, 21)):
        for y in range(2):
            for k in range(3):
                row = (1 + y) * GROUP + row0 + k
                source = (y * 3 + k) * PLANES
                h_ref[pl.ds(row, FLAG0, stride=PLANE), :] = msg[source : source + FLAG0, :]
                fluid[pl.ds(row, SLOTS, stride=PLANE), :] = msg[source + FLAG0 : source + PLANES, :]
    for s in range(SLOTS):
        for slot, msg, row0 in ((low_low, low2_msg, 21), (high_high, high2_msg, 16)):

            @pl.when(slot == s)
            def _():
                for y in range(2):
                    for k in range(3):
                        row = s * SLOT + (1 + y) * GROUP + row0 + k
                        source = (y * 3 + k) * GROUP
                        h_ref[pl.ds(row, POPS, stride=PLANE), :] = msg[source : source + POPS, :]

        for mine in range(SLOTS):
            for slot, x0, row0 in ((low_me, 13, 21), (high_me, 0, 16)):

                @pl.when((slot == s) & (leaving == mine))
                def _():
                    for y in range(2):
                        for k in range(3):
                            row = s * SLOT + (1 + y) * GROUP + row0 + k
                            h_ref[pl.ds(row, POPS, stride=PLANE), :] = own_strip(
                                cells, mine, y, x0 + k
                            )

    for msg, group in ((south_msg, 0), (north_msg, 3)):
        for pair in range(PAIRS):
            for v in range(3):
                value = msg[pair * GROUP + v * 8 : pair * GROUP + v * 8 + 8, :]
                ref, base = home(2 * pair)
                row = base + group * GROUP + v * 8
                ref[row : row + 8, :] = value
                ref, base = home(2 * pair + 1)
                row = base + group * GROUP + v * 8
                ref[row : row + 8, :] = pltpu.roll(value, 64, axis=1)

    def finish(s):
        for x in range(EDGE):
            for y in range(2):
                tile = 2 * x + y
                for p, size in ((0, 8), (8, 8), (16, 3)):
                    row = s * SLOT + (p * PLANE + (1 + y) * GROUP + x)
                    out[s, p : p + size, 128 * tile : 128 * tile + 128] = h_ref[
                        pl.ds(row, size, stride=PLANE), :
                    ]
        pltpu.make_async_copy(out.at[s], out_hbm.at[s], sems.at[s]).start()

    for step in range(STEPS):
        collide_all(h_ref, post_ref, fluid)
        if step == 0:
            table_copy.wait()
        if step < STEPS - 1:
            stream_all(post_ref, h_ref, fluid, table, (0, 1, 2, 3), 3)
        else:
            stream_all(post_ref, h_ref, fluid, table, (1, 2), 2, finish)
    for s in range(SLOTS):
        pltpu.make_async_copy(out.at[s], out_hbm.at[s], sems.at[s]).wait()


def shifted_from(value, axis, step):
    count = lax.axis_size(axis)
    pairs = [(i, i + step) for i in range(count) if 0 <= i + step < count]
    return lax.ppermute(value, axis, pairs)


def rows128(count):
    return jax.ShapeDtypeStruct((count, 128), jnp.float32)


def call(kernel, in_spaces, out_spaces, outs, ins, scratch):
    spaces = {
        "S": pl.BlockSpec(memory_space=pltpu.SMEM),
        "V": pl.BlockSpec(memory_space=pltpu.VMEM),
        "H": pl.BlockSpec(memory_space=pltpu.HBM),
    }
    return pl.pallas_call(
        kernel,
        out_shape=outs,
        in_specs=[spaces[x] for x in in_spaces],
        out_specs=[spaces[x] for x in out_spaces],
        scratch_shapes=scratch,
        compiler_params=pltpu.CompilerParams(vmem_limit_bytes=LIMIT),
    )(*ins)


def per_device(populations, site_flags, neighbours, migrations, counts):
    curve_size = lax.axis_size("curve")
    cross_size = lax.axis_size("cross")
    curve = lax.axis_index("curve")
    cross = lax.axis_index("cross")
    where = jnp.stack([curve, cross]).astype(jnp.int32)
    moves = migrations.T

    sizes = (curve_size, cross_size)
    cells, up_msg, down_msg, up2_msg, down2_msg, inner_msg = call(
        functools.partial(pack_kernel, *sizes),
        "SSSHHV",
        "VVVVVV",
        [
            rows128(PLANES * 32 + 8),
            rows128(STRIP + HALF + 8),
            rows128(STRIP + HALF + 8),
            rows128(6 * GROUP),
            rows128(6 * GROUP),
            rows128(HALF),
        ],
        (moves, where, counts, populations, site_flags, neighbours),
        [
            pltpu.VMEM(populations.shape, jnp.float32),
            pltpu.VMEM(site_flags.shape, jnp.int32),
            pltpu.VMEM((8, 5888), jnp.float32),
            pltpu.VMEM((128, 384), jnp.bfloat16),
            pltpu.VMEM((256, 128), jnp.float32),
            pltpu.VMEM((8, 128), jnp.float32),
            pltpu.SemaphoreType.DMA((SLOTS + 1,)),
        ],
    )
    low_msg = shifted_from(up_msg, "curve", 1)
    high_msg = shifted_from(down_msg, "curve", -1)
    low2_msg = shifted_from(up2_msg, "curve", 2)
    high2_msg = shifted_from(down2_msg, "curve", -2)
    low_inner = shifted_from(inner_msg, "curve", 1)
    high_inner = shifted_from(inner_msg, "curve", -1)
    north_msg, south_msg = call(
        functools.partial(edge_kernel, *sizes),
        "SSVVVVV",
        "VV",
        [rows128(PAIRS * GROUP + 24), rows128(PAIRS * GROUP + 24)],
        (moves, where, cells, low_msg, high_msg, low2_msg, high2_msg),
        [pltpu.VMEM((PLANES * GROUP, 128), jnp.float32)],
    )
    from_south = shifted_from(north_msg, "cross", 1)
    from_north = shifted_from(south_msg, "cross", -1)
    return call(
        functools.partial(steps_kernel, *sizes),
        "SSVVVVVVVVV",
        "H",
        [jax.ShapeDtypeStruct(populations.shape, jnp.float32)],
        (
            moves,
            where,
            cells,
            low_msg,
            high_msg,
            low2_msg,
            high2_msg,
            low_inner,
            high_inner,
            from_south,
            from_north,
        ),
        [
            pltpu.VMEM((SLOTS * SLOT, 128), jnp.float32),
            pltpu.VMEM(((SLOTS + 1) * SLOT, 128), jnp.float32),
            pltpu.VMEM((SLOTS * PLANE, 128), jnp.float32),
            pltpu.VMEM(populations.shape, jnp.float32),
            pltpu.VMEM((72, 128), jnp.int32),
            pltpu.SMEM((72, 128), jnp.int32),
            pltpu.SemaphoreType.DMA((SLOTS + 1,)),
        ],
    )[0]


def solution(mesh):
    return jax.shard_map(
        per_device,
        mesh=mesh,
        in_specs=(
            P(("curve", "cross"), None, None),
            P(("curve", "cross"), None),
            P(("curve", "cross"), None),
            P(),
            P(("curve", "cross")),
        ),
        out_specs=P(("curve", "cross"), None, None),
        check_vma=False,
    )
```

```python
import functools

import jax
import jax.numpy as jnp
import numpy as np
from jax import lax
from jax.experimental import pallas as pl
from jax.experimental.pallas import tpu as pltpu
from jax.sharding import PartitionSpec as P

EDGE = 16
STEPS = 3
SLOTS = 3
POPS = 19
PLANES = SLOTS * POPS + SLOTS
FLAG0 = SLOTS * POPS
GROUP = 24
PLANE = 3 * GROUP
SLOT = POPS * PLANE
OUTWARD = SLOTS * 5 + SLOTS
LAYERS = 2 * PLANES + OUTWARD
HALF = POPS * EDGE
PAIRS = PLANES // 2
TABLE = HALF
STRIPS = HALF + 8
EDGE_TABLE = PAIRS * GROUP
NOWHERE = PLANES * PLANE
LIMIT = 48 * 1024 * 1024
WIDE_LIMIT = 127 * 512 * 1024

VELOCITY = [
    (0, 0, 0),
    (1, 0, 0),
    (-1, 0, 0),
    (0, 1, 0),
    (0, -1, 0),
    (0, 0, 1),
    (0, 0, -1),
    (1, 1, 0),
    (-1, -1, 0),
    (1, -1, 0),
    (-1, 1, 0),
    (1, 0, 1),
    (-1, 0, -1),
    (1, 0, -1),
    (-1, 0, 1),
    (0, 1, 1),
    (0, -1, -1),
    (0, 1, -1),
    (0, -1, 1),
]
OPPOSITE = [0, 2, 1, 4, 3, 6, 5, 8, 7, 10, 9, 12, 11, 14, 13, 16, 15, 18, 17]


def lanes_iota():
    return lax.broadcasted_iota(jnp.int32, (8, 128), 1)


def rows_iota():
    return lax.broadcasted_iota(jnp.int32, (8, 128), 0)


def aligned(start, size=8):
    return pl.ds(pl.multiple_of(start, 8), size)


def move_slots(moves, where, curve_size, cross_size):
    curve, cross = where[0], where[1]

    def landed(source, target):
        inside = (source >= 0) & (source < curve_size) & (target >= 0) & (target < curve_size)
        row = jnp.clip(source, 0, curve_size - 1) * cross_size + cross
        rank = target * cross_size + cross
        hit = inside & (moves[0, row] >= 0) & (moves[1, row] == rank)
        return jnp.where(hit, moves[2, row], -1)

    here = curve * cross_size + cross
    return (
        landed(curve - 1, curve),
        landed(curve + 1, curve),
        landed(curve - 2, curve - 1),
        landed(curve, curve - 1),
        landed(curve + 2, curve + 1),
        landed(curve, curve + 1),
        jnp.maximum(moves[0, here], 0),
    )


def pack_kernel(
    curve_size,
    cross_size,
    moves,
    where,
    counts,
    pops_hbm,
    flags_hbm,
    neighbours,
    cells,
    up_msg,
    down_msg,
    up2_msg,
    down2_msg,
    inner_msg,
    pops,
    flags,
    wide_flags,
    plane_flags,
    site_flags,
    near,
    sems,
):
    flags_copy = pltpu.make_async_copy(flags_hbm, flags, sems.at[SLOTS])
    flags_copy.start()
    copies = [
        pltpu.make_async_copy(pops_hbm.at[s], pops.at[s], sems.at[s]) for s in range(SLOTS)
    ]
    for copy in copies:
        copy.start()

    near[...] = jnp.zeros_like(near)
    named = neighbours[...]
    slot = jnp.where(named >= 0, lax.rem(jnp.maximum(named, 0), SLOTS), SLOTS)
    near[0:SLOTS, 0 : named.shape[1]] = slot.astype(jnp.float32)
    for ref, row in ((cells, PLANES * 32), (up_msg, TABLE), (down_msg, TABLE)):
        ref[row : row + 8, :] = near[...]

    wide_flags[...] = jnp.zeros_like(wide_flags)
    flags_copy.wait()
    wide_flags[0:SLOTS, 0 : flags.shape[1]] = flags[...].astype(jnp.float32)
    span = EDGE + 2
    for x in range(EDGE):
        start = (x + 1) * span * span
        base = start // 128 * 128
        window = wide_flags[:, base : base + 512]
        window = pltpu.roll(window, (512 - (start - base)) % 512, axis=1)
        plane_flags[8 * x : 8 * x + 8, :] = window[:, :384].astype(jnp.bfloat16)
    lane_in = lax.broadcasted_iota(jnp.int32, (384, 256), 0)
    site = lax.broadcasted_iota(jnp.int32, (384, 256), 1)
    chosen = lane_in == (site // EDGE + 1) * span + site % EDGE + 1
    product = jnp.dot(
        plane_flags[...],
        jnp.where(chosen, 1.0, 0.0).astype(jnp.bfloat16),
        preferred_element_type=jnp.float32,
    )
    site_flags[0:128, :] = product[:, :128]
    site_flags[128:256, :] = product[:, 128:]
    for s in range(SLOTS):
        live = s < counts[0]
        for y in range(2):
            piece = site_flags[pl.ds(128 * y + s, EDGE, stride=8), :]
            is_fluid = (piece == 1.0) & live
            row = (FLAG0 + s) * 32 + y * EDGE
            cells[row : row + EDGE, :] = jnp.where(is_fluid, 1.0, 0.0)

    for s in range(SLOTS):
        copies[s].wait()
        for x in range(EDGE):
            for y in range(2):
                tile = 2 * x + y
                for p, size in ((0, 8), (8, 8), (16, 3)):
                    row = (s * POPS + p) * 32 + y * EDGE + x
                    cells[pl.ds(row, size, stride=32), :] = pops[
                        s, p : p + size, 128 * tile : 128 * tile + 128
                    ]

    @pl.loop(0, SLOTS)
    def _(s):
        @pl.loop(0, 4)
        def _(c):
            base = s * (POPS * 32) + c * 8
            h = [cells[aligned(base + p * 32), :] for p in range(POPS)]
            for p, value in enumerate(collided(h, True)):
                cells[aligned(base + p * 32), :] = value

    for y in range(2):
        for msg, x0, first in ((up_msg, 15, 1), (down_msg, 0, 2)):
            step = -1 if x0 else 1
            for k in range(2):
                out = STRIPS + y * LAYERS + k * PLANES
                msg[out : out + PLANES, :] = cells[
                    pl.ds(y * EDGE + x0 + step * k, PLANES, stride=32), :
                ]
            row = y * EDGE + x0 + 2 * step
            out = STRIPS + y * LAYERS + 2 * PLANES
            for s in range(SLOTS):
                base = s * POPS * 32 + row
                msg[out + 5 * s : out + 5 * s + 1, :] = cells[pl.ds(base + first * 32, 1), :]
                msg[out + 5 * s + 1 : out + 5 * s + 5, :] = cells[
                    pl.ds(base + (first + 6) * 32, 4, stride=64), :
                ]
            msg[out + 5 * SLOTS : out + OUTWARD, :] = cells[
                pl.ds(FLAG0 * 32 + row, SLOTS, stride=32), :
            ]

    curve, cross = where[0], where[1]
    leaving = jnp.maximum(moves[0, curve * cross_size + cross], 0)
    low = lanes_iota() < 64
    for p in range(POPS):
        for v in range(2):
            base = leaving * (POPS * 32) + p * 32 + v * 8
            first = cells[aligned(base), :]
            second = cells[aligned(base + EDGE), :]
            outer = jnp.where(low, first, second)
            row = p * EDGE + v * 8
            up_msg[row : row + 8, :] = outer
            down_msg[row : row + 8, :] = outer
            inner_msg[row : row + 8, :] = jnp.where(low, second, first)
    for s in range(SLOTS):

        @pl.when(leaving == s)
        def _():
            for y in range(2):
                for k in range(3):
                    out = (y * 3 + k) * GROUP
                    row = s * POPS * 32 + y * EDGE + k
                    up2_msg[out : out + POPS, :] = cells[pl.ds(row + 13, POPS, stride=32), :]
                    down2_msg[out : out + POPS, :] = cells[pl.ds(row, POPS, stride=32), :]


def strip_rows(first, row0, step):
    pieces = []
    for k in range(2):
        pieces.append(
            (PLANES, lambda size, row: pl.ds(row, PLANES, stride=size), row0 + step * k, STRIPS + k * PLANES)
        )
    row, source = row0 + 2 * step, STRIPS + 2 * PLANES
    for s in range(SLOTS):
        plane = s * POPS + first
        pieces.append((1, lambda size, row, plane=plane: pl.ds(plane * size + row, 1), row, source))
        pieces.append(
            (
                4,
                lambda size, row, plane=plane: pl.ds(
                    (plane + 6) * size + row, 4, stride=2 * size
                ),
                row,
                source + 1,
            )
        )
        source += 5
    pieces.append(
        (SLOTS, lambda size, row: pl.ds(FLAG0 * size + row, SLOTS, stride=size), row, source)
    )
    return pieces


def own_strip(cells, slot, y, x):
    return cells[pl.ds(slot * POPS * 32 + y * EDGE + x, POPS, stride=32), :]


def edge_kernel(
    curve_size,
    cross_size,
    moves,
    where,
    cells,
    low_msg,
    high_msg,
    low2_msg,
    high2_msg,
    north_msg,
    south_msg,
    outer,
):
    from_low, from_high, low_low, low_me, high_high, high_me, leaving = move_slots(
        moves, where, curve_size, cross_size
    )
    low = lanes_iota() < 64
    for q in range(PLANES):
        for v in range(2):
            first = cells[q * 32 + v * 8 : q * 32 + v * 8 + 8, :]
            second = cells[q * 32 + EDGE + v * 8 : q * 32 + EDGE + v * 8 + 8, :]
            outer[q * GROUP + v * 8 : q * GROUP + v * 8 + 8, :] = jnp.where(low, first, second)

    def both(first, second):
        lane = lax.broadcasted_iota(jnp.int32, first.shape, 1)
        return jnp.where(lane < 64, first, second)

    for msg, row0, step, first in ((high_msg, 16, 1, 2), (low_msg, 23, -1, 1)):
        for count, planes, row, source in strip_rows(first, row0, step):
            outer[planes(GROUP, row), :] = both(
                msg[source : source + count, :],
                msg[LAYERS + source : LAYERS + source + count, :],
            )
    for slot, msg in ((from_low, low_msg), (from_high, high_msg)):

        @pl.when(slot >= 0)
        def _():
            for p in range(POPS):
                for v in range(2):
                    row = p * EDGE + v * 8
                    base = slot * (POPS * GROUP) + p * GROUP + v * 8
                    outer[aligned(base), :] = msg[row : row + 8, :]

    for s in range(SLOTS):
        for slot, msg, row0 in ((low_low, low2_msg, 21), (high_high, high2_msg, 16)):

            @pl.when(slot == s)
            def _():
                for k in range(3):
                    outer[pl.ds(s * POPS * GROUP + row0 + k, POPS, stride=GROUP), :] = both(
                        msg[k * GROUP : k * GROUP + POPS, :],
                        msg[(3 + k) * GROUP : (3 + k) * GROUP + POPS, :],
                    )

        for mine in range(SLOTS):
            for slot, x0, row0 in ((low_me, 13, 21), (high_me, 0, 16)):

                @pl.when((slot == s) & (leaving == mine))
                def _():
                    for k in range(3):
                        outer[pl.ds(s * POPS * GROUP + row0 + k, POPS, stride=GROUP), :] = both(
                            own_strip(cells, mine, 0, x0 + k), own_strip(cells, mine, 1, x0 + k)
                        )

    for pair in range(PAIRS):
        for v in range(3):
            row = 2 * pair * GROUP + v * 8
            first = outer[row : row + 8, :]
            second = pltpu.roll(outer[row + GROUP : row + GROUP + 8, :], 64, axis=1)
            out = pair * GROUP + v * 8
            north_msg[out : out + 8, :] = jnp.where(low, second, first)
            south_msg[out : out + 8, :] = jnp.where(low, first, second)
    tables = (low_msg, TABLE), (cells, PLANES * 32), (high_msg, TABLE)
    for i, (ref, row) in enumerate(tables):
        out = EDGE_TABLE + 8 * i
        north_msg[out : out + 8, :] = ref[row : row + 8, :]
        south_msg[out : out + 8, :] = ref[row : row + 8, :]


def collided(h, is_fluid):
    shear = 1.0 / 0.6
    rest = h[0]
    sx, dx = h[1] + h[2], h[1] - h[2]
    sy, dy = h[3] + h[4], h[3] - h[4]
    sz, dz = h[5] + h[6], h[5] - h[6]
    s7, d7 = h[7] + h[8], h[7] - h[8]
    s9, d9 = h[9] + h[10], h[9] - h[10]
    s11, d11 = h[11] + h[12], h[11] - h[12]
    s13, d13 = h[13] + h[14], h[13] - h[14]
    s15, d15 = h[15] + h[16], h[15] - h[16]
    s17, d17 = h[17] + h[18], h[17] - h[18]
    txy, txz, tyz = s7 + s9, s11 + s13, s15 + s17
    pxy, pxz, pyz = s7 - s9, s11 - s13, s15 - s17
    ax, bx = d7 + d9, d11 + d13
    ay, by = d7 - d9, d15 + d17
    az, bz = d11 - d13, d15 - d17
    axes = sx + sy + sz
    diags = txy + txz + tyz
    rho = rest * (1.0 / 3.0) + axes * (1.0 / 18.0) + diags * (1.0 / 36.0)
    fx, fy, fz = ax + bx, ay + by, az + bz
    jx = dx * (1.0 / 18.0) + fx * (1.0 / 36.0)
    jy = dy * (1.0 / 18.0) + fy * (1.0 / 36.0)
    jz = dz * (1.0 / 18.0) + fz * (1.0 / 36.0)
    inverse = 1.0 / jnp.where(is_fluid, rho, 1.0)
    ux, uy, uz = jx * inverse, jy * inverse, jz * inverse
    qxx, qyy, qzz = jx * ux, jy * uy, jz * uz
    total = qxx + qyy + qzz

    energy = -10.0 * rest - axes * (11.0 / 18.0) + diags * (8.0 / 36.0)
    energy = (energy + 11.0 * rho - 19.0 * total) * (1.19 / 2394.0)
    square = 4.0 * rest - axes * (4.0 / 18.0) + diags * (1.0 / 36.0)
    square = (square - 3.0 * rho + 5.5 * total) * (1.4 / 252.0)
    axis_x = (3.0 * sx - axes) * (1.0 / 18.0)
    diag_x = (diags - 3.0 * tyz) * (1.0 / 36.0)
    want_x = 3.0 * qxx - total
    stress_x = (axis_x + diag_x - want_x) * (shear / 36.0)
    third_x = (diag_x - 2.0 * axis_x + 0.5 * want_x) * (1.4 / 72.0)
    axis_w = (sy - sz) * (1.0 / 18.0)
    diag_w = (txy - txz) * (1.0 / 36.0)
    want_w = qyy - qzz
    stress_w = (axis_w + diag_w - want_w) * (shear / 12.0)
    third_w = (diag_w - 2.0 * axis_w + 0.5 * want_w) * (1.4 / 24.0)

    rest_out = rest - 3.0 * (12.0 * square - 30.0 * energy)
    common = -18.0 * (11.0 * energy + 4.0 * square)
    along_x = 18.0 * (stress_x - 2.0 * third_x)
    along_w = 18.0 * (stress_w - 2.0 * third_w)
    ex = common + 2.0 * along_x
    ey = common - along_x + along_w
    ez = common - along_x - along_w
    common = 36.0 * (8.0 * energy + square)
    across_x = 36.0 * (stress_x + third_x)
    across_w = 36.0 * (stress_w + third_w)
    exy = common + across_x + across_w
    exz = common + across_x - across_w
    eyz = common - 2.0 * across_x
    cxy = shear * (0.25 * pxy - 9.0 * jx * uy)
    cxz = shear * (0.25 * pxz - 9.0 * jx * uz)
    cyz = shear * (0.25 * pyz - 9.0 * jy * uz)

    def flux(d, f, j):
        return (f * (1.0 / 36.0) - d * (4.0 / 18.0) + j * (2.0 / 3.0)) * (1.2 / 40.0)

    hx, hy, hz = flux(dx, fx, jx), flux(dy, fy, jy), flux(dz, fz, jz)
    mx = (ax - bx) * (1.98 / 8.0)
    my = (by - ay) * (1.98 / 8.0)
    mz = (az - bz) * (1.98 / 8.0)
    hx36, hy36, hz36 = 36.0 * hx, 36.0 * hy, 36.0 * hz
    xy_x, xz_x = hx36 + mx, hx36 - mx
    yz_y, xy_y = hy36 + my, hy36 - my
    xz_z, yz_z = hz36 + mz, hz36 - mz
    ox, oy, oz = -2.0 * hx36, -2.0 * hy36, -2.0 * hz36

    out = [rest_out]

    def pair(i, even, odd):
        out.append(h[i] - (even + odd))
        out.append(h[i + 1] - (even - odd))

    pair(1, ex, ox)
    pair(3, ey, oy)
    pair(5, ez, oz)
    pair(7, exy + cxy, xy_x + xy_y)
    pair(9, exy - cxy, xy_x - xy_y)
    pair(11, exz + cxz, xz_x + xz_z)
    pair(13, exz - cxz, xz_x - xz_z)
    pair(15, eyz + cyz, yz_y + yz_z)
    pair(17, eyz - cyz, yz_y - yz_z)
    return out


def fluid_at(post_ref, s, row):
    return post_ref[aligned((FLAG0 + s) * PLANE + row), :] > 0.0


def collide_all(h_ref, post_ref):
    @pl.loop(0, SLOTS)
    def _(s):
        @pl.loop(0, PLANE // 8)
        def _(c):
            base = s * SLOT + c * 8
            is_fluid = fluid_at(post_ref, s, c * 8)
            h = [h_ref[aligned(base + p * PLANE), :] for p in range(POPS)]
            for p, value in enumerate(collided(h, is_fluid)):
                post_ref[aligned(base + p * PLANE), :] = jnp.where(is_fluid, value, jnp.nan)


def hide_walls(post_ref):
    @pl.loop(0, SLOTS)
    def _(s):
        @pl.loop(0, PLANE // 8)
        def _(c):
            is_fluid = fluid_at(post_ref, s, c * 8)
            for p in range(POPS):
                place = aligned(s * SLOT + p * PLANE + c * 8)
                post_ref[place, :] = jnp.where(is_fluid, post_ref[place, :], jnp.nan)


def stream_all(post_ref, h_ref, table, groups, vregs, finish=None):
    lane = lanes_iota()
    row = rows_iota()
    low = lane < 64

    def one_slot(s):
        own = s * SLOT

        def shifted(pop, group, j, dy, dz):
            cx = VELOCITY[pop][0]

            def rows(start, v):
                return post_ref[aligned(start + pop * PLANE + group * GROUP + v * 8), :]

            def look(i, j, dx, v):
                if (dx, dy, dz) == (0, 0, 0):
                    return rows(own, v)
                if j is None:
                    return jnp.where(low, look(i, 1, dx, v), look(i, -1, dx, v))
                region = (i + 1) * 3 + j + 1
                return rows(table[region * 8 + s, VELOCITY.index((dx, dy, dz)) - 1], v)

            need_last = vregs == 3
            values = [look(0, j, 0, 0), look(0, j, 0, 1)]
            if need_last:
                if dy == 0 and dz == 0:
                    values.append(rows(own, 2))
                else:
                    values.append(jnp.where(row < 4, look(1, j, 0, 2), look(-1, j, 0, 2)))
            if cx == 0:
                return values
            turn = 1 if cx > 0 else 7
            rolled = [pltpu.roll(value, turn, axis=0) for value in values]
            if cx > 0:
                before = pltpu.roll(look(0, j, -1, 2), 1, axis=0)
                result = [
                    jnp.where(row == 0, before, rolled[0]),
                    jnp.where(row == 0, rolled[0], rolled[1]),
                ]
                if need_last:
                    edge = pltpu.roll(look(1, j, -1, 1), 1, axis=0)
                    result.append(jnp.where(row == 0, edge, rolled[2]))
                return result
            after = pltpu.roll(look(0, j, 1, 2), 7, axis=0)
            result = [
                jnp.where(row == 7, rolled[1], rolled[0]),
                jnp.where(row == 7, after, rolled[1]),
            ]
            if need_last:
                edge = pltpu.roll(look(-1, j, 1, 0), 7, axis=0)
                result.append(jnp.where(row == 7, edge, rolled[2]))
            return result

        for pop in range(POPS):
            cx, cy, cz = VELOCITY[pop]
            kept = {}

            def source(*key):
                if key not in kept:
                    kept[key] = shifted(pop, *key)
                return kept[key]

            def along_y(group, dz):
                values = source(group, None if group == 2 else 0, 0, dz)
                if cy == 0:
                    return values
                other = (group - cy) % 3
                if group != 2 and other != 2:
                    carried = source(other, 0, 0, dz)
                else:
                    carried = source(other, cy if group == 2 else 0, -cy, dz)
                mask = lane >= 112 if cy > 0 else lane < 16
                return [jnp.where(mask, b, a) for a, b in zip(values, carried)]

            for group in groups:
                values = along_y(group, 0)
                turn = (16 * cy + cz) % 128
                if turn:
                    values = [pltpu.roll(value, turn, axis=1) for value in values]
                if cz:
                    turn = (16 * cy - 15 * cz) % 128
                    wrapped = [pltpu.roll(value, turn, axis=1) for value in along_y(group, -cz)]
                    mask = lane % 16 == (0 if cz > 0 else 15)
                    values = [jnp.where(mask, b, a) for a, b in zip(values, wrapped)]
                for v, value in enumerate(values[:vregs]):
                    place = group * GROUP + v * 8
                    if pop:
                        back = post_ref[aligned(own + OPPOSITE[pop] * PLANE + place), :]
                        value = jnp.where(value != value, back, value)
                    is_fluid = fluid_at(post_ref, s, place)
                    h_ref[aligned(own + pop * PLANE + place), :] = jnp.where(is_fluid, value, 0.0)

    @pl.loop(0, SLOTS)
    def _(s):
        one_slot(s)
        if finish is not None:
            finish(s)


def steps_kernel(
    curve_size,
    cross_size,
    moves,
    where,
    cells,
    low_msg,
    high_msg,
    low2_msg,
    high2_msg,
    low_inner,
    high_inner,
    south_msg,
    north_msg,
    out_hbm,
    h_ref,
    post_ref,
    out,
    slots,
    table,
    sems,
):
    for i in range(3):
        for j, (ref, row) in enumerate(
            (
                (south_msg, EDGE_TABLE + 8 * i),
                ((low_msg, TABLE), (cells, PLANES * 32), (high_msg, TABLE))[i],
                (north_msg, EDGE_TABLE + 8 * i),
            )
        ):
            slot = ref[row : row + 8, :].astype(jnp.int32)
            region = 8 * (3 * i + j)
            slots[region : region + 8, :] = jnp.where(slot == SLOTS, NOWHERE, slot * SLOT)
    table_copy = pltpu.make_async_copy(slots, table, sems.at[SLOTS])
    table_copy.start()

    from_low, from_high, low_low, low_me, high_high, high_me, leaving = move_slots(
        moves, where, curve_size, cross_size
    )
    low = lanes_iota() < 64
    post_ref[NOWHERE:, :] = jnp.full((SLOT, 128), jnp.nan, jnp.float32)

    for q in range(PLANES):
        for y in range(2):
            start = q * PLANE + y * GROUP
            post_ref[start : start + EDGE, :] = cells[
                q * 32 + y * EDGE : q * 32 + (y + 1) * EDGE, :
            ]
    for slot, msg, inner in (
        (from_low, low_msg, low_inner),
        (from_high, high_msg, high_inner),
    ):

        @pl.when(slot >= 0)
        def _():
            for p in range(POPS):
                for v in range(2):
                    row = p * EDGE + v * 8
                    outside = msg[row : row + 8, :]
                    inside = inner[row : row + 8, :]
                    start = slot * SLOT + p * PLANE + v * 8
                    post_ref[aligned(start), :] = jnp.where(low, outside, inside)
                    post_ref[aligned(start + GROUP), :] = jnp.where(low, inside, outside)

    for msg, row0, step, first in ((high_msg, 16, 1, 2), (low_msg, 23, -1, 1)):
        for y in range(2):
            for count, planes, row, source in strip_rows(first, row0, step):
                source += y * LAYERS
                post_ref[planes(PLANE, row + y * GROUP), :] = msg[source : source + count, :]
    for s in range(SLOTS):
        for slot, msg, row0 in ((low_low, low2_msg, 21), (high_high, high2_msg, 16)):

            @pl.when(slot == s)
            def _():
                for y in range(2):
                    for k in range(3):
                        row = s * SLOT + y * GROUP + row0 + k
                        source = (y * 3 + k) * GROUP
                        post_ref[pl.ds(row, POPS, stride=PLANE), :] = msg[
                            source : source + POPS, :
                        ]

        for mine in range(SLOTS):
            for slot, x0, row0 in ((low_me, 13, 21), (high_me, 0, 16)):

                @pl.when((slot == s) & (leaving == mine))
                def _():
                    for y in range(2):
                        for k in range(3):
                            row = s * SLOT + y * GROUP + row0 + k
                            post_ref[pl.ds(row, POPS, stride=PLANE), :] = own_strip(
                                cells, mine, y, x0 + k
                            )

    for pair in range(PAIRS):
        for v in range(3):
            row = pair * GROUP + v * 8
            south, north = south_msg[row : row + 8, :], north_msg[row : row + 8, :]
            row = 2 * pair * PLANE + 2 * GROUP + v * 8
            post_ref[row : row + 8, :] = jnp.where(low, north, south)
            post_ref[row + PLANE : row + PLANE + 8, :] = pltpu.roll(
                jnp.where(low, south, north), 64, axis=1
            )

    def finish(s):
        for x in range(EDGE):
            for y in range(2):
                tile = 2 * x + y
                for p, size in ((0, 8), (8, 8), (16, 3)):
                    row = s * SLOT + (p * PLANE + y * GROUP + x)
                    out[s, p : p + size, 128 * tile : 128 * tile + 128] = h_ref[
                        pl.ds(row, size, stride=PLANE), :
                    ]
        pltpu.make_async_copy(out.at[s], out_hbm.at[s], sems.at[s]).start()

    hide_walls(post_ref)
    table_copy.wait()
    for step in range(STEPS - 1):
        stream_all(post_ref, h_ref, table, (0, 1, 2), 3)
        collide_all(h_ref, post_ref)
    stream_all(post_ref, h_ref, table, (0, 1), 2, finish)
    for s in range(SLOTS):
        pltpu.make_async_copy(out.at[s], out_hbm.at[s], sems.at[s]).wait()


def shifted_from(value, axis, step):
    count = lax.axis_size(axis)
    pairs = [(i, i + step) for i in range(count) if 0 <= i + step < count]
    return lax.ppermute(value, axis, pairs)


def rows128(count):
    return jax.ShapeDtypeStruct((count, 128), jnp.float32)


def call(kernel, in_spaces, out_spaces, outs, ins, scratch, limit=LIMIT):
    spaces = {
        "S": pl.BlockSpec(memory_space=pltpu.SMEM),
        "V": pl.BlockSpec(memory_space=pltpu.VMEM),
        "H": pl.BlockSpec(memory_space=pltpu.HBM),
    }
    return pl.pallas_call(
        kernel,
        out_shape=outs,
        in_specs=[spaces[x] for x in in_spaces],
        out_specs=[spaces[x] for x in out_spaces],
        scratch_shapes=scratch,
        compiler_params=pltpu.CompilerParams(vmem_limit_bytes=limit),
    )(*ins)


def per_device(populations, site_flags, neighbours, migrations, counts):
    curve_size = lax.axis_size("curve")
    cross_size = lax.axis_size("cross")
    curve = lax.axis_index("curve")
    cross = lax.axis_index("cross")
    where = jnp.stack([curve, cross]).astype(jnp.int32)
    moves = migrations.T

    sizes = (curve_size, cross_size)
    cells, up_msg, down_msg, up2_msg, down2_msg, inner_msg = call(
        functools.partial(pack_kernel, *sizes),
        "SSSHHV",
        "VVVVVV",
        [
            rows128(PLANES * 32 + 8),
            rows128(STRIPS + 2 * LAYERS),
            rows128(STRIPS + 2 * LAYERS),
            rows128(6 * GROUP),
            rows128(6 * GROUP),
            rows128(HALF),
        ],
        (moves, where, counts, populations, site_flags, neighbours),
        [
            pltpu.VMEM(populations.shape, jnp.float32),
            pltpu.VMEM(site_flags.shape, jnp.int32),
            pltpu.VMEM((8, 5888), jnp.float32),
            pltpu.VMEM((128, 384), jnp.bfloat16),
            pltpu.VMEM((256, 128), jnp.float32),
            pltpu.VMEM((8, 128), jnp.float32),
            pltpu.SemaphoreType.DMA((SLOTS + 1,)),
        ],
        WIDE_LIMIT,
    )
    low_msg = shifted_from(up_msg, "curve", 1)
    high_msg = shifted_from(down_msg, "curve", -1)
    low2_msg = shifted_from(up2_msg, "curve", 2)
    high2_msg = shifted_from(down2_msg, "curve", -2)
    low_inner = shifted_from(inner_msg, "curve", 1)
    high_inner = shifted_from(inner_msg, "curve", -1)
    north_msg, south_msg = call(
        functools.partial(edge_kernel, *sizes),
        "SSVVVVV",
        "VV",
        [rows128(PAIRS * GROUP + 24), rows128(PAIRS * GROUP + 24)],
        (moves, where, cells, low_msg, high_msg, low2_msg, high2_msg),
        [pltpu.VMEM((PLANES * GROUP, 128), jnp.float32)],
    )
    from_south = shifted_from(north_msg, "cross", 1)
    from_north = shifted_from(south_msg, "cross", -1)
    return call(
        functools.partial(steps_kernel, *sizes),
        "SSVVVVVVVVV",
        "H",
        [jax.ShapeDtypeStruct(populations.shape, jnp.float32)],
        (
            moves,
            where,
            cells,
            low_msg,
            high_msg,
            low2_msg,
            high2_msg,
            low_inner,
            high_inner,
            from_south,
            from_north,
        ),
        [
            pltpu.VMEM((SLOTS * SLOT, 128), jnp.float32),
            pltpu.VMEM((NOWHERE + SLOT, 128), jnp.float32),
            pltpu.VMEM(populations.shape, jnp.float32),
            pltpu.VMEM((72, 128), jnp.int32),
            pltpu.SMEM((72, 128), jnp.int32),
            pltpu.SemaphoreType.DMA((SLOTS + 1,)),
        ],
    )[0]


def solution(mesh):
    return jax.shard_map(
        per_device,
        mesh=mesh,
        in_specs=(
            P(("curve", "cross"), None, None),
            P(("curve", "cross"), None),
            P(("curve", "cross"), None),
            P(),
            P(("curve", "cross")),
        ),
        out_specs=P(("curve", "cross"), None, None),
        check_vma=False,
    )
```

```python
import functools

import jax
import jax.numpy as jnp
import numpy as np
from jax import lax
from jax.experimental import pallas as pl
from jax.experimental.pallas import tpu as pltpu
from jax.sharding import PartitionSpec as P

EDGE = 16
STEPS = 3
SLOTS = 3
POPS = 19
PLANES = SLOTS * POPS + SLOTS
FLAG0 = SLOTS * POPS
GROUP = 24
PLANE = 3 * GROUP
SLOT = POPS * PLANE
OUTWARD = SLOTS * 5 + SLOTS
LAYERS = 2 * PLANES + OUTWARD
HALF = POPS * EDGE
PAIRS = PLANES // 2
TABLE = HALF
STRIPS = HALF + 8
EDGE_TABLE = PAIRS * GROUP
NOWHERE = PLANES * PLANE
LIMIT = 20 * 1024 * 1024
WIDE_LIMIT = 127 * 512 * 1024

VELOCITY = [
    (0, 0, 0),
    (1, 0, 0),
    (-1, 0, 0),
    (0, 1, 0),
    (0, -1, 0),
    (0, 0, 1),
    (0, 0, -1),
    (1, 1, 0),
    (-1, -1, 0),
    (1, -1, 0),
    (-1, 1, 0),
    (1, 0, 1),
    (-1, 0, -1),
    (1, 0, -1),
    (-1, 0, 1),
    (0, 1, 1),
    (0, -1, -1),
    (0, 1, -1),
    (0, -1, 1),
]
OPPOSITE = [0, 2, 1, 4, 3, 6, 5, 8, 7, 10, 9, 12, 11, 14, 13, 16, 15, 18, 17]


def lanes_iota():
    return lax.broadcasted_iota(jnp.int32, (8, 128), 1)


def rows_iota():
    return lax.broadcasted_iota(jnp.int32, (8, 128), 0)


def aligned(start, size=8):
    return pl.ds(pl.multiple_of(start, 8), size)


def move_slots(moves, curve_size, cross_size):
    curve, cross = lax.axis_index("curve"), lax.axis_index("cross")

    def landed(source, target):
        inside = (source >= 0) & (source < curve_size) & (target >= 0) & (target < curve_size)
        row = jnp.clip(source, 0, curve_size - 1) * cross_size + cross
        rank = target * cross_size + cross
        hit = inside & (moves[0, row] >= 0) & (moves[1, row] == rank)
        return jnp.where(hit, moves[2, row], -1)

    return (
        landed(curve - 1, curve),
        landed(curve + 1, curve),
        landed(curve - 2, curve - 1),
        landed(curve, curve - 1),
        landed(curve + 2, curve + 1),
        landed(curve, curve + 1),
    )


def pack_kernel(
    cross_size,
    moves_hbm,
    counts_hbm,
    pops_hbm,
    flags_hbm,
    neighbours_hbm,
    cells_hbm,
    up_hbm,
    down_hbm,
    up2_hbm,
    down2_hbm,
    inner_hbm,
    moves,
    counts,
    pops,
    flags,
    neighbours,
    cells,
    up_msg,
    down_msg,
    up2_msg,
    down2_msg,
    inner_msg,
    wide_flags,
    plane_flags,
    site_flags,
    near,
    sems,
):
    started = []

    def copy(source, target):
        one = pltpu.make_async_copy(source, target, sems.at[len(started)])
        one.start()
        started.append(one)
        return one

    flags_copy = copy(flags_hbm, flags)
    copies = [copy(pops_hbm.at[s], pops.at[s]) for s in range(SLOTS)]
    small = [
        copy(neighbours_hbm, neighbours),
        copy(counts_hbm, counts),
        copy(moves_hbm, moves),
    ]
    for one in small:
        one.wait()

    near[...] = jnp.zeros_like(near)
    named = neighbours[...]
    slot = jnp.where(named >= 0, lax.rem(jnp.maximum(named, 0), SLOTS), SLOTS)
    near[0:SLOTS, 0 : named.shape[1]] = slot.astype(jnp.float32)
    for ref, row in ((cells, PLANES * 32), (up_msg, TABLE), (down_msg, TABLE)):
        ref[row : row + 8, :] = near[...]

    wide_flags[...] = jnp.zeros_like(wide_flags)
    flags_copy.wait()
    wide_flags[0:SLOTS, 0 : flags.shape[1]] = flags[...].astype(jnp.float32)
    span = EDGE + 2
    for x in range(EDGE):
        start = (x + 1) * span * span
        base = start // 128 * 128
        window = wide_flags[:, base : base + 512]
        window = pltpu.roll(window, (512 - (start - base)) % 512, axis=1)
        plane_flags[8 * x : 8 * x + 8, :] = window[:, :384].astype(jnp.bfloat16)
    lane_in = lax.broadcasted_iota(jnp.int32, (384, 256), 0)
    site = lax.broadcasted_iota(jnp.int32, (384, 256), 1)
    chosen = lane_in == (site // EDGE + 1) * span + site % EDGE + 1
    product = jnp.dot(
        plane_flags[...],
        jnp.where(chosen, 1.0, 0.0).astype(jnp.bfloat16),
        preferred_element_type=jnp.float32,
    )
    site_flags[0:128, :] = product[:, :128]
    site_flags[128:256, :] = product[:, 128:]
    for s in range(SLOTS):
        live = s < counts[0]
        for y in range(2):
            piece = site_flags[pl.ds(128 * y + s, EDGE, stride=8), :]
            is_fluid = (piece == 1.0) & live
            row = (FLAG0 + s) * 32 + y * EDGE
            cells[row : row + EDGE, :] = jnp.where(is_fluid, 1.0, 0.0)

    for s in range(SLOTS):
        copies[s].wait()
        for x in range(EDGE):
            for y in range(2):
                tile = 2 * x + y
                for p, size in ((0, 8), (8, 8), (16, 3)):
                    row = (s * POPS + p) * 32 + y * EDGE + x
                    cells[pl.ds(row, size, stride=32), :] = pops[
                        s, p : p + size, 128 * tile : 128 * tile + 128
                    ]

    @pl.loop(0, SLOTS)
    def _(s):
        @pl.loop(0, 4)
        def _(c):
            base = s * (POPS * 32) + c * 8
            h = [cells[aligned(base + p * 32), :] for p in range(POPS)]
            for p, value in enumerate(collided(h, True)):
                cells[aligned(base + p * 32), :] = value

    cells_copy = copy(cells, cells_hbm)

    for y in range(2):
        for msg, x0, first in ((up_msg, 15, 1), (down_msg, 0, 2)):
            step = -1 if x0 else 1
            for k in range(2):
                out = STRIPS + y * LAYERS + k * PLANES
                msg[out : out + PLANES, :] = cells[
                    pl.ds(y * EDGE + x0 + step * k, PLANES, stride=32), :
                ]
            row = y * EDGE + x0 + 2 * step
            out = STRIPS + y * LAYERS + 2 * PLANES
            for s in range(SLOTS):
                base = s * POPS * 32 + row
                msg[out + 5 * s : out + 5 * s + 1, :] = cells[pl.ds(base + first * 32, 1), :]
                msg[out + 5 * s + 1 : out + 5 * s + 5, :] = cells[
                    pl.ds(base + (first + 6) * 32, 4, stride=64), :
                ]
            msg[out + 5 * SLOTS : out + OUTWARD, :] = cells[
                pl.ds(FLAG0 * 32 + row, SLOTS, stride=32), :
            ]

    here = lax.axis_index("curve") * cross_size + lax.axis_index("cross")
    leaving = jnp.maximum(moves[0, here], 0)
    low = lanes_iota() < 64
    for p in range(POPS):
        for v in range(2):
            base = leaving * (POPS * 32) + p * 32 + v * 8
            first = cells[aligned(base), :]
            second = cells[aligned(base + EDGE), :]
            outer = jnp.where(low, first, second)
            row = p * EDGE + v * 8
            up_msg[row : row + 8, :] = outer
            down_msg[row : row + 8, :] = outer
            inner_msg[row : row + 8, :] = jnp.where(low, second, first)
    for s in range(SLOTS):

        @pl.when(leaving == s)
        def _():
            for y in range(2):
                for k in range(3):
                    out = (y * 3 + k) * GROUP
                    row = s * POPS * 32 + y * EDGE + k
                    up2_msg[out : out + POPS, :] = cells[pl.ds(row + 13, POPS, stride=32), :]
                    down2_msg[out : out + POPS, :] = cells[pl.ds(row, POPS, stride=32), :]

    last = [
        copy(up_msg, up_hbm),
        copy(down_msg, down_hbm),
        copy(up2_msg, up2_hbm),
        copy(down2_msg, down2_hbm),
        copy(inner_msg, inner_hbm),
    ]
    cells_copy.wait()
    for one in last:
        one.wait()


def spread_kernel(
    curve_size, cross_size, moves, cells, up2_msg, down2_msg, post, outer, own2, landings
):
    low = lanes_iota() < 64
    own2[0 : 6 * GROUP, :] = up2_msg[...]
    own2[6 * GROUP :, :] = down2_msg[...]
    for i, slot in enumerate(move_slots(moves, curve_size, cross_size)):
        landings[i : i + 1, :] = jnp.full((1, 128), slot, jnp.int32)
    post[NOWHERE:, :] = jnp.full((SLOT, 128), jnp.nan, jnp.float32)
    for q in range(PLANES):
        for v in range(2):
            row = q * 32 + v * 8
            first, second = cells[row : row + 8, :], cells[row + EDGE : row + EDGE + 8, :]
            row = q * PLANE + v * 8
            post[row : row + 8, :] = first
            post[row + GROUP : row + GROUP + 8, :] = second
            row = q * GROUP + v * 8
            outer[row : row + 8, :] = jnp.where(low, first, second)
    outer[PLANES * GROUP :, :] = cells[PLANES * 32 :, :]


def strip_rows(first, row0, step):
    pieces = []
    for k in range(2):
        pieces.append(
            (PLANES, lambda size, row: pl.ds(row, PLANES, stride=size), row0 + step * k, STRIPS + k * PLANES)
        )
    row, source = row0 + 2 * step, STRIPS + 2 * PLANES
    for s in range(SLOTS):
        plane = s * POPS + first
        pieces.append((1, lambda size, row, plane=plane: pl.ds(plane * size + row, 1), row, source))
        pieces.append(
            (
                4,
                lambda size, row, plane=plane: pl.ds(
                    (plane + 6) * size + row, 4, stride=2 * size
                ),
                row,
                source + 1,
            )
        )
        source += 5
    pieces.append(
        (SLOTS, lambda size, row: pl.ds(FLAG0 * size + row, SLOTS, stride=size), row, source)
    )
    return pieces


def edge_kernel(
    landings,
    own_outer,
    low_msg,
    high_msg,
    low2_msg,
    high2_msg,
    own2,
    north_msg,
    south_msg,
    outer,
):
    from_low, from_high, low_low, low_me, high_high, high_me = (landings[i, 0] for i in range(6))
    low = lanes_iota() < 64
    for q in range(PLANES):
        for v in range(2):
            row = q * GROUP + v * 8
            outer[row : row + 8, :] = own_outer[row : row + 8, :]

    def both(first, second):
        lane = lax.broadcasted_iota(jnp.int32, first.shape, 1)
        return jnp.where(lane < 64, first, second)

    for msg, row0, step, first in ((high_msg, 16, 1, 2), (low_msg, 23, -1, 1)):
        for count, planes, row, source in strip_rows(first, row0, step):
            outer[planes(GROUP, row), :] = both(
                msg[source : source + count, :],
                msg[LAYERS + source : LAYERS + source + count, :],
            )
    for slot, msg in ((from_low, low_msg), (from_high, high_msg)):

        @pl.when(slot >= 0)
        def _():
            for p in range(POPS):
                for v in range(2):
                    row = p * EDGE + v * 8
                    base = slot * (POPS * GROUP) + p * GROUP + v * 8
                    outer[aligned(base), :] = msg[row : row + 8, :]

    for s in range(SLOTS):
        for slot, msg, row0 in (
            (low_low, low2_msg, 21),
            (low_me, own2, 21),
            (high_high, high2_msg, 16),
            (high_me, own2.at[6 * GROUP :], 16),
        ):

            @pl.when(slot == s)
            def _():
                for k in range(3):
                    outer[pl.ds(s * POPS * GROUP + row0 + k, POPS, stride=GROUP), :] = both(
                        msg[k * GROUP : k * GROUP + POPS, :],
                        msg[(3 + k) * GROUP : (3 + k) * GROUP + POPS, :],
                    )

    for pair in range(PAIRS):
        for v in range(3):
            row = 2 * pair * GROUP + v * 8
            first = outer[row : row + 8, :]
            second = pltpu.roll(outer[row + GROUP : row + GROUP + 8, :], 64, axis=1)
            out = pair * GROUP + v * 8
            north_msg[out : out + 8, :] = jnp.where(low, second, first)
            south_msg[out : out + 8, :] = jnp.where(low, first, second)
    tables = (low_msg, TABLE), (own_outer, PLANES * GROUP), (high_msg, TABLE)
    for i, (ref, row) in enumerate(tables):
        out = EDGE_TABLE + 8 * i
        north_msg[out : out + 8, :] = ref[row : row + 8, :]
        south_msg[out : out + 8, :] = ref[row : row + 8, :]


def collided(h, is_fluid):
    shear = 1.0 / 0.6
    rest = h[0]
    sx, dx = h[1] + h[2], h[1] - h[2]
    sy, dy = h[3] + h[4], h[3] - h[4]
    sz, dz = h[5] + h[6], h[5] - h[6]
    s7, d7 = h[7] + h[8], h[7] - h[8]
    s9, d9 = h[9] + h[10], h[9] - h[10]
    s11, d11 = h[11] + h[12], h[11] - h[12]
    s13, d13 = h[13] + h[14], h[13] - h[14]
    s15, d15 = h[15] + h[16], h[15] - h[16]
    s17, d17 = h[17] + h[18], h[17] - h[18]
    txy, txz, tyz = s7 + s9, s11 + s13, s15 + s17
    pxy, pxz, pyz = s7 - s9, s11 - s13, s15 - s17
    ax, bx = d7 + d9, d11 + d13
    ay, by = d7 - d9, d15 + d17
    az, bz = d11 - d13, d15 - d17
    axes = sx + sy + sz
    diags = txy + txz + tyz
    rho = rest * (1.0 / 3.0) + axes * (1.0 / 18.0) + diags * (1.0 / 36.0)
    fx, fy, fz = ax + bx, ay + by, az + bz
    jx = dx * (1.0 / 18.0) + fx * (1.0 / 36.0)
    jy = dy * (1.0 / 18.0) + fy * (1.0 / 36.0)
    jz = dz * (1.0 / 18.0) + fz * (1.0 / 36.0)
    inverse = 1.0 / jnp.where(is_fluid, rho, 1.0)
    ux, uy, uz = jx * inverse, jy * inverse, jz * inverse
    qxx, qyy, qzz = jx * ux, jy * uy, jz * uz
    total = qxx + qyy + qzz

    energy = -10.0 * rest - axes * (11.0 / 18.0) + diags * (8.0 / 36.0)
    energy = (energy + 11.0 * rho - 19.0 * total) * (1.19 / 2394.0)
    square = 4.0 * rest - axes * (4.0 / 18.0) + diags * (1.0 / 36.0)
    square = (square - 3.0 * rho + 5.5 * total) * (1.4 / 252.0)
    axis_x = (3.0 * sx - axes) * (1.0 / 18.0)
    diag_x = (diags - 3.0 * tyz) * (1.0 / 36.0)
    want_x = 3.0 * qxx - total
    stress_x = (axis_x + diag_x - want_x) * (shear / 36.0)
    third_x = (diag_x - 2.0 * axis_x + 0.5 * want_x) * (1.4 / 72.0)
    axis_w = (sy - sz) * (1.0 / 18.0)
    diag_w = (txy - txz) * (1.0 / 36.0)
    want_w = qyy - qzz
    stress_w = (axis_w + diag_w - want_w) * (shear / 12.0)
    third_w = (diag_w - 2.0 * axis_w + 0.5 * want_w) * (1.4 / 24.0)

    rest_out = rest - 3.0 * (12.0 * square - 30.0 * energy)
    common = -18.0 * (11.0 * energy + 4.0 * square)
    along_x = 18.0 * (stress_x - 2.0 * third_x)
    along_w = 18.0 * (stress_w - 2.0 * third_w)
    ex = common + 2.0 * along_x
    ey = common - along_x + along_w
    ez = common - along_x - along_w
    common = 36.0 * (8.0 * energy + square)
    across_x = 36.0 * (stress_x + third_x)
    across_w = 36.0 * (stress_w + third_w)
    exy = common + across_x + across_w
    exz = common + across_x - across_w
    eyz = common - 2.0 * across_x
    cxy = shear * (0.25 * pxy - 9.0 * jx * uy)
    cxz = shear * (0.25 * pxz - 9.0 * jx * uz)
    cyz = shear * (0.25 * pyz - 9.0 * jy * uz)

    def flux(d, f, j):
        return (f * (1.0 / 36.0) - d * (4.0 / 18.0) + j * (2.0 / 3.0)) * (1.2 / 40.0)

    hx, hy, hz = flux(dx, fx, jx), flux(dy, fy, jy), flux(dz, fz, jz)
    mx = (ax - bx) * (1.98 / 8.0)
    my = (by - ay) * (1.98 / 8.0)
    mz = (az - bz) * (1.98 / 8.0)
    hx36, hy36, hz36 = 36.0 * hx, 36.0 * hy, 36.0 * hz
    xy_x, xz_x = hx36 + mx, hx36 - mx
    yz_y, xy_y = hy36 + my, hy36 - my
    xz_z, yz_z = hz36 + mz, hz36 - mz
    ox, oy, oz = -2.0 * hx36, -2.0 * hy36, -2.0 * hz36

    out = [rest_out]

    def pair(i, even, odd):
        out.append(h[i] - (even + odd))
        out.append(h[i + 1] - (even - odd))

    pair(1, ex, ox)
    pair(3, ey, oy)
    pair(5, ez, oz)
    pair(7, exy + cxy, xy_x + xy_y)
    pair(9, exy - cxy, xy_x - xy_y)
    pair(11, exz + cxz, xz_x + xz_z)
    pair(13, exz - cxz, xz_x - xz_z)
    pair(15, eyz + cyz, yz_y + yz_z)
    pair(17, eyz - cyz, yz_y - yz_z)
    return out


def fluid_at(post_ref, s, row):
    return post_ref[aligned((FLAG0 + s) * PLANE + row), :] > 0.0


def collide_all(h_ref, post_ref, put, chunks):
    @pl.loop(0, SLOTS)
    def _(s):
        @pl.loop(*chunks)
        def _(c):
            base = s * SLOT + c * 8
            is_fluid = fluid_at(post_ref, s, c * 8)
            h = [h_ref[aligned(base + p * PLANE), :] for p in range(POPS)]
            for p, value in enumerate(collided(h, is_fluid)):
                put(s, c, p, jnp.where(is_fluid, value, jnp.nan))


def hide_walls(post_ref):
    @pl.loop(0, SLOTS)
    def _(s):
        @pl.loop(0, PLANE // 8)
        def _(c):
            is_fluid = fluid_at(post_ref, s, c * 8)
            for p in range(POPS):
                place = aligned(s * SLOT + p * PLANE + c * 8)
                post_ref[place, :] = jnp.where(is_fluid, post_ref[place, :], jnp.nan)


def stream_all(post_ref, h_ref, table, groups, vregs, finish=None):
    lane = lanes_iota()
    row = rows_iota()
    low = lane < 64

    def one_slot(s):
        own = s * SLOT

        def shifted(pop, group, j, dy, dz):
            cx = VELOCITY[pop][0]

            def rows(start, v):
                return post_ref[aligned(start + pop * PLANE + group * GROUP + v * 8), :]

            def look(i, j, dx, v):
                if (dx, dy, dz) == (0, 0, 0):
                    return rows(own, v)
                if j is None:
                    return jnp.where(low, look(i, 1, dx, v), look(i, -1, dx, v))
                region = (i + 1) * 3 + j + 1
                return rows(table[region * 8 + s, VELOCITY.index((dx, dy, dz)) - 1], v)

            need_last = vregs == 3
            values = [look(0, j, 0, 0), look(0, j, 0, 1)]
            if need_last:
                if dy == 0 and dz == 0:
                    values.append(rows(own, 2))
                else:
                    values.append(jnp.where(row < 4, look(1, j, 0, 2), look(-1, j, 0, 2)))
            if cx == 0:
                return values
            turn = 1 if cx > 0 else 7
            rolled = [pltpu.roll(value, turn, axis=0) for value in values]
            if cx > 0:
                before = pltpu.roll(look(0, j, -1, 2), 1, axis=0)
                result = [
                    jnp.where(row == 0, before, rolled[0]),
                    jnp.where(row == 0, rolled[0], rolled[1]),
                ]
                if need_last:
                    edge = pltpu.roll(look(1, j, -1, 1), 1, axis=0)
                    result.append(jnp.where(row == 0, edge, rolled[2]))
                return result
            after = pltpu.roll(look(0, j, 1, 2), 7, axis=0)
            result = [
                jnp.where(row == 7, rolled[1], rolled[0]),
                jnp.where(row == 7, after, rolled[1]),
            ]
            if need_last:
                edge = pltpu.roll(look(-1, j, 1, 0), 7, axis=0)
                result.append(jnp.where(row == 7, edge, rolled[2]))
            return result

        for pop in range(POPS):
            cx, cy, cz = VELOCITY[pop]
            kept = {}

            def source(*key):
                if key not in kept:
                    kept[key] = shifted(pop, *key)
                return kept[key]

            def along_y(group, dz):
                values = source(group, None if group == 2 else 0, 0, dz)
                if cy == 0:
                    return values
                other = (group - cy) % 3
                if group != 2 and other != 2:
                    carried = source(other, 0, 0, dz)
                else:
                    carried = source(other, cy if group == 2 else 0, -cy, dz)
                mask = lane >= 112 if cy > 0 else lane < 16
                return [jnp.where(mask, b, a) for a, b in zip(values, carried)]

            for group in groups:
                values = along_y(group, 0)
                turn = (16 * cy + cz) % 128
                if turn:
                    values = [pltpu.roll(value, turn, axis=1) for value in values]
                if cz:
                    turn = (16 * cy - 15 * cz) % 128
                    wrapped = [pltpu.roll(value, turn, axis=1) for value in along_y(group, -cz)]
                    mask = lane % 16 == (0 if cz > 0 else 15)
                    values = [jnp.where(mask, b, a) for a, b in zip(values, wrapped)]
                for v, value in enumerate(values[:vregs]):
                    place = group * GROUP + v * 8
                    if pop:
                        back = post_ref[aligned(own + OPPOSITE[pop] * PLANE + place), :]
                        value = jnp.where(value != value, back, value)
                    is_fluid = fluid_at(post_ref, s, place)
                    h_ref[aligned(own + pop * PLANE + place), :] = jnp.where(is_fluid, value, 0.0)

    @pl.loop(0, SLOTS)
    def _(s):
        one_slot(s)
        if finish is not None:
            finish(s)


def widen_kernel(
    landings,
    own_post,
    own_outer,
    low_msg,
    high_msg,
    low2_msg,
    high2_msg,
    own2,
    south_msg,
    north_msg,
    post_ref,
    slots,
    next_outer,
    h_ref,
    table,
    sem,
):
    for i in range(3):
        for j, (ref, row) in enumerate(
            (
                (south_msg, EDGE_TABLE + 8 * i),
                ((low_msg, TABLE), (own_outer, PLANES * GROUP), (high_msg, TABLE))[i],
                (north_msg, EDGE_TABLE + 8 * i),
            )
        ):
            slot = ref[row : row + 8, :].astype(jnp.int32)
            region = 8 * (3 * i + j)
            slots[region : region + 8, :] = jnp.where(slot == SLOTS, NOWHERE, slot * SLOT)
    table_copy = pltpu.make_async_copy(slots, table, sem)
    table_copy.start()

    from_low, from_high, low_low, low_me, high_high, high_me = (landings[i, 0] for i in range(6))
    low = lanes_iota() < 64
    post_ref[...] = own_post[...]
    for slot, msg in ((from_low, low_msg), (from_high, high_msg)):

        @pl.when(slot >= 0)
        def _():
            for p in range(POPS):
                for v in range(2):
                    row = p * EDGE + v * 8
                    value = msg[row : row + 8, :]
                    start = slot * SLOT + p * PLANE + v * 8
                    post_ref[aligned(start), :] = value
                    post_ref[aligned(start + GROUP), :] = value

    for msg, row0, step, first in ((high_msg, 16, 1, 2), (low_msg, 23, -1, 1)):
        for y in range(2):
            for count, planes, row, source in strip_rows(first, row0, step):
                source += y * LAYERS
                post_ref[planes(PLANE, row + y * GROUP), :] = msg[source : source + count, :]
    for s in range(SLOTS):
        for slot, msg, row0 in (
            (low_low, low2_msg, 21),
            (low_me, own2, 21),
            (high_high, high2_msg, 16),
            (high_me, own2.at[6 * GROUP :], 16),
        ):

            @pl.when(slot == s)
            def _():
                for y in range(2):
                    for k in range(3):
                        row = s * SLOT + y * GROUP + row0 + k
                        source = (y * 3 + k) * GROUP
                        post_ref[pl.ds(row, POPS, stride=PLANE), :] = msg[
                            source : source + POPS, :
                        ]

    for pair in range(PAIRS):
        for v in range(3):
            row = pair * GROUP + v * 8
            south, north = south_msg[row : row + 8, :], north_msg[row : row + 8, :]
            row = 2 * pair * PLANE + 2 * GROUP + v * 8
            post_ref[row : row + 8, :] = jnp.where(low, north, south)
            post_ref[row + PLANE : row + PLANE + 8, :] = pltpu.roll(
                jnp.where(low, south, north), 64, axis=1
            )

    hide_walls(post_ref)
    table_copy.wait()
    stream_all(post_ref, h_ref, table, (2,), 3)

    def put(s, c, p, value):
        next_outer[aligned(s * (POPS * GROUP) + p * GROUP + (c - 6) * 8), :] = value

    collide_all(h_ref, post_ref, put, (6, 9))


def steps_kernel(
    landings,
    table,
    wide_post,
    next_outer,
    low_inner,
    high_inner,
    out_hbm,
    h_ref,
    post_ref,
    out,
    sems,
):
    low = lanes_iota() < 64
    post_ref[...] = wide_post[...]
    for slot, inner in ((landings[0, 0], low_inner), (landings[1, 0], high_inner)):

        @pl.when(slot >= 0)
        def _():
            for v in range(2):
                fluid = [fluid_at(post_ref, slot, y * GROUP + v * 8) for y in range(2)]
                for p in range(POPS):
                    row = p * EDGE + v * 8
                    value = inner[row : row + 8, :]
                    for y in range(2):
                        start = aligned(slot * SLOT + p * PLANE + y * GROUP + v * 8)
                        is_here = low if y else jnp.logical_not(low)
                        hidden = jnp.where(fluid[y], value, jnp.nan)
                        post_ref[start, :] = jnp.where(is_here, hidden, post_ref[start, :])

    def finish(s):
        for x in range(EDGE):
            for y in range(2):
                tile = 2 * x + y
                for p, size in ((0, 8), (8, 8), (16, 3)):
                    row = s * SLOT + (p * PLANE + y * GROUP + x)
                    out[s, p : p + size, 128 * tile : 128 * tile + 128] = h_ref[
                        pl.ds(row, size, stride=PLANE), :
                    ]
        pltpu.make_async_copy(out.at[s], out_hbm.at[s], sems.at[s]).start()

    def put(s, c, p, value):
        post_ref[aligned(s * SLOT + p * PLANE + c * 8), :] = value

    stream_all(post_ref, h_ref, table, (0, 1), 3)
    collide_all(h_ref, post_ref, put, (0, 6))
    for q in range(SLOTS * POPS):
        row = q * PLANE + 2 * GROUP
        post_ref[row : row + GROUP, :] = next_outer[q * GROUP : (q + 1) * GROUP, :]
    for _ in range(STEPS - 2):
        stream_all(post_ref, h_ref, table, (0, 1, 2), 3)
        collide_all(h_ref, post_ref, put, (0, 9))
    stream_all(post_ref, h_ref, table, (0, 1), 2, finish)
    for s in range(SLOTS):
        pltpu.make_async_copy(out.at[s], out_hbm.at[s], sems.at[s]).wait()


def shifted_from(value, axis, step):
    count = lax.axis_size(axis)
    pairs = [(i, i + step) for i in range(count) if 0 <= i + step < count]
    return lax.ppermute(value, axis, pairs)


def rows128(count):
    return jax.ShapeDtypeStruct((count, 128), jnp.float32)


def call(kernel, in_spaces, out_spaces, outs, ins, scratch, limit=LIMIT):
    spaces = {
        "S": pl.BlockSpec(memory_space=pltpu.SMEM),
        "V": pl.BlockSpec(memory_space=pltpu.VMEM),
        "H": pl.BlockSpec(memory_space=pltpu.HBM),
    }
    return pl.pallas_call(
        kernel,
        out_shape=outs,
        in_specs=[spaces[x] for x in in_spaces],
        out_specs=[spaces[x] for x in out_spaces],
        scratch_shapes=scratch,
        compiler_params=pltpu.CompilerParams(vmem_limit_bytes=limit),
    )(*ins)


def per_device(populations, site_flags, neighbours, migrations, counts):
    sizes = (lax.axis_size("curve"), lax.axis_size("cross"))
    moves = migrations.T
    floats = lambda rows: pltpu.VMEM((rows, 128), jnp.float32)
    messages = [
        PLANES * 32 + 8,
        STRIPS + 2 * LAYERS,
        STRIPS + 2 * LAYERS,
        6 * GROUP,
        6 * GROUP,
        HALF,
    ]
    cells, up_msg, down_msg, up2_msg, down2_msg, inner_msg = call(
        functools.partial(pack_kernel, sizes[1]),
        "HHHHH",
        "HHHHHH",
        [rows128(rows) for rows in messages],
        (moves, counts, populations, site_flags, neighbours),
        [
            pltpu.SMEM(moves.shape, jnp.int32),
            pltpu.SMEM(counts.shape, jnp.int32),
            pltpu.VMEM(populations.shape, jnp.float32),
            pltpu.VMEM(site_flags.shape, jnp.int32),
            pltpu.VMEM(neighbours.shape, jnp.int32),
            *[floats(rows) for rows in messages],
            pltpu.VMEM((8, 5888), jnp.float32),
            pltpu.VMEM((128, 384), jnp.bfloat16),
            floats(256),
            floats(8),
            pltpu.SemaphoreType.DMA((4 + SLOTS + 6,)),
        ],
        WIDE_LIMIT,
    )
    low_msg = shifted_from(up_msg, "curve", 1)
    high_msg = shifted_from(down_msg, "curve", -1)
    low2_msg = shifted_from(up2_msg, "curve", 2)
    high2_msg = shifted_from(down2_msg, "curve", -2)
    low_inner = shifted_from(inner_msg, "curve", 1)
    high_inner = shifted_from(inner_msg, "curve", -1)
    post, outer, own2, landings = call(
        functools.partial(spread_kernel, *sizes),
        "SVVV",
        "VVVV",
        [
            rows128(NOWHERE + SLOT),
            rows128(PLANES * GROUP + 8),
            rows128(12 * GROUP),
            jax.ShapeDtypeStruct((8, 128), jnp.int32),
        ],
        (moves, cells, up2_msg, down2_msg),
        [],
    )
    strips = (low_msg, high_msg, low2_msg, high2_msg, own2)
    north_msg, south_msg = call(
        edge_kernel,
        "SVVVVVV",
        "VV",
        [rows128(PAIRS * GROUP + 24), rows128(PAIRS * GROUP + 24)],
        (landings, outer, *strips),
        [floats(PLANES * GROUP)],
    )
    from_south = shifted_from(north_msg, "cross", 1)
    from_north = shifted_from(south_msg, "cross", -1)
    post, table, next_outer = call(
        widen_kernel,
        "SVVVVVVVVV",
        "VVV",
        [
            rows128(NOWHERE + SLOT),
            jax.ShapeDtypeStruct((72, 128), jnp.int32),
            rows128(SLOTS * POPS * GROUP),
        ],
        (landings, post, outer, *strips, from_south, from_north),
        [
            floats(SLOTS * SLOT),
            pltpu.SMEM((72, 128), jnp.int32),
            pltpu.SemaphoreType.DMA,
        ],
    )
    return call(
        steps_kernel,
        "SSVVVV",
        "H",
        [jax.ShapeDtypeStruct(populations.shape, jnp.float32)],
        (landings, table, post, next_outer, low_inner, high_inner),
        [
            floats(SLOTS * SLOT),
            floats(NOWHERE + SLOT),
            pltpu.VMEM(populations.shape, jnp.float32),
            pltpu.SemaphoreType.DMA((SLOTS,)),
        ],
    )[0]


def solution(mesh):
    return jax.shard_map(
        per_device,
        mesh=mesh,
        in_specs=(
            P(("curve", "cross"), None, None),
            P(("curve", "cross"), None),
            P(("curve", "cross"), None),
            P(),
            P(("curve", "cross")),
        ),
        out_specs=P(("curve", "cross"), None, None),
        check_vma=False,
    )
```

```python
import functools

import jax
import jax.numpy as jnp
import numpy as np
from jax import lax
from jax.experimental import pallas as pl
from jax.experimental.pallas import tpu as pltpu
from jax.sharding import PartitionSpec as P

EDGE = 16
STEPS = 3
SLOTS = 3
POPS = 19
PLANES = SLOTS * POPS + SLOTS
FLAG0 = SLOTS * POPS
GROUP = 24
PLANE = 3 * GROUP
SLOT = POPS * PLANE
OUTWARD = SLOTS * 5 + SLOTS
LAYERS = 2 * PLANES + OUTWARD
HALF = POPS * EDGE
PAIRS = PLANES // 2
TABLE = HALF
STRIPS = HALF + 8
EDGE_TABLE = PAIRS * GROUP
NOWHERE = PLANES * PLANE
LIMIT = 20 * 1024 * 1024
WIDE_LIMIT = 127 * 512 * 1024

VELOCITY = [
    (0, 0, 0),
    (1, 0, 0),
    (-1, 0, 0),
    (0, 1, 0),
    (0, -1, 0),
    (0, 0, 1),
    (0, 0, -1),
    (1, 1, 0),
    (-1, -1, 0),
    (1, -1, 0),
    (-1, 1, 0),
    (1, 0, 1),
    (-1, 0, -1),
    (1, 0, -1),
    (-1, 0, 1),
    (0, 1, 1),
    (0, -1, -1),
    (0, 1, -1),
    (0, -1, 1),
]
OPPOSITE = [0, 2, 1, 4, 3, 6, 5, 8, 7, 10, 9, 12, 11, 14, 13, 16, 15, 18, 17]


def lanes_iota():
    return lax.broadcasted_iota(jnp.int32, (8, 128), 1)


def rows_iota():
    return lax.broadcasted_iota(jnp.int32, (8, 128), 0)


def aligned(start, size=8):
    return pl.ds(pl.multiple_of(start, 8), size)


def move_slots(moves, curve_size, cross_size):
    curve, cross = lax.axis_index("curve"), lax.axis_index("cross")

    def landed(source, target):
        inside = (source >= 0) & (source < curve_size) & (target >= 0) & (target < curve_size)
        row = jnp.clip(source, 0, curve_size - 1) * cross_size + cross
        rank = target * cross_size + cross
        hit = inside & (moves[0, row] >= 0) & (moves[1, row] == rank)
        return jnp.where(hit, moves[2, row], -1)

    return (
        landed(curve - 1, curve),
        landed(curve + 1, curve),
        landed(curve - 2, curve - 1),
        landed(curve, curve - 1),
        landed(curve + 2, curve + 1),
        landed(curve, curve + 1),
    )


def pack_kernel(
    cross_size,
    moves_hbm,
    counts_hbm,
    pops_hbm,
    flags_hbm,
    neighbours_hbm,
    cells_hbm,
    up_hbm,
    down_hbm,
    up2_hbm,
    down2_hbm,
    inner_hbm,
    moves,
    counts,
    pops,
    flags,
    neighbours,
    cells,
    up_msg,
    down_msg,
    up2_msg,
    down2_msg,
    inner_msg,
    wide_flags,
    plane_flags,
    site_flags,
    near,
    sems,
):
    started = []

    def copy(source, target):
        one = pltpu.make_async_copy(source, target, sems.at[len(started)])
        one.start()
        started.append(one)
        return one

    flags_copy = copy(flags_hbm, flags)
    copies = [copy(pops_hbm.at[s], pops.at[s]) for s in range(SLOTS)]
    small = [
        copy(neighbours_hbm, neighbours),
        copy(counts_hbm, counts),
        copy(moves_hbm, moves),
    ]
    for one in small:
        one.wait()

    near[...] = jnp.zeros_like(near)
    named = neighbours[...]
    slot = jnp.where(named >= 0, lax.rem(jnp.maximum(named, 0), SLOTS), SLOTS)
    near[0:SLOTS, 0 : named.shape[1]] = slot.astype(jnp.float32)
    for ref, row in ((cells, PLANES * 32), (up_msg, TABLE), (down_msg, TABLE)):
        ref[row : row + 8, :] = near[...]

    wide_flags[...] = jnp.zeros_like(wide_flags)
    flags_copy.wait()
    wide_flags[0:SLOTS, 0 : flags.shape[1]] = flags[...].astype(jnp.float32)
    span = EDGE + 2
    for x in range(EDGE):
        start = (x + 1) * span * span
        base = start // 128 * 128
        window = wide_flags[:, base : base + 512]
        window = pltpu.roll(window, (512 - (start - base)) % 512, axis=1)
        plane_flags[8 * x : 8 * x + 8, :] = window[:, :384].astype(jnp.bfloat16)
    lane_in = lax.broadcasted_iota(jnp.int32, (384, 256), 0)
    site = lax.broadcasted_iota(jnp.int32, (384, 256), 1)
    chosen = lane_in == (site // EDGE + 1) * span + site % EDGE + 1
    product = jnp.dot(
        plane_flags[...],
        jnp.where(chosen, 1.0, 0.0).astype(jnp.bfloat16),
        preferred_element_type=jnp.float32,
    )
    site_flags[0:128, :] = product[:, :128]
    site_flags[128:256, :] = product[:, 128:]
    for s in range(SLOTS):
        live = s < counts[0]
        for y in range(2):
            piece = site_flags[pl.ds(128 * y + s, EDGE, stride=8), :]
            is_fluid = (piece == 1.0) & live
            row = (FLAG0 + s) * 32 + y * EDGE
            cells[row : row + EDGE, :] = jnp.where(is_fluid, 1.0, 0.0)

    for s in range(SLOTS):
        copies[s].wait()
        for x in range(EDGE):
            for y in range(2):
                tile = 2 * x + y
                for p, size in ((0, 8), (8, 8), (16, 3)):
                    row = (s * POPS + p) * 32 + y * EDGE + x
                    cells[pl.ds(row, size, stride=32), :] = pops[
                        s, p : p + size, 128 * tile : 128 * tile + 128
                    ]

    @pl.loop(0, SLOTS)
    def _(s):
        @pl.loop(0, 4, unroll=2)
        def _(c):
            base = s * (POPS * 32) + c * 8
            h = [cells[aligned(base + p * 32), :] for p in range(POPS)]
            for p, value in enumerate(collided(h, True)):
                cells[aligned(base + p * 32), :] = value

    cells_copy = copy(cells, cells_hbm)

    for y in range(2):
        for msg, x0, first in ((up_msg, 15, 1), (down_msg, 0, 2)):
            step = -1 if x0 else 1
            for k in range(2):
                out = STRIPS + y * LAYERS + k * PLANES
                msg[out : out + PLANES, :] = cells[
                    pl.ds(y * EDGE + x0 + step * k, PLANES, stride=32), :
                ]
            row = y * EDGE + x0 + 2 * step
            out = STRIPS + y * LAYERS + 2 * PLANES
            for s in range(SLOTS):
                base = s * POPS * 32 + row
                msg[out + 5 * s : out + 5 * s + 1, :] = cells[pl.ds(base + first * 32, 1), :]
                msg[out + 5 * s + 1 : out + 5 * s + 5, :] = cells[
                    pl.ds(base + (first + 6) * 32, 4, stride=64), :
                ]
            msg[out + 5 * SLOTS : out + OUTWARD, :] = cells[
                pl.ds(FLAG0 * 32 + row, SLOTS, stride=32), :
            ]

    here = lax.axis_index("curve") * cross_size + lax.axis_index("cross")
    leaving = jnp.maximum(moves[0, here], 0)
    low = lanes_iota() < 64
    for p in range(POPS):
        for v in range(2):
            base = leaving * (POPS * 32) + p * 32 + v * 8
            first = cells[aligned(base), :]
            second = cells[aligned(base + EDGE), :]
            outer = jnp.where(low, first, second)
            row = p * EDGE + v * 8
            up_msg[row : row + 8, :] = outer
            down_msg[row : row + 8, :] = outer
            inner_msg[row : row + 8, :] = jnp.where(low, second, first)
    for s in range(SLOTS):

        @pl.when(leaving == s)
        def _():
            for y in range(2):
                for k in range(3):
                    out = (y * 3 + k) * GROUP
                    row = s * POPS * 32 + y * EDGE + k
                    up2_msg[out : out + POPS, :] = cells[pl.ds(row + 13, POPS, stride=32), :]
                    down2_msg[out : out + POPS, :] = cells[pl.ds(row, POPS, stride=32), :]

    last = [
        copy(up_msg, up_hbm),
        copy(down_msg, down_hbm),
        copy(up2_msg, up2_hbm),
        copy(down2_msg, down2_hbm),
        copy(inner_msg, inner_hbm),
    ]
    cells_copy.wait()
    for one in last:
        one.wait()


def spread_kernel(
    curve_size, cross_size, moves, cells, up2_msg, down2_msg, post, outer, own2, landings
):
    low = lanes_iota() < 64
    own2[0 : 6 * GROUP, :] = up2_msg[...]
    own2[6 * GROUP :, :] = down2_msg[...]
    for i, slot in enumerate(move_slots(moves, curve_size, cross_size)):
        landings[i : i + 1, :] = jnp.full((1, 128), slot, jnp.int32)
    post[NOWHERE:, :] = jnp.full((SLOT, 128), jnp.nan, jnp.float32)
    for q in range(PLANES):
        for v in range(2):
            row = q * 32 + v * 8
            first, second = cells[row : row + 8, :], cells[row + EDGE : row + EDGE + 8, :]
            row = q * PLANE + v * 8
            post[row : row + 8, :] = first
            post[row + GROUP : row + GROUP + 8, :] = second
            row = q * GROUP + v * 8
            outer[row : row + 8, :] = jnp.where(low, first, second)
    outer[PLANES * GROUP :, :] = cells[PLANES * 32 :, :]


def strip_rows(first, row0, step):
    pieces = []
    for k in range(2):
        pieces.append(
            (PLANES, lambda size, row: pl.ds(row, PLANES, stride=size), row0 + step * k, STRIPS + k * PLANES)
        )
    row, source = row0 + 2 * step, STRIPS + 2 * PLANES
    for s in range(SLOTS):
        plane = s * POPS + first
        pieces.append((1, lambda size, row, plane=plane: pl.ds(plane * size + row, 1), row, source))
        pieces.append(
            (
                4,
                lambda size, row, plane=plane: pl.ds(
                    (plane + 6) * size + row, 4, stride=2 * size
                ),
                row,
                source + 1,
            )
        )
        source += 5
    pieces.append(
        (SLOTS, lambda size, row: pl.ds(FLAG0 * size + row, SLOTS, stride=size), row, source)
    )
    return pieces


def edge_kernel(
    landings,
    own_outer,
    low_msg,
    high_msg,
    low2_msg,
    high2_msg,
    own2,
    mate_inner,
    north_msg,
    south_msg,
    outer,
):
    from_low, from_high, low_low, low_me, high_high, high_me = (landings[i, 0] for i in range(6))
    low = lanes_iota() < 64
    for q in range(PLANES):
        for v in range(2):
            row = q * GROUP + v * 8
            outer[row : row + 8, :] = own_outer[row : row + 8, :]

    def both(first, second):
        lane = lax.broadcasted_iota(jnp.int32, first.shape, 1)
        return jnp.where(lane < 64, first, second)

    for msg, row0, step, first in ((high_msg, 16, 1, 2), (low_msg, 23, -1, 1)):
        for count, planes, row, source in strip_rows(first, row0, step):
            outer[planes(GROUP, row), :] = both(
                msg[source : source + count, :],
                msg[LAYERS + source : LAYERS + source + count, :],
            )
    for slot, msg in ((from_low, low_msg), (from_high, high_msg)):

        @pl.when(slot >= 0)
        def _():
            for p in range(POPS):
                for v in range(2):
                    row = p * EDGE + v * 8
                    base = slot * (POPS * GROUP) + p * GROUP + v * 8
                    outer[aligned(base), :] = msg[row : row + 8, :]

    for s in range(SLOTS):
        for slot, msg, row0 in (
            (low_low, low2_msg, 21),
            (low_me, own2, 21),
            (high_high, high2_msg, 16),
            (high_me, own2.at[6 * GROUP :], 16),
        ):

            @pl.when(slot == s)
            def _():
                for k in range(3):
                    outer[pl.ds(s * POPS * GROUP + row0 + k, POPS, stride=GROUP), :] = both(
                        msg[k * GROUP : k * GROUP + POPS, :],
                        msg[(3 + k) * GROUP : (3 + k) * GROUP + POPS, :],
                    )

    for pair in range(PAIRS):
        for v in range(3):
            row = 2 * pair * GROUP + v * 8
            first = outer[row : row + 8, :]
            second = pltpu.roll(outer[row + GROUP : row + GROUP + 8, :], 64, axis=1)
            out = pair * GROUP + v * 8
            north_msg[out : out + 8, :] = jnp.where(low, second, first)
            south_msg[out : out + 8, :] = jnp.where(low, first, second)
    tables = (low_msg, TABLE), (own_outer, PLANES * GROUP), (high_msg, TABLE)
    for i, (ref, row) in enumerate(tables):
        out = EDGE_TABLE + 8 * i
        north_msg[out : out + 8, :] = ref[row : row + 8, :]
        south_msg[out : out + 8, :] = ref[row : row + 8, :]


def collided(h, is_fluid):
    shear = 1.0 / 0.6
    rest = h[0]
    sx, dx = h[1] + h[2], h[1] - h[2]
    sy, dy = h[3] + h[4], h[3] - h[4]
    sz, dz = h[5] + h[6], h[5] - h[6]
    s7, d7 = h[7] + h[8], h[7] - h[8]
    s9, d9 = h[9] + h[10], h[9] - h[10]
    s11, d11 = h[11] + h[12], h[11] - h[12]
    s13, d13 = h[13] + h[14], h[13] - h[14]
    s15, d15 = h[15] + h[16], h[15] - h[16]
    s17, d17 = h[17] + h[18], h[17] - h[18]
    txy, txz, tyz = s7 + s9, s11 + s13, s15 + s17
    pxy, pxz, pyz = s7 - s9, s11 - s13, s15 - s17
    ax, bx = d7 + d9, d11 + d13
    ay, by = d7 - d9, d15 + d17
    az, bz = d11 - d13, d15 - d17
    axes = sx + sy + sz
    diags = txy + txz + tyz
    rho = rest * (1.0 / 3.0) + axes * (1.0 / 18.0) + diags * (1.0 / 36.0)
    fx, fy, fz = ax + bx, ay + by, az + bz
    jx = dx * (1.0 / 18.0) + fx * (1.0 / 36.0)
    jy = dy * (1.0 / 18.0) + fy * (1.0 / 36.0)
    jz = dz * (1.0 / 18.0) + fz * (1.0 / 36.0)
    inverse = 1.0 / jnp.where(is_fluid, rho, 1.0)
    ux, uy, uz = jx * inverse, jy * inverse, jz * inverse
    qxx, qyy, qzz = jx * ux, jy * uy, jz * uz
    total = qxx + qyy + qzz

    energy = -10.0 * rest - axes * (11.0 / 18.0) + diags * (8.0 / 36.0)
    energy = (energy + 11.0 * rho - 19.0 * total) * (1.19 / 2394.0)
    square = 4.0 * rest - axes * (4.0 / 18.0) + diags * (1.0 / 36.0)
    square = (square - 3.0 * rho + 5.5 * total) * (1.4 / 252.0)
    axis_x = (3.0 * sx - axes) * (1.0 / 18.0)
    diag_x = (diags - 3.0 * tyz) * (1.0 / 36.0)
    want_x = 3.0 * qxx - total
    stress_x = (axis_x + diag_x - want_x) * (shear / 36.0)
    third_x = (diag_x - 2.0 * axis_x + 0.5 * want_x) * (1.4 / 72.0)
    axis_w = (sy - sz) * (1.0 / 18.0)
    diag_w = (txy - txz) * (1.0 / 36.0)
    want_w = qyy - qzz
    stress_w = (axis_w + diag_w - want_w) * (shear / 12.0)
    third_w = (diag_w - 2.0 * axis_w + 0.5 * want_w) * (1.4 / 24.0)

    rest_out = rest - 3.0 * (12.0 * square - 30.0 * energy)
    common = -18.0 * (11.0 * energy + 4.0 * square)
    along_x = 18.0 * (stress_x - 2.0 * third_x)
    along_w = 18.0 * (stress_w - 2.0 * third_w)
    ex = common + 2.0 * along_x
    ey = common - along_x + along_w
    ez = common - along_x - along_w
    common = 36.0 * (8.0 * energy + square)
    across_x = 36.0 * (stress_x + third_x)
    across_w = 36.0 * (stress_w + third_w)
    exy = common + across_x + across_w
    exz = common + across_x - across_w
    eyz = common - 2.0 * across_x
    cxy = shear * (0.25 * pxy - 9.0 * jx * uy)
    cxz = shear * (0.25 * pxz - 9.0 * jx * uz)
    cyz = shear * (0.25 * pyz - 9.0 * jy * uz)

    def flux(d, f, j):
        return (f * (1.0 / 36.0) - d * (4.0 / 18.0) + j * (2.0 / 3.0)) * (1.2 / 40.0)

    hx, hy, hz = flux(dx, fx, jx), flux(dy, fy, jy), flux(dz, fz, jz)
    mx = (ax - bx) * (1.98 / 8.0)
    my = (by - ay) * (1.98 / 8.0)
    mz = (az - bz) * (1.98 / 8.0)
    hx36, hy36, hz36 = 36.0 * hx, 36.0 * hy, 36.0 * hz
    xy_x, xz_x = hx36 + mx, hx36 - mx
    yz_y, xy_y = hy36 + my, hy36 - my
    xz_z, yz_z = hz36 + mz, hz36 - mz
    ox, oy, oz = -2.0 * hx36, -2.0 * hy36, -2.0 * hz36

    out = [rest_out]

    def pair(i, even, odd):
        out.append(h[i] - (even + odd))
        out.append(h[i + 1] - (even - odd))

    pair(1, ex, ox)
    pair(3, ey, oy)
    pair(5, ez, oz)
    pair(7, exy + cxy, xy_x + xy_y)
    pair(9, exy - cxy, xy_x - xy_y)
    pair(11, exz + cxz, xz_x + xz_z)
    pair(13, exz - cxz, xz_x - xz_z)
    pair(15, eyz + cyz, yz_y + yz_z)
    pair(17, eyz - cyz, yz_y - yz_z)
    return out


def fluid_at(post_ref, s, row):
    return post_ref[aligned((FLAG0 + s) * PLANE + row), :] > 0.0


def collide_all(h_ref, post_ref, put, chunks):
    @pl.loop(0, SLOTS)
    def _(s):
        @pl.loop(*chunks, unroll=3)
        def _(c):
            base = s * SLOT + c * 8
            is_fluid = fluid_at(post_ref, s, c * 8)
            h = [h_ref[aligned(base + p * PLANE), :] for p in range(POPS)]
            for p, value in enumerate(collided(h, is_fluid)):
                put(s, c, p, jnp.where(is_fluid, value, jnp.nan))


def hide_walls(post_ref):
    @pl.loop(0, SLOTS)
    def _(s):
        @pl.loop(0, PLANE // 8)
        def _(c):
            is_fluid = fluid_at(post_ref, s, c * 8)
            for p in range(POPS):
                place = aligned(s * SLOT + p * PLANE + c * 8)
                post_ref[place, :] = jnp.where(is_fluid, post_ref[place, :], jnp.nan)


def stream_all(post_ref, h_ref, table, groups, vregs, finish=None):
    lane = lanes_iota()
    row = rows_iota()
    low = lane < 64

    def one_slot(s):
        own = s * SLOT

        def shifted(pop, group, j, dy, dz):
            cx = VELOCITY[pop][0]

            def rows(start, v):
                return post_ref[aligned(start + pop * PLANE + group * GROUP + v * 8), :]

            def look(i, j, dx, v):
                if (dx, dy, dz) == (0, 0, 0):
                    return rows(own, v)
                if j is None:
                    return jnp.where(low, look(i, 1, dx, v), look(i, -1, dx, v))
                region = (i + 1) * 3 + j + 1
                return rows(table[region * 8 + s, VELOCITY.index((dx, dy, dz)) - 1], v)

            need_last = vregs == 3
            values = [look(0, j, 0, 0), look(0, j, 0, 1)]
            if need_last:
                if dy == 0 and dz == 0:
                    values.append(rows(own, 2))
                else:
                    values.append(jnp.where(row < 4, look(1, j, 0, 2), look(-1, j, 0, 2)))
            if cx == 0:
                return values
            turn = 1 if cx > 0 else 7
            rolled = [pltpu.roll(value, turn, axis=0) for value in values]
            if cx > 0:
                before = pltpu.roll(look(0, j, -1, 2), 1, axis=0)
                result = [
                    jnp.where(row == 0, before, rolled[0]),
                    jnp.where(row == 0, rolled[0], rolled[1]),
                ]
                if need_last:
                    edge = pltpu.roll(look(1, j, -1, 1), 1, axis=0)
                    result.append(jnp.where(row == 0, edge, rolled[2]))
                return result
            after = pltpu.roll(look(0, j, 1, 2), 7, axis=0)
            result = [
                jnp.where(row == 7, rolled[1], rolled[0]),
                jnp.where(row == 7, after, rolled[1]),
            ]
            if need_last:
                edge = pltpu.roll(look(-1, j, 1, 0), 7, axis=0)
                result.append(jnp.where(row == 7, edge, rolled[2]))
            return result

        for pop in range(POPS):
            cx, cy, cz = VELOCITY[pop]
            kept = {}

            def source(*key):
                if key not in kept:
                    kept[key] = shifted(pop, *key)
                return kept[key]

            def along_y(group, dz):
                values = source(group, None if group == 2 else 0, 0, dz)
                if cy == 0:
                    return values
                other = (group - cy) % 3
                if group != 2 and other != 2:
                    carried = source(other, 0, 0, dz)
                else:
                    carried = source(other, cy if group == 2 else 0, -cy, dz)
                mask = lane >= 112 if cy > 0 else lane < 16
                return [jnp.where(mask, b, a) for a, b in zip(values, carried)]

            for group in groups:
                values = along_y(group, 0)
                turn = (16 * cy + cz) % 128
                if turn:
                    values = [pltpu.roll(value, turn, axis=1) for value in values]
                if cz:
                    turn = (16 * cy - 15 * cz) % 128
                    wrapped = [pltpu.roll(value, turn, axis=1) for value in along_y(group, -cz)]
                    mask = lane % 16 == (0 if cz > 0 else 15)
                    values = [jnp.where(mask, b, a) for a, b in zip(values, wrapped)]
                for v, value in enumerate(values[:vregs]):
                    place = group * GROUP + v * 8
                    if pop:
                        back = post_ref[aligned(own + OPPOSITE[pop] * PLANE + place), :]
                        value = jnp.where(value != value, back, value)
                    is_fluid = fluid_at(post_ref, s, place)
                    h_ref[aligned(own + pop * PLANE + place), :] = jnp.where(is_fluid, value, 0.0)

    @pl.loop(0, SLOTS)
    def _(s):
        one_slot(s)
        if finish is not None:
            finish(s)


def widen_kernel(
    landings,
    own_post,
    own_outer,
    low_msg,
    high_msg,
    low2_msg,
    high2_msg,
    own2,
    south_msg,
    north_msg,
    post_ref,
    slots,
    next_outer,
    h_ref,
    table,
    sem,
):
    for i in range(3):
        for j, (ref, row) in enumerate(
            (
                (south_msg, EDGE_TABLE + 8 * i),
                ((low_msg, TABLE), (own_outer, PLANES * GROUP), (high_msg, TABLE))[i],
                (north_msg, EDGE_TABLE + 8 * i),
            )
        ):
            slot = ref[row : row + 8, :].astype(jnp.int32)
            region = 8 * (3 * i + j)
            slots[region : region + 8, :] = jnp.where(slot == SLOTS, NOWHERE, slot * SLOT)
    table_copy = pltpu.make_async_copy(slots, table, sem)
    table_copy.start()

    from_low, from_high, low_low, low_me, high_high, high_me = (landings[i, 0] for i in range(6))
    low = lanes_iota() < 64
    post_ref[...] = own_post[...]
    for slot, msg in ((from_low, low_msg), (from_high, high_msg)):

        @pl.when(slot >= 0)
        def _():
            for p in range(POPS):
                for v in range(2):
                    row = p * EDGE + v * 8
                    value = msg[row : row + 8, :]
                    start = slot * SLOT + p * PLANE + v * 8
                    post_ref[aligned(start), :] = value
                    post_ref[aligned(start + GROUP), :] = value

    for msg, row0, step, first in ((high_msg, 16, 1, 2), (low_msg, 23, -1, 1)):
        for y in range(2):
            for count, planes, row, source in strip_rows(first, row0, step):
                source += y * LAYERS
                post_ref[planes(PLANE, row + y * GROUP), :] = msg[source : source + count, :]
    for s in range(SLOTS):
        for slot, msg, row0 in (
            (low_low, low2_msg, 21),
            (low_me, own2, 21),
            (high_high, high2_msg, 16),
            (high_me, own2.at[6 * GROUP :], 16),
        ):

            @pl.when(slot == s)
            def _():
                for y in range(2):
                    for k in range(3):
                        row = s * SLOT + y * GROUP + row0 + k
                        source = (y * 3 + k) * GROUP
                        post_ref[pl.ds(row, POPS, stride=PLANE), :] = msg[
                            source : source + POPS, :
                        ]

    for pair in range(PAIRS):
        for v in range(3):
            row = pair * GROUP + v * 8
            south, north = south_msg[row : row + 8, :], north_msg[row : row + 8, :]
            row = 2 * pair * PLANE + 2 * GROUP + v * 8
            post_ref[row : row + 8, :] = jnp.where(low, north, south)
            post_ref[row + PLANE : row + PLANE + 8, :] = pltpu.roll(
                jnp.where(low, south, north), 64, axis=1
            )

    hide_walls(post_ref)
    table_copy.wait()
    stream_all(post_ref, h_ref, table, (2,), 3)

    def put(s, c, p, value):
        next_outer[aligned(s * (POPS * GROUP) + p * GROUP + (c - 6) * 8), :] = value

    collide_all(h_ref, post_ref, put, (6, 9))


def steps_kernel(
    landings,
    table,
    wide_post,
    next_outer,
    mate_inner,
    passed_inner,
    out_hbm,
    h_ref,
    post_ref,
    out,
    sems,
):
    low = lanes_iota() < 64
    post_ref[...] = wide_post[...]
    odd = lax.rem(lax.axis_index("curve"), 2) == 1
    even = jnp.logical_not(odd)
    for slot, wanted, inner in (
        (landings[0, 0], odd, mate_inner),
        (landings[0, 0], even, passed_inner),
        (landings[1, 0], even, mate_inner),
        (landings[1, 0], odd, passed_inner),
    ):

        @pl.when((slot >= 0) & wanted)
        def _():
            for v in range(2):
                fluid = [fluid_at(post_ref, slot, y * GROUP + v * 8) for y in range(2)]
                for p in range(POPS):
                    row = p * EDGE + v * 8
                    value = inner[row : row + 8, :]
                    for y in range(2):
                        start = aligned(slot * SLOT + p * PLANE + y * GROUP + v * 8)
                        is_here = low if y else jnp.logical_not(low)
                        hidden = jnp.where(fluid[y], value, jnp.nan)
                        post_ref[start, :] = jnp.where(is_here, hidden, post_ref[start, :])

    def finish(s):
        for x in range(EDGE):
            for y in range(2):
                tile = 2 * x + y
                for p, size in ((0, 8), (8, 8), (16, 3)):
                    row = s * SLOT + (p * PLANE + y * GROUP + x)
                    out[s, p : p + size, 128 * tile : 128 * tile + 128] = h_ref[
                        pl.ds(row, size, stride=PLANE), :
                    ]
        pltpu.make_async_copy(out.at[s], out_hbm.at[s], sems.at[s]).start()

    def put(s, c, p, value):
        post_ref[aligned(s * SLOT + p * PLANE + c * 8), :] = value

    stream_all(post_ref, h_ref, table, (0, 1), 3)
    collide_all(h_ref, post_ref, put, (0, 6))
    for q in range(SLOTS * POPS):
        row = q * PLANE + 2 * GROUP
        post_ref[row : row + GROUP, :] = next_outer[q * GROUP : (q + 1) * GROUP, :]
    for _ in range(STEPS - 2):
        stream_all(post_ref, h_ref, table, (0, 1, 2), 3)
        collide_all(h_ref, post_ref, put, (0, 9))
    stream_all(post_ref, h_ref, table, (0, 1), 2, finish)
    for s in range(SLOTS):
        pltpu.make_async_copy(out.at[s], out_hbm.at[s], sems.at[s]).wait()


def shifted_from(value, axis, step):
    count = lax.axis_size(axis)
    pairs = [(i, i + step) for i in range(count) if 0 <= i + step < count]
    return lax.ppermute(value, axis, pairs)


def rows128(count):
    return jax.ShapeDtypeStruct((count, 128), jnp.float32)


def call(kernel, in_spaces, out_spaces, outs, ins, scratch, limit=LIMIT):
    spaces = {
        "S": pl.BlockSpec(memory_space=pltpu.SMEM),
        "V": pl.BlockSpec(memory_space=pltpu.VMEM),
        "H": pl.BlockSpec(memory_space=pltpu.HBM),
    }
    return pl.pallas_call(
        kernel,
        out_shape=outs,
        in_specs=[spaces[x] for x in in_spaces],
        out_specs=[spaces[x] for x in out_spaces],
        scratch_shapes=scratch,
        compiler_params=pltpu.CompilerParams(vmem_limit_bytes=limit),
    )(*ins)


def per_device(populations, site_flags, neighbours, migrations, counts):
    sizes = (lax.axis_size("curve"), lax.axis_size("cross"))
    moves = migrations.T
    floats = lambda rows: pltpu.VMEM((rows, 128), jnp.float32)
    messages = [
        PLANES * 32 + 8,
        STRIPS + 2 * LAYERS,
        STRIPS + 2 * LAYERS,
        6 * GROUP,
        6 * GROUP,
        HALF,
    ]
    cells, up_msg, down_msg, up2_msg, down2_msg, inner_msg = call(
        functools.partial(pack_kernel, sizes[1]),
        "HHHHH",
        "HHHHHH",
        [rows128(rows) for rows in messages],
        (moves, counts, populations, site_flags, neighbours),
        [
            pltpu.SMEM(moves.shape, jnp.int32),
            pltpu.SMEM(counts.shape, jnp.int32),
            pltpu.VMEM(populations.shape, jnp.float32),
            pltpu.VMEM(site_flags.shape, jnp.int32),
            pltpu.VMEM(neighbours.shape, jnp.int32),
            *[floats(rows) for rows in messages],
            pltpu.VMEM((8, 5888), jnp.float32),
            pltpu.VMEM((128, 384), jnp.bfloat16),
            floats(256),
            floats(8),
            pltpu.SemaphoreType.DMA((4 + SLOTS + 6,)),
        ],
        WIDE_LIMIT,
    )
    low_msg = shifted_from(up_msg, "curve", 1)
    high_msg = shifted_from(down_msg, "curve", -1)
    low2_msg = shifted_from(up2_msg, "curve", 2)
    high2_msg = shifted_from(down2_msg, "curve", -2)
    assert sizes[0] % 2 == 0
    pairs = [(i, i ^ 1) for i in range(sizes[0])]
    mate_inner = lax.ppermute(inner_msg, "curve", pairs)
    pairs = [(i, i - 2 if i % 2 else i + 2) for i in range(sizes[0])]
    pairs = [pair for pair in pairs if 0 <= pair[1] < sizes[0]]
    passed_inner = lax.ppermute(mate_inner, "curve", pairs)
    post, outer, own2, landings = call(
        functools.partial(spread_kernel, *sizes),
        "SVVV",
        "VVVV",
        [
            rows128(NOWHERE + SLOT),
            rows128(PLANES * GROUP + 8),
            rows128(12 * GROUP),
            jax.ShapeDtypeStruct((8, 128), jnp.int32),
        ],
        (moves, cells, up2_msg, down2_msg),
        [],
    )
    strips = (low_msg, high_msg, low2_msg, high2_msg, own2)
    north_msg, south_msg = call(
        edge_kernel,
        "SVVVVVVV",
        "VV",
        [rows128(PAIRS * GROUP + 24), rows128(PAIRS * GROUP + 24)],
        (landings, outer, *strips, mate_inner),
        [floats(PLANES * GROUP)],
    )
    from_south = shifted_from(north_msg, "cross", 1)
    from_north = shifted_from(south_msg, "cross", -1)
    post, table, next_outer = call(
        widen_kernel,
        "SVVVVVVVVV",
        "VVV",
        [
            rows128(NOWHERE + SLOT),
            jax.ShapeDtypeStruct((72, 128), jnp.int32),
            rows128(SLOTS * POPS * GROUP),
        ],
        (landings, post, outer, *strips, from_south, from_north),
        [
            floats(SLOTS * SLOT),
            pltpu.SMEM((72, 128), jnp.int32),
            pltpu.SemaphoreType.DMA,
        ],
    )
    return call(
        steps_kernel,
        "SSVVVV",
        "H",
        [jax.ShapeDtypeStruct(populations.shape, jnp.float32)],
        (landings, table, post, next_outer, mate_inner, passed_inner),
        [
            floats(SLOTS * SLOT),
            floats(NOWHERE + SLOT),
            pltpu.VMEM(populations.shape, jnp.float32),
            pltpu.SemaphoreType.DMA((SLOTS,)),
        ],
    )[0]


def solution(mesh):
    return jax.shard_map(
        per_device,
        mesh=mesh,
        in_specs=(
            P(("curve", "cross"), None, None),
            P(("curve", "cross"), None),
            P(("curve", "cross"), None),
            P(),
            P(("curve", "cross")),
        ),
        out_specs=P(("curve", "cross"), None, None),
        check_vma=False,
    )
```

```python
import functools

import jax
import jax.numpy as jnp
import numpy as np
from jax import lax
from jax.experimental import pallas as pl
from jax.experimental.pallas import tpu as pltpu
from jax.sharding import PartitionSpec as P

EDGE = 16
STEPS = 3
SLOTS = 3
POPS = 19
PLANES = SLOTS * POPS + SLOTS
FLAG0 = SLOTS * POPS
GROUP = 24
PLANE = 3 * GROUP
SLOT = POPS * PLANE
OUTWARD = SLOTS * 5 + SLOTS
LAYERS = 2 * PLANES + OUTWARD
HALF = POPS * EDGE
QUADS = PLANES // 4
TABLE = HALF
STRIPS = HALF + 8
FAR = QUADS * GROUP
EDGE_TABLE = FAR + 3 * GROUP
EDGE_ROWS = EDGE_TABLE + 24
NOWHERE = PLANES * PLANE
LIMIT = 20 * 1024 * 1024
WIDE_LIMIT = 127 * 512 * 1024

VELOCITY = [
    (0, 0, 0),
    (1, 0, 0),
    (-1, 0, 0),
    (0, 1, 0),
    (0, -1, 0),
    (0, 0, 1),
    (0, 0, -1),
    (1, 1, 0),
    (-1, -1, 0),
    (1, -1, 0),
    (-1, 1, 0),
    (1, 0, 1),
    (-1, 0, -1),
    (1, 0, -1),
    (-1, 0, 1),
    (0, 1, 1),
    (0, -1, -1),
    (0, 1, -1),
    (0, -1, 1),
]
NORTHWARD, SOUTHWARD = (
    [s * POPS + p for s in range(SLOTS) for p in range(POPS) if VELOCITY[p][1] == side]
    + [FLAG0 + s for s in range(SLOTS)]
    for side in (1, -1)
)
OPPOSITE = [0, 2, 1, 4, 3, 6, 5, 8, 7, 10, 9, 12, 11, 14, 13, 16, 15, 18, 17]


def lanes_iota():
    return lax.broadcasted_iota(jnp.int32, (8, 128), 1)


def is_even(axis, unit=1):
    return lax.rem(lax.axis_index(axis) // unit, 2) == 0


def rows_iota():
    return lax.broadcasted_iota(jnp.int32, (8, 128), 0)


def aligned(start, size=8):
    return pl.ds(pl.multiple_of(start, 8), size)


def move_slots(moves, curve_size, cross_size):
    curve, cross = lax.axis_index("curve"), lax.axis_index("cross")

    def landed(source, target):
        inside = (source >= 0) & (source < curve_size) & (target >= 0) & (target < curve_size)
        row = jnp.clip(source, 0, curve_size - 1) * cross_size + cross
        rank = target * cross_size + cross
        hit = inside & (moves[0, row] >= 0) & (moves[1, row] == rank)
        return jnp.where(hit, moves[2, row], -1)

    return (
        landed(curve - 1, curve),
        landed(curve + 1, curve),
        landed(curve - 2, curve - 1),
        landed(curve, curve - 1),
        landed(curve + 2, curve + 1),
        landed(curve, curve + 1),
    )


def pack_kernel(
    cross_size,
    moves_hbm,
    counts_hbm,
    pops_hbm,
    flags_hbm,
    neighbours_hbm,
    cells_hbm,
    mate_hbm,
    other_hbm,
    mate2_hbm,
    other2_hbm,
    up2_hbm,
    down2_hbm,
    inner_hbm,
    moves,
    counts,
    pops,
    flags,
    neighbours,
    cells,
    up_msg,
    down_msg,
    up2_msg,
    down2_msg,
    inner_msg,
    wide_flags,
    plane_flags,
    site_flags,
    near,
    sems,
):
    started = []

    def copy(source, target):
        one = pltpu.make_async_copy(source, target, sems.at[len(started)])
        one.start()
        started.append(one)
        return one

    flags_copy = copy(flags_hbm, flags)
    copies = [copy(pops_hbm.at[s], pops.at[s]) for s in range(SLOTS)]
    small = [
        copy(neighbours_hbm, neighbours),
        copy(counts_hbm, counts),
        copy(moves_hbm, moves),
    ]
    for one in small:
        one.wait()

    near[...] = jnp.zeros_like(near)
    named = neighbours[...]
    slot = jnp.where(named >= 0, lax.rem(jnp.maximum(named, 0), SLOTS), SLOTS)
    near[0:SLOTS, 0 : named.shape[1]] = slot.astype(jnp.float32)
    for ref, row in ((cells, PLANES * 32), (up_msg, TABLE), (down_msg, TABLE)):
        ref[row : row + 8, :] = near[...]

    wide_flags[...] = jnp.zeros_like(wide_flags)
    flags_copy.wait()
    wide_flags[0:SLOTS, 0 : flags.shape[1]] = flags[...].astype(jnp.float32)
    span = EDGE + 2
    for x in range(EDGE):
        start = (x + 1) * span * span
        base = start // 128 * 128
        window = wide_flags[:, base : base + 512]
        window = pltpu.roll(window, (512 - (start - base)) % 512, axis=1)
        plane_flags[8 * x : 8 * x + 8, :] = window[:, :384].astype(jnp.bfloat16)
    lane_in = lax.broadcasted_iota(jnp.int32, (384, 256), 0)
    site = lax.broadcasted_iota(jnp.int32, (384, 256), 1)
    chosen = lane_in == (site // EDGE + 1) * span + site % EDGE + 1
    product = jnp.dot(
        plane_flags[...],
        jnp.where(chosen, 1.0, 0.0).astype(jnp.bfloat16),
        preferred_element_type=jnp.float32,
    )
    site_flags[0:128, :] = product[:, :128]
    site_flags[128:256, :] = product[:, 128:]
    for s in range(SLOTS):
        live = s < counts[0]
        for y in range(2):
            piece = site_flags[pl.ds(128 * y + s, EDGE, stride=8), :]
            is_fluid = (piece == 1.0) & live
            row = (FLAG0 + s) * 32 + y * EDGE
            cells[row : row + EDGE, :] = jnp.where(is_fluid, 1.0, 0.0)

    for s in range(SLOTS):
        copies[s].wait()
        for x in range(EDGE):
            for y in range(2):
                tile = 2 * x + y
                for p, size in ((0, 8), (8, 8), (16, 3)):
                    row = (s * POPS + p) * 32 + y * EDGE + x
                    cells[pl.ds(row, size, stride=32), :] = pops[
                        s, p : p + size, 128 * tile : 128 * tile + 128
                    ]

    @pl.loop(0, SLOTS)
    def _(s):
        @pl.loop(0, 4, unroll=2)
        def _(c):
            base = s * (POPS * 32) + c * 8
            h = [cells[aligned(base + p * 32), :] for p in range(POPS)]
            for p, value in enumerate(collided(h, True)):
                cells[aligned(base + p * 32), :] = value

    cells_copy = copy(cells, cells_hbm)

    for y in range(2):
        for msg, x0, first in ((up_msg, 15, 1), (down_msg, 0, 2)):
            step = -1 if x0 else 1
            for k in range(2):
                out = STRIPS + y * LAYERS + k * PLANES
                msg[out : out + PLANES, :] = cells[
                    pl.ds(y * EDGE + x0 + step * k, PLANES, stride=32), :
                ]
            row = y * EDGE + x0 + 2 * step
            out = STRIPS + y * LAYERS + 2 * PLANES
            for s in range(SLOTS):
                base = s * POPS * 32 + row
                msg[out + 5 * s : out + 5 * s + 1, :] = cells[pl.ds(base + first * 32, 1), :]
                msg[out + 5 * s + 1 : out + 5 * s + 5, :] = cells[
                    pl.ds(base + (first + 6) * 32, 4, stride=64), :
                ]
            msg[out + 5 * SLOTS : out + OUTWARD, :] = cells[
                pl.ds(FLAG0 * 32 + row, SLOTS, stride=32), :
            ]

    here = lax.axis_index("curve") * cross_size + lax.axis_index("cross")
    leaving = jnp.maximum(moves[0, here], 0)
    low = lanes_iota() < 64
    for p in range(POPS):
        for v in range(2):
            base = leaving * (POPS * 32) + p * 32 + v * 8
            first = cells[aligned(base), :]
            second = cells[aligned(base + EDGE), :]
            outer = jnp.where(low, first, second)
            row = p * EDGE + v * 8
            up_msg[row : row + 8, :] = outer
            down_msg[row : row + 8, :] = outer
            inner_msg[row : row + 8, :] = jnp.where(low, second, first)
    for s in range(SLOTS):

        @pl.when(leaving == s)
        def _():
            for y in range(2):
                for k in range(3):
                    out = (y * 3 + k) * GROUP
                    row = s * POPS * 32 + y * EDGE + k
                    up2_msg[out : out + POPS, :] = cells[pl.ds(row + 13, POPS, stride=32), :]
                    down2_msg[out : out + POPS, :] = cells[pl.ds(row, POPS, stride=32), :]

    last = [copy(up2_msg, up2_hbm), copy(down2_msg, down2_hbm), copy(inner_msg, inner_hbm)]
    count = len(started)
    for i, (up, down, mate, other, unit) in enumerate(
        ((up_msg, down_msg, mate_hbm, other_hbm, 1), (up2_msg, down2_msg, mate2_hbm, other2_hbm, 2))
    ):
        first, second = sems.at[count + 2 * i], sems.at[count + 2 * i + 1]
        even = is_even("curve", unit)

        @pl.when(even)
        def _():
            pltpu.make_async_copy(up, mate, first).start()
            pltpu.make_async_copy(down, other, second).start()

        @pl.when(jnp.logical_not(even))
        def _():
            pltpu.make_async_copy(down, mate, first).start()
            pltpu.make_async_copy(up, other, second).start()

        last.append(pltpu.make_async_copy(up, mate, first))
        last.append(pltpu.make_async_copy(down, other, second))
    cells_copy.wait()
    for one in last:
        one.wait()


def spread_kernel(
    curve_size, cross_size, moves, cells, up2_msg, down2_msg, post, outer, own2, landings
):
    low = lanes_iota() < 64
    own2[0 : 6 * GROUP, :] = up2_msg[...]
    own2[6 * GROUP :, :] = down2_msg[...]
    for i, slot in enumerate(move_slots(moves, curve_size, cross_size)):
        landings[i : i + 1, :] = jnp.full((1, 128), slot, jnp.int32)
    post[NOWHERE:, :] = jnp.full((SLOT, 128), jnp.nan, jnp.float32)
    for q in range(PLANES):
        for v in range(2):
            row = q * 32 + v * 8
            first, second = cells[row : row + 8, :], cells[row + EDGE : row + EDGE + 8, :]
            row = q * PLANE + v * 8
            post[row : row + 8, :] = first
            post[row + GROUP : row + GROUP + 8, :] = second
            row = q * GROUP + v * 8
            outer[row : row + 8, :] = jnp.where(low, first, second)
    outer[PLANES * GROUP :, :] = cells[PLANES * 32 :, :]


def sort_messages(mate_msg, other_msg, mate2_msg, other2_msg, low_msg, high_msg, low2, high2):
    for mate, other, low, high, unit in (
        (mate_msg, other_msg, low_msg, high_msg, 1),
        (mate2_msg, other2_msg, low2, high2, 2),
    ):
        even = is_even("curve", unit)

        @pl.when(even)
        def _():
            low[...] = other[...]
            high[...] = mate[...]

        @pl.when(jnp.logical_not(even))
        def _():
            low[...] = mate[...]
            high[...] = other[...]


def sel4(parts, lane):
    first = jnp.where(lane < 32, parts[0], parts[1])
    second = jnp.where(lane < 96, parts[2], parts[3])
    return jnp.where(lane < 64, first, second)


def strip_rows(first, row0, step):
    pieces = []
    for k in range(2):
        pieces.append(
            (PLANES, lambda size, row: pl.ds(row, PLANES, stride=size), row0 + step * k, STRIPS + k * PLANES)
        )
    row, source = row0 + 2 * step, STRIPS + 2 * PLANES
    for s in range(SLOTS):
        plane = s * POPS + first
        pieces.append((1, lambda size, row, plane=plane: pl.ds(plane * size + row, 1), row, source))
        pieces.append(
            (
                4,
                lambda size, row, plane=plane: pl.ds(
                    (plane + 6) * size + row, 4, stride=2 * size
                ),
                row,
                source + 1,
            )
        )
        source += 5
    pieces.append(
        (SLOTS, lambda size, row: pl.ds(FLAG0 * size + row, SLOTS, stride=size), row, source)
    )
    return pieces


def edge_kernel(
    landings,
    own_outer,
    mate_msg,
    other_msg,
    mate2_msg,
    other2_msg,
    own2,
    near_msg,
    far_msg,
    outer,
    low_msg,
    high_msg,
    low2_msg,
    high2_msg,
):
    sort_messages(
        mate_msg, other_msg, mate2_msg, other2_msg, low_msg, high_msg, low2_msg, high2_msg
    )
    from_low, from_high, low_low, low_me, high_high, high_me = (landings[i, 0] for i in range(6))
    low = lanes_iota() < 64
    for q in range(PLANES):
        for v in range(2):
            row = q * GROUP + v * 8
            outer[row : row + 8, :] = own_outer[row : row + 8, :]

    def both(first, second):
        lane = lax.broadcasted_iota(jnp.int32, first.shape, 1)
        return jnp.where(lane < 64, first, second)

    for msg, row0, step, first in ((high_msg, 16, 1, 2), (low_msg, 23, -1, 1)):
        for count, planes, row, source in strip_rows(first, row0, step):
            outer[planes(GROUP, row), :] = both(
                msg[source : source + count, :],
                msg[LAYERS + source : LAYERS + source + count, :],
            )
    for slot, msg in ((from_low, low_msg), (from_high, high_msg)):

        @pl.when(slot >= 0)
        def _():
            for p in range(POPS):
                for v in range(2):
                    row = p * EDGE + v * 8
                    base = slot * (POPS * GROUP) + p * GROUP + v * 8
                    outer[aligned(base), :] = msg[row : row + 8, :]

    for s in range(SLOTS):
        for slot, msg, row0 in (
            (low_low, low2_msg, 21),
            (low_me, own2, 21),
            (high_high, high2_msg, 16),
            (high_me, own2.at[6 * GROUP :], 16),
        ):

            @pl.when(slot == s)
            def _():
                for k in range(3):
                    outer[pl.ds(s * POPS * GROUP + row0 + k, POPS, stride=GROUP), :] = both(
                        msg[k * GROUP : k * GROUP + POPS, :],
                        msg[(3 + k) * GROUP : (3 + k) * GROUP + POPS, :],
                    )

    even = is_even("cross")
    lane = lanes_iota()

    def send(row, north, south):
        near_msg[row : row + 8, :] = jnp.where(even, north, south)
        far_msg[row : row + 8, :] = jnp.where(even, south, north)

    for v in range(3):

        def plane(q):
            return outer[q * GROUP + v * 8 : q * GROUP + v * 8 + 8, :]

        for quad in range(QUADS):
            parts = [plane(4 * quad)]
            parts += [pltpu.roll(plane(4 * quad + k), 32 * k, axis=1) for k in (1, 2, 3)]
            send(quad * GROUP + v * 8, sel4(parts[1:] + parts[:1], lane), sel4(parts, lane))
        for part in range(3):
            values = []
            for planes, source in ((NORTHWARD, 80), (SOUTHWARD, 32)):
                value = None
                for k, q in enumerate(planes[8 * part : 8 * part + 8]):
                    moved = pltpu.roll(plane(q), (16 * k - source) % 128, axis=1)
                    value = moved if value is None else jnp.where(lane < 16 * k, value, moved)
                values.append(value)
            send(FAR + part * GROUP + v * 8, *values)
    tables = (low_msg, TABLE), (own_outer, PLANES * GROUP), (high_msg, TABLE)
    for i, (ref, row) in enumerate(tables):
        value = ref[row : row + 8, :]
        send(EDGE_TABLE + 8 * i, value, value)


def collided(h, is_fluid):
    shear = 1.0 / 0.6
    rest = h[0]
    sx, dx = h[1] + h[2], h[1] - h[2]
    sy, dy = h[3] + h[4], h[3] - h[4]
    sz, dz = h[5] + h[6], h[5] - h[6]
    s7, d7 = h[7] + h[8], h[7] - h[8]
    s9, d9 = h[9] + h[10], h[9] - h[10]
    s11, d11 = h[11] + h[12], h[11] - h[12]
    s13, d13 = h[13] + h[14], h[13] - h[14]
    s15, d15 = h[15] + h[16], h[15] - h[16]
    s17, d17 = h[17] + h[18], h[17] - h[18]
    txy, txz, tyz = s7 + s9, s11 + s13, s15 + s17
    pxy, pxz, pyz = s7 - s9, s11 - s13, s15 - s17
    ax, bx = d7 + d9, d11 + d13
    ay, by = d7 - d9, d15 + d17
    az, bz = d11 - d13, d15 - d17
    axes = sx + sy + sz
    diags = txy + txz + tyz
    rho = rest * (1.0 / 3.0) + axes * (1.0 / 18.0) + diags * (1.0 / 36.0)
    fx, fy, fz = ax + bx, ay + by, az + bz
    jx = dx * (1.0 / 18.0) + fx * (1.0 / 36.0)
    jy = dy * (1.0 / 18.0) + fy * (1.0 / 36.0)
    jz = dz * (1.0 / 18.0) + fz * (1.0 / 36.0)
    inverse = 1.0 / jnp.where(is_fluid, rho, 1.0)
    ux, uy, uz = jx * inverse, jy * inverse, jz * inverse
    qxx, qyy, qzz = jx * ux, jy * uy, jz * uz
    total = qxx + qyy + qzz

    energy = -10.0 * rest - axes * (11.0 / 18.0) + diags * (8.0 / 36.0)
    energy = (energy + 11.0 * rho - 19.0 * total) * (1.19 / 2394.0)
    square = 4.0 * rest - axes * (4.0 / 18.0) + diags * (1.0 / 36.0)
    square = (square - 3.0 * rho + 5.5 * total) * (1.4 / 252.0)
    axis_x = (3.0 * sx - axes) * (1.0 / 18.0)
    diag_x = (diags - 3.0 * tyz) * (1.0 / 36.0)
    want_x = 3.0 * qxx - total
    stress_x = (axis_x + diag_x - want_x) * (shear / 36.0)
    third_x = (diag_x - 2.0 * axis_x + 0.5 * want_x) * (1.4 / 72.0)
    axis_w = (sy - sz) * (1.0 / 18.0)
    diag_w = (txy - txz) * (1.0 / 36.0)
    want_w = qyy - qzz
    stress_w = (axis_w + diag_w - want_w) * (shear / 12.0)
    third_w = (diag_w - 2.0 * axis_w + 0.5 * want_w) * (1.4 / 24.0)

    rest_out = rest - 3.0 * (12.0 * square - 30.0 * energy)
    common = -18.0 * (11.0 * energy + 4.0 * square)
    along_x = 18.0 * (stress_x - 2.0 * third_x)
    along_w = 18.0 * (stress_w - 2.0 * third_w)
    ex = common + 2.0 * along_x
    ey = common - along_x + along_w
    ez = common - along_x - along_w
    common = 36.0 * (8.0 * energy + square)
    across_x = 36.0 * (stress_x + third_x)
    across_w = 36.0 * (stress_w + third_w)
    exy = common + across_x + across_w
    exz = common + across_x - across_w
    eyz = common - 2.0 * across_x
    cxy = shear * (0.25 * pxy - 9.0 * jx * uy)
    cxz = shear * (0.25 * pxz - 9.0 * jx * uz)
    cyz = shear * (0.25 * pyz - 9.0 * jy * uz)

    def flux(d, f, j):
        return (f * (1.0 / 36.0) - d * (4.0 / 18.0) + j * (2.0 / 3.0)) * (1.2 / 40.0)

    hx, hy, hz = flux(dx, fx, jx), flux(dy, fy, jy), flux(dz, fz, jz)
    mx = (ax - bx) * (1.98 / 8.0)
    my = (by - ay) * (1.98 / 8.0)
    mz = (az - bz) * (1.98 / 8.0)
    hx36, hy36, hz36 = 36.0 * hx, 36.0 * hy, 36.0 * hz
    xy_x, xz_x = hx36 + mx, hx36 - mx
    yz_y, xy_y = hy36 + my, hy36 - my
    xz_z, yz_z = hz36 + mz, hz36 - mz
    ox, oy, oz = -2.0 * hx36, -2.0 * hy36, -2.0 * hz36

    out = [rest_out]

    def pair(i, even, odd):
        out.append(h[i] - (even + odd))
        out.append(h[i + 1] - (even - odd))

    pair(1, ex, ox)
    pair(3, ey, oy)
    pair(5, ez, oz)
    pair(7, exy + cxy, xy_x + xy_y)
    pair(9, exy - cxy, xy_x - xy_y)
    pair(11, exz + cxz, xz_x + xz_z)
    pair(13, exz - cxz, xz_x - xz_z)
    pair(15, eyz + cyz, yz_y + yz_z)
    pair(17, eyz - cyz, yz_y - yz_z)
    return out


def fluid_at(post_ref, s, row):
    return post_ref[aligned((FLAG0 + s) * PLANE + row), :] > 0.0


def collide_all(h_ref, post_ref, put, chunks):
    @pl.loop(0, SLOTS)
    def _(s):
        @pl.loop(*chunks, unroll=3)
        def _(c):
            base = s * SLOT + c * 8
            is_fluid = fluid_at(post_ref, s, c * 8)
            h = [h_ref[aligned(base + p * PLANE), :] for p in range(POPS)]
            for p, value in enumerate(collided(h, is_fluid)):
                put(s, c, p, jnp.where(is_fluid, value, jnp.nan))


def hide_walls(post_ref):
    @pl.loop(0, SLOTS)
    def _(s):
        @pl.loop(0, PLANE // 8)
        def _(c):
            is_fluid = fluid_at(post_ref, s, c * 8)
            for p in range(POPS):
                place = aligned(s * SLOT + p * PLANE + c * 8)
                post_ref[place, :] = jnp.where(is_fluid, post_ref[place, :], jnp.nan)


def stream_all(post_ref, h_ref, table, groups, vregs, finish=None):
    lane = lanes_iota()
    row = rows_iota()
    low = lane < 64

    def one_slot(s):
        own = s * SLOT

        def shifted(pop, group, j, dy, dz):
            cx = VELOCITY[pop][0]

            def rows(start, v):
                return post_ref[aligned(start + pop * PLANE + group * GROUP + v * 8), :]

            def look(i, j, dx, v):
                if (dx, dy, dz) == (0, 0, 0):
                    return rows(own, v)
                if j is None:
                    return jnp.where(low, look(i, 1, dx, v), look(i, -1, dx, v))
                region = (i + 1) * 3 + j + 1
                return rows(table[region * 8 + s, VELOCITY.index((dx, dy, dz)) - 1], v)

            need_last = vregs == 3
            values = [look(0, j, 0, 0), look(0, j, 0, 1)]
            if need_last:
                if dy == 0 and dz == 0:
                    values.append(rows(own, 2))
                else:
                    values.append(jnp.where(row < 4, look(1, j, 0, 2), look(-1, j, 0, 2)))
            if cx == 0:
                return values
            turn = 1 if cx > 0 else 7
            rolled = [pltpu.roll(value, turn, axis=0) for value in values]
            if cx > 0:
                before = pltpu.roll(look(0, j, -1, 2), 1, axis=0)
                result = [
                    jnp.where(row == 0, before, rolled[0]),
                    jnp.where(row == 0, rolled[0], rolled[1]),
                ]
                if need_last:
                    edge = pltpu.roll(look(1, j, -1, 1), 1, axis=0)
                    result.append(jnp.where(row == 0, edge, rolled[2]))
                return result
            after = pltpu.roll(look(0, j, 1, 2), 7, axis=0)
            result = [
                jnp.where(row == 7, rolled[1], rolled[0]),
                jnp.where(row == 7, after, rolled[1]),
            ]
            if need_last:
                edge = pltpu.roll(look(-1, j, 1, 0), 7, axis=0)
                result.append(jnp.where(row == 7, edge, rolled[2]))
            return result

        for pop in range(POPS):
            cx, cy, cz = VELOCITY[pop]
            kept = {}

            def source(*key):
                if key not in kept:
                    kept[key] = shifted(pop, *key)
                return kept[key]

            def along_y(group, dz):
                values = source(group, None if group == 2 else 0, 0, dz)
                if cy == 0:
                    return values
                other = (group - cy) % 3
                if group != 2 and other != 2:
                    carried = source(other, 0, 0, dz)
                else:
                    carried = source(other, cy if group == 2 else 0, -cy, dz)
                mask = lane >= 112 if cy > 0 else lane < 16
                return [jnp.where(mask, b, a) for a, b in zip(values, carried)]

            for group in groups:
                values = along_y(group, 0)
                turn = (16 * cy + cz) % 128
                if turn:
                    values = [pltpu.roll(value, turn, axis=1) for value in values]
                if cz:
                    turn = (16 * cy - 15 * cz) % 128
                    wrapped = [pltpu.roll(value, turn, axis=1) for value in along_y(group, -cz)]
                    mask = lane % 16 == (0 if cz > 0 else 15)
                    values = [jnp.where(mask, b, a) for a, b in zip(values, wrapped)]
                for v, value in enumerate(values[:vregs]):
                    place = group * GROUP + v * 8
                    if pop:
                        back = post_ref[aligned(own + OPPOSITE[pop] * PLANE + place), :]
                        value = jnp.where(value != value, back, value)
                    is_fluid = fluid_at(post_ref, s, place)
                    h_ref[aligned(own + pop * PLANE + place), :] = jnp.where(is_fluid, value, 0.0)

    @pl.loop(0, SLOTS)
    def _(s):
        one_slot(s)
        if finish is not None:
            finish(s)


def widen_kernel(
    landings,
    own_post,
    own_outer,
    mate_msg,
    other_msg,
    mate2_msg,
    other2_msg,
    own2,
    near_msg,
    far_msg,
    post_ref,
    slots,
    next_outer,
    h_ref,
    low_msg,
    high_msg,
    low2_msg,
    high2_msg,
    table,
    sem,
):
    sort_messages(
        mate_msg, other_msg, mate2_msg, other2_msg, low_msg, high_msg, low2_msg, high2_msg
    )
    even = is_even("cross")

    def received(row):
        near, far = near_msg[row : row + 8, :], far_msg[row : row + 8, :]
        return jnp.where(even, far, near), jnp.where(even, near, far)

    for i in range(3):
        south, north = received(EDGE_TABLE + 8 * i)
        ref, row = ((low_msg, TABLE), (own_outer, PLANES * GROUP), (high_msg, TABLE))[i]
        for j, value in enumerate((south, ref[row : row + 8, :], north)):
            slot = value.astype(jnp.int32)
            region = 8 * (3 * i + j)
            slots[region : region + 8, :] = jnp.where(slot == SLOTS, NOWHERE, slot * SLOT)
    table_copy = pltpu.make_async_copy(slots, table, sem)
    table_copy.start()

    from_low, from_high, low_low, low_me, high_high, high_me = (landings[i, 0] for i in range(6))
    low = lanes_iota() < 64
    post_ref[...] = own_post[...]
    for slot, msg in ((from_low, low_msg), (from_high, high_msg)):

        @pl.when(slot >= 0)
        def _():
            for p in range(POPS):
                for v in range(2):
                    row = p * EDGE + v * 8
                    value = msg[row : row + 8, :]
                    start = slot * SLOT + p * PLANE + v * 8
                    post_ref[aligned(start), :] = value
                    post_ref[aligned(start + GROUP), :] = value

    for msg, row0, step, first in ((high_msg, 16, 1, 2), (low_msg, 23, -1, 1)):
        for y in range(2):
            for count, planes, row, source in strip_rows(first, row0, step):
                source += y * LAYERS
                post_ref[planes(PLANE, row + y * GROUP), :] = msg[source : source + count, :]
    for s in range(SLOTS):
        for slot, msg, row0 in (
            (low_low, low2_msg, 21),
            (low_me, own2, 21),
            (high_high, high2_msg, 16),
            (high_me, own2.at[6 * GROUP :], 16),
        ):

            @pl.when(slot == s)
            def _():
                for y in range(2):
                    for k in range(3):
                        row = s * SLOT + y * GROUP + row0 + k
                        source = (y * 3 + k) * GROUP
                        post_ref[pl.ds(row, POPS, stride=PLANE), :] = msg[
                            source : source + POPS, :
                        ]

    lane = lanes_iota()
    for v in range(3):

        def place(q):
            row = q * PLANE + 2 * GROUP + v * 8
            return slice(row, row + 8)

        for quad in range(QUADS):
            south, north = received(quad * GROUP + v * 8)
            for k in range(4):
                value = jnp.where(lane // 32 == (k + 3) % 4, south, north)
                if k:
                    value = pltpu.roll(value, 128 - 32 * k, axis=1)
                post_ref[place(4 * quad + k), :] = value
        for part in range(3):
            values = received(FAR + part * GROUP + v * 8)
            for planes, target, value in zip((NORTHWARD, SOUTHWARD), (80, 32), values):
                for k, q in enumerate(planes[8 * part : 8 * part + 8]):
                    moved = pltpu.roll(value, (target - 16 * k) % 128, axis=1)
                    post_ref[place(q), :] = jnp.where(
                        lane // 16 == target // 16, moved, post_ref[place(q), :]
                    )

    hide_walls(post_ref)
    table_copy.wait()
    stream_all(post_ref, h_ref, table, (2,), 3)

    def put(s, c, p, value):
        next_outer[aligned(s * (POPS * GROUP) + p * GROUP + (c - 6) * 8), :] = value

    collide_all(h_ref, post_ref, put, (6, 9))


def steps_kernel(
    landings,
    table,
    wide_post,
    next_outer,
    mate_inner,
    other_inner,
    out_hbm,
    h_ref,
    post_ref,
    out,
    sems,
):
    low = lanes_iota() < 64
    post_ref[...] = wide_post[...]
    even = is_even("curve")
    odd = jnp.logical_not(even)
    for slot, wanted, inner in (
        (landings[0, 0], odd, mate_inner),
        (landings[0, 0], even, other_inner),
        (landings[1, 0], even, mate_inner),
        (landings[1, 0], odd, other_inner),
    ):

        @pl.when((slot >= 0) & wanted)
        def _():
            for v in range(2):
                fluid = [fluid_at(post_ref, slot, y * GROUP + v * 8) for y in range(2)]
                for p in range(POPS):
                    row = p * EDGE + v * 8
                    value = inner[row : row + 8, :]
                    for y in range(2):
                        start = aligned(slot * SLOT + p * PLANE + y * GROUP + v * 8)
                        is_here = low if y else jnp.logical_not(low)
                        hidden = jnp.where(fluid[y], value, jnp.nan)
                        post_ref[start, :] = jnp.where(is_here, hidden, post_ref[start, :])

    def finish(s):
        for x in range(EDGE):
            for y in range(2):
                tile = 2 * x + y
                for p, size in ((0, 8), (8, 8), (16, 3)):
                    row = s * SLOT + (p * PLANE + y * GROUP + x)
                    out[s, p : p + size, 128 * tile : 128 * tile + 128] = h_ref[
                        pl.ds(row, size, stride=PLANE), :
                    ]
        pltpu.make_async_copy(out.at[s], out_hbm.at[s], sems.at[s]).start()

    def put(s, c, p, value):
        post_ref[aligned(s * SLOT + p * PLANE + c * 8), :] = value

    stream_all(post_ref, h_ref, table, (0, 1), 3)
    collide_all(h_ref, post_ref, put, (0, 6))
    for q in range(SLOTS * POPS):
        row = q * PLANE + 2 * GROUP
        post_ref[row : row + GROUP, :] = next_outer[q * GROUP : (q + 1) * GROUP, :]
    for _ in range(STEPS - 2):
        stream_all(post_ref, h_ref, table, (0, 1, 2), 3)
        collide_all(h_ref, post_ref, put, (0, 9))
    stream_all(post_ref, h_ref, table, (0, 1), 2, finish)
    for s in range(SLOTS):
        pltpu.make_async_copy(out.at[s], out_hbm.at[s], sems.at[s]).wait()


def swapped(value, axis, unit=1):
    count = lax.axis_size(axis)
    results = []
    for which in (0, 1):
        sides = [unit if i // unit % 2 == which else -unit for i in range(count)]
        pairs = [(i, i + side) for i, side in enumerate(sides) if 0 <= i + side < count]
        results.append(lax.ppermute(value[which], axis, pairs))
    return results


def rows128(count):
    return jax.ShapeDtypeStruct((count, 128), jnp.float32)


def call(kernel, in_spaces, out_spaces, outs, ins, scratch, limit=LIMIT):
    spaces = {
        "S": pl.BlockSpec(memory_space=pltpu.SMEM),
        "V": pl.BlockSpec(memory_space=pltpu.VMEM),
        "H": pl.BlockSpec(memory_space=pltpu.HBM),
    }
    return pl.pallas_call(
        kernel,
        out_shape=outs,
        in_specs=[spaces[x] for x in in_spaces],
        out_specs=[spaces[x] for x in out_spaces],
        scratch_shapes=scratch,
        compiler_params=pltpu.CompilerParams(vmem_limit_bytes=limit),
    )(*ins)


def per_device(populations, site_flags, neighbours, migrations, counts):
    sizes = (lax.axis_size("curve"), lax.axis_size("cross"))
    moves = migrations.T
    floats = lambda rows: pltpu.VMEM((rows, 128), jnp.float32)
    messages = [
        PLANES * 32 + 8,
        STRIPS + 2 * LAYERS,
        STRIPS + 2 * LAYERS,
        6 * GROUP,
        6 * GROUP,
        HALF,
    ]
    results = messages[:5] + messages[3:]
    cells, mate_msg, other_msg, mate2_msg, other2_msg, up2_msg, down2_msg, inner_msg = call(
        functools.partial(pack_kernel, sizes[1]),
        "HHHHH",
        "HHHHHHHH",
        [rows128(rows) for rows in results],
        (moves, counts, populations, site_flags, neighbours),
        [
            pltpu.SMEM(moves.shape, jnp.int32),
            pltpu.SMEM(counts.shape, jnp.int32),
            pltpu.VMEM(populations.shape, jnp.float32),
            pltpu.VMEM(site_flags.shape, jnp.int32),
            pltpu.VMEM(neighbours.shape, jnp.int32),
            *[floats(rows) for rows in messages],
            pltpu.VMEM((8, 5888), jnp.float32),
            pltpu.VMEM((128, 384), jnp.bfloat16),
            floats(256),
            floats(8),
            pltpu.SemaphoreType.DMA((4 + SLOTS + 8,)),
        ],
        WIDE_LIMIT,
    )
    mate_msg, other_msg = swapped((mate_msg, other_msg), "curve")
    mate2_msg, other2_msg = swapped((mate2_msg, other2_msg), "curve", 2)
    mate_inner, other_inner = swapped((inner_msg, inner_msg), "curve")
    post, outer, own2, landings = call(
        functools.partial(spread_kernel, *sizes),
        "SVVV",
        "VVVV",
        [
            rows128(NOWHERE + SLOT),
            rows128(PLANES * GROUP + 8),
            rows128(12 * GROUP),
            jax.ShapeDtypeStruct((8, 128), jnp.int32),
        ],
        (moves, cells, up2_msg, down2_msg),
        [],
    )
    strips = (mate_msg, other_msg, mate2_msg, other2_msg, own2)
    sorted_rows = [messages[1], messages[1], messages[3], messages[3]]
    near_msg, far_msg = call(
        edge_kernel,
        "SVVVVVV",
        "VV",
        [rows128(EDGE_ROWS), rows128(EDGE_ROWS)],
        (landings, outer, *strips),
        [floats(rows) for rows in [PLANES * GROUP] + sorted_rows],
    )
    near_msg, far_msg = swapped((near_msg, far_msg), "cross")
    post, table, next_outer = call(
        widen_kernel,
        "SVVVVVVVVV",
        "VVV",
        [
            rows128(NOWHERE + SLOT),
            jax.ShapeDtypeStruct((72, 128), jnp.int32),
            rows128(SLOTS * POPS * GROUP),
        ],
        (landings, post, outer, *strips, near_msg, far_msg),
        [
            *[floats(rows) for rows in [SLOTS * SLOT] + sorted_rows],
            pltpu.SMEM((72, 128), jnp.int32),
            pltpu.SemaphoreType.DMA,
        ],
    )
    return call(
        steps_kernel,
        "SSVVVV",
        "H",
        [jax.ShapeDtypeStruct(populations.shape, jnp.float32)],
        (landings, table, post, next_outer, mate_inner, other_inner),
        [
            floats(SLOTS * SLOT),
            floats(NOWHERE + SLOT),
            pltpu.VMEM(populations.shape, jnp.float32),
            pltpu.SemaphoreType.DMA((SLOTS,)),
        ],
    )[0]


def solution(mesh):
    return jax.shard_map(
        per_device,
        mesh=mesh,
        in_specs=(
            P(("curve", "cross"), None, None),
            P(("curve", "cross"), None),
            P(("curve", "cross"), None),
            P(),
            P(("curve", "cross")),
        ),
        out_specs=P(("curve", "cross"), None, None),
        check_vma=False,
    )
```

```python
import functools

import jax
import jax.numpy as jnp
import numpy as np
from jax import lax
from jax.experimental import pallas as pl
from jax.experimental.pallas import tpu as pltpu
from jax.sharding import PartitionSpec as P

EDGE = 16
STEPS = 3
SLOTS = 3
POPS = 19
PLANES = SLOTS * POPS + SLOTS
FLAG0 = SLOTS * POPS
GROUP = 24
PLANE = 3 * GROUP
SLOT = POPS * PLANE
OUTWARD = SLOTS * 5 + SLOTS
LAYERS = 2 * PLANES + OUTWARD
RIM = 11 * EDGE
REST = POPS * EDGE + 10 * EDGE
PAIR = 2 * GROUP
QUADS = PLANES // 4
TABLE = RIM
STRIPS = RIM + 8
FAR = QUADS * GROUP
EDGE_TABLE = FAR + 3 * GROUP
EDGE_ROWS = EDGE_TABLE + 24
NOWHERE = PLANES * GROUP
ALL_PLANES = PLANES + POPS
LIMIT = 20 * 1024 * 1024
WIDE_LIMIT = 127 * 512 * 1024

VELOCITY = [
    (0, 0, 0),
    (1, 0, 0),
    (-1, 0, 0),
    (0, 1, 0),
    (0, -1, 0),
    (0, 0, 1),
    (0, 0, -1),
    (1, 1, 0),
    (-1, -1, 0),
    (1, -1, 0),
    (-1, 1, 0),
    (1, 0, 1),
    (-1, 0, -1),
    (1, 0, -1),
    (-1, 0, 1),
    (0, 1, 1),
    (0, -1, -1),
    (0, 1, -1),
    (0, -1, 1),
]
NORTHWARD, SOUTHWARD = (
    [s * POPS + p for s in range(SLOTS) for p in range(POPS) if VELOCITY[p][1] == side]
    + [FLAG0 + s for s in range(SLOTS)]
    for side in (1, -1)
)
THIRD = [
    (pop, source, *((32 + 16 * k, 9) if k < 4 else (16 * (k - 4), 10)))
    for k, (pop, source) in enumerate(
        [(p, 32) for p in (4, 8, 9, 16, 18)] + [(p, 80) for p in (3, 7, 10, 15, 17)]
    )
]
OPPOSITE = [0, 2, 1, 4, 3, 6, 5, 8, 7, 10, 9, 12, 11, 14, 13, 16, 15, 18, 17]


def lanes_iota():
    return lax.broadcasted_iota(jnp.int32, (8, 128), 1)


def is_even(axis, unit=1):
    return lax.rem(lax.axis_index(axis) // unit, 2) == 0


def rows_iota():
    return lax.broadcasted_iota(jnp.int32, (8, 128), 0)


def aligned(start, size=8):
    return pl.ds(pl.multiple_of(start, 8), size)


def move_slots(moves, curve_size, cross_size):
    curve, cross = lax.axis_index("curve"), lax.axis_index("cross")

    def landed(source, target):
        inside = (source >= 0) & (source < curve_size) & (target >= 0) & (target < curve_size)
        row = jnp.clip(source, 0, curve_size - 1) * cross_size + cross
        rank = target * cross_size + cross
        hit = inside & (moves[0, row] >= 0) & (moves[1, row] == rank)
        return jnp.where(hit, moves[2, row], -1)

    return (
        landed(curve - 1, curve),
        landed(curve + 1, curve),
        landed(curve - 2, curve - 1),
        landed(curve, curve - 1),
        landed(curve + 2, curve + 1),
        landed(curve, curve + 1),
    )


def pack_kernel(
    cross_size,
    moves_hbm,
    counts_hbm,
    pops_hbm,
    flags_hbm,
    neighbours_hbm,
    cells_hbm,
    mate_hbm,
    other_hbm,
    mate2_hbm,
    other2_hbm,
    up2_hbm,
    down2_hbm,
    rest_hbm,
    moves,
    counts,
    pops,
    flags,
    neighbours,
    cells,
    up_msg,
    down_msg,
    up2_msg,
    down2_msg,
    rest_msg,
    wide_flags,
    plane_flags,
    site_flags,
    near,
    sems,
):
    started = []

    def copy(source, target):
        one = pltpu.make_async_copy(source, target, sems.at[len(started)])
        one.start()
        started.append(one)
        return one

    flags_copy = copy(flags_hbm, flags)
    copies = [copy(pops_hbm.at[s], pops.at[s]) for s in range(SLOTS)]
    small = [
        copy(neighbours_hbm, neighbours),
        copy(counts_hbm, counts),
        copy(moves_hbm, moves),
    ]
    for one in small:
        one.wait()

    near[...] = jnp.zeros_like(near)
    named = neighbours[...]
    slot = jnp.where(named >= 0, lax.rem(jnp.maximum(named, 0), SLOTS), SLOTS)
    near[0:SLOTS, 0 : named.shape[1]] = slot.astype(jnp.float32)
    for ref, row in ((cells, PLANES * 32), (up_msg, TABLE), (down_msg, TABLE)):
        ref[row : row + 8, :] = near[...]

    wide_flags[...] = jnp.zeros_like(wide_flags)
    flags_copy.wait()
    wide_flags[0:SLOTS, 0 : flags.shape[1]] = flags[...].astype(jnp.float32)
    span = EDGE + 2
    for x in range(EDGE):
        start = (x + 1) * span * span
        base = start // 128 * 128
        window = wide_flags[:, base : base + 512]
        window = pltpu.roll(window, (512 - (start - base)) % 512, axis=1)
        plane_flags[8 * x : 8 * x + 8, :] = window[:, :384].astype(jnp.bfloat16)
    lane_in = lax.broadcasted_iota(jnp.int32, (384, 256), 0)
    site = lax.broadcasted_iota(jnp.int32, (384, 256), 1)
    chosen = lane_in == (site // EDGE + 1) * span + site % EDGE + 1
    product = jnp.dot(
        plane_flags[...],
        jnp.where(chosen, 1.0, 0.0).astype(jnp.bfloat16),
        preferred_element_type=jnp.float32,
    )
    site_flags[0:128, :] = product[:, :128]
    site_flags[128:256, :] = product[:, 128:]
    for s in range(SLOTS):
        live = s < counts[0]
        for y in range(2):
            piece = site_flags[pl.ds(128 * y + s, EDGE, stride=8), :]
            is_fluid = (piece == 1.0) & live
            row = (FLAG0 + s) * 32 + y * EDGE
            cells[row : row + EDGE, :] = jnp.where(is_fluid, 1.0, 0.0)

    for s in range(SLOTS):
        copies[s].wait()
        for x in range(EDGE):
            for y in range(2):
                tile = 2 * x + y
                for p, size in ((0, 8), (8, 8), (16, 3)):
                    row = (s * POPS + p) * 32 + y * EDGE + x
                    cells[pl.ds(row, size, stride=32), :] = pops[
                        s, p : p + size, 128 * tile : 128 * tile + 128
                    ]

    @pl.loop(0, SLOTS)
    def _(s):
        @pl.loop(0, 4, unroll=2)
        def _(c):
            base = s * (POPS * 32) + c * 8
            h = [cells[aligned(base + p * 32), :] for p in range(POPS)]
            for p, value in enumerate(collided(h, True)):
                cells[aligned(base + p * 32), :] = value

    cells_copy = copy(cells, cells_hbm)

    for y in range(2):
        for msg, x0, first in ((up_msg, 15, 1), (down_msg, 0, 2)):
            step = -1 if x0 else 1
            for k in range(2):
                out = STRIPS + y * LAYERS + k * PLANES
                msg[out : out + PLANES, :] = cells[
                    pl.ds(y * EDGE + x0 + step * k, PLANES, stride=32), :
                ]
            row = y * EDGE + x0 + 2 * step
            out = STRIPS + y * LAYERS + 2 * PLANES
            for s in range(SLOTS):
                base = s * POPS * 32 + row
                msg[out + 5 * s : out + 5 * s + 1, :] = cells[pl.ds(base + first * 32, 1), :]
                msg[out + 5 * s + 1 : out + 5 * s + 5, :] = cells[
                    pl.ds(base + (first + 6) * 32, 4, stride=64), :
                ]
            msg[out + 5 * SLOTS : out + OUTWARD, :] = cells[
                pl.ds(FLAG0 * 32 + row, SLOTS, stride=32), :
            ]

    here = lax.axis_index("curve") * cross_size + lax.axis_index("cross")
    leaving = jnp.maximum(moves[0, here], 0)
    lane = lanes_iota()
    for v in range(2):
        halves = [
            [cells[aligned(leaving * (POPS * 32) + p * 32 + y * EDGE + v * 8), :] for y in (0, 1)]
            for p in range(POPS)
        ]
        outer = [jnp.where(lane < 64, first, second) for first, second in halves]
        middle = (lane >= 32) & (lane < 96)
        sets = [
            jnp.where(middle, pltpu.roll(outer[p + 1], 64, axis=1), outer[p])
            for p in range(0, POPS - 1, 2)
        ]
        sets += [outer[POPS - 1], jnp.zeros_like(outer[0])]
        for pop, source, target, which in THIRD:
            moved = pltpu.roll(outer[pop], (target - source) % 128, axis=1)
            sets[which] = jnp.where(lane // 16 == target // 16, moved, sets[which])
        for k, value in enumerate(sets):
            row = k * EDGE + v * 8
            up_msg[row : row + 8, :] = value
            down_msg[row : row + 8, :] = value
        for p, (first, second) in enumerate(halves):
            row = p * EDGE + v * 8
            rest_msg[row : row + 8, :] = jnp.where(lane < 32, second, first)
        for p in range(0, POPS, 2):
            value = halves[p][1]
            if p + 1 < POPS:
                value = jnp.where(middle, value, pltpu.roll(halves[p + 1][1], 64, axis=1))
            row = (POPS + p // 2) * EDGE + v * 8
            rest_msg[row : row + 8, :] = value
    for s in range(SLOTS):

        @pl.when(leaving == s)
        def _():
            for y in range(2):
                for k in range(3):
                    out = (y * 3 + k) * GROUP
                    row = s * POPS * 32 + y * EDGE + k
                    up2_msg[out : out + POPS, :] = cells[pl.ds(row + 13, POPS, stride=32), :]
                    down2_msg[out : out + POPS, :] = cells[pl.ds(row, POPS, stride=32), :]

    last = [copy(up2_msg, up2_hbm), copy(down2_msg, down2_hbm), copy(rest_msg, rest_hbm)]
    count = len(started)
    for i, (up, down, mate, other, unit) in enumerate(
        ((up_msg, down_msg, mate_hbm, other_hbm, 1), (up2_msg, down2_msg, mate2_hbm, other2_hbm, 2))
    ):
        first, second = sems.at[count + 2 * i], sems.at[count + 2 * i + 1]
        even = is_even("curve", unit)

        @pl.when(even)
        def _():
            pltpu.make_async_copy(up, mate, first).start()
            pltpu.make_async_copy(down, other, second).start()

        @pl.when(jnp.logical_not(even))
        def _():
            pltpu.make_async_copy(down, mate, first).start()
            pltpu.make_async_copy(up, other, second).start()

        last.append(pltpu.make_async_copy(up, mate, first))
        last.append(pltpu.make_async_copy(down, other, second))
    cells_copy.wait()
    for one in last:
        one.wait()


def spread_kernel(
    curve_size, cross_size, moves, cells, up2_msg, down2_msg, outer, own2, landings
):
    low = lanes_iota() < 64
    own2[0 : 6 * GROUP, :] = up2_msg[...]
    own2[6 * GROUP :, :] = down2_msg[...]
    for i, slot in enumerate(move_slots(moves, curve_size, cross_size)):
        landings[i : i + 1, :] = jnp.full((1, 128), slot, jnp.int32)
    for q in range(PLANES):
        for v in range(2):
            row = q * 32 + v * 8
            first, second = cells[row : row + 8, :], cells[row + EDGE : row + EDGE + 8, :]
            row = q * GROUP + v * 8
            outer[row : row + 8, :] = jnp.where(low, first, second)
    outer[PLANES * GROUP :, :] = cells[PLANES * 32 :, :]


def sort_messages(mate_msg, other_msg, mate2_msg, other2_msg, low_msg, high_msg, low2, high2):
    for mate, other, low, high, unit in (
        (mate_msg, other_msg, low_msg, high_msg, 1),
        (mate2_msg, other2_msg, low2, high2, 2),
    ):
        even = is_even("curve", unit)

        @pl.when(even)
        def _():
            low[...] = other[...]
            high[...] = mate[...]

        @pl.when(jnp.logical_not(even))
        def _():
            low[...] = mate[...]
            high[...] = other[...]


def rim_of(msg, p, v):
    row = p // 2 * EDGE + v * 8
    value = msg[row : row + 8, :]
    return pltpu.roll(value, 64, axis=1) if p % 2 else value


def sel4(parts, lane):
    first = jnp.where(lane < 32, parts[0], parts[1])
    second = jnp.where(lane < 96, parts[2], parts[3])
    return jnp.where(lane < 64, first, second)


def strip_rows(first, row0, step):
    pieces = []
    for k in range(2):
        pieces.append(
            (PLANES, lambda size, row: pl.ds(row, PLANES, stride=size), row0 + step * k, STRIPS + k * PLANES)
        )
    row, source = row0 + 2 * step, STRIPS + 2 * PLANES
    for s in range(SLOTS):
        plane = s * POPS + first
        pieces.append((1, lambda size, row, plane=plane: pl.ds(plane * size + row, 1), row, source))
        pieces.append(
            (
                4,
                lambda size, row, plane=plane: pl.ds(
                    (plane + 6) * size + row, 4, stride=2 * size
                ),
                row,
                source + 1,
            )
        )
        source += 5
    pieces.append(
        (SLOTS, lambda size, row: pl.ds(FLAG0 * size + row, SLOTS, stride=size), row, source)
    )
    return pieces


def edge_kernel(
    landings,
    own_outer,
    mate_msg,
    other_msg,
    mate2_msg,
    other2_msg,
    own2,
    near_msg,
    far_msg,
    outer,
    low_msg,
    high_msg,
    low2_msg,
    high2_msg,
):
    sort_messages(
        mate_msg, other_msg, mate2_msg, other2_msg, low_msg, high_msg, low2_msg, high2_msg
    )
    from_low, from_high, low_low, low_me, high_high, high_me = (landings[i, 0] for i in range(6))
    low = lanes_iota() < 64
    for q in range(PLANES):
        for v in range(2):
            row = q * GROUP + v * 8
            outer[row : row + 8, :] = own_outer[row : row + 8, :]

    def both(first, second):
        lane = lax.broadcasted_iota(jnp.int32, first.shape, 1)
        return jnp.where(lane < 64, first, second)

    for msg, row0, step, first in ((high_msg, 16, 1, 2), (low_msg, 23, -1, 1)):
        for count, planes, row, source in strip_rows(first, row0, step):
            outer[planes(GROUP, row), :] = both(
                msg[source : source + count, :],
                msg[LAYERS + source : LAYERS + source + count, :],
            )
    lane = lanes_iota()
    for slot, msg in ((from_low, low_msg), (from_high, high_msg)):

        @pl.when(slot >= 0)
        def _():
            for v in range(2):
                values = [rim_of(msg, p, v) for p in range(POPS)]
                for pop, target, source, which in THIRD:
                    row = which * EDGE + v * 8
                    moved = pltpu.roll(msg[row : row + 8, :], (target - source) % 128, axis=1)
                    values[pop] = jnp.where(lane // 16 == target // 16, moved, values[pop])
                for p, value in enumerate(values):
                    base = slot * (POPS * GROUP) + p * GROUP + v * 8
                    outer[aligned(base), :] = value

    for s in range(SLOTS):
        for slot, msg, row0 in (
            (low_low, low2_msg, 21),
            (low_me, own2, 21),
            (high_high, high2_msg, 16),
            (high_me, own2.at[6 * GROUP :], 16),
        ):

            @pl.when(slot == s)
            def _():
                for k in range(3):
                    outer[pl.ds(s * POPS * GROUP + row0 + k, POPS, stride=GROUP), :] = both(
                        msg[k * GROUP : k * GROUP + POPS, :],
                        msg[(3 + k) * GROUP : (3 + k) * GROUP + POPS, :],
                    )

    even = is_even("cross")

    def send(row, north, south):
        near_msg[row : row + 8, :] = jnp.where(even, north, south)
        far_msg[row : row + 8, :] = jnp.where(even, south, north)

    for v in range(3):

        def plane(q):
            return outer[q * GROUP + v * 8 : q * GROUP + v * 8 + 8, :]

        for quad in range(QUADS):
            parts = [plane(4 * quad)]
            parts += [pltpu.roll(plane(4 * quad + k), 32 * k, axis=1) for k in (1, 2, 3)]
            send(quad * GROUP + v * 8, sel4(parts[1:] + parts[:1], lane), sel4(parts, lane))
        for part in range(3):
            values = []
            for planes, source in ((NORTHWARD, 80), (SOUTHWARD, 32)):
                value = None
                for k, q in enumerate(planes[8 * part : 8 * part + 8]):
                    moved = pltpu.roll(plane(q), (16 * k - source) % 128, axis=1)
                    value = moved if value is None else jnp.where(lane < 16 * k, value, moved)
                values.append(value)
            send(FAR + part * GROUP + v * 8, *values)
    tables = (low_msg, TABLE), (own_outer, PLANES * GROUP), (high_msg, TABLE)
    for i, (ref, row) in enumerate(tables):
        value = ref[row : row + 8, :]
        send(EDGE_TABLE + 8 * i, value, value)


def collided(h, is_fluid):
    shear = 1.0 / 0.6
    rest = h[0]
    sx, dx = h[1] + h[2], h[1] - h[2]
    sy, dy = h[3] + h[4], h[3] - h[4]
    sz, dz = h[5] + h[6], h[5] - h[6]
    s7, d7 = h[7] + h[8], h[7] - h[8]
    s9, d9 = h[9] + h[10], h[9] - h[10]
    s11, d11 = h[11] + h[12], h[11] - h[12]
    s13, d13 = h[13] + h[14], h[13] - h[14]
    s15, d15 = h[15] + h[16], h[15] - h[16]
    s17, d17 = h[17] + h[18], h[17] - h[18]
    txy, txz, tyz = s7 + s9, s11 + s13, s15 + s17
    pxy, pxz, pyz = s7 - s9, s11 - s13, s15 - s17
    ax, bx = d7 + d9, d11 + d13
    ay, by = d7 - d9, d15 + d17
    az, bz = d11 - d13, d15 - d17
    axes = sx + sy + sz
    diags = txy + txz + tyz
    rho = rest * (1.0 / 3.0) + axes * (1.0 / 18.0) + diags * (1.0 / 36.0)
    fx, fy, fz = ax + bx, ay + by, az + bz
    jx = dx * (1.0 / 18.0) + fx * (1.0 / 36.0)
    jy = dy * (1.0 / 18.0) + fy * (1.0 / 36.0)
    jz = dz * (1.0 / 18.0) + fz * (1.0 / 36.0)
    inverse = 1.0 / jnp.where(is_fluid, rho, 1.0)
    ux, uy, uz = jx * inverse, jy * inverse, jz * inverse
    qxx, qyy, qzz = jx * ux, jy * uy, jz * uz
    total = qxx + qyy + qzz

    energy = -10.0 * rest - axes * (11.0 / 18.0) + diags * (8.0 / 36.0)
    energy = (energy + 11.0 * rho - 19.0 * total) * (1.19 / 2394.0)
    square = 4.0 * rest - axes * (4.0 / 18.0) + diags * (1.0 / 36.0)
    square = (square - 3.0 * rho + 5.5 * total) * (1.4 / 252.0)
    axis_x = (3.0 * sx - axes) * (1.0 / 18.0)
    diag_x = (diags - 3.0 * tyz) * (1.0 / 36.0)
    want_x = 3.0 * qxx - total
    stress_x = (axis_x + diag_x - want_x) * (shear / 36.0)
    third_x = (diag_x - 2.0 * axis_x + 0.5 * want_x) * (1.4 / 72.0)
    axis_w = (sy - sz) * (1.0 / 18.0)
    diag_w = (txy - txz) * (1.0 / 36.0)
    want_w = qyy - qzz
    stress_w = (axis_w + diag_w - want_w) * (shear / 12.0)
    third_w = (diag_w - 2.0 * axis_w + 0.5 * want_w) * (1.4 / 24.0)

    rest_out = rest - 3.0 * (12.0 * square - 30.0 * energy)
    common = -18.0 * (11.0 * energy + 4.0 * square)
    along_x = 18.0 * (stress_x - 2.0 * third_x)
    along_w = 18.0 * (stress_w - 2.0 * third_w)
    ex = common + 2.0 * along_x
    ey = common - along_x + along_w
    ez = common - along_x - along_w
    common = 36.0 * (8.0 * energy + square)
    across_x = 36.0 * (stress_x + third_x)
    across_w = 36.0 * (stress_w + third_w)
    exy = common + across_x + across_w
    exz = common + across_x - across_w
    eyz = common - 2.0 * across_x
    cxy = shear * (0.25 * pxy - 9.0 * jx * uy)
    cxz = shear * (0.25 * pxz - 9.0 * jx * uz)
    cyz = shear * (0.25 * pyz - 9.0 * jy * uz)

    def flux(d, f, j):
        return (f * (1.0 / 36.0) - d * (4.0 / 18.0) + j * (2.0 / 3.0)) * (1.2 / 40.0)

    hx, hy, hz = flux(dx, fx, jx), flux(dy, fy, jy), flux(dz, fz, jz)
    mx = (ax - bx) * (1.98 / 8.0)
    my = (by - ay) * (1.98 / 8.0)
    mz = (az - bz) * (1.98 / 8.0)
    hx36, hy36, hz36 = 36.0 * hx, 36.0 * hy, 36.0 * hz
    xy_x, xz_x = hx36 + mx, hx36 - mx
    yz_y, xy_y = hy36 + my, hy36 - my
    xz_z, yz_z = hz36 + mz, hz36 - mz
    ox, oy, oz = -2.0 * hx36, -2.0 * hy36, -2.0 * hz36

    out = [rest_out]

    def pair(i, even, odd):
        out.append(h[i] - (even + odd))
        out.append(h[i + 1] - (even - odd))

    pair(1, ex, ox)
    pair(3, ey, oy)
    pair(5, ez, oz)
    pair(7, exy + cxy, xy_x + xy_y)
    pair(9, exy - cxy, xy_x - xy_y)
    pair(11, exz + cxz, xz_x + xz_z)
    pair(13, exz - cxz, xz_x - xz_z)
    pair(15, eyz + cyz, yz_y + yz_z)
    pair(17, eyz - cyz, yz_y - yz_z)
    return out


def place(group, start, plane, v):
    if group == 2:
        return aligned(start + plane * GROUP + v * 8)
    return aligned(2 * start + plane * PAIR + group * GROUP + v * 8)


def fluid_at(ref, group, s, v):
    return ref[place(group, s * GROUP, FLAG0, v), :] > 0.0


def collide_all(h_ref, flags, posts):
    for groups in ((0, 1), (2,)):
        ref = posts[groups[0] // 2]
        size = len(groups) * GROUP

        @pl.loop(0, SLOTS)
        def _(s):
            @pl.loop(0, size // 8, unroll=3)
            def _(c):
                base = s * SLOT + groups[0] * GROUP + c * 8
                is_fluid = flags[groups[0] // 2][aligned((FLAG0 + s) * size + c * 8), :] > 0.0
                h = [h_ref[aligned(base + p * PLANE), :] for p in range(POPS)]
                for p, value in enumerate(collided(h, is_fluid)):
                    row = aligned((s * POPS + p) * size + c * 8)
                    ref[row, :] = jnp.where(is_fluid, value, jnp.nan)


def hide_walls(ref, size):
    @pl.loop(0, SLOTS)
    def _(s):
        @pl.loop(0, size // 8)
        def _(c):
            is_fluid = ref[aligned((FLAG0 + s) * size + c * 8), :] > 0.0
            for p in range(POPS):
                row = aligned((s * POPS + p) * size + c * 8)
                ref[row, :] = jnp.where(is_fluid, ref[row, :], jnp.nan)


def stream_all(posts, h_ref, flags, table, groups, vregs, finish=None):
    lane = lanes_iota()
    row = rows_iota()
    low = lane < 64

    def one_slot(s):
        own = s * (POPS * GROUP)

        def shifted(pop, group, j, dy, dz):
            cx = VELOCITY[pop][0]

            def rows(start, v):
                return posts[group // 2][place(group, start, pop, v), :]

            def look(i, j, dx, v):
                if (dx, dy, dz) == (0, 0, 0):
                    return rows(own, v)
                if j is None:
                    return jnp.where(low, look(i, 1, dx, v), look(i, -1, dx, v))
                region = (i + 1) * 3 + j + 1
                return rows(table[region * 8 + s, VELOCITY.index((dx, dy, dz)) - 1], v)

            need_last = vregs == 3
            values = [look(0, j, 0, 0), look(0, j, 0, 1)]
            if need_last:
                if dy == 0 and dz == 0:
                    values.append(rows(own, 2))
                else:
                    values.append(jnp.where(row < 4, look(1, j, 0, 2), look(-1, j, 0, 2)))
            if cx == 0:
                return values
            turn = 1 if cx > 0 else 7
            rolled = [pltpu.roll(value, turn, axis=0) for value in values]
            if cx > 0:
                before = pltpu.roll(look(0, j, -1, 2), 1, axis=0)
                result = [
                    jnp.where(row == 0, before, rolled[0]),
                    jnp.where(row == 0, rolled[0], rolled[1]),
                ]
                if need_last:
                    edge = pltpu.roll(look(1, j, -1, 1), 1, axis=0)
                    result.append(jnp.where(row == 0, edge, rolled[2]))
                return result
            after = pltpu.roll(look(0, j, 1, 2), 7, axis=0)
            result = [
                jnp.where(row == 7, rolled[1], rolled[0]),
                jnp.where(row == 7, after, rolled[1]),
            ]
            if need_last:
                edge = pltpu.roll(look(-1, j, 1, 0), 7, axis=0)
                result.append(jnp.where(row == 7, edge, rolled[2]))
            return result

        for pop in range(POPS):
            cx, cy, cz = VELOCITY[pop]
            kept = {}

            def source(*key):
                if key not in kept:
                    kept[key] = shifted(pop, *key)
                return kept[key]

            def along_y(group, dz):
                values = source(group, None if group == 2 else 0, 0, dz)
                if cy == 0:
                    return values
                other = (group - cy) % 3
                if group != 2 and other != 2:
                    carried = source(other, 0, 0, dz)
                else:
                    carried = source(other, cy if group == 2 else 0, -cy, dz)
                mask = lane >= 112 if cy > 0 else lane < 16
                return [jnp.where(mask, b, a) for a, b in zip(values, carried)]

            for group in groups:
                values = along_y(group, 0)
                turn = (16 * cy + cz) % 128
                if turn:
                    values = [pltpu.roll(value, turn, axis=1) for value in values]
                if cz:
                    turn = (16 * cy - 15 * cz) % 128
                    wrapped = [pltpu.roll(value, turn, axis=1) for value in along_y(group, -cz)]
                    mask = lane % 16 == (0 if cz > 0 else 15)
                    values = [jnp.where(mask, b, a) for a, b in zip(values, wrapped)]
                for v, value in enumerate(values[:vregs]):
                    if pop:
                        back = posts[group // 2][place(group, own, OPPOSITE[pop], v), :]
                        value = jnp.where(value != value, back, value)
                    is_fluid = fluid_at(flags[group // 2], group, s, v)
                    target = aligned(s * SLOT + pop * PLANE + group * GROUP + v * 8)
                    h_ref[target, :] = jnp.where(is_fluid, value, 0.0)

    @pl.loop(0, SLOTS)
    def _(s):
        one_slot(s)
        if finish is not None:
            finish(s)


def join_kernel(
    landings,
    cells,
    mate_msg,
    other_msg,
    mate2_msg,
    other2_msg,
    own2,
    mate_rest,
    other_rest,
    post_ref,
    slots,
    low_msg,
    high_msg,
    low2_msg,
    high2_msg,
):
    sort_messages(
        mate_msg, other_msg, mate2_msg, other2_msg, low_msg, high_msg, low2_msg, high2_msg
    )
    for i, (ref, row) in enumerate(((low_msg, TABLE), (cells, PLANES * 32), (high_msg, TABLE))):
        slots[8 * i : 8 * i + 8, :] = first_rows(ref[row : row + 8, :])

    from_low, from_high, low_low, low_me, high_high, high_me = (landings[i, 0] for i in range(6))
    lane = lanes_iota()
    post_ref[PLANES * PAIR :, :] = jnp.full((POPS * PAIR, 128), jnp.nan, jnp.float32)
    for q in range(PLANES):
        for y in range(2):
            start = q * PAIR + y * GROUP
            post_ref[start : start + EDGE, :] = cells[
                q * 32 + y * EDGE : q * 32 + (y + 1) * EDGE, :
            ]
    even = is_even("curve")
    odd = jnp.logical_not(even)
    for slot, msg, wanted, rest in (
        (from_low, low_msg, odd, mate_rest),
        (from_low, low_msg, even, other_rest),
        (from_high, high_msg, even, mate_rest),
        (from_high, high_msg, odd, other_rest),
    ):

        @pl.when((slot >= 0) & wanted)
        def _():
            for p in range(POPS):
                for v in range(2):
                    rim = rim_of(msg, p, v)
                    row = p * EDGE + v * 8
                    wide = rest[row : row + 8, :]
                    row = (POPS + p // 2) * EDGE + v * 8
                    middle = rest[row : row + 8, :]
                    if p % 2:
                        middle = pltpu.roll(middle, 64, axis=1)
                    second = jnp.where(lane < 32, wide, jnp.where(lane < 96, middle, rim))
                    start = slot * (POPS * PAIR) + p * PAIR + v * 8
                    post_ref[aligned(start), :] = jnp.where(lane < 32, rim, wide)
                    post_ref[aligned(start + GROUP), :] = second

    for msg, row0, step, first in ((high_msg, 16, 1, 2), (low_msg, 23, -1, 1)):
        for y in range(2):
            for count, planes, row, source in strip_rows(first, row0, step):
                source += y * LAYERS
                post_ref[planes(PAIR, row + y * GROUP), :] = msg[source : source + count, :]
    for s in range(SLOTS):
        for slot, msg, row0 in (
            (low_low, low2_msg, 21),
            (low_me, own2, 21),
            (high_high, high2_msg, 16),
            (high_me, own2.at[6 * GROUP :], 16),
        ):

            @pl.when(slot == s)
            def _():
                for y in range(2):
                    for k in range(3):
                        row = s * POPS * PAIR + y * GROUP + row0 + k
                        source = (y * 3 + k) * GROUP
                        post_ref[pl.ds(row, POPS, stride=PAIR), :] = msg[source : source + POPS, :]
    hide_walls(post_ref, PAIR)


def first_rows(slot):
    slot = slot.astype(jnp.int32)
    return jnp.where(slot == SLOTS, NOWHERE, slot * (POPS * GROUP))


def steps_kernel(
    own_slots,
    first_post,
    near_msg,
    far_msg,
    out_hbm,
    h_ref,
    post_ref,
    outer_ref,
    out,
    slots,
    table,
    sems,
):
    even = is_even("cross")

    def received(row):
        near, far = near_msg[row : row + 8, :], far_msg[row : row + 8, :]
        return jnp.where(even, far, near), jnp.where(even, near, far)

    for i in range(3):
        south, north = received(EDGE_TABLE + 8 * i)
        slots[24 * i : 24 * i + 8, :] = first_rows(south)
        slots[24 * i + 8 : 24 * i + 16, :] = own_slots[8 * i : 8 * i + 8, :]
        slots[24 * i + 16 : 24 * i + 24, :] = first_rows(north)
    table_copy = pltpu.make_async_copy(slots, table, sems.at[SLOTS])
    table_copy.start()

    nothing = jnp.full((8, 128), jnp.nan, jnp.float32)
    for row in range(0, POPS * GROUP, 8):
        outer_ref[NOWHERE + row : NOWHERE + row + 8, :] = nothing
    for row in range(PLANES * PAIR, ALL_PLANES * PAIR, 8):
        post_ref[row : row + 8, :] = nothing
    lane = lanes_iota()
    for v in range(3):

        def rows(q):
            return slice(q * GROUP + v * 8, q * GROUP + v * 8 + 8)

        for quad in range(QUADS):
            south, north = received(quad * GROUP + v * 8)
            for k in range(4):
                value = jnp.where(lane // 32 == (k + 3) % 4, south, north)
                if k:
                    value = pltpu.roll(value, 128 - 32 * k, axis=1)
                outer_ref[rows(4 * quad + k), :] = value
        for part in range(3):
            values = received(FAR + part * GROUP + v * 8)
            for planes, target, value in zip((NORTHWARD, SOUTHWARD), (80, 32), values):
                for k, q in enumerate(planes[8 * part : 8 * part + 8]):
                    moved = pltpu.roll(value, (target - 16 * k) % 128, axis=1)
                    outer_ref[rows(q), :] = jnp.where(
                        lane // 16 == target // 16, moved, outer_ref[rows(q), :]
                    )
    hide_walls(outer_ref, GROUP)
    table_copy.wait()

    def finish(s):
        for x in range(EDGE):
            for y in range(2):
                tile = 2 * x + y
                for p, size in ((0, 8), (8, 8), (16, 3)):
                    row = s * SLOT + (p * PLANE + y * GROUP + x)
                    out[s, p : p + size, 128 * tile : 128 * tile + 128] = h_ref[
                        pl.ds(row, size, stride=PLANE), :
                    ]
        pltpu.make_async_copy(out.at[s], out_hbm.at[s], sems.at[s]).start()

    flags = (first_post, outer_ref)
    posts = flags
    for _ in range(STEPS - 1):
        stream_all(posts, h_ref, flags, table, (0, 1, 2), 3)
        posts = (post_ref, outer_ref)
        collide_all(h_ref, flags, posts)
    stream_all(posts, h_ref, flags, table, (0, 1), 2, finish)
    for s in range(SLOTS):
        pltpu.make_async_copy(out.at[s], out_hbm.at[s], sems.at[s]).wait()


def swapped(value, axis, unit=1):
    count = lax.axis_size(axis)
    results = []
    for which in (0, 1):
        sides = [unit if i // unit % 2 == which else -unit for i in range(count)]
        pairs = [(i, i + side) for i, side in enumerate(sides) if 0 <= i + side < count]
        results.append(lax.ppermute(value[which], axis, pairs))
    return results


def rows128(count):
    return jax.ShapeDtypeStruct((count, 128), jnp.float32)


def call(kernel, in_spaces, out_spaces, outs, ins, scratch, limit=LIMIT):
    spaces = {
        "S": pl.BlockSpec(memory_space=pltpu.SMEM),
        "V": pl.BlockSpec(memory_space=pltpu.VMEM),
        "H": pl.BlockSpec(memory_space=pltpu.HBM),
    }
    return pl.pallas_call(
        kernel,
        out_shape=outs,
        in_specs=[spaces[x] for x in in_spaces],
        out_specs=[spaces[x] for x in out_spaces],
        scratch_shapes=scratch,
        compiler_params=pltpu.CompilerParams(vmem_limit_bytes=limit),
    )(*ins)


def per_device(populations, site_flags, neighbours, migrations, counts):
    sizes = (lax.axis_size("curve"), lax.axis_size("cross"))
    moves = migrations.T
    floats = lambda rows: pltpu.VMEM((rows, 128), jnp.float32)
    messages = [
        PLANES * 32 + 8,
        STRIPS + 2 * LAYERS,
        STRIPS + 2 * LAYERS,
        6 * GROUP,
        6 * GROUP,
        REST,
    ]
    results = messages[:5] + messages[3:]
    cells, mate_msg, other_msg, mate2_msg, other2_msg, up2_msg, down2_msg, rest_msg = call(
        functools.partial(pack_kernel, sizes[1]),
        "HHHHH",
        "HHHHHHHH",
        [rows128(rows) for rows in results],
        (moves, counts, populations, site_flags, neighbours),
        [
            pltpu.SMEM(moves.shape, jnp.int32),
            pltpu.SMEM(counts.shape, jnp.int32),
            pltpu.VMEM(populations.shape, jnp.float32),
            pltpu.VMEM(site_flags.shape, jnp.int32),
            pltpu.VMEM(neighbours.shape, jnp.int32),
            *[floats(rows) for rows in messages],
            pltpu.VMEM((8, 5888), jnp.float32),
            pltpu.VMEM((128, 384), jnp.bfloat16),
            floats(256),
            floats(8),
            pltpu.SemaphoreType.DMA((4 + SLOTS + 8,)),
        ],
        WIDE_LIMIT,
    )
    mate_msg, other_msg = swapped((mate_msg, other_msg), "curve")
    mate2_msg, other2_msg = swapped((mate2_msg, other2_msg), "curve", 2)
    mate_rest, other_rest = swapped((rest_msg, rest_msg), "curve")
    outer, own2, landings = call(
        functools.partial(spread_kernel, *sizes),
        "SVVV",
        "VVV",
        [
            rows128(PLANES * GROUP + 8),
            rows128(12 * GROUP),
            jax.ShapeDtypeStruct((8, 128), jnp.int32),
        ],
        (moves, cells, up2_msg, down2_msg),
        [],
    )
    strips = (mate_msg, other_msg, mate2_msg, other2_msg, own2)
    sorted_rows = [messages[1], messages[1], messages[3], messages[3]]
    near_msg, far_msg = call(
        edge_kernel,
        "SVVVVVV",
        "VV",
        [rows128(EDGE_ROWS), rows128(EDGE_ROWS)],
        (landings, outer, *strips),
        [floats(rows) for rows in [PLANES * GROUP] + sorted_rows],
    )
    near_msg, far_msg = swapped((near_msg, far_msg), "cross")
    post, own_slots = call(
        join_kernel,
        "SVVVVVVVV",
        "VV",
        [rows128(ALL_PLANES * PAIR), jax.ShapeDtypeStruct((24, 128), jnp.int32)],
        (landings, cells, *strips, mate_rest, other_rest),
        [floats(rows) for rows in sorted_rows],
    )
    return call(
        steps_kernel,
        "VVVV",
        "H",
        [jax.ShapeDtypeStruct(populations.shape, jnp.float32)],
        (own_slots, post, near_msg, far_msg),
        [
            floats(SLOTS * SLOT),
            floats(ALL_PLANES * PAIR),
            floats(ALL_PLANES * GROUP),
            pltpu.VMEM(populations.shape, jnp.float32),
            pltpu.VMEM((72, 128), jnp.int32),
            pltpu.SMEM((72, 128), jnp.int32),
            pltpu.SemaphoreType.DMA((SLOTS + 1,)),
        ],
    )[0]


def solution(mesh):
    return jax.shard_map(
        per_device,
        mesh=mesh,
        in_specs=(
            P(("curve", "cross"), None, None),
            P(("curve", "cross"), None),
            P(("curve", "cross"), None),
            P(),
            P(("curve", "cross")),
        ),
        out_specs=P(("curve", "cross"), None, None),
        check_vma=False,
    )
```

```python
import functools

import jax
import jax.numpy as jnp
import numpy as np
from jax import lax
from jax.experimental import pallas as pl
from jax.experimental.pallas import tpu as pltpu
from jax.sharding import PartitionSpec as P

EDGE = 16
STEPS = 3
SLOTS = 3
POPS = 19
PLANES = SLOTS * POPS + SLOTS
FLAG0 = SLOTS * POPS
GROUP = 24
PLANE = 3 * GROUP
SLOT = POPS * PLANE
CELLS = PLANES * 32
LANDINGS = CELLS + 8
OWN2 = LANDINGS + 8
OUTWARD = SLOTS * 5 + SLOTS
LAYERS = 2 * PLANES + OUTWARD
RIM = 11 * EDGE
REST = POPS * EDGE + 10 * EDGE
PAIR = 2 * GROUP
QUADS = PLANES // 4
TABLE = RIM
STRIPS = RIM + 8
FAR = QUADS * GROUP
EDGE_TABLE = FAR + 3 * GROUP
EDGE_ROWS = EDGE_TABLE + 24
NOWHERE = PLANES * GROUP
ALL_PLANES = PLANES + POPS
LIMIT = 20 * 1024 * 1024
WIDE_LIMIT = 127 * 512 * 1024

VELOCITY = [
    (0, 0, 0),
    (1, 0, 0),
    (-1, 0, 0),
    (0, 1, 0),
    (0, -1, 0),
    (0, 0, 1),
    (0, 0, -1),
    (1, 1, 0),
    (-1, -1, 0),
    (1, -1, 0),
    (-1, 1, 0),
    (1, 0, 1),
    (-1, 0, -1),
    (1, 0, -1),
    (-1, 0, 1),
    (0, 1, 1),
    (0, -1, -1),
    (0, 1, -1),
    (0, -1, 1),
]
NORTHWARD, SOUTHWARD = (
    [s * POPS + p for s in range(SLOTS) for p in range(POPS) if VELOCITY[p][1] == side]
    + [FLAG0 + s for s in range(SLOTS)]
    for side in (1, -1)
)
THIRD = [
    (pop, source, *((32 + 16 * k, 9) if k < 4 else (16 * (k - 4), 10)))
    for k, (pop, source) in enumerate(
        [(p, 32) for p in (4, 8, 9, 16, 18)] + [(p, 80) for p in (3, 7, 10, 15, 17)]
    )
]
OPPOSITE = [0, 2, 1, 4, 3, 6, 5, 8, 7, 10, 9, 12, 11, 14, 13, 16, 15, 18, 17]


def lanes_iota():
    return lax.broadcasted_iota(jnp.int32, (8, 128), 1)


def is_even(axis, unit=1):
    return lax.rem(lax.axis_index(axis) // unit, 2) == 0


def rows_iota():
    return lax.broadcasted_iota(jnp.int32, (8, 128), 0)


def aligned(start, size=8):
    return pl.ds(pl.multiple_of(start, 8), size)


def move_slots(moves, curve_size, cross_size):
    curve, cross = lax.axis_index("curve"), lax.axis_index("cross")

    def landed(source, target):
        inside = (source >= 0) & (source < curve_size) & (target >= 0) & (target < curve_size)
        row = jnp.clip(source, 0, curve_size - 1) * cross_size + cross
        rank = target * cross_size + cross
        hit = inside & (moves[0, row] >= 0) & (moves[1, row] == rank)
        return jnp.where(hit, moves[2, row], -1)

    return (
        landed(curve - 1, curve),
        landed(curve + 1, curve),
        landed(curve - 2, curve - 1),
        landed(curve, curve - 1),
        landed(curve + 2, curve + 1),
        landed(curve, curve + 1),
    )


def pack_kernel(
    curve_size,
    cross_size,
    moves_hbm,
    counts_hbm,
    pops_hbm,
    flags_hbm,
    neighbours_hbm,
    cells_hbm,
    mate_hbm,
    other_hbm,
    mate2_hbm,
    other2_hbm,
    rest_hbm,
    moves,
    counts,
    pops,
    flags,
    neighbours,
    cells,
    up_msg,
    down_msg,
    up2_msg,
    down2_msg,
    rest_msg,
    wide_flags,
    plane_flags,
    site_flags,
    near,
    sems,
):
    started = []

    def copy(source, target):
        one = pltpu.make_async_copy(source, target, sems.at[len(started)])
        one.start()
        started.append(one)
        return one

    flags_copy = copy(flags_hbm, flags)
    copies = [copy(pops_hbm.at[s], pops.at[s]) for s in range(SLOTS)]
    small = [
        copy(neighbours_hbm, neighbours),
        copy(counts_hbm, counts),
        copy(moves_hbm, moves),
    ]
    for one in small:
        one.wait()

    near[...] = jnp.zeros_like(near)
    named = neighbours[...]
    slot = jnp.where(named >= 0, lax.rem(jnp.maximum(named, 0), SLOTS), SLOTS)
    near[0:SLOTS, 0 : named.shape[1]] = slot.astype(jnp.float32)
    for ref, row in ((cells, CELLS), (up_msg, TABLE), (down_msg, TABLE)):
        ref[row : row + 8, :] = near[...]

    wide_flags[...] = jnp.zeros_like(wide_flags)
    flags_copy.wait()
    wide_flags[0:SLOTS, 0 : flags.shape[1]] = flags[...].astype(jnp.float32)
    span = EDGE + 2
    for x in range(EDGE):
        start = (x + 1) * span * span
        base = start // 128 * 128
        window = wide_flags[:, base : base + 512]
        window = pltpu.roll(window, (512 - (start - base)) % 512, axis=1)
        plane_flags[8 * x : 8 * x + 8, :] = window[:, :384].astype(jnp.bfloat16)
    lane_in = lax.broadcasted_iota(jnp.int32, (384, 256), 0)
    site = lax.broadcasted_iota(jnp.int32, (384, 256), 1)
    chosen = lane_in == (site // EDGE + 1) * span + site % EDGE + 1
    product = jnp.dot(
        plane_flags[...],
        jnp.where(chosen, 1.0, 0.0).astype(jnp.bfloat16),
        preferred_element_type=jnp.float32,
    )
    site_flags[0:128, :] = product[:, :128]
    site_flags[128:256, :] = product[:, 128:]
    for s in range(SLOTS):
        live = s < counts[0]
        for y in range(2):
            piece = site_flags[pl.ds(128 * y + s, EDGE, stride=8), :]
            is_fluid = (piece == 1.0) & live
            row = (FLAG0 + s) * 32 + y * EDGE
            cells[row : row + EDGE, :] = jnp.where(is_fluid, 1.0, 0.0)

    for s in range(SLOTS):
        copies[s].wait()
        for x in range(EDGE):
            for y in range(2):
                tile = 2 * x + y
                for p, size in ((0, 8), (8, 8), (16, 3)):
                    row = (s * POPS + p) * 32 + y * EDGE + x
                    cells[pl.ds(row, size, stride=32), :] = pops[
                        s, p : p + size, 128 * tile : 128 * tile + 128
                    ]

    @pl.loop(0, SLOTS)
    def _(s):
        @pl.loop(0, 4, unroll=2)
        def _(c):
            base = s * (POPS * 32) + c * 8
            view = cells.at[aligned(base, (POPS - 1) * 32 + 8), :]
            h = [view[p * 32 : p * 32 + 8, :] for p in range(POPS)]
            for p, value in enumerate(collided(h)):
                view[p * 32 : p * 32 + 8, :] = value

    for i, slot in enumerate(move_slots(moves, curve_size, cross_size)):
        value = jnp.full((1, 128), slot, jnp.int32)
        cells[LANDINGS + i : LANDINGS + i + 1, :] = value.astype(jnp.float32)

    body_copy = copy(cells.at[:OWN2], cells_hbm.at[:OWN2])

    for y in range(2):
        for msg, x0, first in ((up_msg, 15, 1), (down_msg, 0, 2)):
            step = -1 if x0 else 1
            for k in range(2):
                out = STRIPS + y * LAYERS + k * PLANES
                msg[out : out + PLANES, :] = cells[
                    pl.ds(y * EDGE + x0 + step * k, PLANES, stride=32), :
                ]
            row = y * EDGE + x0 + 2 * step
            out = STRIPS + y * LAYERS + 2 * PLANES
            for s in range(SLOTS):
                base = s * POPS * 32 + row
                msg[out + 5 * s : out + 5 * s + 1, :] = cells[pl.ds(base + first * 32, 1), :]
                msg[out + 5 * s + 1 : out + 5 * s + 5, :] = cells[
                    pl.ds(base + (first + 6) * 32, 4, stride=64), :
                ]
            msg[out + 5 * SLOTS : out + OUTWARD, :] = cells[
                pl.ds(FLAG0 * 32 + row, SLOTS, stride=32), :
            ]

    here = lax.axis_index("curve") * cross_size + lax.axis_index("cross")
    leaving = jnp.maximum(moves[0, here], 0)
    lane = lanes_iota()
    for v in range(2):
        halves = [
            [cells[aligned(leaving * (POPS * 32) + p * 32 + y * EDGE + v * 8), :] for y in (0, 1)]
            for p in range(POPS)
        ]
        outer = [jnp.where(lane < 64, first, second) for first, second in halves]
        middle = (lane >= 32) & (lane < 96)
        sets = [
            jnp.where(middle, pltpu.roll(outer[p + 1], 64, axis=1), outer[p])
            for p in range(0, POPS - 1, 2)
        ]
        sets += [outer[POPS - 1], jnp.zeros_like(outer[0])]
        for pop, source, target, which in THIRD:
            moved = pltpu.roll(outer[pop], (target - source) % 128, axis=1)
            sets[which] = jnp.where(lane // 16 == target // 16, moved, sets[which])
        for k, value in enumerate(sets):
            row = k * EDGE + v * 8
            up_msg[row : row + 8, :] = value
            down_msg[row : row + 8, :] = value
        for p, (first, second) in enumerate(halves):
            row = p * EDGE + v * 8
            rest_msg[row : row + 8, :] = jnp.where(lane < 32, second, first)
        for p in range(0, POPS, 2):
            value = halves[p][1]
            if p + 1 < POPS:
                value = jnp.where(middle, value, pltpu.roll(halves[p + 1][1], 64, axis=1))
            row = (POPS + p // 2) * EDGE + v * 8
            rest_msg[row : row + 8, :] = value
    for s in range(SLOTS):

        @pl.when(leaving == s)
        def _():
            for y in range(2):
                for k in range(3):
                    out = (y * 3 + k) * GROUP
                    row = s * POPS * 32 + y * EDGE + k
                    up2_msg[out : out + POPS, :] = cells[pl.ds(row + 13, POPS, stride=32), :]
                    down2_msg[out : out + POPS, :] = cells[pl.ds(row, POPS, stride=32), :]

    cells[OWN2 : OWN2 + 6 * GROUP, :] = up2_msg[...]
    cells[OWN2 + 6 * GROUP :, :] = down2_msg[...]
    last = [copy(cells.at[OWN2:], cells_hbm.at[OWN2:]), copy(rest_msg, rest_hbm)]
    count = len(started)
    for i, (up, down, mate, other, unit) in enumerate(
        ((up_msg, down_msg, mate_hbm, other_hbm, 1), (up2_msg, down2_msg, mate2_hbm, other2_hbm, 2))
    ):
        first, second = sems.at[count + 2 * i], sems.at[count + 2 * i + 1]
        even = is_even("curve", unit)

        @pl.when(even)
        def _():
            pltpu.make_async_copy(up, mate, first).start()
            pltpu.make_async_copy(down, other, second).start()

        @pl.when(jnp.logical_not(even))
        def _():
            pltpu.make_async_copy(down, mate, first).start()
            pltpu.make_async_copy(up, other, second).start()

        last.append(pltpu.make_async_copy(up, mate, first))
        last.append(pltpu.make_async_copy(down, other, second))
    body_copy.wait()
    for one in last:
        one.wait()


def spread_kernel(cells, outer, landings):
    low = lanes_iota() < 64
    landings[...] = cells[LANDINGS : LANDINGS + 8, :].astype(jnp.int32)
    for q in range(PLANES):
        for v in range(2):
            row = q * 32 + v * 8
            first, second = cells[row : row + 8, :], cells[row + EDGE : row + EDGE + 8, :]
            row = q * GROUP + v * 8
            outer[row : row + 8, :] = jnp.where(low, first, second)


def sort_messages(mate_msg, other_msg, mate2_msg, other2_msg, low_msg, high_msg, low2, high2):
    for mate, other, low, high, unit in (
        (mate_msg, other_msg, low_msg, high_msg, 1),
        (mate2_msg, other2_msg, low2, high2, 2),
    ):
        even = is_even("curve", unit)

        @pl.when(even)
        def _():
            low[...] = other[...]
            high[...] = mate[...]

        @pl.when(jnp.logical_not(even))
        def _():
            low[...] = mate[...]
            high[...] = other[...]


def rim_of(msg, p, v):
    row = p // 2 * EDGE + v * 8
    value = msg[row : row + 8, :]
    return pltpu.roll(value, 64, axis=1) if p % 2 else value


def sel4(parts, lane):
    first = jnp.where(lane < 32, parts[0], parts[1])
    second = jnp.where(lane < 96, parts[2], parts[3])
    return jnp.where(lane < 64, first, second)


def strip_rows(first, row0, step):
    pieces = []
    for k in range(2):
        pieces.append(
            (PLANES, lambda size, row: pl.ds(row, PLANES, stride=size), row0 + step * k, STRIPS + k * PLANES)
        )
    row, source = row0 + 2 * step, STRIPS + 2 * PLANES
    for s in range(SLOTS):
        plane = s * POPS + first
        pieces.append((1, lambda size, row, plane=plane: pl.ds(plane * size + row, 1), row, source))
        pieces.append(
            (
                4,
                lambda size, row, plane=plane: pl.ds(
                    (plane + 6) * size + row, 4, stride=2 * size
                ),
                row,
                source + 1,
            )
        )
        source += 5
    pieces.append(
        (SLOTS, lambda size, row: pl.ds(FLAG0 * size + row, SLOTS, stride=size), row, source)
    )
    return pieces


def edge_kernel(
    landings,
    own_outer,
    cells,
    mate_msg,
    other_msg,
    mate2_msg,
    other2_msg,
    near_msg,
    far_msg,
    outer,
    low_msg,
    high_msg,
    low2_msg,
    high2_msg,
):
    sort_messages(
        mate_msg, other_msg, mate2_msg, other2_msg, low_msg, high_msg, low2_msg, high2_msg
    )
    from_low, from_high, low_low, low_me, high_high, high_me = (landings[i, 0] for i in range(6))
    low = lanes_iota() < 64
    for q in range(PLANES):
        for v in range(2):
            row = q * GROUP + v * 8
            outer[row : row + 8, :] = own_outer[row : row + 8, :]

    def both(first, second):
        lane = lax.broadcasted_iota(jnp.int32, first.shape, 1)
        return jnp.where(lane < 64, first, second)

    for msg, row0, step, first in ((high_msg, 16, 1, 2), (low_msg, 23, -1, 1)):
        for count, planes, row, source in strip_rows(first, row0, step):
            outer[planes(GROUP, row), :] = both(
                msg[source : source + count, :],
                msg[LAYERS + source : LAYERS + source + count, :],
            )
    lane = lanes_iota()
    for slot, msg in ((from_low, low_msg), (from_high, high_msg)):

        @pl.when(slot >= 0)
        def _():
            for v in range(2):
                values = [rim_of(msg, p, v) for p in range(POPS)]
                for pop, target, source, which in THIRD:
                    row = which * EDGE + v * 8
                    moved = pltpu.roll(msg[row : row + 8, :], (target - source) % 128, axis=1)
                    values[pop] = jnp.where(lane // 16 == target // 16, moved, values[pop])
                for p, value in enumerate(values):
                    base = slot * (POPS * GROUP) + p * GROUP + v * 8
                    outer[aligned(base), :] = value

    for s in range(SLOTS):
        for slot, msg, row0 in (
            (low_low, low2_msg, 21),
            (low_me, cells.at[OWN2:], 21),
            (high_high, high2_msg, 16),
            (high_me, cells.at[OWN2 + 6 * GROUP :], 16),
        ):

            @pl.when(slot == s)
            def _():
                for k in range(3):
                    outer[pl.ds(s * POPS * GROUP + row0 + k, POPS, stride=GROUP), :] = both(
                        msg[k * GROUP : k * GROUP + POPS, :],
                        msg[(3 + k) * GROUP : (3 + k) * GROUP + POPS, :],
                    )

    even = is_even("cross")

    def send(row, north, south):
        near_msg[row : row + 8, :] = jnp.where(even, north, south)
        far_msg[row : row + 8, :] = jnp.where(even, south, north)

    for v in range(3):

        def plane(q):
            return outer[q * GROUP + v * 8 : q * GROUP + v * 8 + 8, :]

        for quad in range(QUADS):
            parts = [plane(4 * quad)]
            parts += [pltpu.roll(plane(4 * quad + k), 32 * k, axis=1) for k in (1, 2, 3)]
            send(quad * GROUP + v * 8, sel4(parts[1:] + parts[:1], lane), sel4(parts, lane))
        for part in range(3):
            values = []
            for planes, source in ((NORTHWARD, 80), (SOUTHWARD, 32)):
                value = None
                for k, q in enumerate(planes[8 * part : 8 * part + 8]):
                    moved = pltpu.roll(plane(q), (16 * k - source) % 128, axis=1)
                    value = moved if value is None else jnp.where(lane < 16 * k, value, moved)
                values.append(value)
            send(FAR + part * GROUP + v * 8, *values)
    tables = (low_msg, TABLE), (cells, CELLS), (high_msg, TABLE)
    for i, (ref, row) in enumerate(tables):
        value = ref[row : row + 8, :]
        send(EDGE_TABLE + 8 * i, value, value)


def collided(h):
    shear = 1.0 / 0.6
    rest = h[0]
    sx, dx = h[1] + h[2], h[1] - h[2]
    sy, dy = h[3] + h[4], h[3] - h[4]
    sz, dz = h[5] + h[6], h[5] - h[6]
    s7, d7 = h[7] + h[8], h[7] - h[8]
    s9, d9 = h[9] + h[10], h[9] - h[10]
    s11, d11 = h[11] + h[12], h[11] - h[12]
    s13, d13 = h[13] + h[14], h[13] - h[14]
    s15, d15 = h[15] + h[16], h[15] - h[16]
    s17, d17 = h[17] + h[18], h[17] - h[18]
    txy, txz, tyz = s7 + s9, s11 + s13, s15 + s17
    pxy, pxz, pyz = s7 - s9, s11 - s13, s15 - s17
    ax, bx = d7 + d9, d11 + d13
    ay, by = d7 - d9, d15 + d17
    az, bz = d11 - d13, d15 - d17
    axes = sx + sy + sz
    diags = txy + txz + tyz
    rho = rest * (1.0 / 3.0) + axes * (1.0 / 18.0) + diags * (1.0 / 36.0)
    fx, fy, fz = ax + bx, ay + by, az + bz
    jx = dx * (1.0 / 18.0) + fx * (1.0 / 36.0)
    jy = dy * (1.0 / 18.0) + fy * (1.0 / 36.0)
    jz = dz * (1.0 / 18.0) + fz * (1.0 / 36.0)
    inverse = 1.0 / rho
    ux, uy, uz = jx * inverse, jy * inverse, jz * inverse
    qxx, qyy, qzz = jx * ux, jy * uy, jz * uz
    total = qxx + qyy + qzz

    energy = -10.0 * rest - axes * (11.0 / 18.0) + diags * (8.0 / 36.0)
    energy = (energy + 11.0 * rho - 19.0 * total) * (1.19 / 2394.0)
    square = 4.0 * rest - axes * (4.0 / 18.0) + diags * (1.0 / 36.0)
    square = (square - 3.0 * rho + 5.5 * total) * (1.4 / 252.0)
    axis_x = (3.0 * sx - axes) * (1.0 / 18.0)
    diag_x = (diags - 3.0 * tyz) * (1.0 / 36.0)
    want_x = 3.0 * qxx - total
    stress_x = (axis_x + diag_x - want_x) * (shear / 36.0)
    third_x = (diag_x - 2.0 * axis_x + 0.5 * want_x) * (1.4 / 72.0)
    axis_w = (sy - sz) * (1.0 / 18.0)
    diag_w = (txy - txz) * (1.0 / 36.0)
    want_w = qyy - qzz
    stress_w = (axis_w + diag_w - want_w) * (shear / 12.0)
    third_w = (diag_w - 2.0 * axis_w + 0.5 * want_w) * (1.4 / 24.0)

    rest_out = rest - 3.0 * (12.0 * square - 30.0 * energy)
    common = -18.0 * (11.0 * energy + 4.0 * square)
    along_x = 18.0 * (stress_x - 2.0 * third_x)
    along_w = 18.0 * (stress_w - 2.0 * third_w)
    ex = common + 2.0 * along_x
    ey = common - along_x + along_w
    ez = common - along_x - along_w
    common = 36.0 * (8.0 * energy + square)
    across_x = 36.0 * (stress_x + third_x)
    across_w = 36.0 * (stress_w + third_w)
    exy = common + across_x + across_w
    exz = common + across_x - across_w
    eyz = common - 2.0 * across_x
    cxy = shear * (0.25 * pxy - 9.0 * jx * uy)
    cxz = shear * (0.25 * pxz - 9.0 * jx * uz)
    cyz = shear * (0.25 * pyz - 9.0 * jy * uz)

    def flux(d, f, j):
        return (f * (1.0 / 36.0) - d * (4.0 / 18.0) + j * (2.0 / 3.0)) * (1.2 / 40.0)

    hx, hy, hz = flux(dx, fx, jx), flux(dy, fy, jy), flux(dz, fz, jz)
    mx = (ax - bx) * (1.98 / 8.0)
    my = (by - ay) * (1.98 / 8.0)
    mz = (az - bz) * (1.98 / 8.0)
    hx36, hy36, hz36 = 36.0 * hx, 36.0 * hy, 36.0 * hz
    xy_x, xz_x = hx36 + mx, hx36 - mx
    yz_y, xy_y = hy36 + my, hy36 - my
    xz_z, yz_z = hz36 + mz, hz36 - mz
    ox, oy, oz = -2.0 * hx36, -2.0 * hy36, -2.0 * hz36

    out = [rest_out]

    def pair(i, even, odd):
        out.append(h[i] - (even + odd))
        out.append(h[i + 1] - (even - odd))

    pair(1, ex, ox)
    pair(3, ey, oy)
    pair(5, ez, oz)
    pair(7, exy + cxy, xy_x + xy_y)
    pair(9, exy - cxy, xy_x - xy_y)
    pair(11, exz + cxz, xz_x + xz_z)
    pair(13, exz - cxz, xz_x - xz_z)
    pair(15, eyz + cyz, yz_y + yz_z)
    pair(17, eyz - cyz, yz_y - yz_z)
    return out


def collide_all(h_ref, flags, posts):
    for groups in ((0, 1), (2,)):
        ref = posts[groups[0] // 2]
        size = len(groups) * GROUP

        @pl.loop(0, SLOTS)
        def _(s):
            @pl.loop(0, size // 8, unroll=3)
            def _(c):
                is_fluid = flags[groups[0] // 2][aligned((FLAG0 + s) * size + c * 8), :] > 0.0
                start = s * SLOT + groups[0] * GROUP + c * 8
                h_view = h_ref.at[aligned(start, (POPS - 1) * PLANE + 8), :]
                start = s * (POPS * size) + c * 8
                view = ref.at[aligned(start, (POPS - 1) * size + 8), :]
                h = [h_view[p * PLANE : p * PLANE + 8, :] for p in range(POPS)]
                for p, value in enumerate(collided(h)):
                    view[p * size : p * size + 8, :] = jnp.where(is_fluid, value, jnp.nan)


def hide_walls(ref, size):
    @pl.loop(0, SLOTS)
    def _(s):
        @pl.loop(0, size // 8)
        def _(c):
            is_fluid = ref[aligned((FLAG0 + s) * size + c * 8), :] > 0.0
            start = s * (POPS * size) + c * 8
            view = ref.at[aligned(start, (POPS - 1) * size + 8), :]
            for p in range(POPS):
                row = p * size
                view[row : row + 8, :] = jnp.where(is_fluid, view[row : row + 8, :], jnp.nan)


def stream_all(posts, h_ref, flags, table, groups, vregs, finish=None):
    lane = lanes_iota()
    row = rows_iota()
    low = lane < 64

    def one_slot(s):
        views = {}

        def view(which, key):
            if (which, key) not in views:
                start = s * (POPS * GROUP) if key == "own" else table[key[0] * 8 + s, key[1]]
                start = start if which else 2 * start
                views[which, key] = posts[which].at[
                    aligned(start, POPS * (GROUP if which else PAIR)), :
                ]
            return views[which, key]

        def load(key, pop, group, v):
            if group == 2:
                row = pop * GROUP + v * 8
            else:
                row = pop * PAIR + group * GROUP + v * 8
            return view(group // 2, key)[row : row + 8, :]

        h_view = h_ref.at[aligned(s * SLOT, SLOT), :]

        def shifted(pop, group, j, dy, dz):
            cx = VELOCITY[pop][0]

            def rows(key, v):
                return load(key, pop, group, v)

            def look(i, j, dx, v):
                if (dx, dy, dz) == (0, 0, 0):
                    return rows("own", v)
                if j is None:
                    return jnp.where(low, look(i, 1, dx, v), look(i, -1, dx, v))
                region = (i + 1) * 3 + j + 1
                return rows((region, VELOCITY.index((dx, dy, dz)) - 1), v)

            need_last = vregs == 3
            values = [look(0, j, 0, 0), look(0, j, 0, 1)]
            if need_last:
                if dy == 0 and dz == 0:
                    values.append(rows("own", 2))
                else:
                    values.append(jnp.where(row < 4, look(1, j, 0, 2), look(-1, j, 0, 2)))
            if cx == 0:
                return values
            turn = 1 if cx > 0 else 7
            rolled = [pltpu.roll(value, turn, axis=0) for value in values]
            if cx > 0:
                before = pltpu.roll(look(0, j, -1, 2), 1, axis=0)
                result = [
                    jnp.where(row == 0, before, rolled[0]),
                    jnp.where(row == 0, rolled[0], rolled[1]),
                ]
                if need_last:
                    edge = pltpu.roll(look(1, j, -1, 1), 1, axis=0)
                    result.append(jnp.where(row == 0, edge, rolled[2]))
                return result
            after = pltpu.roll(look(0, j, 1, 2), 7, axis=0)
            result = [
                jnp.where(row == 7, rolled[1], rolled[0]),
                jnp.where(row == 7, after, rolled[1]),
            ]
            if need_last:
                edge = pltpu.roll(look(-1, j, 1, 0), 7, axis=0)
                result.append(jnp.where(row == 7, edge, rolled[2]))
            return result

        for pop in range(POPS):
            cx, cy, cz = VELOCITY[pop]
            kept = {}

            def source(*key):
                if key not in kept:
                    kept[key] = shifted(pop, *key)
                return kept[key]

            def along_y(group, dz):
                values = source(group, None if group == 2 else 0, 0, dz)
                if cy == 0:
                    return values
                other = (group - cy) % 3
                if group != 2 and other != 2:
                    carried = source(other, 0, 0, dz)
                else:
                    carried = source(other, cy if group == 2 else 0, -cy, dz)
                mask = lane >= 112 if cy > 0 else lane < 16
                return [jnp.where(mask, b, a) for a, b in zip(values, carried)]

            for group in groups:
                values = along_y(group, 0)
                turn = (16 * cy + cz) % 128
                if turn:
                    values = [pltpu.roll(value, turn, axis=1) for value in values]
                if cz:
                    turn = (16 * cy - 15 * cz) % 128
                    wrapped = [pltpu.roll(value, turn, axis=1) for value in along_y(group, -cz)]
                    mask = lane % 16 == (0 if cz > 0 else 15)
                    values = [jnp.where(mask, b, a) for a, b in zip(values, wrapped)]
                for v, value in enumerate(values[:vregs]):
                    if pop:
                        value = jnp.where(value != value, load("own", OPPOSITE[pop], group, v), value)
                    if finish is not None:
                        is_fluid = flags[group // 2][
                            aligned((FLAG0 + s) * PAIR + group * GROUP + v * 8), :
                        ]
                        value = jnp.where(is_fluid > 0.0, value, 0.0)
                    target = pop * PLANE + group * GROUP + v * 8
                    h_view[target : target + 8, :] = value

    @pl.loop(0, SLOTS)
    def _(s):
        one_slot(s)
        if finish is not None:
            finish(s)


def join_kernel(
    landings,
    cells,
    mate_msg,
    other_msg,
    mate2_msg,
    other2_msg,
    mate_rest,
    passed_rest,
    post_ref,
    slots,
    low_msg,
    high_msg,
    low2_msg,
    high2_msg,
):
    sort_messages(
        mate_msg, other_msg, mate2_msg, other2_msg, low_msg, high_msg, low2_msg, high2_msg
    )
    for i, (ref, row) in enumerate(((low_msg, TABLE), (cells, CELLS), (high_msg, TABLE))):
        slots[8 * i : 8 * i + 8, :] = first_rows(ref[row : row + 8, :])

    from_low, from_high, low_low, low_me, high_high, high_me = (landings[i, 0] for i in range(6))
    lane = lanes_iota()
    post_ref[PLANES * PAIR :, :] = jnp.full((POPS * PAIR, 128), jnp.nan, jnp.float32)
    for q in range(PLANES):
        for y in range(2):
            start = q * PAIR + y * GROUP
            post_ref[start : start + EDGE, :] = cells[
                q * 32 + y * EDGE : q * 32 + (y + 1) * EDGE, :
            ]
    even = is_even("curve")
    odd = jnp.logical_not(even)
    for slot, msg, wanted, rest in (
        (from_low, low_msg, odd, mate_rest),
        (from_low, low_msg, even, passed_rest),
        (from_high, high_msg, even, mate_rest),
        (from_high, high_msg, odd, passed_rest),
    ):

        @pl.when((slot >= 0) & wanted)
        def _():
            for p in range(POPS):
                for v in range(2):
                    rim = rim_of(msg, p, v)
                    row = p * EDGE + v * 8
                    wide = rest[row : row + 8, :]
                    row = (POPS + p // 2) * EDGE + v * 8
                    middle = rest[row : row + 8, :]
                    if p % 2:
                        middle = pltpu.roll(middle, 64, axis=1)
                    second = jnp.where(lane < 32, wide, jnp.where(lane < 96, middle, rim))
                    start = slot * (POPS * PAIR) + p * PAIR + v * 8
                    post_ref[aligned(start), :] = jnp.where(lane < 32, rim, wide)
                    post_ref[aligned(start + GROUP), :] = second

    for msg, row0, step, first in ((high_msg, 16, 1, 2), (low_msg, 23, -1, 1)):
        for y in range(2):
            for count, planes, row, source in strip_rows(first, row0, step):
                source += y * LAYERS
                post_ref[planes(PAIR, row + y * GROUP), :] = msg[source : source + count, :]
    for s in range(SLOTS):
        for slot, msg, row0 in (
            (low_low, low2_msg, 21),
            (low_me, cells.at[OWN2:], 21),
            (high_high, high2_msg, 16),
            (high_me, cells.at[OWN2 + 6 * GROUP :], 16),
        ):

            @pl.when(slot == s)
            def _():
                for y in range(2):
                    for k in range(3):
                        row = s * POPS * PAIR + y * GROUP + row0 + k
                        source = (y * 3 + k) * GROUP
                        post_ref[pl.ds(row, POPS, stride=PAIR), :] = msg[source : source + POPS, :]
    hide_walls(post_ref, PAIR)


def first_rows(slot):
    slot = slot.astype(jnp.int32)
    return jnp.where(slot == SLOTS, NOWHERE, slot * (POPS * GROUP))


def steps_kernel(
    own_slots,
    first_post,
    near_msg,
    far_msg,
    out_hbm,
    h_ref,
    post_ref,
    outer_ref,
    out,
    slots,
    table,
    sems,
):
    even = is_even("cross")

    def received(row):
        near, far = near_msg[row : row + 8, :], far_msg[row : row + 8, :]
        return jnp.where(even, far, near), jnp.where(even, near, far)

    for i in range(3):
        south, north = received(EDGE_TABLE + 8 * i)
        slots[24 * i : 24 * i + 8, :] = first_rows(south)
        slots[24 * i + 8 : 24 * i + 16, :] = own_slots[8 * i : 8 * i + 8, :]
        slots[24 * i + 16 : 24 * i + 24, :] = first_rows(north)
    table_copy = pltpu.make_async_copy(slots, table, sems.at[SLOTS])
    table_copy.start()

    nothing = jnp.full((8, 128), jnp.nan, jnp.float32)
    for row in range(0, POPS * GROUP, 8):
        outer_ref[NOWHERE + row : NOWHERE + row + 8, :] = nothing
    for row in range(PLANES * PAIR, ALL_PLANES * PAIR, 8):
        post_ref[row : row + 8, :] = nothing
    lane = lanes_iota()
    for v in range(3):

        def rows(q):
            return slice(q * GROUP + v * 8, q * GROUP + v * 8 + 8)

        for quad in range(QUADS):
            south, north = received(quad * GROUP + v * 8)
            for k in range(4):
                value = jnp.where(lane // 32 == (k + 3) % 4, south, north)
                if k:
                    value = pltpu.roll(value, 128 - 32 * k, axis=1)
                outer_ref[rows(4 * quad + k), :] = value
        for part in range(3):
            values = received(FAR + part * GROUP + v * 8)
            for planes, target, value in zip((NORTHWARD, SOUTHWARD), (80, 32), values):
                for k, q in enumerate(planes[8 * part : 8 * part + 8]):
                    moved = pltpu.roll(value, (target - 16 * k) % 128, axis=1)
                    outer_ref[rows(q), :] = jnp.where(
                        lane // 16 == target // 16, moved, outer_ref[rows(q), :]
                    )
    hide_walls(outer_ref, GROUP)
    table_copy.wait()

    def finish(s):
        for x in range(EDGE):
            for y in range(2):
                tile = 2 * x + y
                for p, size in ((0, 8), (8, 8), (16, 3)):
                    row = s * SLOT + (p * PLANE + y * GROUP + x)
                    out[s, p : p + size, 128 * tile : 128 * tile + 128] = h_ref[
                        pl.ds(row, size, stride=PLANE), :
                    ]
        pltpu.make_async_copy(out.at[s], out_hbm.at[s], sems.at[s]).start()

    flags = (first_post, outer_ref)
    posts = flags
    for _ in range(STEPS - 1):
        stream_all(posts, h_ref, flags, table, (0, 1, 2), 3)
        posts = (post_ref, outer_ref)
        collide_all(h_ref, flags, posts)
    stream_all(posts, h_ref, flags, table, (0, 1), 2, finish)
    for s in range(SLOTS):
        pltpu.make_async_copy(out.at[s], out_hbm.at[s], sems.at[s]).wait()


def swapped(value, axis, unit=1):
    count = lax.axis_size(axis)
    results = []
    for which in (0, 1):
        sides = [unit if i // unit % 2 == which else -unit for i in range(count)]
        pairs = [(i, i + side) for i, side in enumerate(sides) if 0 <= i + side < count]
        results.append(lax.ppermute(value[which], axis, pairs))
    return results


def rows128(count):
    return jax.ShapeDtypeStruct((count, 128), jnp.float32)


def call(kernel, in_spaces, out_spaces, outs, ins, scratch, limit=LIMIT):
    spaces = {
        "S": pl.BlockSpec(memory_space=pltpu.SMEM),
        "V": pl.BlockSpec(memory_space=pltpu.VMEM),
        "H": pl.BlockSpec(memory_space=pltpu.HBM),
    }
    return pl.pallas_call(
        kernel,
        out_shape=outs,
        in_specs=[spaces[x] for x in in_spaces],
        out_specs=[spaces[x] for x in out_spaces],
        scratch_shapes=scratch,
        compiler_params=pltpu.CompilerParams(vmem_limit_bytes=limit),
    )(*ins)


def per_device(populations, site_flags, neighbours, migrations, counts):
    sizes = (lax.axis_size("curve"), lax.axis_size("cross"))
    moves = migrations.T
    floats = lambda rows: pltpu.VMEM((rows, 128), jnp.float32)
    messages = [
        OWN2 + 12 * GROUP,
        STRIPS + 2 * LAYERS,
        STRIPS + 2 * LAYERS,
        6 * GROUP,
        6 * GROUP,
        REST,
    ]
    cells, mate_msg, other_msg, mate2_msg, other2_msg, rest_msg = call(
        functools.partial(pack_kernel, *sizes),
        "HHHHH",
        "HHHHHH",
        [rows128(rows) for rows in messages],
        (moves, counts, populations, site_flags, neighbours),
        [
            pltpu.SMEM(moves.shape, jnp.int32),
            pltpu.SMEM(counts.shape, jnp.int32),
            pltpu.VMEM(populations.shape, jnp.float32),
            pltpu.VMEM(site_flags.shape, jnp.int32),
            pltpu.VMEM(neighbours.shape, jnp.int32),
            *[floats(rows) for rows in messages],
            pltpu.VMEM((8, 5888), jnp.float32),
            pltpu.VMEM((128, 384), jnp.bfloat16),
            floats(256),
            floats(8),
            pltpu.SemaphoreType.DMA((4 + SLOTS + 8,)),
        ],
        WIDE_LIMIT,
    )
    mate_msg, other_msg = swapped((mate_msg, other_msg), "curve")
    mate2_msg, other2_msg = swapped((mate2_msg, other2_msg), "curve", 2)
    assert sizes[0] % 2 == 0
    pairs = [(i, i ^ 1) for i in range(sizes[0])]
    mate_rest = lax.ppermute(rest_msg, "curve", pairs)
    pairs = [(i, i - 2 if i % 2 else i + 2) for i in range(sizes[0])]
    pairs = [pair for pair in pairs if 0 <= pair[1] < sizes[0]]
    passed_rest = lax.ppermute(mate_rest, "curve", pairs)
    outer, landings = call(
        spread_kernel,
        "V",
        "VV",
        [rows128(PLANES * GROUP), jax.ShapeDtypeStruct((8, 128), jnp.int32)],
        (cells,),
        [],
    )
    strips = (cells, mate_msg, other_msg, mate2_msg, other2_msg)
    sorted_rows = [messages[1], messages[1], messages[3], messages[3]]
    near_msg, far_msg = call(
        edge_kernel,
        "SVVVVVV",
        "VV",
        [rows128(EDGE_ROWS), rows128(EDGE_ROWS)],
        (landings, outer, *strips),
        [floats(rows) for rows in [PLANES * GROUP] + sorted_rows],
    )
    near_msg, far_msg = swapped((near_msg, far_msg), "cross")
    post, own_slots = call(
        join_kernel,
        "SVVVVVVV",
        "VV",
        [rows128(ALL_PLANES * PAIR), jax.ShapeDtypeStruct((24, 128), jnp.int32)],
        (landings, *strips, mate_rest, passed_rest),
        [floats(rows) for rows in sorted_rows],
    )
    return call(
        steps_kernel,
        "VVVV",
        "H",
        [jax.ShapeDtypeStruct(populations.shape, jnp.float32)],
        (own_slots, post, near_msg, far_msg),
        [
            floats(SLOTS * SLOT),
            floats(ALL_PLANES * PAIR),
            floats(ALL_PLANES * GROUP),
            pltpu.VMEM(populations.shape, jnp.float32),
            pltpu.VMEM((72, 128), jnp.int32),
            pltpu.SMEM((72, 128), jnp.int32),
            pltpu.SemaphoreType.DMA((SLOTS + 1,)),
        ],
    )[0]


def solution(mesh):
    return jax.shard_map(
        per_device,
        mesh=mesh,
        in_specs=(
            P(("curve", "cross"), None, None),
            P(("curve", "cross"), None),
            P(("curve", "cross"), None),
            P(),
            P(("curve", "cross")),
        ),
        out_specs=P(("curve", "cross"), None, None),
        check_vma=False,
    )
```

```python
import functools
import itertools

import jax
import jax.numpy as jnp
import numpy as np
from jax import lax
from jax.experimental import pallas as pl
from jax.experimental.pallas import tpu as pltpu
from jax.sharding import PartitionSpec as P

EDGE = 16
STEPS = 3
SLOTS = 3
POPS = 19
PLANES = SLOTS * POPS + SLOTS
FLAG0 = SLOTS * POPS
GROUP = 24
PLANE = 3 * GROUP
SLOT = POPS * PLANE
CELLS = PLANES * 32
LANDINGS = CELLS + 8
OWN2 = LANDINGS + 8
OUTWARD = SLOTS * 5 + SLOTS
LAYERS = 2 * PLANES + OUTWARD
RIM = 11 * EDGE
REST = POPS * EDGE + 10 * EDGE
PAIR = 2 * GROUP
QUADS = PLANES // 4
TABLE = RIM
STRIPS = RIM + 8
FAR = QUADS * GROUP
EDGE_TABLE = FAR + 3 * GROUP
EDGE_ROWS = EDGE_TABLE + 24
CUT = EDGE_ROWS // 16 * 8
NOWHERE = PLANES * GROUP
ALL_PLANES = PLANES + POPS
LIMIT = 20 * 1024 * 1024
WIDE_LIMIT = 127 * 512 * 1024

VELOCITY = [
    (0, 0, 0),
    (1, 0, 0),
    (-1, 0, 0),
    (0, 1, 0),
    (0, -1, 0),
    (0, 0, 1),
    (0, 0, -1),
    (1, 1, 0),
    (-1, -1, 0),
    (1, -1, 0),
    (-1, 1, 0),
    (1, 0, 1),
    (-1, 0, -1),
    (1, 0, -1),
    (-1, 0, 1),
    (0, 1, 1),
    (0, -1, -1),
    (0, 1, -1),
    (0, -1, 1),
]
NORTHWARD, SOUTHWARD = (
    [s * POPS + p for s in range(SLOTS) for p in range(POPS) if VELOCITY[p][1] == side]
    + [FLAG0 + s for s in range(SLOTS)]
    for side in (1, -1)
)
THIRD = [
    (pop, source, *((32 + 16 * k, 9) if k < 4 else (16 * (k - 4), 10)))
    for k, (pop, source) in enumerate(
        [(p, 32) for p in (4, 8, 9, 16, 18)] + [(p, 80) for p in (3, 7, 10, 15, 17)]
    )
]
OPPOSITE = [0, 2, 1, 4, 3, 6, 5, 8, 7, 10, 9, 12, 11, 14, 13, 16, 15, 18, 17]


def lanes_iota():
    return lax.broadcasted_iota(jnp.int32, (8, 128), 1)


def is_even(axis, unit=1):
    return lax.rem(lax.axis_index(axis) // unit, 2) == 0


def rows_iota():
    return lax.broadcasted_iota(jnp.int32, (8, 128), 0)


def aligned(start, size=8):
    return pl.ds(pl.multiple_of(start, 8), size)


def move_slots(moves, curve_size, cross_size):
    curve, cross = lax.axis_index("curve"), lax.axis_index("cross")

    def landed(source, target):
        inside = (source >= 0) & (source < curve_size) & (target >= 0) & (target < curve_size)
        row = jnp.clip(source, 0, curve_size - 1) * cross_size + cross
        rank = target * cross_size + cross
        hit = inside & (moves[0, row] >= 0) & (moves[1, row] == rank)
        return jnp.where(hit, moves[2, row], -1)

    return (
        landed(curve - 1, curve),
        landed(curve + 1, curve),
        landed(curve - 2, curve - 1),
        landed(curve, curve - 1),
        landed(curve + 2, curve + 1),
        landed(curve, curve + 1),
    )


def pack_kernel(
    curve_size,
    cross_size,
    moves_hbm,
    counts_hbm,
    pops_hbm,
    flags_hbm,
    neighbours_hbm,
    cells_hbm,
    mate_hbm,
    other_hbm,
    mate2_hbm,
    other2_hbm,
    rest_hbm,
    moves,
    counts,
    pops,
    flags,
    neighbours,
    cells,
    up_msg,
    down_msg,
    up2_msg,
    down2_msg,
    rest_msg,
    wide_flags,
    plane_flags,
    site_flags,
    near,
    sems,
):
    started = []

    def copy(source, target):
        one = pltpu.make_async_copy(source, target, sems.at[len(started)])
        one.start()
        started.append(one)
        return one

    flags_copy = copy(flags_hbm, flags)
    copies = [copy(pops_hbm.at[s], pops.at[s]) for s in range(SLOTS)]
    small = [
        copy(neighbours_hbm, neighbours),
        copy(counts_hbm, counts),
        copy(moves_hbm, moves),
    ]
    for one in small:
        one.wait()

    near[...] = jnp.zeros_like(near)
    named = neighbours[...]
    slot = jnp.where(named >= 0, lax.rem(jnp.maximum(named, 0), SLOTS), SLOTS)
    near[0:SLOTS, 0 : named.shape[1]] = slot.astype(jnp.float32)
    for ref, row in ((cells, CELLS), (up_msg, TABLE), (down_msg, TABLE)):
        ref[row : row + 8, :] = near[...]

    wide_flags[...] = jnp.zeros_like(wide_flags)
    flags_copy.wait()
    wide_flags[0:SLOTS, 0 : flags.shape[1]] = flags[...].astype(jnp.float32)
    span = EDGE + 2
    for x in range(EDGE):
        start = (x + 1) * span * span
        base = start // 128 * 128
        window = wide_flags[:, base : base + 512]
        window = pltpu.roll(window, (512 - (start - base)) % 512, axis=1)
        plane_flags[8 * x : 8 * x + 8, :] = window[:, :384].astype(jnp.bfloat16)
    lane_in = lax.broadcasted_iota(jnp.int32, (384, 256), 0)
    site = lax.broadcasted_iota(jnp.int32, (384, 256), 1)
    chosen = lane_in == (site // EDGE + 1) * span + site % EDGE + 1
    product = jnp.dot(
        plane_flags[...],
        jnp.where(chosen, 1.0, 0.0).astype(jnp.bfloat16),
        preferred_element_type=jnp.float32,
    )
    site_flags[0:128, :] = product[:, :128]
    site_flags[128:256, :] = product[:, 128:]
    for s in range(SLOTS):
        live = s < counts[0]
        for y in range(2):
            piece = site_flags[pl.ds(128 * y + s, EDGE, stride=8), :]
            is_fluid = (piece == 1.0) & live
            row = (FLAG0 + s) * 32 + y * EDGE
            cells[row : row + EDGE, :] = jnp.where(is_fluid, 1.0, 0.0)

    for s in range(SLOTS):
        copies[s].wait()
        for x in range(EDGE):
            for y in range(2):
                tile = 2 * x + y
                for p, size in ((0, 8), (8, 8), (16, 3)):
                    row = (s * POPS + p) * 32 + y * EDGE + x
                    cells[pl.ds(row, size, stride=32), :] = pops[
                        s, p : p + size, 128 * tile : 128 * tile + 128
                    ]

    @pl.loop(0, SLOTS)
    def _(s):
        @pl.loop(0, 4, unroll=2)
        def _(c):
            base = s * (POPS * 32) + c * 8
            view = cells.at[aligned(base, (POPS - 1) * 32 + 8), :]
            h = [view[p * 32 : p * 32 + 8, :] for p in range(POPS)]
            for p, value in enumerate(collided(h)):
                view[p * 32 : p * 32 + 8, :] = value

    for i, slot in enumerate(move_slots(moves, curve_size, cross_size)):
        value = jnp.full((1, 128), slot, jnp.int32)
        cells[LANDINGS + i : LANDINGS + i + 1, :] = value.astype(jnp.float32)

    body_copy = copy(cells.at[:OWN2], cells_hbm.at[:OWN2])

    for y in range(2):
        for msg, x0, first in ((up_msg, 15, 1), (down_msg, 0, 2)):
            step = -1 if x0 else 1
            for k in range(2):
                out = STRIPS + y * LAYERS + k * PLANES
                msg[out : out + PLANES, :] = cells[
                    pl.ds(y * EDGE + x0 + step * k, PLANES, stride=32), :
                ]
            row = y * EDGE + x0 + 2 * step
            out = STRIPS + y * LAYERS + 2 * PLANES
            for s in range(SLOTS):
                base = s * POPS * 32 + row
                msg[out + 5 * s : out + 5 * s + 1, :] = cells[pl.ds(base + first * 32, 1), :]
                msg[out + 5 * s + 1 : out + 5 * s + 5, :] = cells[
                    pl.ds(base + (first + 6) * 32, 4, stride=64), :
                ]
            msg[out + 5 * SLOTS : out + OUTWARD, :] = cells[
                pl.ds(FLAG0 * 32 + row, SLOTS, stride=32), :
            ]

    here = lax.axis_index("curve") * cross_size + lax.axis_index("cross")
    leaving = jnp.maximum(moves[0, here], 0)
    lane = lanes_iota()
    for v in range(2):
        halves = [
            [cells[aligned(leaving * (POPS * 32) + p * 32 + y * EDGE + v * 8), :] for y in (0, 1)]
            for p in range(POPS)
        ]
        outer = [jnp.where(lane < 64, first, second) for first, second in halves]
        middle = (lane >= 32) & (lane < 96)
        sets = [
            jnp.where(middle, pltpu.roll(outer[p + 1], 64, axis=1), outer[p])
            for p in range(0, POPS - 1, 2)
        ]
        sets += [outer[POPS - 1], jnp.zeros_like(outer[0])]
        for pop, source, target, which in THIRD:
            moved = pltpu.roll(outer[pop], (target - source) % 128, axis=1)
            sets[which] = jnp.where(lane // 16 == target // 16, moved, sets[which])
        for k, value in enumerate(sets):
            row = k * EDGE + v * 8
            up_msg[row : row + 8, :] = value
            down_msg[row : row + 8, :] = value
        for p, (first, second) in enumerate(halves):
            row = p * EDGE + v * 8
            rest_msg[row : row + 8, :] = jnp.where(lane < 32, second, first)
        for p in range(0, POPS, 2):
            value = halves[p][1]
            if p + 1 < POPS:
                value = jnp.where(middle, value, pltpu.roll(halves[p + 1][1], 64, axis=1))
            row = (POPS + p // 2) * EDGE + v * 8
            rest_msg[row : row + 8, :] = value
    for s in range(SLOTS):

        @pl.when(leaving == s)
        def _():
            for y in range(2):
                for k in range(3):
                    out = (y * 3 + k) * GROUP
                    row = s * POPS * 32 + y * EDGE + k
                    up2_msg[out : out + POPS, :] = cells[pl.ds(row + 13, POPS, stride=32), :]
                    down2_msg[out : out + POPS, :] = cells[pl.ds(row, POPS, stride=32), :]

    cells[OWN2 : OWN2 + 6 * GROUP, :] = up2_msg[...]
    cells[OWN2 + 6 * GROUP :, :] = down2_msg[...]
    last = [copy(cells.at[OWN2:], cells_hbm.at[OWN2:]), copy(rest_msg, rest_hbm)]
    count = len(started)
    for i, (up, down, mate, other, unit) in enumerate(
        ((up_msg, down_msg, mate_hbm, other_hbm, 1), (up2_msg, down2_msg, mate2_hbm, other2_hbm, 2))
    ):
        first, second = sems.at[count + 2 * i], sems.at[count + 2 * i + 1]
        even = is_even("curve", unit)

        @pl.when(even)
        def _():
            pltpu.make_async_copy(up, mate, first).start()
            pltpu.make_async_copy(down, other, second).start()

        @pl.when(jnp.logical_not(even))
        def _():
            pltpu.make_async_copy(down, mate, first).start()
            pltpu.make_async_copy(up, other, second).start()

        last.append(pltpu.make_async_copy(up, mate, first))
        last.append(pltpu.make_async_copy(down, other, second))
    body_copy.wait()
    for one in last:
        one.wait()


def spread_kernel(cells, outer):
    low = lanes_iota() < 64
    for q in range(PLANES):
        for v in range(2):
            row = q * 32 + v * 8
            first, second = cells[row : row + 8, :], cells[row + EDGE : row + EDGE + 8, :]
            row = q * GROUP + v * 8
            outer[row : row + 8, :] = jnp.where(low, first, second)


def sort_messages(mate_msg, other_msg, mate2_msg, other2_msg, low_msg, high_msg, low2, high2):
    for mate, other, low, high, unit in (
        (mate_msg, other_msg, low_msg, high_msg, 1),
        (mate2_msg, other2_msg, low2, high2, 2),
    ):
        even = is_even("curve", unit)

        @pl.when(even)
        def _():
            low[...] = other[...]
            high[...] = mate[...]

        @pl.when(jnp.logical_not(even))
        def _():
            low[...] = mate[...]
            high[...] = other[...]


def landed_slots(cells):
    return [jnp.max(cells[LANDINGS + i : LANDINGS + i + 1, :]) for i in range(6)]


def rim_of(msg, p, v):
    row = p // 2 * EDGE + v * 8
    value = msg[row : row + 8, :]
    return pltpu.roll(value, 64, axis=1) if p % 2 else value


def sel4(parts, lane):
    first = jnp.where(lane < 32, parts[0], parts[1])
    second = jnp.where(lane < 96, parts[2], parts[3])
    return jnp.where(lane < 64, first, second)


def strip_rows(first, row0, step):
    pieces = []
    for k in range(2):
        pieces.append(
            (PLANES, lambda size, row: pl.ds(row, PLANES, stride=size), row0 + step * k, STRIPS + k * PLANES)
        )
    row, source = row0 + 2 * step, STRIPS + 2 * PLANES
    for s in range(SLOTS):
        plane = s * POPS + first
        pieces.append((1, lambda size, row, plane=plane: pl.ds(plane * size + row, 1), row, source))
        pieces.append(
            (
                4,
                lambda size, row, plane=plane: pl.ds(
                    (plane + 6) * size + row, 4, stride=2 * size
                ),
                row,
                source + 1,
            )
        )
        source += 5
    pieces.append(
        (SLOTS, lambda size, row: pl.ds(FLAG0 * size + row, SLOTS, stride=size), row, source)
    )
    return pieces


def edge_kernel(
    own_outer,
    cells,
    mate_msg,
    other_msg,
    mate2_msg,
    other2_msg,
    near_msg,
    far_msg,
    far2_msg,
    outer,
    low_msg,
    high_msg,
    low2_msg,
    high2_msg,
):
    sort_messages(
        mate_msg, other_msg, mate2_msg, other2_msg, low_msg, high_msg, low2_msg, high2_msg
    )
    from_low, from_high, low_low, low_me, high_high, high_me = landed_slots(cells)
    low = lanes_iota() < 64
    for q in range(PLANES):
        for v in range(2):
            row = q * GROUP + v * 8
            outer[row : row + 8, :] = own_outer[row : row + 8, :]

    def both(first, second):
        lane = lax.broadcasted_iota(jnp.int32, first.shape, 1)
        return jnp.where(lane < 64, first, second)

    for msg, row0, step, first in ((high_msg, 16, 1, 2), (low_msg, 23, -1, 1)):
        for count, planes, row, source in strip_rows(first, row0, step):
            outer[planes(GROUP, row), :] = both(
                msg[source : source + count, :],
                msg[LAYERS + source : LAYERS + source + count, :],
            )
    lane = lanes_iota()
    for s, (slot, msg) in itertools.product(
        range(SLOTS), ((from_low, low_msg), (from_high, high_msg))
    ):

        @pl.when(slot == s)
        def _():
            for v in range(2):
                values = [rim_of(msg, p, v) for p in range(POPS)]
                for pop, target, source, which in THIRD:
                    row = which * EDGE + v * 8
                    moved = pltpu.roll(msg[row : row + 8, :], (target - source) % 128, axis=1)
                    values[pop] = jnp.where(lane // 16 == target // 16, moved, values[pop])
                for p, value in enumerate(values):
                    row = (s * POPS + p) * GROUP + v * 8
                    outer[row : row + 8, :] = value

    for s in range(SLOTS):
        for slot, msg, row0 in (
            (low_low, low2_msg, 21),
            (low_me, cells.at[OWN2:], 21),
            (high_high, high2_msg, 16),
            (high_me, cells.at[OWN2 + 6 * GROUP :], 16),
        ):

            @pl.when(slot == s)
            def _():
                for k in range(3):
                    outer[pl.ds(s * POPS * GROUP + row0 + k, POPS, stride=GROUP), :] = both(
                        msg[k * GROUP : k * GROUP + POPS, :],
                        msg[(3 + k) * GROUP : (3 + k) * GROUP + POPS, :],
                    )

    even = is_even("cross")

    def send(row, north, south):
        near_msg[row : row + 8, :] = jnp.where(even, north, south)
        ref, row = (far_msg, row) if row < CUT else (far2_msg, row - CUT)
        ref[row : row + 8, :] = jnp.where(even, south, north)

    for v in range(3):

        def plane(q):
            return outer[q * GROUP + v * 8 : q * GROUP + v * 8 + 8, :]

        for quad in range(QUADS):
            parts = [plane(4 * quad)]
            parts += [pltpu.roll(plane(4 * quad + k), 32 * k, axis=1) for k in (1, 2, 3)]
            send(quad * GROUP + v * 8, sel4(parts[1:] + parts[:1], lane), sel4(parts, lane))
        for part in range(3):
            values = []
            for planes, source in ((NORTHWARD, 80), (SOUTHWARD, 32)):
                value = None
                for k, q in enumerate(planes[8 * part : 8 * part + 8]):
                    moved = pltpu.roll(plane(q), (16 * k - source) % 128, axis=1)
                    value = moved if value is None else jnp.where(lane < 16 * k, value, moved)
                values.append(value)
            send(FAR + part * GROUP + v * 8, *values)
    tables = (low_msg, TABLE), (cells, CELLS), (high_msg, TABLE)
    for i, (ref, row) in enumerate(tables):
        value = ref[row : row + 8, :]
        send(EDGE_TABLE + 8 * i, value, value)


def collided(h):
    shear = 1.0 / 0.6
    rest = h[0]
    sx, dx = h[1] + h[2], h[1] - h[2]
    sy, dy = h[3] + h[4], h[3] - h[4]
    sz, dz = h[5] + h[6], h[5] - h[6]
    s7, d7 = h[7] + h[8], h[7] - h[8]
    s9, d9 = h[9] + h[10], h[9] - h[10]
    s11, d11 = h[11] + h[12], h[11] - h[12]
    s13, d13 = h[13] + h[14], h[13] - h[14]
    s15, d15 = h[15] + h[16], h[15] - h[16]
    s17, d17 = h[17] + h[18], h[17] - h[18]
    txy, txz, tyz = s7 + s9, s11 + s13, s15 + s17
    pxy, pxz, pyz = s7 - s9, s11 - s13, s15 - s17
    ax, bx = d7 + d9, d11 + d13
    ay, by = d7 - d9, d15 + d17
    az, bz = d11 - d13, d15 - d17
    axes = sx + sy + sz
    diags = txy + txz + tyz
    rho = rest * (1.0 / 3.0) + axes * (1.0 / 18.0) + diags * (1.0 / 36.0)
    fx, fy, fz = ax + bx, ay + by, az + bz
    jx = dx * (1.0 / 18.0) + fx * (1.0 / 36.0)
    jy = dy * (1.0 / 18.0) + fy * (1.0 / 36.0)
    jz = dz * (1.0 / 18.0) + fz * (1.0 / 36.0)
    inverse = 1.0 / rho
    ux, uy, uz = jx * inverse, jy * inverse, jz * inverse
    qxx, qyy, qzz = jx * ux, jy * uy, jz * uz
    total = qxx + qyy + qzz

    energy = -10.0 * rest - axes * (11.0 / 18.0) + diags * (8.0 / 36.0)
    energy = (energy + 11.0 * rho - 19.0 * total) * (1.19 / 2394.0)
    square = 4.0 * rest - axes * (4.0 / 18.0) + diags * (1.0 / 36.0)
    square = (square - 3.0 * rho + 5.5 * total) * (1.4 / 252.0)
    axis_x = (3.0 * sx - axes) * (1.0 / 18.0)
    diag_x = (diags - 3.0 * tyz) * (1.0 / 36.0)
    want_x = 3.0 * qxx - total
    stress_x = (axis_x + diag_x - want_x) * (shear / 36.0)
    third_x = (diag_x - 2.0 * axis_x + 0.5 * want_x) * (1.4 / 72.0)
    axis_w = (sy - sz) * (1.0 / 18.0)
    diag_w = (txy - txz) * (1.0 / 36.0)
    want_w = qyy - qzz
    stress_w = (axis_w + diag_w - want_w) * (shear / 12.0)
    third_w = (diag_w - 2.0 * axis_w + 0.5 * want_w) * (1.4 / 24.0)

    rest_out = rest - 3.0 * (12.0 * square - 30.0 * energy)
    common = -18.0 * (11.0 * energy + 4.0 * square)
    along_x = 18.0 * (stress_x - 2.0 * third_x)
    along_w = 18.0 * (stress_w - 2.0 * third_w)
    ex = common + 2.0 * along_x
    ey = common - along_x + along_w
    ez = common - along_x - along_w
    common = 36.0 * (8.0 * energy + square)
    across_x = 36.0 * (stress_x + third_x)
    across_w = 36.0 * (stress_w + third_w)
    exy = common + across_x + across_w
    exz = common + across_x - across_w
    eyz = common - 2.0 * across_x
    cxy = shear * (0.25 * pxy - 9.0 * jx * uy)
    cxz = shear * (0.25 * pxz - 9.0 * jx * uz)
    cyz = shear * (0.25 * pyz - 9.0 * jy * uz)

    def flux(d, f, j):
        return (f * (1.0 / 36.0) - d * (4.0 / 18.0) + j * (2.0 / 3.0)) * (1.2 / 40.0)

    hx, hy, hz = flux(dx, fx, jx), flux(dy, fy, jy), flux(dz, fz, jz)
    mx = (ax - bx) * (1.98 / 8.0)
    my = (by - ay) * (1.98 / 8.0)
    mz = (az - bz) * (1.98 / 8.0)
    hx36, hy36, hz36 = 36.0 * hx, 36.0 * hy, 36.0 * hz
    xy_x, xz_x = hx36 + mx, hx36 - mx
    yz_y, xy_y = hy36 + my, hy36 - my
    xz_z, yz_z = hz36 + mz, hz36 - mz
    ox, oy, oz = -2.0 * hx36, -2.0 * hy36, -2.0 * hz36

    out = [rest_out]

    def pair(i, even, odd):
        out.append(h[i] - (even + odd))
        out.append(h[i + 1] - (even - odd))

    pair(1, ex, ox)
    pair(3, ey, oy)
    pair(5, ez, oz)
    pair(7, exy + cxy, xy_x + xy_y)
    pair(9, exy - cxy, xy_x - xy_y)
    pair(11, exz + cxz, xz_x + xz_z)
    pair(13, exz - cxz, xz_x - xz_z)
    pair(15, eyz + cyz, yz_y + yz_z)
    pair(17, eyz - cyz, yz_y - yz_z)
    return out


def collide_all(h_ref, flags, posts):
    for groups in ((0, 1), (2,)):
        ref = posts[groups[0] // 2]
        size = len(groups) * GROUP

        @pl.loop(0, SLOTS)
        def _(s):
            @pl.loop(0, size // 8, unroll=3)
            def _(c):
                is_fluid = flags[groups[0] // 2][aligned((FLAG0 + s) * size + c * 8), :] > 0.0
                start = s * SLOT + groups[0] * GROUP + c * 8
                h_view = h_ref.at[aligned(start, (POPS - 1) * PLANE + 8), :]
                start = s * (POPS * size) + c * 8
                view = ref.at[aligned(start, (POPS - 1) * size + 8), :]
                h = [h_view[p * PLANE : p * PLANE + 8, :] for p in range(POPS)]
                for p, value in enumerate(collided(h)):
                    view[p * size : p * size + 8, :] = jnp.where(is_fluid, value, jnp.nan)


def hide_walls(ref, size):
    @pl.loop(0, SLOTS)
    def _(s):
        @pl.loop(0, size // 8)
        def _(c):
            is_fluid = ref[aligned((FLAG0 + s) * size + c * 8), :] > 0.0
            start = s * (POPS * size) + c * 8
            view = ref.at[aligned(start, (POPS - 1) * size + 8), :]
            for p in range(POPS):
                row = p * size
                view[row : row + 8, :] = jnp.where(is_fluid, view[row : row + 8, :], jnp.nan)


def stream_all(posts, h_ref, flags, table, groups, vregs, finish=None):
    lane = lanes_iota()
    row = rows_iota()
    low = lane < 64

    def one_slot(s):
        views = {}

        def view(which, key):
            if (which, key) not in views:
                start = s * (POPS * GROUP) if key == "own" else table[key[0] * 8 + s, key[1]]
                start = start if which else 2 * start
                views[which, key] = posts[which].at[
                    aligned(start, POPS * (GROUP if which else PAIR)), :
                ]
            return views[which, key]

        def load(key, pop, group, v):
            if group == 2:
                row = pop * GROUP + v * 8
            else:
                row = pop * PAIR + group * GROUP + v * 8
            return view(group // 2, key)[row : row + 8, :]

        h_view = h_ref.at[aligned(s * SLOT, SLOT), :]

        def shifted(pop, group, j, dy, dz):
            cx = VELOCITY[pop][0]

            def rows(key, v):
                return load(key, pop, group, v)

            def look(i, j, dx, v):
                if (dx, dy, dz) == (0, 0, 0):
                    return rows("own", v)
                if j is None:
                    return jnp.where(low, look(i, 1, dx, v), look(i, -1, dx, v))
                region = (i + 1) * 3 + j + 1
                return rows((region, VELOCITY.index((dx, dy, dz)) - 1), v)

            need_last = vregs == 3
            values = [look(0, j, 0, 0), look(0, j, 0, 1)]
            if need_last:
                if dy == 0 and dz == 0:
                    values.append(rows("own", 2))
                else:
                    values.append(jnp.where(row < 4, look(1, j, 0, 2), look(-1, j, 0, 2)))
            if cx == 0:
                return values
            turn = 1 if cx > 0 else 7
            rolled = [pltpu.roll(value, turn, axis=0) for value in values]
            if cx > 0:
                before = pltpu.roll(look(0, j, -1, 2), 1, axis=0)
                result = [
                    jnp.where(row == 0, before, rolled[0]),
                    jnp.where(row == 0, rolled[0], rolled[1]),
                ]
                if need_last:
                    edge = pltpu.roll(look(1, j, -1, 1), 1, axis=0)
                    result.append(jnp.where(row == 0, edge, rolled[2]))
                return result
            after = pltpu.roll(look(0, j, 1, 2), 7, axis=0)
            result = [
                jnp.where(row == 7, rolled[1], rolled[0]),
                jnp.where(row == 7, after, rolled[1]),
            ]
            if need_last:
                edge = pltpu.roll(look(-1, j, 1, 0), 7, axis=0)
                result.append(jnp.where(row == 7, edge, rolled[2]))
            return result

        for pop in range(POPS):
            cx, cy, cz = VELOCITY[pop]
            kept = {}

            def source(*key):
                if key not in kept:
                    kept[key] = shifted(pop, *key)
                return kept[key]

            def along_y(group, dz):
                values = source(group, None if group == 2 else 0, 0, dz)
                if cy == 0:
                    return values
                other = (group - cy) % 3
                if group != 2 and other != 2:
                    carried = source(other, 0, 0, dz)
                else:
                    carried = source(other, cy if group == 2 else 0, -cy, dz)
                mask = lane >= 112 if cy > 0 else lane < 16
                return [jnp.where(mask, b, a) for a, b in zip(values, carried)]

            for group in groups:
                values = along_y(group, 0)
                turn = (16 * cy + cz) % 128
                if turn:
                    values = [pltpu.roll(value, turn, axis=1) for value in values]
                if cz:
                    turn = (16 * cy - 15 * cz) % 128
                    wrapped = [pltpu.roll(value, turn, axis=1) for value in along_y(group, -cz)]
                    mask = lane % 16 == (0 if cz > 0 else 15)
                    values = [jnp.where(mask, b, a) for a, b in zip(values, wrapped)]
                for v, value in enumerate(values[:vregs]):
                    if pop:
                        value = jnp.where(value != value, load("own", OPPOSITE[pop], group, v), value)
                    if finish is not None:
                        is_fluid = flags[group // 2][
                            aligned((FLAG0 + s) * PAIR + group * GROUP + v * 8), :
                        ]
                        value = jnp.where(is_fluid > 0.0, value, 0.0)
                    target = pop * PLANE + group * GROUP + v * 8
                    h_view[target : target + 8, :] = value

    @pl.loop(0, SLOTS)
    def _(s):
        one_slot(s)
        if finish is not None:
            finish(s)


def join_kernel(
    cells,
    mate_msg,
    other_msg,
    mate2_msg,
    other2_msg,
    mate_rest,
    passed_rest,
    post_ref,
    slots,
    low_msg,
    high_msg,
    low2_msg,
    high2_msg,
):
    sort_messages(
        mate_msg, other_msg, mate2_msg, other2_msg, low_msg, high_msg, low2_msg, high2_msg
    )
    for i, (ref, row) in enumerate(((low_msg, TABLE), (cells, CELLS), (high_msg, TABLE))):
        slots[8 * i : 8 * i + 8, :] = first_rows(ref[row : row + 8, :])

    from_low, from_high, low_low, low_me, high_high, high_me = landed_slots(cells)
    lane = lanes_iota()
    post_ref[PLANES * PAIR :, :] = jnp.full((POPS * PAIR, 128), jnp.nan, jnp.float32)
    for q in range(PLANES):
        for y in range(2):
            start = q * PAIR + y * GROUP
            post_ref[start : start + EDGE, :] = cells[
                q * 32 + y * EDGE : q * 32 + (y + 1) * EDGE, :
            ]
    even = is_even("curve")
    odd = jnp.logical_not(even)
    for s, (slot, msg, wanted, rest) in itertools.product(
        range(SLOTS),
        (
            (from_low, low_msg, odd, mate_rest),
            (from_low, low_msg, even, passed_rest),
            (from_high, high_msg, even, mate_rest),
            (from_high, high_msg, odd, passed_rest),
        ),
    ):

        @pl.when((slot == s) & wanted)
        def _():
            for p in range(POPS):
                for v in range(2):
                    rim = rim_of(msg, p, v)
                    row = p * EDGE + v * 8
                    wide = rest[row : row + 8, :]
                    row = (POPS + p // 2) * EDGE + v * 8
                    middle = rest[row : row + 8, :]
                    if p % 2:
                        middle = pltpu.roll(middle, 64, axis=1)
                    second = jnp.where(lane < 32, wide, jnp.where(lane < 96, middle, rim))
                    row = (s * POPS + p) * PAIR + v * 8
                    post_ref[row : row + 8, :] = jnp.where(lane < 32, rim, wide)
                    post_ref[row + GROUP : row + GROUP + 8, :] = second

    for msg, row0, step, first in ((high_msg, 16, 1, 2), (low_msg, 23, -1, 1)):
        for y in range(2):
            for count, planes, row, source in strip_rows(first, row0, step):
                source += y * LAYERS
                post_ref[planes(PAIR, row + y * GROUP), :] = msg[source : source + count, :]
    for s in range(SLOTS):
        for slot, msg, row0 in (
            (low_low, low2_msg, 21),
            (low_me, cells.at[OWN2:], 21),
            (high_high, high2_msg, 16),
            (high_me, cells.at[OWN2 + 6 * GROUP :], 16),
        ):

            @pl.when(slot == s)
            def _():
                for y in range(2):
                    for k in range(3):
                        row = s * POPS * PAIR + y * GROUP + row0 + k
                        source = (y * 3 + k) * GROUP
                        post_ref[pl.ds(row, POPS, stride=PAIR), :] = msg[source : source + POPS, :]
    hide_walls(post_ref, PAIR)


def first_rows(slot):
    slot = slot.astype(jnp.int32)
    return jnp.where(slot == SLOTS, NOWHERE, slot * (POPS * GROUP))


def steps_kernel(
    own_slots,
    first_post,
    near_msg,
    far_msg,
    far2_msg,
    out_hbm,
    h_ref,
    post_ref,
    outer_ref,
    out,
    slots,
    table,
    sems,
):
    even = is_even("cross")

    def received(row):
        near = near_msg[row : row + 8, :]
        ref, row = (far_msg, row) if row < CUT else (far2_msg, row - CUT)
        far = ref[row : row + 8, :]
        return jnp.where(even, far, near), jnp.where(even, near, far)

    for i in range(3):
        south, north = received(EDGE_TABLE + 8 * i)
        slots[24 * i : 24 * i + 8, :] = first_rows(south)
        slots[24 * i + 8 : 24 * i + 16, :] = own_slots[8 * i : 8 * i + 8, :]
        slots[24 * i + 16 : 24 * i + 24, :] = first_rows(north)
    table_copy = pltpu.make_async_copy(slots, table, sems.at[SLOTS])
    table_copy.start()

    nothing = jnp.full((8, 128), jnp.nan, jnp.float32)
    for row in range(0, POPS * GROUP, 8):
        outer_ref[NOWHERE + row : NOWHERE + row + 8, :] = nothing
    for row in range(PLANES * PAIR, ALL_PLANES * PAIR, 8):
        post_ref[row : row + 8, :] = nothing
    lane = lanes_iota()
    for v in range(3):

        def rows(q):
            return slice(q * GROUP + v * 8, q * GROUP + v * 8 + 8)

        for quad in range(QUADS):
            south, north = received(quad * GROUP + v * 8)
            for k in range(4):
                value = jnp.where(lane // 32 == (k + 3) % 4, south, north)
                if k:
                    value = pltpu.roll(value, 128 - 32 * k, axis=1)
                outer_ref[rows(4 * quad + k), :] = value
        for part in range(3):
            values = received(FAR + part * GROUP + v * 8)
            for planes, target, value in zip((NORTHWARD, SOUTHWARD), (80, 32), values):
                for k, q in enumerate(planes[8 * part : 8 * part + 8]):
                    moved = pltpu.roll(value, (target - 16 * k) % 128, axis=1)
                    outer_ref[rows(q), :] = jnp.where(
                        lane // 16 == target // 16, moved, outer_ref[rows(q), :]
                    )
    hide_walls(outer_ref, GROUP)
    table_copy.wait()

    def finish(s):
        for x in range(EDGE):
            for y in range(2):
                tile = 2 * x + y
                for p, size in ((0, 8), (8, 8), (16, 3)):
                    row = s * SLOT + (p * PLANE + y * GROUP + x)
                    out[s, p : p + size, 128 * tile : 128 * tile + 128] = h_ref[
                        pl.ds(row, size, stride=PLANE), :
                    ]
        pltpu.make_async_copy(out.at[s], out_hbm.at[s], sems.at[s]).start()

    flags = (first_post, outer_ref)
    posts = flags
    for _ in range(STEPS - 1):
        stream_all(posts, h_ref, flags, table, (0, 1, 2), 3)
        posts = (post_ref, outer_ref)
        collide_all(h_ref, flags, posts)
    stream_all(posts, h_ref, flags, table, (0, 1), 2, finish)
    for s in range(SLOTS):
        pltpu.make_async_copy(out.at[s], out_hbm.at[s], sems.at[s]).wait()


def swapped(value, axis, unit=1):
    count = lax.axis_size(axis)
    results = []
    for which in (0, 1):
        if value[which] is None:
            continue
        sides = [unit if i // unit % 2 == which else -unit for i in range(count)]
        pairs = [(i, i + side) for i, side in enumerate(sides) if 0 <= i + side < count]
        results.append(lax.ppermute(value[which], axis, pairs))
    return results


def rows128(count):
    return jax.ShapeDtypeStruct((count, 128), jnp.float32)


def call(kernel, in_spaces, out_spaces, outs, ins, scratch, limit=LIMIT):
    spaces = {
        "S": pl.BlockSpec(memory_space=pltpu.SMEM),
        "V": pl.BlockSpec(memory_space=pltpu.VMEM),
        "H": pl.BlockSpec(memory_space=pltpu.HBM),
    }
    return pl.pallas_call(
        kernel,
        out_shape=outs,
        in_specs=[spaces[x] for x in in_spaces],
        out_specs=[spaces[x] for x in out_spaces],
        scratch_shapes=scratch,
        compiler_params=pltpu.CompilerParams(vmem_limit_bytes=limit),
    )(*ins)


def per_device(populations, site_flags, neighbours, migrations, counts):
    sizes = (lax.axis_size("curve"), lax.axis_size("cross"))
    moves = migrations.T
    floats = lambda rows: pltpu.VMEM((rows, 128), jnp.float32)
    messages = [
        OWN2 + 12 * GROUP,
        STRIPS + 2 * LAYERS,
        STRIPS + 2 * LAYERS,
        6 * GROUP,
        6 * GROUP,
        REST,
    ]
    cells, mate_msg, other_msg, mate2_msg, other2_msg, rest_msg = call(
        functools.partial(pack_kernel, *sizes),
        "HHHHH",
        "HHHHHH",
        [rows128(rows) for rows in messages],
        (moves, counts, populations, site_flags, neighbours),
        [
            pltpu.SMEM(moves.shape, jnp.int32),
            pltpu.SMEM(counts.shape, jnp.int32),
            pltpu.VMEM(populations.shape, jnp.float32),
            pltpu.VMEM(site_flags.shape, jnp.int32),
            pltpu.VMEM(neighbours.shape, jnp.int32),
            *[floats(rows) for rows in messages],
            pltpu.VMEM((8, 5888), jnp.float32),
            pltpu.VMEM((128, 384), jnp.bfloat16),
            floats(256),
            floats(8),
            pltpu.SemaphoreType.DMA((4 + SLOTS + 8,)),
        ],
        WIDE_LIMIT,
    )
    mate_msg, other_msg = swapped((mate_msg, other_msg), "curve")
    mate2_msg, other2_msg = swapped((mate2_msg, other2_msg), "curve", 2)
    assert sizes[0] % 2 == 0
    pairs = [(i, i ^ 1) for i in range(sizes[0])]
    mate_rest = lax.ppermute(rest_msg, "curve", pairs)
    pairs = [(i, i - 2 if i % 2 else i + 2) for i in range(sizes[0])]
    pairs = [pair for pair in pairs if 0 <= pair[1] < sizes[0]]
    passed_rest = lax.ppermute(mate_rest, "curve", pairs)
    (outer,) = call(spread_kernel, "V", "V", [rows128(PLANES * GROUP)], (cells,), [])
    strips = (cells, mate_msg, other_msg, mate2_msg, other2_msg)
    sorted_rows = [messages[1], messages[1], messages[3], messages[3]]
    near_msg, far_msg, far2_msg = call(
        edge_kernel,
        "VVVVVV",
        "VVV",
        [rows128(EDGE_ROWS), rows128(CUT), rows128(EDGE_ROWS - CUT)],
        (outer, *strips),
        [floats(rows) for rows in [PLANES * GROUP] + sorted_rows],
    )
    near_msg, far_msg = swapped((near_msg, far_msg), "cross")
    (far2_msg,) = swapped((None, far2_msg), "cross")
    post, own_slots = call(
        join_kernel,
        "VVVVVVV",
        "VV",
        [rows128(ALL_PLANES * PAIR), jax.ShapeDtypeStruct((24, 128), jnp.int32)],
        (*strips, mate_rest, passed_rest),
        [floats(rows) for rows in sorted_rows],
    )
    return call(
        steps_kernel,
        "VVVVV",
        "H",
        [jax.ShapeDtypeStruct(populations.shape, jnp.float32)],
        (own_slots, post, near_msg, far_msg, far2_msg),
        [
            floats(SLOTS * SLOT),
            floats(ALL_PLANES * PAIR),
            floats(ALL_PLANES * GROUP),
            pltpu.VMEM(populations.shape, jnp.float32),
            pltpu.VMEM((72, 128), jnp.int32),
            pltpu.SMEM((72, 128), jnp.int32),
            pltpu.SemaphoreType.DMA((SLOTS + 1,)),
        ],
    )[0]


def solution(mesh):
    return jax.shard_map(
        per_device,
        mesh=mesh,
        in_specs=(
            P(("curve", "cross"), None, None),
            P(("curve", "cross"), None),
            P(("curve", "cross"), None),
            P(),
            P(("curve", "cross")),
        ),
        out_specs=P(("curve", "cross"), None, None),
        check_vma=False,
    )
```

```python
import functools
import itertools

import jax
import jax.numpy as jnp
import numpy as np
from jax import lax
from jax.experimental import pallas as pl
from jax.experimental.pallas import tpu as pltpu
from jax.sharding import PartitionSpec as P

EDGE = 16
STEPS = 3
SLOTS = 3
POPS = 19
PLANES = SLOTS * POPS + SLOTS
FLAG0 = SLOTS * POPS
GROUP = 24
PLANE = 3 * GROUP
SLOT = POPS * PLANE
CELLS = PLANES * 32
LANDINGS = CELLS + 8
OWN2 = LANDINGS + 8
OUTWARD = SLOTS * 5 + SLOTS
LAYERS = 2 * PLANES + OUTWARD
RIM = 11 * EDGE
REST = POPS * EDGE + 10 * EDGE
PAIR = 2 * GROUP
QUADS = PLANES // 4
TABLE = RIM
STRIPS = RIM + 8
FAR = QUADS * GROUP
EDGE_TABLE = FAR + 3 * GROUP
EDGE_ROWS = EDGE_TABLE + 24
NOWHERE = PLANES * GROUP
ALL_PLANES = PLANES + POPS
LIMIT = 20 * 1024 * 1024
WIDE_LIMIT = 127 * 512 * 1024

VELOCITY = [
    (0, 0, 0),
    (1, 0, 0),
    (-1, 0, 0),
    (0, 1, 0),
    (0, -1, 0),
    (0, 0, 1),
    (0, 0, -1),
    (1, 1, 0),
    (-1, -1, 0),
    (1, -1, 0),
    (-1, 1, 0),
    (1, 0, 1),
    (-1, 0, -1),
    (1, 0, -1),
    (-1, 0, 1),
    (0, 1, 1),
    (0, -1, -1),
    (0, 1, -1),
    (0, -1, 1),
]
NORTHWARD, SOUTHWARD = (
    [s * POPS + p for s in range(SLOTS) for p in range(POPS) if VELOCITY[p][1] == side]
    + [FLAG0 + s for s in range(SLOTS)]
    for side in (1, -1)
)
THIRD = [
    (pop, source, *((32 + 16 * k, 9) if k < 4 else (16 * (k - 4), 10)))
    for k, (pop, source) in enumerate(
        [(p, 32) for p in (4, 8, 9, 16, 18)] + [(p, 80) for p in (3, 7, 10, 15, 17)]
    )
]
OPPOSITE = [0, 2, 1, 4, 3, 6, 5, 8, 7, 10, 9, 12, 11, 14, 13, 16, 15, 18, 17]


def lanes_iota():
    return lax.broadcasted_iota(jnp.int32, (8, 128), 1)


def is_even(axis, unit=1):
    return lax.rem(lax.axis_index(axis) // unit, 2) == 0


def rows_iota():
    return lax.broadcasted_iota(jnp.int32, (8, 128), 0)


def aligned(start, size=8):
    return pl.ds(pl.multiple_of(start, 8), size)


def move_slots(moves, curve_size, cross_size):
    curve, cross = lax.axis_index("curve"), lax.axis_index("cross")

    def landed(source, target):
        inside = (source >= 0) & (source < curve_size) & (target >= 0) & (target < curve_size)
        row = jnp.clip(source, 0, curve_size - 1) * cross_size + cross
        rank = target * cross_size + cross
        hit = inside & (moves[0, row] >= 0) & (moves[1, row] == rank)
        return jnp.where(hit, moves[2, row], -1)

    return (
        landed(curve - 1, curve),
        landed(curve + 1, curve),
        landed(curve - 2, curve - 1),
        landed(curve, curve - 1),
        landed(curve + 2, curve + 1),
        landed(curve, curve + 1),
    )


def pack_kernel(
    curve_size,
    cross_size,
    moves_hbm,
    counts_hbm,
    pops_hbm,
    flags_hbm,
    neighbours_hbm,
    cells_hbm,
    mate_hbm,
    other_hbm,
    mate2_hbm,
    other2_hbm,
    rest_hbm,
    moves,
    counts,
    pops,
    flags,
    neighbours,
    cells,
    up_msg,
    down_msg,
    up2_msg,
    down2_msg,
    rest_msg,
    wide_flags,
    plane_flags,
    site_flags,
    near,
    sems,
):
    started = []

    def copy(source, target):
        one = pltpu.make_async_copy(source, target, sems.at[len(started)])
        one.start()
        started.append(one)
        return one

    flags_copy = copy(flags_hbm, flags)
    copies = [copy(pops_hbm.at[s], pops.at[s]) for s in range(SLOTS)]
    small = [
        copy(neighbours_hbm, neighbours),
        copy(counts_hbm, counts),
        copy(moves_hbm, moves),
    ]
    for one in small:
        one.wait()

    near[...] = jnp.zeros_like(near)
    named = neighbours[...]
    slot = jnp.where(named >= 0, lax.rem(jnp.maximum(named, 0), SLOTS), SLOTS)
    near[0:SLOTS, 0 : named.shape[1]] = slot.astype(jnp.float32)
    for ref, row in ((cells, CELLS), (up_msg, TABLE), (down_msg, TABLE)):
        ref[row : row + 8, :] = near[...]

    wide_flags[...] = jnp.zeros_like(wide_flags)
    flags_copy.wait()
    wide_flags[0:SLOTS, 0 : flags.shape[1]] = flags[...].astype(jnp.float32)
    span = EDGE + 2
    for x in range(EDGE):
        start = (x + 1) * span * span
        base = start // 128 * 128
        window = wide_flags[:, base : base + 512]
        window = pltpu.roll(window, (512 - (start - base)) % 512, axis=1)
        plane_flags[8 * x : 8 * x + 8, :] = window[:, :384].astype(jnp.bfloat16)
    lane_in = lax.broadcasted_iota(jnp.int32, (384, 256), 0)
    site = lax.broadcasted_iota(jnp.int32, (384, 256), 1)
    chosen = lane_in == (site // EDGE + 1) * span + site % EDGE + 1
    product = jnp.dot(
        plane_flags[...],
        jnp.where(chosen, 1.0, 0.0).astype(jnp.bfloat16),
        preferred_element_type=jnp.float32,
    )
    site_flags[0:128, :] = product[:, :128]
    site_flags[128:256, :] = product[:, 128:]
    for s in range(SLOTS):
        live = s < counts[0]
        for y in range(2):
            piece = site_flags[pl.ds(128 * y + s, EDGE, stride=8), :]
            is_fluid = (piece == 1.0) & live
            row = (FLAG0 + s) * 32 + y * EDGE
            cells[row : row + EDGE, :] = jnp.where(is_fluid, 1.0, 0.0)

    for s in range(SLOTS):
        copies[s].wait()
        for x in range(EDGE):
            for y in range(2):
                tile = 2 * x + y
                for p, size in ((0, 8), (8, 8), (16, 3)):
                    row = (s * POPS + p) * 32 + y * EDGE + x
                    cells[pl.ds(row, size, stride=32), :] = pops[
                        s, p : p + size, 128 * tile : 128 * tile + 128
                    ]

    @pl.loop(0, SLOTS)
    def _(s):
        @pl.loop(0, 4, unroll=2)
        def _(c):
            base = s * (POPS * 32) + c * 8
            view = cells.at[aligned(base, (POPS - 1) * 32 + 8), :]
            h = [view[p * 32 : p * 32 + 8, :] for p in range(POPS)]
            for p, value in enumerate(collided(h)):
                view[p * 32 : p * 32 + 8, :] = value

    for i, slot in enumerate(move_slots(moves, curve_size, cross_size)):
        value = jnp.full((1, 128), slot, jnp.int32)
        cells[LANDINGS + i : LANDINGS + i + 1, :] = value.astype(jnp.float32)

    body_copy = copy(cells.at[:OWN2], cells_hbm.at[:OWN2])

    for y in range(2):
        for msg, x0, first in ((up_msg, 15, 1), (down_msg, 0, 2)):
            step = -1 if x0 else 1
            for k in range(2):
                out = STRIPS + y * LAYERS + k * PLANES
                msg[out : out + PLANES, :] = cells[
                    pl.ds(y * EDGE + x0 + step * k, PLANES, stride=32), :
                ]
            row = y * EDGE + x0 + 2 * step
            out = STRIPS + y * LAYERS + 2 * PLANES
            for s in range(SLOTS):
                base = s * POPS * 32 + row
                msg[out + 5 * s : out + 5 * s + 1, :] = cells[pl.ds(base + first * 32, 1), :]
                msg[out + 5 * s + 1 : out + 5 * s + 5, :] = cells[
                    pl.ds(base + (first + 6) * 32, 4, stride=64), :
                ]
            msg[out + 5 * SLOTS : out + OUTWARD, :] = cells[
                pl.ds(FLAG0 * 32 + row, SLOTS, stride=32), :
            ]

    here = lax.axis_index("curve") * cross_size + lax.axis_index("cross")
    leaving = jnp.maximum(moves[0, here], 0)
    lane = lanes_iota()
    for v in range(2):
        halves = [
            [cells[aligned(leaving * (POPS * 32) + p * 32 + y * EDGE + v * 8), :] for y in (0, 1)]
            for p in range(POPS)
        ]
        outer = [jnp.where(lane < 64, first, second) for first, second in halves]
        middle = (lane >= 32) & (lane < 96)
        sets = [
            jnp.where(middle, pltpu.roll(outer[p + 1], 64, axis=1), outer[p])
            for p in range(0, POPS - 1, 2)
        ]
        sets += [outer[POPS - 1], jnp.zeros_like(outer[0])]
        for pop, source, target, which in THIRD:
            moved = pltpu.roll(outer[pop], (target - source) % 128, axis=1)
            sets[which] = jnp.where(lane // 16 == target // 16, moved, sets[which])
        for k, value in enumerate(sets):
            row = k * EDGE + v * 8
            up_msg[row : row + 8, :] = value
            down_msg[row : row + 8, :] = value
        for p, (first, second) in enumerate(halves):
            row = p * EDGE + v * 8
            rest_msg[row : row + 8, :] = jnp.where(lane < 32, second, first)
        for p in range(0, POPS, 2):
            value = halves[p][1]
            if p + 1 < POPS:
                value = jnp.where(middle, value, pltpu.roll(halves[p + 1][1], 64, axis=1))
            row = (POPS + p // 2) * EDGE + v * 8
            rest_msg[row : row + 8, :] = value
    for s in range(SLOTS):

        @pl.when(leaving == s)
        def _():
            for y in range(2):
                for k in range(3):
                    out = (y * 3 + k) * GROUP
                    row = s * POPS * 32 + y * EDGE + k
                    up2_msg[out : out + POPS, :] = cells[pl.ds(row + 13, POPS, stride=32), :]
                    down2_msg[out : out + POPS, :] = cells[pl.ds(row, POPS, stride=32), :]

    cells[OWN2 : OWN2 + 6 * GROUP, :] = up2_msg[...]
    cells[OWN2 + 6 * GROUP :, :] = down2_msg[...]
    last = [copy(cells.at[OWN2:], cells_hbm.at[OWN2:]), copy(rest_msg, rest_hbm)]
    count = len(started)
    for i, (up, down, mate, other, unit) in enumerate(
        ((up_msg, down_msg, mate_hbm, other_hbm, 1), (up2_msg, down2_msg, mate2_hbm, other2_hbm, 2))
    ):
        first, second = sems.at[count + 2 * i], sems.at[count + 2 * i + 1]
        even = is_even("curve", unit)

        @pl.when(even)
        def _():
            pltpu.make_async_copy(up, mate, first).start()
            pltpu.make_async_copy(down, other, second).start()

        @pl.when(jnp.logical_not(even))
        def _():
            pltpu.make_async_copy(down, mate, first).start()
            pltpu.make_async_copy(up, other, second).start()

        last.append(pltpu.make_async_copy(up, mate, first))
        last.append(pltpu.make_async_copy(down, other, second))
    body_copy.wait()
    for one in last:
        one.wait()


def spread_kernel(cells, outer):
    low = lanes_iota() < 64
    for q in range(PLANES):
        for v in range(2):
            row = q * 32 + v * 8
            first, second = cells[row : row + 8, :], cells[row + EDGE : row + EDGE + 8, :]
            row = q * GROUP + v * 8
            outer[row : row + 8, :] = jnp.where(low, first, second)


def sort_messages(mate_msg, other_msg, mate2_msg, other2_msg, low_msg, high_msg, low2, high2):
    for mate, other, low, high, unit in (
        (mate_msg, other_msg, low_msg, high_msg, 1),
        (mate2_msg, other2_msg, low2, high2, 2),
    ):
        even = is_even("curve", unit)

        @pl.when(even)
        def _():
            low[...] = other[...]
            high[...] = mate[...]

        @pl.when(jnp.logical_not(even))
        def _():
            low[...] = mate[...]
            high[...] = other[...]


def landed_slots(cells):
    return [jnp.max(cells[LANDINGS + i : LANDINGS + i + 1, :]) for i in range(6)]


def rim_of(msg, p, v):
    row = p // 2 * EDGE + v * 8
    value = msg[row : row + 8, :]
    return pltpu.roll(value, 64, axis=1) if p % 2 else value


def sel4(parts, lane):
    first = jnp.where(lane < 32, parts[0], parts[1])
    second = jnp.where(lane < 96, parts[2], parts[3])
    return jnp.where(lane < 64, first, second)


def strip_rows(first, row0, step):
    pieces = []
    for k in range(2):
        pieces.append(
            (PLANES, lambda size, row: pl.ds(row, PLANES, stride=size), row0 + step * k, STRIPS + k * PLANES)
        )
    row, source = row0 + 2 * step, STRIPS + 2 * PLANES
    for s in range(SLOTS):
        plane = s * POPS + first
        pieces.append((1, lambda size, row, plane=plane: pl.ds(plane * size + row, 1), row, source))
        pieces.append(
            (
                4,
                lambda size, row, plane=plane: pl.ds(
                    (plane + 6) * size + row, 4, stride=2 * size
                ),
                row,
                source + 1,
            )
        )
        source += 5
    pieces.append(
        (SLOTS, lambda size, row: pl.ds(FLAG0 * size + row, SLOTS, stride=size), row, source)
    )
    return pieces


def edge_kernel(
    own_outer,
    cells,
    mate_msg,
    other_msg,
    mate2_msg,
    other2_msg,
    near_msg,
    far_msg,
    outer,
    low_msg,
    high_msg,
    low2_msg,
    high2_msg,
):
    sort_messages(
        mate_msg, other_msg, mate2_msg, other2_msg, low_msg, high_msg, low2_msg, high2_msg
    )
    from_low, from_high, low_low, low_me, high_high, high_me = landed_slots(cells)
    low = lanes_iota() < 64
    for q in range(PLANES):
        for v in range(2):
            row = q * GROUP + v * 8
            outer[row : row + 8, :] = own_outer[row : row + 8, :]

    def both(first, second):
        lane = lax.broadcasted_iota(jnp.int32, first.shape, 1)
        return jnp.where(lane < 64, first, second)

    for msg, row0, step, first in ((high_msg, 16, 1, 2), (low_msg, 23, -1, 1)):
        for count, planes, row, source in strip_rows(first, row0, step):
            outer[planes(GROUP, row), :] = both(
                msg[source : source + count, :],
                msg[LAYERS + source : LAYERS + source + count, :],
            )
    lane = lanes_iota()
    for s, (slot, msg) in itertools.product(
        range(SLOTS), ((from_low, low_msg), (from_high, high_msg))
    ):

        @pl.when(slot == s)
        def _():
            for v in range(2):
                values = [rim_of(msg, p, v) for p in range(POPS)]
                for pop, target, source, which in THIRD:
                    row = which * EDGE + v * 8
                    moved = pltpu.roll(msg[row : row + 8, :], (target - source) % 128, axis=1)
                    values[pop] = jnp.where(lane // 16 == target // 16, moved, values[pop])
                for p, value in enumerate(values):
                    row = (s * POPS + p) * GROUP + v * 8
                    outer[row : row + 8, :] = value

    for s in range(SLOTS):
        for slot, msg, row0 in (
            (low_low, low2_msg, 21),
            (low_me, cells.at[OWN2:], 21),
            (high_high, high2_msg, 16),
            (high_me, cells.at[OWN2 + 6 * GROUP :], 16),
        ):

            @pl.when(slot == s)
            def _():
                for k in range(3):
                    outer[pl.ds(s * POPS * GROUP + row0 + k, POPS, stride=GROUP), :] = both(
                        msg[k * GROUP : k * GROUP + POPS, :],
                        msg[(3 + k) * GROUP : (3 + k) * GROUP + POPS, :],
                    )

    even = is_even("cross")

    def send(row, north, south):
        near_msg[row : row + 8, :] = jnp.where(even, north, south)
        far_msg[row : row + 8, :] = jnp.where(even, south, north)

    for v in range(3):

        def plane(q):
            return outer[q * GROUP + v * 8 : q * GROUP + v * 8 + 8, :]

        for quad in range(QUADS):
            parts = [plane(4 * quad)]
            parts += [pltpu.roll(plane(4 * quad + k), 32 * k, axis=1) for k in (1, 2, 3)]
            send(quad * GROUP + v * 8, sel4(parts[1:] + parts[:1], lane), sel4(parts, lane))
        for part in range(3):
            values = []
            for planes, source in ((NORTHWARD, 80), (SOUTHWARD, 32)):
                value = None
                for k, q in enumerate(planes[8 * part : 8 * part + 8]):
                    moved = pltpu.roll(plane(q), (16 * k - source) % 128, axis=1)
                    value = moved if value is None else jnp.where(lane < 16 * k, value, moved)
                values.append(value)
            send(FAR + part * GROUP + v * 8, *values)
    tables = (low_msg, TABLE), (cells, CELLS), (high_msg, TABLE)
    for i, (ref, row) in enumerate(tables):
        value = ref[row : row + 8, :]
        send(EDGE_TABLE + 8 * i, value, value)


def collided(h):
    shear = 1.0 / 0.6
    rest = h[0]
    sx, dx = h[1] + h[2], h[1] - h[2]
    sy, dy = h[3] + h[4], h[3] - h[4]
    sz, dz = h[5] + h[6], h[5] - h[6]
    s7, d7 = h[7] + h[8], h[7] - h[8]
    s9, d9 = h[9] + h[10], h[9] - h[10]
    s11, d11 = h[11] + h[12], h[11] - h[12]
    s13, d13 = h[13] + h[14], h[13] - h[14]
    s15, d15 = h[15] + h[16], h[15] - h[16]
    s17, d17 = h[17] + h[18], h[17] - h[18]
    txy, txz, tyz = s7 + s9, s11 + s13, s15 + s17
    pxy, pxz, pyz = s7 - s9, s11 - s13, s15 - s17
    ax, bx = d7 + d9, d11 + d13
    ay, by = d7 - d9, d15 + d17
    az, bz = d11 - d13, d15 - d17
    axes = sx + sy + sz
    diags = txy + txz + tyz
    rho = rest * (1.0 / 3.0) + axes * (1.0 / 18.0) + diags * (1.0 / 36.0)
    fx, fy, fz = ax + bx, ay + by, az + bz
    jx = dx * (1.0 / 18.0) + fx * (1.0 / 36.0)
    jy = dy * (1.0 / 18.0) + fy * (1.0 / 36.0)
    jz = dz * (1.0 / 18.0) + fz * (1.0 / 36.0)
    inverse = 1.0 / rho
    ux, uy, uz = jx * inverse, jy * inverse, jz * inverse
    qxx, qyy, qzz = jx * ux, jy * uy, jz * uz
    total = qxx + qyy + qzz

    energy = -10.0 * rest - axes * (11.0 / 18.0) + diags * (8.0 / 36.0)
    energy = (energy + 11.0 * rho - 19.0 * total) * (1.19 / 2394.0)
    square = 4.0 * rest - axes * (4.0 / 18.0) + diags * (1.0 / 36.0)
    square = (square - 3.0 * rho + 5.5 * total) * (1.4 / 252.0)
    axis_x = (3.0 * sx - axes) * (1.0 / 18.0)
    diag_x = (diags - 3.0 * tyz) * (1.0 / 36.0)
    want_x = 3.0 * qxx - total
    stress_x = (axis_x + diag_x - want_x) * (shear / 36.0)
    third_x = (diag_x - 2.0 * axis_x + 0.5 * want_x) * (1.4 / 72.0)
    axis_w = (sy - sz) * (1.0 / 18.0)
    diag_w = (txy - txz) * (1.0 / 36.0)
    want_w = qyy - qzz
    stress_w = (axis_w + diag_w - want_w) * (shear / 12.0)
    third_w = (diag_w - 2.0 * axis_w + 0.5 * want_w) * (1.4 / 24.0)

    rest_out = rest - 3.0 * (12.0 * square - 30.0 * energy)
    common = -18.0 * (11.0 * energy + 4.0 * square)
    along_x = 18.0 * (stress_x - 2.0 * third_x)
    along_w = 18.0 * (stress_w - 2.0 * third_w)
    ex = common + 2.0 * along_x
    ey = common - along_x + along_w
    ez = common - along_x - along_w
    common = 36.0 * (8.0 * energy + square)
    across_x = 36.0 * (stress_x + third_x)
    across_w = 36.0 * (stress_w + third_w)
    exy = common + across_x + across_w
    exz = common + across_x - across_w
    eyz = common - 2.0 * across_x
    cxy = shear * (0.25 * pxy - 9.0 * jx * uy)
    cxz = shear * (0.25 * pxz - 9.0 * jx * uz)
    cyz = shear * (0.25 * pyz - 9.0 * jy * uz)

    def flux(d, f, j):
        return (f * (1.0 / 36.0) - d * (4.0 / 18.0) + j * (2.0 / 3.0)) * (1.2 / 40.0)

    hx, hy, hz = flux(dx, fx, jx), flux(dy, fy, jy), flux(dz, fz, jz)
    mx = (ax - bx) * (1.98 / 8.0)
    my = (by - ay) * (1.98 / 8.0)
    mz = (az - bz) * (1.98 / 8.0)
    hx36, hy36, hz36 = 36.0 * hx, 36.0 * hy, 36.0 * hz
    xy_x, xz_x = hx36 + mx, hx36 - mx
    yz_y, xy_y = hy36 + my, hy36 - my
    xz_z, yz_z = hz36 + mz, hz36 - mz
    ox, oy, oz = -2.0 * hx36, -2.0 * hy36, -2.0 * hz36

    out = [rest_out]

    def pair(i, even, odd):
        out.append(h[i] - (even + odd))
        out.append(h[i + 1] - (even - odd))

    pair(1, ex, ox)
    pair(3, ey, oy)
    pair(5, ez, oz)
    pair(7, exy + cxy, xy_x + xy_y)
    pair(9, exy - cxy, xy_x - xy_y)
    pair(11, exz + cxz, xz_x + xz_z)
    pair(13, exz - cxz, xz_x - xz_z)
    pair(15, eyz + cyz, yz_y + yz_z)
    pair(17, eyz - cyz, yz_y - yz_z)
    return out


def collide_all(h_ref, flags, posts):
    for groups in ((0, 1), (2,)):
        ref = posts[groups[0] // 2]
        size = len(groups) * GROUP

        @pl.loop(0, SLOTS)
        def _(s):
            @pl.loop(0, size // 8, unroll=3)
            def _(c):
                is_fluid = flags[groups[0] // 2][aligned((FLAG0 + s) * size + c * 8), :] > 0.0
                start = s * SLOT + groups[0] * GROUP + c * 8
                h_view = h_ref.at[aligned(start, (POPS - 1) * PLANE + 8), :]
                start = s * (POPS * size) + c * 8
                view = ref.at[aligned(start, (POPS - 1) * size + 8), :]
                h = [h_view[p * PLANE : p * PLANE + 8, :] for p in range(POPS)]
                for p, value in enumerate(collided(h)):
                    view[p * size : p * size + 8, :] = jnp.where(is_fluid, value, jnp.nan)


def hide_walls(ref, size):
    @pl.loop(0, SLOTS)
    def _(s):
        @pl.loop(0, size // 8)
        def _(c):
            is_fluid = ref[aligned((FLAG0 + s) * size + c * 8), :] > 0.0
            start = s * (POPS * size) + c * 8
            view = ref.at[aligned(start, (POPS - 1) * size + 8), :]
            for p in range(POPS):
                row = p * size
                view[row : row + 8, :] = jnp.where(is_fluid, view[row : row + 8, :], jnp.nan)


def stream_all(posts, h_ref, flags, table, groups, vregs, finish=None):
    lane = lanes_iota()
    row = rows_iota()
    low = lane < 64

    def one_slot(s):
        views = {}

        def view(which, key):
            if (which, key) not in views:
                start = s * (POPS * GROUP) if key == "own" else table[key[0] * 8 + s, key[1]]
                start = start if which else 2 * start
                views[which, key] = posts[which].at[
                    aligned(start, POPS * (GROUP if which else PAIR)), :
                ]
            return views[which, key]

        def load(key, pop, group, v):
            if group == 2:
                row = pop * GROUP + v * 8
            else:
                row = pop * PAIR + group * GROUP + v * 8
            return view(group // 2, key)[row : row + 8, :]

        h_view = h_ref.at[aligned(s * SLOT, SLOT), :]

        def shifted(pop, group, j, dy, dz):
            cx = VELOCITY[pop][0]

            def rows(key, v):
                return load(key, pop, group, v)

            def look(i, j, dx, v):
                if (dx, dy, dz) == (0, 0, 0):
                    return rows("own", v)
                if j is None:
                    return jnp.where(low, look(i, 1, dx, v), look(i, -1, dx, v))
                region = (i + 1) * 3 + j + 1
                return rows((region, VELOCITY.index((dx, dy, dz)) - 1), v)

            need_last = vregs == 3
            values = [look(0, j, 0, 0), look(0, j, 0, 1)]
            if need_last:
                if dy == 0 and dz == 0:
                    values.append(rows("own", 2))
                else:
                    values.append(jnp.where(row < 4, look(1, j, 0, 2), look(-1, j, 0, 2)))
            if cx == 0:
                return values
            turn = 1 if cx > 0 else 7
            rolled = [pltpu.roll(value, turn, axis=0) for value in values]
            if cx > 0:
                before = pltpu.roll(look(0, j, -1, 2), 1, axis=0)
                result = [
                    jnp.where(row == 0, before, rolled[0]),
                    jnp.where(row == 0, rolled[0], rolled[1]),
                ]
                if need_last:
                    edge = pltpu.roll(look(1, j, -1, 1), 1, axis=0)
                    result.append(jnp.where(row == 0, edge, rolled[2]))
                return result
            after = pltpu.roll(look(0, j, 1, 2), 7, axis=0)
            result = [
                jnp.where(row == 7, rolled[1], rolled[0]),
                jnp.where(row == 7, after, rolled[1]),
            ]
            if need_last:
                edge = pltpu.roll(look(-1, j, 1, 0), 7, axis=0)
                result.append(jnp.where(row == 7, edge, rolled[2]))
            return result

        for pop in range(POPS):
            cx, cy, cz = VELOCITY[pop]
            kept = {}

            def source(*key):
                if key not in kept:
                    kept[key] = shifted(pop, *key)
                return kept[key]

            def along_y(group, dz):
                values = source(group, None if group == 2 else 0, 0, dz)
                if cy == 0:
                    return values
                other = (group - cy) % 3
                if group != 2 and other != 2:
                    carried = source(other, 0, 0, dz)
                else:
                    carried = source(other, cy if group == 2 else 0, -cy, dz)
                mask = lane >= 112 if cy > 0 else lane < 16
                return [jnp.where(mask, b, a) for a, b in zip(values, carried)]

            for group in groups:
                values = along_y(group, 0)
                turn = (16 * cy + cz) % 128
                if turn:
                    values = [pltpu.roll(value, turn, axis=1) for value in values]
                if cz:
                    turn = (16 * cy - 15 * cz) % 128
                    wrapped = [pltpu.roll(value, turn, axis=1) for value in along_y(group, -cz)]
                    mask = lane % 16 == (0 if cz > 0 else 15)
                    values = [jnp.where(mask, b, a) for a, b in zip(values, wrapped)]
                for v, value in enumerate(values[:vregs]):
                    if pop:
                        value = jnp.where(value != value, load("own", OPPOSITE[pop], group, v), value)
                    if finish is not None:
                        is_fluid = flags[group // 2][
                            aligned((FLAG0 + s) * PAIR + group * GROUP + v * 8), :
                        ]
                        value = jnp.where(is_fluid > 0.0, value, 0.0)
                    target = pop * PLANE + group * GROUP + v * 8
                    h_view[target : target + 8, :] = value

    @pl.loop(0, SLOTS)
    def _(s):
        one_slot(s)
        if finish is not None:
            finish(s)


def join_kernel(
    cells,
    mate_msg,
    other_msg,
    mate2_msg,
    other2_msg,
    mate_rest,
    passed_rest,
    post_ref,
    slots,
    low_msg,
    high_msg,
    low2_msg,
    high2_msg,
):
    sort_messages(
        mate_msg, other_msg, mate2_msg, other2_msg, low_msg, high_msg, low2_msg, high2_msg
    )
    for i, (ref, row) in enumerate(((low_msg, TABLE), (cells, CELLS), (high_msg, TABLE))):
        slots[8 * i : 8 * i + 8, :] = first_rows(ref[row : row + 8, :])

    from_low, from_high, low_low, low_me, high_high, high_me = landed_slots(cells)
    lane = lanes_iota()
    post_ref[PLANES * PAIR :, :] = jnp.full((POPS * PAIR, 128), jnp.nan, jnp.float32)
    for q in range(PLANES):
        for y in range(2):
            start = q * PAIR + y * GROUP
            post_ref[start : start + EDGE, :] = cells[
                q * 32 + y * EDGE : q * 32 + (y + 1) * EDGE, :
            ]
    even = is_even("curve")
    odd = jnp.logical_not(even)
    for s, (slot, msg, wanted, rest) in itertools.product(
        range(SLOTS),
        (
            (from_low, low_msg, odd, mate_rest),
            (from_low, low_msg, even, passed_rest),
            (from_high, high_msg, even, mate_rest),
            (from_high, high_msg, odd, passed_rest),
        ),
    ):

        @pl.when((slot == s) & wanted)
        def _():
            for p in range(POPS):
                for v in range(2):
                    rim = rim_of(msg, p, v)
                    row = p * EDGE + v * 8
                    wide = rest[row : row + 8, :]
                    row = (POPS + p // 2) * EDGE + v * 8
                    middle = rest[row : row + 8, :]
                    if p % 2:
                        middle = pltpu.roll(middle, 64, axis=1)
                    second = jnp.where(lane < 32, wide, jnp.where(lane < 96, middle, rim))
                    row = (s * POPS + p) * PAIR + v * 8
                    post_ref[row : row + 8, :] = jnp.where(lane < 32, rim, wide)
                    post_ref[row + GROUP : row + GROUP + 8, :] = second

    for msg, row0, step, first in ((high_msg, 16, 1, 2), (low_msg, 23, -1, 1)):
        for y in range(2):
            for count, planes, row, source in strip_rows(first, row0, step):
                source += y * LAYERS
                post_ref[planes(PAIR, row + y * GROUP), :] = msg[source : source + count, :]
    for s in range(SLOTS):
        for slot, msg, row0 in (
            (low_low, low2_msg, 21),
            (low_me, cells.at[OWN2:], 21),
            (high_high, high2_msg, 16),
            (high_me, cells.at[OWN2 + 6 * GROUP :], 16),
        ):

            @pl.when(slot == s)
            def _():
                for y in range(2):
                    for k in range(3):
                        row = s * POPS * PAIR + y * GROUP + row0 + k
                        source = (y * 3 + k) * GROUP
                        post_ref[pl.ds(row, POPS, stride=PAIR), :] = msg[source : source + POPS, :]
    hide_walls(post_ref, PAIR)


def first_rows(slot):
    slot = slot.astype(jnp.int32)
    return jnp.where(slot == SLOTS, NOWHERE, slot * (POPS * GROUP))


def steps_kernel(
    own_slots,
    first_post,
    near_msg,
    far_msg,
    out_hbm,
    h_ref,
    post_ref,
    outer_ref,
    out,
    slots,
    table,
    sems,
):
    even = is_even("cross")

    def received(row):
        near, far = near_msg[row : row + 8, :], far_msg[row : row + 8, :]
        return jnp.where(even, far, near), jnp.where(even, near, far)

    for i in range(3):
        south, north = received(EDGE_TABLE + 8 * i)
        slots[24 * i : 24 * i + 8, :] = first_rows(south)
        slots[24 * i + 8 : 24 * i + 16, :] = own_slots[8 * i : 8 * i + 8, :]
        slots[24 * i + 16 : 24 * i + 24, :] = first_rows(north)
    table_copy = pltpu.make_async_copy(slots, table, sems.at[SLOTS])
    table_copy.start()

    nothing = jnp.full((8, 128), jnp.nan, jnp.float32)
    for row in range(0, POPS * GROUP, 8):
        outer_ref[NOWHERE + row : NOWHERE + row + 8, :] = nothing
    for row in range(PLANES * PAIR, ALL_PLANES * PAIR, 8):
        post_ref[row : row + 8, :] = nothing
    lane = lanes_iota()
    for v in range(3):

        def rows(q):
            return slice(q * GROUP + v * 8, q * GROUP + v * 8 + 8)

        for quad in range(QUADS):
            south, north = received(quad * GROUP + v * 8)
            for k in range(4):
                value = jnp.where(lane // 32 == (k + 3) % 4, south, north)
                if k:
                    value = pltpu.roll(value, 128 - 32 * k, axis=1)
                outer_ref[rows(4 * quad + k), :] = value
        for part in range(3):
            values = received(FAR + part * GROUP + v * 8)
            for planes, target, value in zip((NORTHWARD, SOUTHWARD), (80, 32), values):
                for k, q in enumerate(planes[8 * part : 8 * part + 8]):
                    moved = pltpu.roll(value, (target - 16 * k) % 128, axis=1)
                    outer_ref[rows(q), :] = jnp.where(
                        lane // 16 == target // 16, moved, outer_ref[rows(q), :]
                    )
    hide_walls(outer_ref, GROUP)
    table_copy.wait()

    def finish(s):
        for x in range(EDGE):
            for y in range(2):
                tile = 2 * x + y
                for p, size in ((0, 8), (8, 8), (16, 3)):
                    row = s * SLOT + (p * PLANE + y * GROUP + x)
                    out[s, p : p + size, 128 * tile : 128 * tile + 128] = h_ref[
                        pl.ds(row, size, stride=PLANE), :
                    ]
        pltpu.make_async_copy(out.at[s], out_hbm.at[s], sems.at[s]).start()

    flags = (first_post, outer_ref)
    posts = flags
    for _ in range(STEPS - 1):
        stream_all(posts, h_ref, flags, table, (0, 1, 2), 3)
        posts = (post_ref, outer_ref)
        collide_all(h_ref, flags, posts)
    stream_all(posts, h_ref, flags, table, (0, 1), 2, finish)
    for s in range(SLOTS):
        pltpu.make_async_copy(out.at[s], out_hbm.at[s], sems.at[s]).wait()


def swapped(value, axis, unit=1):
    count = lax.axis_size(axis)
    results = []
    for which in (0, 1):
        others = [i + (unit if i // unit % 2 == which else -unit) for i in range(count)]
        pairs = [(i, j if 0 <= j < count else i) for i, j in enumerate(others)]
        results.append(lax.ppermute(value[which], axis, pairs))
    return results


def rows128(count):
    return jax.ShapeDtypeStruct((count, 128), jnp.float32)


def call(kernel, in_spaces, out_spaces, outs, ins, scratch, limit=LIMIT):
    spaces = {
        "S": pl.BlockSpec(memory_space=pltpu.SMEM),
        "V": pl.BlockSpec(memory_space=pltpu.VMEM),
        "H": pl.BlockSpec(memory_space=pltpu.HBM),
    }
    return pl.pallas_call(
        kernel,
        out_shape=outs,
        in_specs=[spaces[x] for x in in_spaces],
        out_specs=[spaces[x] for x in out_spaces],
        scratch_shapes=scratch,
        compiler_params=pltpu.CompilerParams(vmem_limit_bytes=limit),
    )(*ins)


def per_device(populations, site_flags, neighbours, migrations, counts):
    sizes = (lax.axis_size("curve"), lax.axis_size("cross"))
    moves = migrations.T
    floats = lambda rows: pltpu.VMEM((rows, 128), jnp.float32)
    messages = [
        OWN2 + 12 * GROUP,
        STRIPS + 2 * LAYERS,
        STRIPS + 2 * LAYERS,
        6 * GROUP,
        6 * GROUP,
        REST,
    ]
    cells, mate_msg, other_msg, mate2_msg, other2_msg, rest_msg = call(
        functools.partial(pack_kernel, *sizes),
        "HHHHH",
        "HHHHHH",
        [rows128(rows) for rows in messages],
        (moves, counts, populations, site_flags, neighbours),
        [
            pltpu.SMEM(moves.shape, jnp.int32),
            pltpu.SMEM(counts.shape, jnp.int32),
            pltpu.VMEM(populations.shape, jnp.float32),
            pltpu.VMEM(site_flags.shape, jnp.int32),
            pltpu.VMEM(neighbours.shape, jnp.int32),
            *[floats(rows) for rows in messages],
            pltpu.VMEM((8, 5888), jnp.float32),
            pltpu.VMEM((128, 384), jnp.bfloat16),
            floats(256),
            floats(8),
            pltpu.SemaphoreType.DMA((4 + SLOTS + 8,)),
        ],
        WIDE_LIMIT,
    )
    mate_msg, other_msg = swapped((mate_msg, other_msg), "curve")
    mate2_msg, other2_msg = swapped((mate2_msg, other2_msg), "curve", 2)
    assert sizes[0] % 2 == 0
    pairs = [(i, i ^ 1) for i in range(sizes[0])]
    mate_rest = lax.ppermute(rest_msg, "curve", pairs)
    pairs = [(i, (i - 2 if i % 2 else i + 2) % sizes[0]) for i in range(sizes[0])]
    passed_rest = lax.ppermute(mate_rest, "curve", pairs)
    (outer,) = call(spread_kernel, "V", "V", [rows128(PLANES * GROUP)], (cells,), [])
    strips = (cells, mate_msg, other_msg, mate2_msg, other2_msg)
    sorted_rows = [messages[1], messages[1], messages[3], messages[3]]
    near_msg, far_msg = call(
        edge_kernel,
        "VVVVVV",
        "VV",
        [rows128(EDGE_ROWS), rows128(EDGE_ROWS)],
        (outer, *strips),
        [floats(rows) for rows in [PLANES * GROUP] + sorted_rows],
    )
    near_msg, far_msg = swapped((near_msg, far_msg), "cross")
    post, own_slots = call(
        join_kernel,
        "VVVVVVV",
        "VV",
        [rows128(ALL_PLANES * PAIR), jax.ShapeDtypeStruct((24, 128), jnp.int32)],
        (*strips, mate_rest, passed_rest),
        [floats(rows) for rows in sorted_rows],
    )
    return call(
        steps_kernel,
        "VVVV",
        "H",
        [jax.ShapeDtypeStruct(populations.shape, jnp.float32)],
        (own_slots, post, near_msg, far_msg),
        [
            floats(SLOTS * SLOT),
            floats(ALL_PLANES * PAIR),
            floats(ALL_PLANES * GROUP),
            pltpu.VMEM(populations.shape, jnp.float32),
            pltpu.VMEM((72, 128), jnp.int32),
            pltpu.SMEM((72, 128), jnp.int32),
            pltpu.SemaphoreType.DMA((SLOTS + 1,)),
        ],
    )[0]


def solution(mesh):
    return jax.shard_map(
        per_device,
        mesh=mesh,
        in_specs=(
            P(("curve", "cross"), None, None),
            P(("curve", "cross"), None),
            P(("curve", "cross"), None),
            P(),
            P(("curve", "cross")),
        ),
        out_specs=P(("curve", "cross"), None, None),
        check_vma=False,
    )
```

```python
import functools
import itertools

import jax
import jax.numpy as jnp
import numpy as np
from jax import lax
from jax.experimental import pallas as pl
from jax.experimental.pallas import tpu as pltpu
from jax.sharding import PartitionSpec as P

EDGE = 16
STEPS = 3
SLOTS = 3
POPS = 19
PLANES = SLOTS * POPS + SLOTS
FLAG0 = SLOTS * POPS
GROUP = 24
PLANE = 3 * GROUP
SLOT = POPS * PLANE
CELLS = PLANES * 32
LANDINGS = CELLS + 8
OWN2 = LANDINGS + 8
OUTWARD = SLOTS * 5 + SLOTS
LAYERS = 2 * PLANES + OUTWARD
RIM = 11 * EDGE
REST = POPS * EDGE + 10 * EDGE
PAIR = 2 * GROUP
QUADS = PLANES // 4
TABLE = RIM
STRIPS = RIM + 8
FAR = QUADS * GROUP
EDGE_TABLE = FAR + 3 * GROUP
EDGE_ROWS = EDGE_TABLE + 24
NEAR_ROWS, FAR_ROWS = EDGE_ROWS + 16, EDGE_ROWS + 24
NOWHERE = PLANES * GROUP
ALL_PLANES = PLANES + POPS
LIMIT = 20 * 1024 * 1024
WIDE_LIMIT = 127 * 512 * 1024

VELOCITY = [
    (0, 0, 0),
    (1, 0, 0),
    (-1, 0, 0),
    (0, 1, 0),
    (0, -1, 0),
    (0, 0, 1),
    (0, 0, -1),
    (1, 1, 0),
    (-1, -1, 0),
    (1, -1, 0),
    (-1, 1, 0),
    (1, 0, 1),
    (-1, 0, -1),
    (1, 0, -1),
    (-1, 0, 1),
    (0, 1, 1),
    (0, -1, -1),
    (0, 1, -1),
    (0, -1, 1),
]
NORTHWARD, SOUTHWARD = (
    [s * POPS + p for s in range(SLOTS) for p in range(POPS) if VELOCITY[p][1] == side]
    + [FLAG0 + s for s in range(SLOTS)]
    for side in (1, -1)
)
THIRD = [
    (pop, source, *((32 + 16 * k, 9) if k < 4 else (16 * (k - 4), 10)))
    for k, (pop, source) in enumerate(
        [(p, 32) for p in (4, 8, 9, 16, 18)] + [(p, 80) for p in (3, 7, 10, 15, 17)]
    )
]
OPPOSITE = [0, 2, 1, 4, 3, 6, 5, 8, 7, 10, 9, 12, 11, 14, 13, 16, 15, 18, 17]


def lanes_iota():
    return lax.broadcasted_iota(jnp.int32, (8, 128), 1)


def is_even(axis, unit=1):
    return lax.rem(lax.axis_index(axis) // unit, 2) == 0


def rows_iota():
    return lax.broadcasted_iota(jnp.int32, (8, 128), 0)


def aligned(start, size=8):
    return pl.ds(pl.multiple_of(start, 8), size)


def move_slots(moves, curve_size, cross_size):
    curve, cross = lax.axis_index("curve"), lax.axis_index("cross")

    def landed(source, target):
        inside = (source >= 0) & (source < curve_size) & (target >= 0) & (target < curve_size)
        row = jnp.clip(source, 0, curve_size - 1) * cross_size + cross
        rank = target * cross_size + cross
        hit = inside & (moves[0, row] >= 0) & (moves[1, row] == rank)
        return jnp.where(hit, moves[2, row], -1)

    return (
        landed(curve - 1, curve),
        landed(curve + 1, curve),
        landed(curve - 2, curve - 1),
        landed(curve, curve - 1),
        landed(curve + 2, curve + 1),
        landed(curve, curve + 1),
    )


def pack_kernel(
    curve_size,
    cross_size,
    moves_hbm,
    counts_hbm,
    pops_hbm,
    flags_hbm,
    neighbours_hbm,
    cells_hbm,
    mate_hbm,
    other_hbm,
    mate2_hbm,
    other2_hbm,
    rest_hbm,
    moves,
    counts,
    pops,
    flags,
    neighbours,
    cells,
    up_msg,
    down_msg,
    up2_msg,
    down2_msg,
    rest_msg,
    wide_flags,
    plane_flags,
    site_flags,
    near,
    sems,
):
    started = []

    def copy(source, target):
        one = pltpu.make_async_copy(source, target, sems.at[len(started)])
        one.start()
        started.append(one)
        return one

    flags_copy = copy(flags_hbm, flags)
    copies = [copy(pops_hbm.at[s], pops.at[s]) for s in range(SLOTS)]
    small = [
        copy(neighbours_hbm, neighbours),
        copy(counts_hbm, counts),
        copy(moves_hbm, moves),
    ]
    for one in small:
        one.wait()

    near[...] = jnp.zeros_like(near)
    named = neighbours[...]
    slot = jnp.where(named >= 0, lax.rem(jnp.maximum(named, 0), SLOTS), SLOTS)
    near[0:SLOTS, 0 : named.shape[1]] = slot.astype(jnp.float32)
    for ref, row in ((cells, CELLS), (up_msg, TABLE), (down_msg, TABLE)):
        ref[row : row + 8, :] = near[...]

    wide_flags[...] = jnp.zeros_like(wide_flags)
    flags_copy.wait()
    wide_flags[0:SLOTS, 0 : flags.shape[1]] = flags[...].astype(jnp.float32)
    span = EDGE + 2
    for x in range(EDGE):
        start = (x + 1) * span * span
        base = start // 128 * 128
        window = wide_flags[:, base : base + 512]
        window = pltpu.roll(window, (512 - (start - base)) % 512, axis=1)
        plane_flags[8 * x : 8 * x + 8, :] = window[:, :384].astype(jnp.bfloat16)
    lane_in = lax.broadcasted_iota(jnp.int32, (384, 256), 0)
    site = lax.broadcasted_iota(jnp.int32, (384, 256), 1)
    chosen = lane_in == (site // EDGE + 1) * span + site % EDGE + 1
    product = jnp.dot(
        plane_flags[...],
        jnp.where(chosen, 1.0, 0.0).astype(jnp.bfloat16),
        preferred_element_type=jnp.float32,
    )
    site_flags[0:128, :] = product[:, :128]
    site_flags[128:256, :] = product[:, 128:]
    for s in range(SLOTS):
        live = s < counts[0]
        for y in range(2):
            piece = site_flags[pl.ds(128 * y + s, EDGE, stride=8), :]
            is_fluid = (piece == 1.0) & live
            row = (FLAG0 + s) * 32 + y * EDGE
            cells[row : row + EDGE, :] = jnp.where(is_fluid, 1.0, 0.0)

    for s in range(SLOTS):
        copies[s].wait()
        for x in range(EDGE):
            for y in range(2):
                tile = 2 * x + y
                for p, size in ((0, 8), (8, 8), (16, 3)):
                    row = (s * POPS + p) * 32 + y * EDGE + x
                    cells[pl.ds(row, size, stride=32), :] = pops[
                        s, p : p + size, 128 * tile : 128 * tile + 128
                    ]

    @pl.loop(0, SLOTS)
    def _(s):
        @pl.loop(0, 4, unroll=2)
        def _(c):
            base = s * (POPS * 32) + c * 8
            view = cells.at[aligned(base, (POPS - 1) * 32 + 8), :]
            h = [view[p * 32 : p * 32 + 8, :] for p in range(POPS)]
            for p, value in enumerate(collided(h)):
                view[p * 32 : p * 32 + 8, :] = value

    for i, slot in enumerate(move_slots(moves, curve_size, cross_size)):
        value = jnp.full((1, 128), slot, jnp.int32)
        cells[LANDINGS + i : LANDINGS + i + 1, :] = value.astype(jnp.float32)

    body_copy = copy(cells.at[:OWN2], cells_hbm.at[:OWN2])

    for y in range(2):
        for msg, x0, first in ((up_msg, 15, 1), (down_msg, 0, 2)):
            step = -1 if x0 else 1
            for k in range(2):
                out = STRIPS + y * LAYERS + k * PLANES
                msg[out : out + PLANES, :] = cells[
                    pl.ds(y * EDGE + x0 + step * k, PLANES, stride=32), :
                ]
            row = y * EDGE + x0 + 2 * step
            out = STRIPS + y * LAYERS + 2 * PLANES
            for s in range(SLOTS):
                base = s * POPS * 32 + row
                msg[out + 5 * s : out + 5 * s + 1, :] = cells[pl.ds(base + first * 32, 1), :]
                msg[out + 5 * s + 1 : out + 5 * s + 5, :] = cells[
                    pl.ds(base + (first + 6) * 32, 4, stride=64), :
                ]
            msg[out + 5 * SLOTS : out + OUTWARD, :] = cells[
                pl.ds(FLAG0 * 32 + row, SLOTS, stride=32), :
            ]

    here = lax.axis_index("curve") * cross_size + lax.axis_index("cross")
    leaving = jnp.maximum(moves[0, here], 0)
    lane = lanes_iota()
    for v in range(2):
        halves = [
            [cells[aligned(leaving * (POPS * 32) + p * 32 + y * EDGE + v * 8), :] for y in (0, 1)]
            for p in range(POPS)
        ]
        outer = [jnp.where(lane < 64, first, second) for first, second in halves]
        middle = (lane >= 32) & (lane < 96)
        sets = [
            jnp.where(middle, pltpu.roll(outer[p + 1], 64, axis=1), outer[p])
            for p in range(0, POPS - 1, 2)
        ]
        sets += [outer[POPS - 1], jnp.zeros_like(outer[0])]
        for pop, source, target, which in THIRD:
            moved = pltpu.roll(outer[pop], (target - source) % 128, axis=1)
            sets[which] = jnp.where(lane // 16 == target // 16, moved, sets[which])
        for k, value in enumerate(sets):
            row = k * EDGE + v * 8
            up_msg[row : row + 8, :] = value
            down_msg[row : row + 8, :] = value
        for p, (first, second) in enumerate(halves):
            row = p * EDGE + v * 8
            rest_msg[row : row + 8, :] = jnp.where(lane < 32, second, first)
        for p in range(0, POPS, 2):
            value = halves[p][1]
            if p + 1 < POPS:
                value = jnp.where(middle, value, pltpu.roll(halves[p + 1][1], 64, axis=1))
            row = (POPS + p // 2) * EDGE + v * 8
            rest_msg[row : row + 8, :] = value
    for s in range(SLOTS):

        @pl.when(leaving == s)
        def _():
            for y in range(2):
                for k in range(3):
                    out = (y * 3 + k) * GROUP
                    row = s * POPS * 32 + y * EDGE + k
                    up2_msg[out : out + POPS, :] = cells[pl.ds(row + 13, POPS, stride=32), :]
                    down2_msg[out : out + POPS, :] = cells[pl.ds(row, POPS, stride=32), :]

    cells[OWN2 : OWN2 + 6 * GROUP, :] = up2_msg[...]
    cells[OWN2 + 6 * GROUP :, :] = down2_msg[...]
    last = [copy(cells.at[OWN2:], cells_hbm.at[OWN2:]), copy(rest_msg, rest_hbm)]
    count = len(started)
    for i, (up, down, mate, other, unit) in enumerate(
        ((up_msg, down_msg, mate_hbm, other_hbm, 1), (up2_msg, down2_msg, mate2_hbm, other2_hbm, 2))
    ):
        first, second = sems.at[count + 2 * i], sems.at[count + 2 * i + 1]
        even = is_even("curve", unit)

        @pl.when(even)
        def _():
            pltpu.make_async_copy(up, mate, first).start()
            pltpu.make_async_copy(down, other, second).start()

        @pl.when(jnp.logical_not(even))
        def _():
            pltpu.make_async_copy(down, mate, first).start()
            pltpu.make_async_copy(up, other, second).start()

        last.append(pltpu.make_async_copy(up, mate, first))
        last.append(pltpu.make_async_copy(down, other, second))
    body_copy.wait()
    for one in last:
        one.wait()


def spread_kernel(cells, outer):
    low = lanes_iota() < 64
    for q in range(PLANES):
        for v in range(2):
            row = q * 32 + v * 8
            first, second = cells[row : row + 8, :], cells[row + EDGE : row + EDGE + 8, :]
            row = q * GROUP + v * 8
            outer[row : row + 8, :] = jnp.where(low, first, second)


def sort_messages(mate_msg, other_msg, mate2_msg, other2_msg, low_msg, high_msg, low2, high2):
    for mate, other, low, high, unit in (
        (mate_msg, other_msg, low_msg, high_msg, 1),
        (mate2_msg, other2_msg, low2, high2, 2),
    ):
        even = is_even("curve", unit)

        @pl.when(even)
        def _():
            low[...] = other[...]
            high[...] = mate[...]

        @pl.when(jnp.logical_not(even))
        def _():
            low[...] = mate[...]
            high[...] = other[...]


def landed_slots(cells):
    return [jnp.max(cells[LANDINGS + i : LANDINGS + i + 1, :]) for i in range(6)]


def rim_of(msg, p, v):
    row = p // 2 * EDGE + v * 8
    value = msg[row : row + 8, :]
    return pltpu.roll(value, 64, axis=1) if p % 2 else value


def sel4(parts, lane):
    first = jnp.where(lane < 32, parts[0], parts[1])
    second = jnp.where(lane < 96, parts[2], parts[3])
    return jnp.where(lane < 64, first, second)


def strip_rows(first, row0, step):
    pieces = []
    for k in range(2):
        pieces.append(
            (PLANES, lambda size, row: pl.ds(row, PLANES, stride=size), row0 + step * k, STRIPS + k * PLANES)
        )
    row, source = row0 + 2 * step, STRIPS + 2 * PLANES
    for s in range(SLOTS):
        plane = s * POPS + first
        pieces.append((1, lambda size, row, plane=plane: pl.ds(plane * size + row, 1), row, source))
        pieces.append(
            (
                4,
                lambda size, row, plane=plane: pl.ds(
                    (plane + 6) * size + row, 4, stride=2 * size
                ),
                row,
                source + 1,
            )
        )
        source += 5
    pieces.append(
        (SLOTS, lambda size, row: pl.ds(FLAG0 * size + row, SLOTS, stride=size), row, source)
    )
    return pieces


def edge_kernel(
    own_outer,
    cells,
    mate_msg,
    other_msg,
    mate2_msg,
    other2_msg,
    near_msg,
    far_msg,
    outer,
    low_msg,
    high_msg,
    low2_msg,
    high2_msg,
):
    sort_messages(
        mate_msg, other_msg, mate2_msg, other2_msg, low_msg, high_msg, low2_msg, high2_msg
    )
    from_low, from_high, low_low, low_me, high_high, high_me = landed_slots(cells)
    low = lanes_iota() < 64
    for q in range(PLANES):
        for v in range(2):
            row = q * GROUP + v * 8
            outer[row : row + 8, :] = own_outer[row : row + 8, :]

    def both(first, second):
        lane = lax.broadcasted_iota(jnp.int32, first.shape, 1)
        return jnp.where(lane < 64, first, second)

    for msg, row0, step, first in ((high_msg, 16, 1, 2), (low_msg, 23, -1, 1)):
        for count, planes, row, source in strip_rows(first, row0, step):
            outer[planes(GROUP, row), :] = both(
                msg[source : source + count, :],
                msg[LAYERS + source : LAYERS + source + count, :],
            )
    lane = lanes_iota()
    for s, (slot, msg) in itertools.product(
        range(SLOTS), ((from_low, low_msg), (from_high, high_msg))
    ):

        @pl.when(slot == s)
        def _():
            for v in range(2):
                values = [rim_of(msg, p, v) for p in range(POPS)]
                for pop, target, source, which in THIRD:
                    row = which * EDGE + v * 8
                    moved = pltpu.roll(msg[row : row + 8, :], (target - source) % 128, axis=1)
                    values[pop] = jnp.where(lane // 16 == target // 16, moved, values[pop])
                for p, value in enumerate(values):
                    row = (s * POPS + p) * GROUP + v * 8
                    outer[row : row + 8, :] = value

    for s in range(SLOTS):
        for slot, msg, row0 in (
            (low_low, low2_msg, 21),
            (low_me, cells.at[OWN2:], 21),
            (high_high, high2_msg, 16),
            (high_me, cells.at[OWN2 + 6 * GROUP :], 16),
        ):

            @pl.when(slot == s)
            def _():
                for k in range(3):
                    outer[pl.ds(s * POPS * GROUP + row0 + k, POPS, stride=GROUP), :] = both(
                        msg[k * GROUP : k * GROUP + POPS, :],
                        msg[(3 + k) * GROUP : (3 + k) * GROUP + POPS, :],
                    )

    even = is_even("cross")

    def send(row, north, south):
        near_msg[row : row + 8, :] = jnp.where(even, north, south)
        far_msg[row : row + 8, :] = jnp.where(even, south, north)

    for v in range(3):

        def plane(q):
            return outer[q * GROUP + v * 8 : q * GROUP + v * 8 + 8, :]

        for quad in range(QUADS):
            parts = [plane(4 * quad)]
            parts += [pltpu.roll(plane(4 * quad + k), 32 * k, axis=1) for k in (1, 2, 3)]
            send(quad * GROUP + v * 8, sel4(parts[1:] + parts[:1], lane), sel4(parts, lane))
        for part in range(3):
            values = []
            for planes, source in ((NORTHWARD, 80), (SOUTHWARD, 32)):
                value = None
                for k, q in enumerate(planes[8 * part : 8 * part + 8]):
                    moved = pltpu.roll(plane(q), (16 * k - source) % 128, axis=1)
                    value = moved if value is None else jnp.where(lane < 16 * k, value, moved)
                values.append(value)
            send(FAR + part * GROUP + v * 8, *values)
    tables = (low_msg, TABLE), (cells, CELLS), (high_msg, TABLE)
    for i, (ref, row) in enumerate(tables):
        value = ref[row : row + 8, :]
        send(EDGE_TABLE + 8 * i, value, value)


def collided(h):
    shear = 1.0 / 0.6
    rest = h[0]
    sx, dx = h[1] + h[2], h[1] - h[2]
    sy, dy = h[3] + h[4], h[3] - h[4]
    sz, dz = h[5] + h[6], h[5] - h[6]
    s7, d7 = h[7] + h[8], h[7] - h[8]
    s9, d9 = h[9] + h[10], h[9] - h[10]
    s11, d11 = h[11] + h[12], h[11] - h[12]
    s13, d13 = h[13] + h[14], h[13] - h[14]
    s15, d15 = h[15] + h[16], h[15] - h[16]
    s17, d17 = h[17] + h[18], h[17] - h[18]
    txy, txz, tyz = s7 + s9, s11 + s13, s15 + s17
    pxy, pxz, pyz = s7 - s9, s11 - s13, s15 - s17
    ax, bx = d7 + d9, d11 + d13
    ay, by = d7 - d9, d15 + d17
    az, bz = d11 - d13, d15 - d17
    axes = sx + sy + sz
    diags = txy + txz + tyz
    rho = rest * (1.0 / 3.0) + axes * (1.0 / 18.0) + diags * (1.0 / 36.0)
    fx, fy, fz = ax + bx, ay + by, az + bz
    jx = dx * (1.0 / 18.0) + fx * (1.0 / 36.0)
    jy = dy * (1.0 / 18.0) + fy * (1.0 / 36.0)
    jz = dz * (1.0 / 18.0) + fz * (1.0 / 36.0)
    inverse = 1.0 / rho
    ux, uy, uz = jx * inverse, jy * inverse, jz * inverse
    qxx, qyy, qzz = jx * ux, jy * uy, jz * uz
    total = qxx + qyy + qzz

    energy = -10.0 * rest - axes * (11.0 / 18.0) + diags * (8.0 / 36.0)
    energy = (energy + 11.0 * rho - 19.0 * total) * (1.19 / 2394.0)
    square = 4.0 * rest - axes * (4.0 / 18.0) + diags * (1.0 / 36.0)
    square = (square - 3.0 * rho + 5.5 * total) * (1.4 / 252.0)
    axis_x = (3.0 * sx - axes) * (1.0 / 18.0)
    diag_x = (diags - 3.0 * tyz) * (1.0 / 36.0)
    want_x = 3.0 * qxx - total
    stress_x = (axis_x + diag_x - want_x) * (shear / 36.0)
    third_x = (diag_x - 2.0 * axis_x + 0.5 * want_x) * (1.4 / 72.0)
    axis_w = (sy - sz) * (1.0 / 18.0)
    diag_w = (txy - txz) * (1.0 / 36.0)
    want_w = qyy - qzz
    stress_w = (axis_w + diag_w - want_w) * (shear / 12.0)
    third_w = (diag_w - 2.0 * axis_w + 0.5 * want_w) * (1.4 / 24.0)

    rest_out = rest - 3.0 * (12.0 * square - 30.0 * energy)
    common = -18.0 * (11.0 * energy + 4.0 * square)
    along_x = 18.0 * (stress_x - 2.0 * third_x)
    along_w = 18.0 * (stress_w - 2.0 * third_w)
    ex = common + 2.0 * along_x
    ey = common - along_x + along_w
    ez = common - along_x - along_w
    common = 36.0 * (8.0 * energy + square)
    across_x = 36.0 * (stress_x + third_x)
    across_w = 36.0 * (stress_w + third_w)
    exy = common + across_x + across_w
    exz = common + across_x - across_w
    eyz = common - 2.0 * across_x
    cxy = shear * (0.25 * pxy - 9.0 * jx * uy)
    cxz = shear * (0.25 * pxz - 9.0 * jx * uz)
    cyz = shear * (0.25 * pyz - 9.0 * jy * uz)

    def flux(d, f, j):
        return (f * (1.0 / 36.0) - d * (4.0 / 18.0) + j * (2.0 / 3.0)) * (1.2 / 40.0)

    hx, hy, hz = flux(dx, fx, jx), flux(dy, fy, jy), flux(dz, fz, jz)
    mx = (ax - bx) * (1.98 / 8.0)
    my = (by - ay) * (1.98 / 8.0)
    mz = (az - bz) * (1.98 / 8.0)
    hx36, hy36, hz36 = 36.0 * hx, 36.0 * hy, 36.0 * hz
    xy_x, xz_x = hx36 + mx, hx36 - mx
    yz_y, xy_y = hy36 + my, hy36 - my
    xz_z, yz_z = hz36 + mz, hz36 - mz
    ox, oy, oz = -2.0 * hx36, -2.0 * hy36, -2.0 * hz36

    out = [rest_out]

    def pair(i, even, odd):
        out.append(h[i] - (even + odd))
        out.append(h[i + 1] - (even - odd))

    pair(1, ex, ox)
    pair(3, ey, oy)
    pair(5, ez, oz)
    pair(7, exy + cxy, xy_x + xy_y)
    pair(9, exy - cxy, xy_x - xy_y)
    pair(11, exz + cxz, xz_x + xz_z)
    pair(13, exz - cxz, xz_x - xz_z)
    pair(15, eyz + cyz, yz_y + yz_z)
    pair(17, eyz - cyz, yz_y - yz_z)
    return out


def collide_all(h_ref, flags, posts):
    for groups in ((0, 1), (2,)):
        ref = posts[groups[0] // 2]
        size = len(groups) * GROUP

        @pl.loop(0, SLOTS)
        def _(s):
            @pl.loop(0, size // 8, unroll=3)
            def _(c):
                is_fluid = flags[groups[0] // 2][aligned((FLAG0 + s) * size + c * 8), :] > 0.0
                start = s * SLOT + groups[0] * GROUP + c * 8
                h_view = h_ref.at[aligned(start, (POPS - 1) * PLANE + 8), :]
                start = s * (POPS * size) + c * 8
                view = ref.at[aligned(start, (POPS - 1) * size + 8), :]
                h = [h_view[p * PLANE : p * PLANE + 8, :] for p in range(POPS)]
                for p, value in enumerate(collided(h)):
                    view[p * size : p * size + 8, :] = jnp.where(is_fluid, value, jnp.nan)


def hide_walls(ref, size):
    @pl.loop(0, SLOTS)
    def _(s):
        @pl.loop(0, size // 8)
        def _(c):
            is_fluid = ref[aligned((FLAG0 + s) * size + c * 8), :] > 0.0
            start = s * (POPS * size) + c * 8
            view = ref.at[aligned(start, (POPS - 1) * size + 8), :]
            for p in range(POPS):
                row = p * size
                view[row : row + 8, :] = jnp.where(is_fluid, view[row : row + 8, :], jnp.nan)


def stream_all(posts, h_ref, flags, table, groups, vregs, finish=None):
    lane = lanes_iota()
    row = rows_iota()
    low = lane < 64

    def one_slot(s):
        views = {}

        def view(which, key):
            if (which, key) not in views:
                start = s * (POPS * GROUP) if key == "own" else table[key[0] * 8 + s, key[1]]
                start = start if which else 2 * start
                views[which, key] = posts[which].at[
                    aligned(start, POPS * (GROUP if which else PAIR)), :
                ]
            return views[which, key]

        def load(key, pop, group, v):
            if group == 2:
                row = pop * GROUP + v * 8
            else:
                row = pop * PAIR + group * GROUP + v * 8
            return view(group // 2, key)[row : row + 8, :]

        h_view = h_ref.at[aligned(s * SLOT, SLOT), :]

        def shifted(pop, group, j, dy, dz):
            cx = VELOCITY[pop][0]

            def rows(key, v):
                return load(key, pop, group, v)

            def look(i, j, dx, v):
                if (dx, dy, dz) == (0, 0, 0):
                    return rows("own", v)
                if j is None:
                    return jnp.where(low, look(i, 1, dx, v), look(i, -1, dx, v))
                region = (i + 1) * 3 + j + 1
                return rows((region, VELOCITY.index((dx, dy, dz)) - 1), v)

            need_last = vregs == 3
            values = [look(0, j, 0, 0), look(0, j, 0, 1)]
            if need_last:
                if dy == 0 and dz == 0:
                    values.append(rows("own", 2))
                else:
                    values.append(jnp.where(row < 4, look(1, j, 0, 2), look(-1, j, 0, 2)))
            if cx == 0:
                return values
            turn = 1 if cx > 0 else 7
            rolled = [pltpu.roll(value, turn, axis=0) for value in values]
            if cx > 0:
                before = pltpu.roll(look(0, j, -1, 2), 1, axis=0)
                result = [
                    jnp.where(row == 0, before, rolled[0]),
                    jnp.where(row == 0, rolled[0], rolled[1]),
                ]
                if need_last:
                    edge = pltpu.roll(look(1, j, -1, 1), 1, axis=0)
                    result.append(jnp.where(row == 0, edge, rolled[2]))
                return result
            after = pltpu.roll(look(0, j, 1, 2), 7, axis=0)
            result = [
                jnp.where(row == 7, rolled[1], rolled[0]),
                jnp.where(row == 7, after, rolled[1]),
            ]
            if need_last:
                edge = pltpu.roll(look(-1, j, 1, 0), 7, axis=0)
                result.append(jnp.where(row == 7, edge, rolled[2]))
            return result

        for pop in range(POPS):
            cx, cy, cz = VELOCITY[pop]
            kept = {}

            def source(*key):
                if key not in kept:
                    kept[key] = shifted(pop, *key)
                return kept[key]

            def along_y(group, dz):
                values = source(group, None if group == 2 else 0, 0, dz)
                if cy == 0:
                    return values
                other = (group - cy) % 3
                if group != 2 and other != 2:
                    carried = source(other, 0, 0, dz)
                else:
                    carried = source(other, cy if group == 2 else 0, -cy, dz)
                mask = lane >= 112 if cy > 0 else lane < 16
                return [jnp.where(mask, b, a) for a, b in zip(values, carried)]

            for group in groups:
                values = along_y(group, 0)
                turn = (16 * cy + cz) % 128
                if turn:
                    values = [pltpu.roll(value, turn, axis=1) for value in values]
                if cz:
                    turn = (16 * cy - 15 * cz) % 128
                    wrapped = [pltpu.roll(value, turn, axis=1) for value in along_y(group, -cz)]
                    mask = lane % 16 == (0 if cz > 0 else 15)
                    values = [jnp.where(mask, b, a) for a, b in zip(values, wrapped)]
                for v, value in enumerate(values[:vregs]):
                    if pop:
                        value = jnp.where(value != value, load("own", OPPOSITE[pop], group, v), value)
                    if finish is not None:
                        is_fluid = flags[group // 2][
                            aligned((FLAG0 + s) * PAIR + group * GROUP + v * 8), :
                        ]
                        value = jnp.where(is_fluid > 0.0, value, 0.0)
                    target = pop * PLANE + group * GROUP + v * 8
                    h_view[target : target + 8, :] = value

    @pl.loop(0, SLOTS)
    def _(s):
        one_slot(s)
        if finish is not None:
            finish(s)


def join_kernel(
    cells,
    mate_msg,
    other_msg,
    mate2_msg,
    other2_msg,
    mate_rest,
    passed_rest,
    post_ref,
    slots,
    low_msg,
    high_msg,
    low2_msg,
    high2_msg,
):
    sort_messages(
        mate_msg, other_msg, mate2_msg, other2_msg, low_msg, high_msg, low2_msg, high2_msg
    )
    for i, (ref, row) in enumerate(((low_msg, TABLE), (cells, CELLS), (high_msg, TABLE))):
        slots[8 * i : 8 * i + 8, :] = first_rows(ref[row : row + 8, :])

    from_low, from_high, low_low, low_me, high_high, high_me = landed_slots(cells)
    lane = lanes_iota()
    post_ref[PLANES * PAIR :, :] = jnp.full((POPS * PAIR, 128), jnp.nan, jnp.float32)
    for q in range(PLANES):
        for y in range(2):
            start = q * PAIR + y * GROUP
            post_ref[start : start + EDGE, :] = cells[
                q * 32 + y * EDGE : q * 32 + (y + 1) * EDGE, :
            ]
    even = is_even("curve")
    odd = jnp.logical_not(even)
    for s, (slot, msg, wanted, rest) in itertools.product(
        range(SLOTS),
        (
            (from_low, low_msg, odd, mate_rest),
            (from_low, low_msg, even, passed_rest),
            (from_high, high_msg, even, mate_rest),
            (from_high, high_msg, odd, passed_rest),
        ),
    ):

        @pl.when((slot == s) & wanted)
        def _():
            for p in range(POPS):
                for v in range(2):
                    rim = rim_of(msg, p, v)
                    row = p * EDGE + v * 8
                    wide = rest[row : row + 8, :]
                    row = (POPS + p // 2) * EDGE + v * 8
                    middle = rest[row : row + 8, :]
                    if p % 2:
                        middle = pltpu.roll(middle, 64, axis=1)
                    second = jnp.where(lane < 32, wide, jnp.where(lane < 96, middle, rim))
                    row = (s * POPS + p) * PAIR + v * 8
                    post_ref[row : row + 8, :] = jnp.where(lane < 32, rim, wide)
                    post_ref[row + GROUP : row + GROUP + 8, :] = second

    for msg, row0, step, first in ((high_msg, 16, 1, 2), (low_msg, 23, -1, 1)):
        for y in range(2):
            for count, planes, row, source in strip_rows(first, row0, step):
                source += y * LAYERS
                post_ref[planes(PAIR, row + y * GROUP), :] = msg[source : source + count, :]
    for s in range(SLOTS):
        for slot, msg, row0 in (
            (low_low, low2_msg, 21),
            (low_me, cells.at[OWN2:], 21),
            (high_high, high2_msg, 16),
            (high_me, cells.at[OWN2 + 6 * GROUP :], 16),
        ):

            @pl.when(slot == s)
            def _():
                for y in range(2):
                    for k in range(3):
                        row = s * POPS * PAIR + y * GROUP + row0 + k
                        source = (y * 3 + k) * GROUP
                        post_ref[pl.ds(row, POPS, stride=PAIR), :] = msg[source : source + POPS, :]
    hide_walls(post_ref, PAIR)


def first_rows(slot):
    slot = slot.astype(jnp.int32)
    return jnp.where(slot == SLOTS, NOWHERE, slot * (POPS * GROUP))


def steps_kernel(
    own_slots,
    first_post,
    near_msg,
    far_msg,
    out_hbm,
    h_ref,
    post_ref,
    outer_ref,
    out,
    slots,
    table,
    sems,
):
    even = is_even("cross")

    def received(row):
        near, far = near_msg[row : row + 8, :], far_msg[row : row + 8, :]
        return jnp.where(even, far, near), jnp.where(even, near, far)

    for i in range(3):
        south, north = received(EDGE_TABLE + 8 * i)
        slots[24 * i : 24 * i + 8, :] = first_rows(south)
        slots[24 * i + 8 : 24 * i + 16, :] = own_slots[8 * i : 8 * i + 8, :]
        slots[24 * i + 16 : 24 * i + 24, :] = first_rows(north)
    table_copy = pltpu.make_async_copy(slots, table, sems.at[SLOTS])
    table_copy.start()

    nothing = jnp.full((8, 128), jnp.nan, jnp.float32)
    for row in range(0, POPS * GROUP, 8):
        outer_ref[NOWHERE + row : NOWHERE + row + 8, :] = nothing
    for row in range(PLANES * PAIR, ALL_PLANES * PAIR, 8):
        post_ref[row : row + 8, :] = nothing
    lane = lanes_iota()
    for v in range(3):

        def rows(q):
            return slice(q * GROUP + v * 8, q * GROUP + v * 8 + 8)

        for quad in range(QUADS):
            south, north = received(quad * GROUP + v * 8)
            for k in range(4):
                value = jnp.where(lane // 32 == (k + 3) % 4, south, north)
                if k:
                    value = pltpu.roll(value, 128 - 32 * k, axis=1)
                outer_ref[rows(4 * quad + k), :] = value
        for part in range(3):
            values = received(FAR + part * GROUP + v * 8)
            for planes, target, value in zip((NORTHWARD, SOUTHWARD), (80, 32), values):
                for k, q in enumerate(planes[8 * part : 8 * part + 8]):
                    moved = pltpu.roll(value, (target - 16 * k) % 128, axis=1)
                    outer_ref[rows(q), :] = jnp.where(
                        lane // 16 == target // 16, moved, outer_ref[rows(q), :]
                    )
    hide_walls(outer_ref, GROUP)
    table_copy.wait()

    def finish(s):
        for x in range(EDGE):
            for y in range(2):
                tile = 2 * x + y
                for p, size in ((0, 8), (8, 8), (16, 3)):
                    row = s * SLOT + (p * PLANE + y * GROUP + x)
                    out[s, p : p + size, 128 * tile : 128 * tile + 128] = h_ref[
                        pl.ds(row, size, stride=PLANE), :
                    ]
        pltpu.make_async_copy(out.at[s], out_hbm.at[s], sems.at[s]).start()

    flags = (first_post, outer_ref)
    posts = flags
    for _ in range(STEPS - 1):
        stream_all(posts, h_ref, flags, table, (0, 1, 2), 3)
        posts = (post_ref, outer_ref)
        collide_all(h_ref, flags, posts)
    stream_all(posts, h_ref, flags, table, (0, 1), 2, finish)
    for s in range(SLOTS):
        pltpu.make_async_copy(out.at[s], out_hbm.at[s], sems.at[s]).wait()


def swapped(value, axis, unit=1):
    count = lax.axis_size(axis)
    results = []
    for which in (0, 1):
        others = [i + (unit if i // unit % 2 == which else -unit) for i in range(count)]
        pairs = [(i, j if 0 <= j < count else i) for i, j in enumerate(others)]
        results.append(lax.ppermute(value[which], axis, pairs))
    return results


def rows128(count):
    return jax.ShapeDtypeStruct((count, 128), jnp.float32)


def call(kernel, in_spaces, out_spaces, outs, ins, scratch, limit=LIMIT, cost=None):
    spaces = {
        "S": pl.BlockSpec(memory_space=pltpu.SMEM),
        "V": pl.BlockSpec(memory_space=pltpu.VMEM),
        "H": pl.BlockSpec(memory_space=pltpu.HBM),
    }
    return pl.pallas_call(
        kernel,
        out_shape=outs,
        in_specs=[spaces[x] for x in in_spaces],
        out_specs=[spaces[x] for x in out_spaces],
        scratch_shapes=scratch,
        compiler_params=pltpu.CompilerParams(vmem_limit_bytes=limit),
        cost_estimate=cost,
    )(*ins)


def per_device(populations, site_flags, neighbours, migrations, counts):
    sizes = (lax.axis_size("curve"), lax.axis_size("cross"))
    moves = migrations.T
    floats = lambda rows: pltpu.VMEM((rows, 128), jnp.float32)
    messages = [
        OWN2 + 12 * GROUP,
        STRIPS + 2 * LAYERS,
        STRIPS + 2 * LAYERS,
        6 * GROUP,
        6 * GROUP,
        REST,
    ]
    cells, mate_msg, other_msg, mate2_msg, other2_msg, rest_msg = call(
        functools.partial(pack_kernel, *sizes),
        "HHHHH",
        "HHHHHH",
        [rows128(rows) for rows in messages],
        (moves, counts, populations, site_flags, neighbours),
        [
            pltpu.SMEM(moves.shape, jnp.int32),
            pltpu.SMEM(counts.shape, jnp.int32),
            pltpu.VMEM(populations.shape, jnp.float32),
            pltpu.VMEM(site_flags.shape, jnp.int32),
            pltpu.VMEM(neighbours.shape, jnp.int32),
            *[floats(rows) for rows in messages],
            pltpu.VMEM((8, 5888), jnp.float32),
            pltpu.VMEM((128, 384), jnp.bfloat16),
            floats(256),
            floats(8),
            pltpu.SemaphoreType.DMA((4 + SLOTS + 8,)),
        ],
        WIDE_LIMIT,
    )
    mate_msg, other_msg = swapped((mate_msg, other_msg), "curve")
    mate2_msg, other2_msg = swapped((mate2_msg, other2_msg), "curve", 2)
    assert sizes[0] % 2 == 0
    pairs = [(i, i ^ 1) for i in range(sizes[0])]
    mate_rest = lax.ppermute(rest_msg, "curve", pairs)
    pairs = [(i, (i - 2 if i % 2 else i + 2) % sizes[0]) for i in range(sizes[0])]
    passed_rest = lax.ppermute(mate_rest, "curve", pairs)
    (outer,) = call(spread_kernel, "V", "V", [rows128(PLANES * GROUP)], (cells,), [])
    strips = (cells, mate_msg, other_msg, mate2_msg, other2_msg)
    sorted_rows = [messages[1], messages[1], messages[3], messages[3]]
    near_msg, far_msg = call(
        edge_kernel,
        "VVVVVV",
        "VV",
        [rows128(NEAR_ROWS), rows128(FAR_ROWS)],
        (outer, *strips),
        [floats(rows) for rows in [PLANES * GROUP] + sorted_rows],
        cost=pl.CostEstimate(flops=10**10, bytes_accessed=0, transcendentals=0),
    )
    near_msg, far_msg = swapped((near_msg, far_msg), "cross")
    post, own_slots = call(
        join_kernel,
        "VVVVVVV",
        "VV",
        [rows128(ALL_PLANES * PAIR), jax.ShapeDtypeStruct((24, 128), jnp.int32)],
        (*strips, mate_rest, passed_rest),
        [floats(rows) for rows in sorted_rows],
    )
    return call(
        steps_kernel,
        "VVVV",
        "H",
        [jax.ShapeDtypeStruct(populations.shape, jnp.float32)],
        (own_slots, post, near_msg, far_msg),
        [
            floats(SLOTS * SLOT),
            floats(ALL_PLANES * PAIR),
            floats(ALL_PLANES * GROUP),
            pltpu.VMEM(populations.shape, jnp.float32),
            pltpu.VMEM((72, 128), jnp.int32),
            pltpu.SMEM((72, 128), jnp.int32),
            pltpu.SemaphoreType.DMA((SLOTS + 1,)),
        ],
    )[0]


def solution(mesh):
    return jax.shard_map(
        per_device,
        mesh=mesh,
        in_specs=(
            P(("curve", "cross"), None, None),
            P(("curve", "cross"), None),
            P(("curve", "cross"), None),
            P(),
            P(("curve", "cross")),
        ),
        out_specs=P(("curve", "cross"), None, None),
        check_vma=False,
    )
```

```python
import functools
import itertools

import jax
import jax.numpy as jnp
import numpy as np
from jax import lax
from jax.experimental import pallas as pl
from jax.experimental.pallas import tpu as pltpu
from jax.sharding import PartitionSpec as P

EDGE = 16
STEPS = 3
SLOTS = 3
POPS = 19
PLANES = SLOTS * POPS + SLOTS
FLAG0 = SLOTS * POPS
GROUP = 24
PLANE = 3 * GROUP
SLOT = POPS * PLANE
CELLS = PLANES * 32
LANDINGS = CELLS + 8
OWN2 = LANDINGS + 8
OUTWARD = SLOTS * 5 + SLOTS
LAYERS = 2 * PLANES + OUTWARD
RIM = 11 * EDGE
REST = POPS * EDGE + 10 * EDGE
PAIR = 2 * GROUP
QUADS = PLANES // 4
TABLE = RIM
STRIPS = RIM + 8
FAR = QUADS * GROUP
EDGE_TABLE = FAR + 3 * GROUP
EDGE_ROWS = EDGE_TABLE + 24
NEAR_ROWS, FAR_ROWS = EDGE_ROWS + 16, EDGE_ROWS + 24
NOWHERE = PLANES * GROUP
ALL_PLANES = PLANES + POPS
LIMIT = 20 * 1024 * 1024
WIDE_LIMIT = 127 * 512 * 1024

VELOCITY = [
    (0, 0, 0),
    (1, 0, 0),
    (-1, 0, 0),
    (0, 1, 0),
    (0, -1, 0),
    (0, 0, 1),
    (0, 0, -1),
    (1, 1, 0),
    (-1, -1, 0),
    (1, -1, 0),
    (-1, 1, 0),
    (1, 0, 1),
    (-1, 0, -1),
    (1, 0, -1),
    (-1, 0, 1),
    (0, 1, 1),
    (0, -1, -1),
    (0, 1, -1),
    (0, -1, 1),
]
NORTHWARD, SOUTHWARD = (
    [s * POPS + p for s in range(SLOTS) for p in range(POPS) if VELOCITY[p][1] == side]
    + [FLAG0 + s for s in range(SLOTS)]
    for side in (1, -1)
)
THIRD = [
    (pop, source, *((32 + 16 * k, 9) if k < 4 else (16 * (k - 4), 10)))
    for k, (pop, source) in enumerate(
        [(p, 32) for p in (4, 8, 9, 16, 18)] + [(p, 80) for p in (3, 7, 10, 15, 17)]
    )
]
OPPOSITE = [0, 2, 1, 4, 3, 6, 5, 8, 7, 10, 9, 12, 11, 14, 13, 16, 15, 18, 17]


def lanes_iota():
    return lax.broadcasted_iota(jnp.int32, (8, 128), 1)


def is_even(axis, unit=1):
    return lax.rem(lax.axis_index(axis) // unit, 2) == 0


def rows_iota():
    return lax.broadcasted_iota(jnp.int32, (8, 128), 0)


def aligned(start, size=8):
    return pl.ds(pl.multiple_of(start, 8), size)


def move_slots(moves, curve_size, cross_size):
    curve, cross = lax.axis_index("curve"), lax.axis_index("cross")

    def landed(source, target):
        inside = (source >= 0) & (source < curve_size) & (target >= 0) & (target < curve_size)
        row = jnp.clip(source, 0, curve_size - 1) * cross_size + cross
        rank = target * cross_size + cross
        hit = inside & (moves[0, row] >= 0) & (moves[1, row] == rank)
        return jnp.where(hit, moves[2, row], -1)

    return (
        landed(curve - 1, curve),
        landed(curve + 1, curve),
        landed(curve - 2, curve - 1),
        landed(curve, curve - 1),
        landed(curve + 2, curve + 1),
        landed(curve, curve + 1),
    )


def pack_kernel(
    curve_size,
    cross_size,
    moves_hbm,
    counts_hbm,
    pops_hbm,
    flags_hbm,
    neighbours_hbm,
    cells_hbm,
    mate_hbm,
    other_hbm,
    mate2_hbm,
    other2_hbm,
    rest_hbm,
    moves,
    counts,
    pops,
    flags,
    neighbours,
    cells,
    up_msg,
    down_msg,
    up2_msg,
    down2_msg,
    rest_msg,
    wide_flags,
    plane_flags,
    site_flags,
    near,
    sems,
):
    started = []

    def copy(source, target):
        one = pltpu.make_async_copy(source, target, sems.at[len(started)])
        one.start()
        started.append(one)
        return one

    flags_copy = copy(flags_hbm, flags)
    copies = [copy(pops_hbm.at[s], pops.at[s]) for s in range(SLOTS)]
    small = [
        copy(neighbours_hbm, neighbours),
        copy(counts_hbm, counts),
        copy(moves_hbm, moves),
    ]
    for one in small:
        one.wait()

    near[...] = jnp.zeros_like(near)
    named = neighbours[...]
    slot = jnp.where(named >= 0, lax.rem(jnp.maximum(named, 0), SLOTS), SLOTS)
    near[0:SLOTS, 0 : named.shape[1]] = slot.astype(jnp.float32)
    for ref, row in ((cells, CELLS), (up_msg, TABLE), (down_msg, TABLE)):
        ref[row : row + 8, :] = near[...]

    wide_flags[...] = jnp.zeros_like(wide_flags)
    flags_copy.wait()
    wide_flags[0:SLOTS, 0 : flags.shape[1]] = flags[...].astype(jnp.float32)
    span = EDGE + 2
    for x in range(EDGE):
        start = (x + 1) * span * span
        base = start // 128 * 128
        window = wide_flags[:, base : base + 512]
        window = pltpu.roll(window, (512 - (start - base)) % 512, axis=1)
        plane_flags[8 * x : 8 * x + 8, :] = window[:, :384].astype(jnp.bfloat16)
    lane_in = lax.broadcasted_iota(jnp.int32, (384, 256), 0)
    site = lax.broadcasted_iota(jnp.int32, (384, 256), 1)
    chosen = lane_in == (site // EDGE + 1) * span + site % EDGE + 1
    product = jnp.dot(
        plane_flags[...],
        jnp.where(chosen, 1.0, 0.0).astype(jnp.bfloat16),
        preferred_element_type=jnp.float32,
    )
    site_flags[0:128, :] = product[:, :128]
    site_flags[128:256, :] = product[:, 128:]
    for s in range(SLOTS):
        live = s < counts[0]
        for y in range(2):
            piece = site_flags[pl.ds(128 * y + s, EDGE, stride=8), :]
            is_fluid = (piece == 1.0) & live
            row = (FLAG0 + s) * 32 + y * EDGE
            cells[row : row + EDGE, :] = jnp.where(is_fluid, 1.0, 0.0)

    for s in range(SLOTS):
        copies[s].wait()
        for x in range(EDGE):
            for y in range(2):
                tile = 2 * x + y
                for p, size in ((0, 8), (8, 8), (16, 3)):
                    row = (s * POPS + p) * 32 + y * EDGE + x
                    cells[pl.ds(row, size, stride=32), :] = pops[
                        s, p : p + size, 128 * tile : 128 * tile + 128
                    ]

    @pl.loop(0, SLOTS)
    def _(s):
        @pl.loop(0, 4, unroll=2)
        def _(c):
            base = s * (POPS * 32) + c * 8
            view = cells.at[aligned(base, (POPS - 1) * 32 + 8), :]
            h = [view[p * 32 : p * 32 + 8, :] for p in range(POPS)]
            for p, value in enumerate(collided(h)):
                view[p * 32 : p * 32 + 8, :] = value

    for i, slot in enumerate(move_slots(moves, curve_size, cross_size)):
        value = jnp.full((1, 128), slot, jnp.int32)
        cells[LANDINGS + i : LANDINGS + i + 1, :] = value.astype(jnp.float32)

    body_copy = copy(cells.at[:OWN2], cells_hbm.at[:OWN2])

    for y in range(2):
        for msg, x0, first in ((up_msg, 15, 1), (down_msg, 0, 2)):
            step = -1 if x0 else 1
            for k in range(2):
                out = STRIPS + y * LAYERS + k * PLANES
                msg[out : out + PLANES, :] = cells[
                    pl.ds(y * EDGE + x0 + step * k, PLANES, stride=32), :
                ]
            row = y * EDGE + x0 + 2 * step
            out = STRIPS + y * LAYERS + 2 * PLANES
            for s in range(SLOTS):
                base = s * POPS * 32 + row
                msg[out + 5 * s : out + 5 * s + 1, :] = cells[pl.ds(base + first * 32, 1), :]
                msg[out + 5 * s + 1 : out + 5 * s + 5, :] = cells[
                    pl.ds(base + (first + 6) * 32, 4, stride=64), :
                ]
            msg[out + 5 * SLOTS : out + OUTWARD, :] = cells[
                pl.ds(FLAG0 * 32 + row, SLOTS, stride=32), :
            ]

    here = lax.axis_index("curve") * cross_size + lax.axis_index("cross")
    leaving = jnp.maximum(moves[0, here], 0)
    lane = lanes_iota()
    for v in range(2):
        halves = [
            [cells[aligned(leaving * (POPS * 32) + p * 32 + y * EDGE + v * 8), :] for y in (0, 1)]
            for p in range(POPS)
        ]
        outer = [jnp.where(lane < 64, first, second) for first, second in halves]
        middle = (lane >= 32) & (lane < 96)
        sets = [
            jnp.where(middle, pltpu.roll(outer[p + 1], 64, axis=1), outer[p])
            for p in range(0, POPS - 1, 2)
        ]
        sets += [outer[POPS - 1], jnp.zeros_like(outer[0])]
        for pop, source, target, which in THIRD:
            moved = pltpu.roll(outer[pop], (target - source) % 128, axis=1)
            sets[which] = jnp.where(lane // 16 == target // 16, moved, sets[which])
        for k, value in enumerate(sets):
            row = k * EDGE + v * 8
            up_msg[row : row + 8, :] = value
            down_msg[row : row + 8, :] = value
        for p, (first, second) in enumerate(halves):
            row = p * EDGE + v * 8
            rest_msg[row : row + 8, :] = jnp.where(lane < 32, second, first)
        for p in range(0, POPS, 2):
            value = halves[p][1]
            if p + 1 < POPS:
                value = jnp.where(middle, value, pltpu.roll(halves[p + 1][1], 64, axis=1))
            row = (POPS + p // 2) * EDGE + v * 8
            rest_msg[row : row + 8, :] = value
    for s in range(SLOTS):

        @pl.when(leaving == s)
        def _():
            for y in range(2):
                for k in range(3):
                    out = (y * 3 + k) * GROUP
                    row = s * POPS * 32 + y * EDGE + k
                    up2_msg[out : out + POPS, :] = cells[pl.ds(row + 13, POPS, stride=32), :]
                    down2_msg[out : out + POPS, :] = cells[pl.ds(row, POPS, stride=32), :]

    cells[OWN2 : OWN2 + 6 * GROUP, :] = up2_msg[...]
    cells[OWN2 + 6 * GROUP :, :] = down2_msg[...]
    last = [copy(cells.at[OWN2:], cells_hbm.at[OWN2:]), copy(rest_msg, rest_hbm)]
    count = len(started)
    for i, (up, down, mate, other, unit) in enumerate(
        ((up_msg, down_msg, mate_hbm, other_hbm, 1), (up2_msg, down2_msg, mate2_hbm, other2_hbm, 2))
    ):
        first, second = sems.at[count + 2 * i], sems.at[count + 2 * i + 1]
        even = is_even("curve", unit)

        @pl.when(even)
        def _():
            pltpu.make_async_copy(up, mate, first).start()
            pltpu.make_async_copy(down, other, second).start()

        @pl.when(jnp.logical_not(even))
        def _():
            pltpu.make_async_copy(down, mate, first).start()
            pltpu.make_async_copy(up, other, second).start()

        last.append(pltpu.make_async_copy(up, mate, first))
        last.append(pltpu.make_async_copy(down, other, second))
    body_copy.wait()
    for one in last:
        one.wait()


def spread_kernel(cells, outer):
    low = lanes_iota() < 64
    for q in range(PLANES):
        for v in range(2):
            row = q * 32 + v * 8
            first, second = cells[row : row + 8, :], cells[row + EDGE : row + EDGE + 8, :]
            row = q * GROUP + v * 8
            outer[row : row + 8, :] = jnp.where(low, first, second)


def sort_messages(mate_msg, other_msg, mate2_msg, other2_msg, low_msg, high_msg, low2, high2):
    for mate, other, low, high, unit in (
        (mate_msg, other_msg, low_msg, high_msg, 1),
        (mate2_msg, other2_msg, low2, high2, 2),
    ):
        even = is_even("curve", unit)

        @pl.when(even)
        def _():
            low[...] = other[...]
            high[...] = mate[...]

        @pl.when(jnp.logical_not(even))
        def _():
            low[...] = mate[...]
            high[...] = other[...]


def landed_slots(cells):
    return [jnp.max(cells[LANDINGS + i : LANDINGS + i + 1, :]) for i in range(6)]


def rim_of(msg, p, v):
    row = p // 2 * EDGE + v * 8
    value = msg[row : row + 8, :]
    return pltpu.roll(value, 64, axis=1) if p % 2 else value


def sel4(parts, lane):
    first = jnp.where(lane < 32, parts[0], parts[1])
    second = jnp.where(lane < 96, parts[2], parts[3])
    return jnp.where(lane < 64, first, second)


def strip_rows(first, row0, step):
    pieces = []
    for k in range(2):
        pieces.append(
            (PLANES, lambda size, row: pl.ds(row, PLANES, stride=size), row0 + step * k, STRIPS + k * PLANES)
        )
    row, source = row0 + 2 * step, STRIPS + 2 * PLANES
    for s in range(SLOTS):
        plane = s * POPS + first
        pieces.append((1, lambda size, row, plane=plane: pl.ds(plane * size + row, 1), row, source))
        pieces.append(
            (
                4,
                lambda size, row, plane=plane: pl.ds(
                    (plane + 6) * size + row, 4, stride=2 * size
                ),
                row,
                source + 1,
            )
        )
        source += 5
    pieces.append(
        (SLOTS, lambda size, row: pl.ds(FLAG0 * size + row, SLOTS, stride=size), row, source)
    )
    return pieces


def edge_kernel(
    own_outer,
    cells,
    mate_msg,
    other_msg,
    mate2_msg,
    other2_msg,
    near_msg,
    far_msg,
    outer,
    low_msg,
    high_msg,
    low2_msg,
    high2_msg,
):
    sort_messages(
        mate_msg, other_msg, mate2_msg, other2_msg, low_msg, high_msg, low2_msg, high2_msg
    )
    from_low, from_high, low_low, low_me, high_high, high_me = landed_slots(cells)
    low = lanes_iota() < 64
    for q in range(PLANES):
        for v in range(2):
            row = q * GROUP + v * 8
            outer[row : row + 8, :] = own_outer[row : row + 8, :]

    def both(first, second):
        lane = lax.broadcasted_iota(jnp.int32, first.shape, 1)
        return jnp.where(lane < 64, first, second)

    for msg, row0, step, first in ((high_msg, 16, 1, 2), (low_msg, 23, -1, 1)):
        for count, planes, row, source in strip_rows(first, row0, step):
            outer[planes(GROUP, row), :] = both(
                msg[source : source + count, :],
                msg[LAYERS + source : LAYERS + source + count, :],
            )
    lane = lanes_iota()
    for s, (slot, msg) in itertools.product(
        range(SLOTS), ((from_low, low_msg), (from_high, high_msg))
    ):

        @pl.when(slot == s)
        def _():
            for v in range(2):
                values = [rim_of(msg, p, v) for p in range(POPS)]
                for pop, target, source, which in THIRD:
                    row = which * EDGE + v * 8
                    moved = pltpu.roll(msg[row : row + 8, :], (target - source) % 128, axis=1)
                    values[pop] = jnp.where(lane // 16 == target // 16, moved, values[pop])
                for p, value in enumerate(values):
                    row = (s * POPS + p) * GROUP + v * 8
                    outer[row : row + 8, :] = value

    for s in range(SLOTS):
        for slot, msg, row0 in (
            (low_low, low2_msg, 21),
            (low_me, cells.at[OWN2:], 21),
            (high_high, high2_msg, 16),
            (high_me, cells.at[OWN2 + 6 * GROUP :], 16),
        ):

            @pl.when(slot == s)
            def _():
                for k in range(3):
                    outer[pl.ds(s * POPS * GROUP + row0 + k, POPS, stride=GROUP), :] = both(
                        msg[k * GROUP : k * GROUP + POPS, :],
                        msg[(3 + k) * GROUP : (3 + k) * GROUP + POPS, :],
                    )

    even = is_even("cross")

    def send(row, north, south):
        near_msg[row : row + 8, :] = jnp.where(even, north, south)
        far_msg[row : row + 8, :] = jnp.where(even, south, north)

    for v in range(3):

        def plane(q):
            return outer[q * GROUP + v * 8 : q * GROUP + v * 8 + 8, :]

        for quad in range(QUADS):
            parts = [plane(4 * quad)]
            parts += [pltpu.roll(plane(4 * quad + k), 32 * k, axis=1) for k in (1, 2, 3)]
            send(quad * GROUP + v * 8, sel4(parts[1:] + parts[:1], lane), sel4(parts, lane))
        for part in range(3):
            values = []
            for planes, source in ((NORTHWARD, 80), (SOUTHWARD, 32)):
                value = None
                for k, q in enumerate(planes[8 * part : 8 * part + 8]):
                    moved = pltpu.roll(plane(q), (16 * k - source) % 128, axis=1)
                    value = moved if value is None else jnp.where(lane < 16 * k, value, moved)
                values.append(value)
            send(FAR + part * GROUP + v * 8, *values)
    tables = (low_msg, TABLE), (cells, CELLS), (high_msg, TABLE)
    for i, (ref, row) in enumerate(tables):
        value = ref[row : row + 8, :]
        send(EDGE_TABLE + 8 * i, value, value)


def collided(h):
    shear = 1.0 / 0.6
    rest = h[0]
    sx, dx = h[1] + h[2], h[1] - h[2]
    sy, dy = h[3] + h[4], h[3] - h[4]
    sz, dz = h[5] + h[6], h[5] - h[6]
    s7, d7 = h[7] + h[8], h[7] - h[8]
    s9, d9 = h[9] + h[10], h[9] - h[10]
    s11, d11 = h[11] + h[12], h[11] - h[12]
    s13, d13 = h[13] + h[14], h[13] - h[14]
    s15, d15 = h[15] + h[16], h[15] - h[16]
    s17, d17 = h[17] + h[18], h[17] - h[18]
    txy, txz, tyz = s7 + s9, s11 + s13, s15 + s17
    pxy, pxz, pyz = s7 - s9, s11 - s13, s15 - s17
    ax, bx = d7 + d9, d11 + d13
    ay, by = d7 - d9, d15 + d17
    az, bz = d11 - d13, d15 - d17
    axes = sx + sy + sz
    diags = txy + txz + tyz
    rho = rest * (1.0 / 3.0) + axes * (1.0 / 18.0) + diags * (1.0 / 36.0)
    fx, fy, fz = ax + bx, ay + by, az + bz
    jx = dx * (1.0 / 18.0) + fx * (1.0 / 36.0)
    jy = dy * (1.0 / 18.0) + fy * (1.0 / 36.0)
    jz = dz * (1.0 / 18.0) + fz * (1.0 / 36.0)
    inverse = 1.0 / rho
    ux, uy, uz = jx * inverse, jy * inverse, jz * inverse
    qxx, qyy, qzz = jx * ux, jy * uy, jz * uz
    total = qxx + qyy + qzz

    energy = -10.0 * rest - axes * (11.0 / 18.0) + diags * (8.0 / 36.0)
    energy = (energy + 11.0 * rho - 19.0 * total) * (1.19 / 2394.0)
    square = 4.0 * rest - axes * (4.0 / 18.0) + diags * (1.0 / 36.0)
    square = (square - 3.0 * rho + 5.5 * total) * (1.4 / 252.0)
    axis_x = (3.0 * sx - axes) * (1.0 / 18.0)
    diag_x = (diags - 3.0 * tyz) * (1.0 / 36.0)
    want_x = 3.0 * qxx - total
    stress_x = (axis_x + diag_x - want_x) * (shear / 36.0)
    third_x = (diag_x - 2.0 * axis_x + 0.5 * want_x) * (1.4 / 72.0)
    axis_w = (sy - sz) * (1.0 / 18.0)
    diag_w = (txy - txz) * (1.0 / 36.0)
    want_w = qyy - qzz
    stress_w = (axis_w + diag_w - want_w) * (shear / 12.0)
    third_w = (diag_w - 2.0 * axis_w + 0.5 * want_w) * (1.4 / 24.0)

    rest_out = rest - 3.0 * (12.0 * square - 30.0 * energy)
    common = -18.0 * (11.0 * energy + 4.0 * square)
    along_x = 18.0 * (stress_x - 2.0 * third_x)
    along_w = 18.0 * (stress_w - 2.0 * third_w)
    ex = common + 2.0 * along_x
    ey = common - along_x + along_w
    ez = common - along_x - along_w
    common = 36.0 * (8.0 * energy + square)
    across_x = 36.0 * (stress_x + third_x)
    across_w = 36.0 * (stress_w + third_w)
    exy = common + across_x + across_w
    exz = common + across_x - across_w
    eyz = common - 2.0 * across_x
    cxy = shear * (0.25 * pxy - 9.0 * jx * uy)
    cxz = shear * (0.25 * pxz - 9.0 * jx * uz)
    cyz = shear * (0.25 * pyz - 9.0 * jy * uz)

    def flux(d, f, j):
        return (f * (1.0 / 36.0) - d * (4.0 / 18.0) + j * (2.0 / 3.0)) * (1.2 / 40.0)

    hx, hy, hz = flux(dx, fx, jx), flux(dy, fy, jy), flux(dz, fz, jz)
    mx = (ax - bx) * (1.98 / 8.0)
    my = (by - ay) * (1.98 / 8.0)
    mz = (az - bz) * (1.98 / 8.0)
    hx36, hy36, hz36 = 36.0 * hx, 36.0 * hy, 36.0 * hz
    xy_x, xz_x = hx36 + mx, hx36 - mx
    yz_y, xy_y = hy36 + my, hy36 - my
    xz_z, yz_z = hz36 + mz, hz36 - mz
    ox, oy, oz = -2.0 * hx36, -2.0 * hy36, -2.0 * hz36

    out = [rest_out]

    def pair(i, even, odd):
        out.append(h[i] - (even + odd))
        out.append(h[i + 1] - (even - odd))

    pair(1, ex, ox)
    pair(3, ey, oy)
    pair(5, ez, oz)
    pair(7, exy + cxy, xy_x + xy_y)
    pair(9, exy - cxy, xy_x - xy_y)
    pair(11, exz + cxz, xz_x + xz_z)
    pair(13, exz - cxz, xz_x - xz_z)
    pair(15, eyz + cyz, yz_y + yz_z)
    pair(17, eyz - cyz, yz_y - yz_z)
    return out


def collide_all(h_ref, flags, posts, parts=((0, 1), (2,))):
    for groups in parts:
        ref = posts[groups[0] // 2]
        size = len(groups) * GROUP

        @pl.loop(0, SLOTS)
        def _(s):
            @pl.loop(0, size // 8, unroll=3)
            def _(c):
                is_fluid = flags[groups[0] // 2][aligned((FLAG0 + s) * size + c * 8), :] > 0.0
                start = s * SLOT + groups[0] * GROUP + c * 8
                h_view = h_ref.at[aligned(start, (POPS - 1) * PLANE + 8), :]
                start = s * (POPS * size) + c * 8
                view = ref.at[aligned(start, (POPS - 1) * size + 8), :]
                h = [h_view[p * PLANE : p * PLANE + 8, :] for p in range(POPS)]
                for p, value in enumerate(collided(h)):
                    view[p * size : p * size + 8, :] = jnp.where(is_fluid, value, jnp.nan)


def hide_walls(ref, size):
    @pl.loop(0, SLOTS)
    def _(s):
        @pl.loop(0, size // 8)
        def _(c):
            is_fluid = ref[aligned((FLAG0 + s) * size + c * 8), :] > 0.0
            start = s * (POPS * size) + c * 8
            view = ref.at[aligned(start, (POPS - 1) * size + 8), :]
            for p in range(POPS):
                row = p * size
                view[row : row + 8, :] = jnp.where(is_fluid, view[row : row + 8, :], jnp.nan)


def stream_all(posts, h_ref, flags, table, groups, vregs, finish=None):
    lane = lanes_iota()
    row = rows_iota()
    low = lane < 64

    def one_slot(s):
        views = {}

        def view(which, key):
            if (which, key) not in views:
                start = s * (POPS * GROUP) if key == "own" else table[key[0] * 8 + s, key[1]]
                start = start if which else 2 * start
                views[which, key] = posts[which].at[
                    aligned(start, POPS * (GROUP if which else PAIR)), :
                ]
            return views[which, key]

        def load(key, pop, group, v):
            if group == 2:
                row = pop * GROUP + v * 8
            else:
                row = pop * PAIR + group * GROUP + v * 8
            return view(group // 2, key)[row : row + 8, :]

        h_view = h_ref.at[aligned(s * SLOT, SLOT), :]

        def shifted(pop, group, j, dy, dz):
            cx = VELOCITY[pop][0]

            def rows(key, v):
                return load(key, pop, group, v)

            def look(i, j, dx, v):
                if (dx, dy, dz) == (0, 0, 0):
                    return rows("own", v)
                if j is None:
                    return jnp.where(low, look(i, 1, dx, v), look(i, -1, dx, v))
                region = (i + 1) * 3 + j + 1
                return rows((region, VELOCITY.index((dx, dy, dz)) - 1), v)

            need_last = vregs == 3
            values = [look(0, j, 0, 0), look(0, j, 0, 1)]
            if need_last:
                if dy == 0 and dz == 0:
                    values.append(rows("own", 2))
                else:
                    values.append(jnp.where(row < 4, look(1, j, 0, 2), look(-1, j, 0, 2)))
            if cx == 0:
                return values
            turn = 1 if cx > 0 else 7
            rolled = [pltpu.roll(value, turn, axis=0) for value in values]
            if cx > 0:
                before = pltpu.roll(look(0, j, -1, 2), 1, axis=0)
                result = [
                    jnp.where(row == 0, before, rolled[0]),
                    jnp.where(row == 0, rolled[0], rolled[1]),
                ]
                if need_last:
                    edge = pltpu.roll(look(1, j, -1, 1), 1, axis=0)
                    result.append(jnp.where(row == 0, edge, rolled[2]))
                return result
            after = pltpu.roll(look(0, j, 1, 2), 7, axis=0)
            result = [
                jnp.where(row == 7, rolled[1], rolled[0]),
                jnp.where(row == 7, after, rolled[1]),
            ]
            if need_last:
                edge = pltpu.roll(look(-1, j, 1, 0), 7, axis=0)
                result.append(jnp.where(row == 7, edge, rolled[2]))
            return result

        for pop in range(POPS):
            cx, cy, cz = VELOCITY[pop]
            kept = {}

            def source(*key):
                if key not in kept:
                    kept[key] = shifted(pop, *key)
                return kept[key]

            def along_y(group, dz):
                values = source(group, None if group == 2 else 0, 0, dz)
                if cy == 0:
                    return values
                other = (group - cy) % 3
                if group != 2 and other != 2:
                    carried = source(other, 0, 0, dz)
                else:
                    carried = source(other, cy if group == 2 else 0, -cy, dz)
                mask = lane >= 112 if cy > 0 else lane < 16
                return [jnp.where(mask, b, a) for a, b in zip(values, carried)]

            for group in groups:
                values = along_y(group, 0)
                turn = (16 * cy + cz) % 128
                if turn:
                    values = [pltpu.roll(value, turn, axis=1) for value in values]
                if cz:
                    turn = (16 * cy - 15 * cz) % 128
                    wrapped = [pltpu.roll(value, turn, axis=1) for value in along_y(group, -cz)]
                    mask = lane % 16 == (0 if cz > 0 else 15)
                    values = [jnp.where(mask, b, a) for a, b in zip(values, wrapped)]
                for v, value in enumerate(values[:vregs]):
                    if pop:
                        value = jnp.where(value != value, load("own", OPPOSITE[pop], group, v), value)
                    if finish is not None:
                        is_fluid = flags[group // 2][
                            aligned((FLAG0 + s) * PAIR + group * GROUP + v * 8), :
                        ]
                        value = jnp.where(is_fluid > 0.0, value, 0.0)
                    target = pop * PLANE + group * GROUP + v * 8
                    h_view[target : target + 8, :] = value

    @pl.loop(0, SLOTS)
    def _(s):
        one_slot(s)
        if finish is not None:
            finish(s)


def join_kernel(
    cells,
    mate_msg,
    other_msg,
    mate2_msg,
    other2_msg,
    post_ref,
    slots,
    low_msg,
    high_msg,
    low2_msg,
    high2_msg,
):
    sort_messages(
        mate_msg, other_msg, mate2_msg, other2_msg, low_msg, high_msg, low2_msg, high2_msg
    )
    for i, (ref, row) in enumerate(((low_msg, TABLE), (cells, CELLS), (high_msg, TABLE))):
        slots[8 * i : 8 * i + 8, :] = first_rows(ref[row : row + 8, :])

    from_low, from_high, low_low, low_me, high_high, high_me = landed_slots(cells)
    post_ref[PLANES * PAIR :, :] = jnp.full((POPS * PAIR, 128), jnp.nan, jnp.float32)
    for q in range(PLANES):
        for y in range(2):
            start = q * PAIR + y * GROUP
            post_ref[start : start + EDGE, :] = cells[
                q * 32 + y * EDGE : q * 32 + (y + 1) * EDGE, :
            ]
    for s, (slot, msg) in itertools.product(
        range(SLOTS), ((from_low, low_msg), (from_high, high_msg))
    ):

        @pl.when(slot == s)
        def _():
            for p in range(POPS):
                for v in range(2):
                    rim = rim_of(msg, p, v)
                    row = (s * POPS + p) * PAIR + v * 8
                    post_ref[row : row + 8, :] = rim
                    post_ref[row + GROUP : row + GROUP + 8, :] = rim

    for msg, row0, step, first in ((high_msg, 16, 1, 2), (low_msg, 23, -1, 1)):
        for y in range(2):
            for count, planes, row, source in strip_rows(first, row0, step):
                source += y * LAYERS
                post_ref[planes(PAIR, row + y * GROUP), :] = msg[source : source + count, :]
    for s in range(SLOTS):
        for slot, msg, row0 in (
            (low_low, low2_msg, 21),
            (low_me, cells.at[OWN2:], 21),
            (high_high, high2_msg, 16),
            (high_me, cells.at[OWN2 + 6 * GROUP :], 16),
        ):

            @pl.when(slot == s)
            def _():
                for y in range(2):
                    for k in range(3):
                        row = s * POPS * PAIR + y * GROUP + row0 + k
                        source = (y * 3 + k) * GROUP
                        post_ref[pl.ds(row, POPS, stride=PAIR), :] = msg[source : source + POPS, :]
    hide_walls(post_ref, PAIR)


def first_rows(slot):
    slot = slot.astype(jnp.int32)
    return jnp.where(slot == SLOTS, NOWHERE, slot * (POPS * GROUP))


def outer_kernel(
    own_slots, first_post, near_msg, far_msg, slots, outer_ref, next_ref, h_ref, table, sem
):
    even = is_even("cross")

    def received(row):
        near, far = near_msg[row : row + 8, :], far_msg[row : row + 8, :]
        return jnp.where(even, far, near), jnp.where(even, near, far)

    for i in range(3):
        south, north = received(EDGE_TABLE + 8 * i)
        slots[24 * i : 24 * i + 8, :] = first_rows(south)
        slots[24 * i + 8 : 24 * i + 16, :] = own_slots[8 * i : 8 * i + 8, :]
        slots[24 * i + 16 : 24 * i + 24, :] = first_rows(north)
    table_copy = pltpu.make_async_copy(slots, table, sem)
    table_copy.start()

    nothing = jnp.full((8, 128), jnp.nan, jnp.float32)
    for row in range(0, POPS * GROUP, 8):
        outer_ref[NOWHERE + row : NOWHERE + row + 8, :] = nothing
        next_ref[NOWHERE + row : NOWHERE + row + 8, :] = nothing
    lane = lanes_iota()
    for v in range(3):

        def rows(q):
            return slice(q * GROUP + v * 8, q * GROUP + v * 8 + 8)

        for quad in range(QUADS):
            south, north = received(quad * GROUP + v * 8)
            for k in range(4):
                value = jnp.where(lane // 32 == (k + 3) % 4, south, north)
                if k:
                    value = pltpu.roll(value, 128 - 32 * k, axis=1)
                outer_ref[rows(4 * quad + k), :] = value
        for part in range(3):
            values = received(FAR + part * GROUP + v * 8)
            for planes, target, value in zip((NORTHWARD, SOUTHWARD), (80, 32), values):
                for k, q in enumerate(planes[8 * part : 8 * part + 8]):
                    moved = pltpu.roll(value, (target - 16 * k) % 128, axis=1)
                    outer_ref[rows(q), :] = jnp.where(
                        lane // 16 == target // 16, moved, outer_ref[rows(q), :]
                    )
    for row in range(FLAG0 * GROUP, NOWHERE, 8):
        next_ref[row : row + 8, :] = outer_ref[row : row + 8, :]
    hide_walls(outer_ref, GROUP)
    table_copy.wait()
    flags = (first_post, outer_ref)
    stream_all(flags, h_ref, flags, table, (2,), 3)
    collide_all(h_ref, flags, (None, next_ref), ((2,),))


def steps_kernel(
    slots,
    first_post,
    first_outer,
    next_outer,
    cells,
    mate_msg,
    other_msg,
    mate_rest,
    passed_rest,
    out_hbm,
    h_ref,
    post_ref,
    outer_ref,
    out,
    table,
    sems,
):
    table_copy = pltpu.make_async_copy(slots, table, sems.at[SLOTS])
    table_copy.start()
    post_ref[...] = first_post[...]
    nothing = jnp.full((8, 128), jnp.nan, jnp.float32)
    for row in range(0, POPS * GROUP, 8):
        outer_ref[NOWHERE + row : NOWHERE + row + 8, :] = nothing

    from_low, from_high = landed_slots(cells)[:2]
    lane = lanes_iota()
    even = is_even("curve")
    odd = jnp.logical_not(even)
    for s, (slot, wanted, msg, rest) in itertools.product(
        range(SLOTS),
        (
            (from_low, odd, mate_msg, mate_rest),
            (from_low, even, other_msg, passed_rest),
            (from_high, even, mate_msg, mate_rest),
            (from_high, odd, other_msg, passed_rest),
        ),
    ):

        @pl.when((slot == s) & wanted)
        def _():
            for v in range(2):
                starts = [(FLAG0 + s) * PAIR + y * GROUP + v * 8 for y in range(2)]
                fluid = [first_post[row : row + 8, :] > 0.0 for row in starts]
                for p in range(POPS):
                    rim = rim_of(msg, p, v)
                    row = p * EDGE + v * 8
                    wide = rest[row : row + 8, :]
                    row = (POPS + p // 2) * EDGE + v * 8
                    middle = rest[row : row + 8, :]
                    if p % 2:
                        middle = pltpu.roll(middle, 64, axis=1)
                    first = jnp.where(lane < 32, rim, wide)
                    second = jnp.where(lane < 32, wide, jnp.where(lane < 96, middle, rim))
                    row = (s * POPS + p) * PAIR + v * 8
                    post_ref[row : row + 8, :] = jnp.where(fluid[0], first, jnp.nan)
                    row += GROUP
                    post_ref[row : row + 8, :] = jnp.where(fluid[1], second, jnp.nan)

    def finish(s):
        for x in range(EDGE):
            for y in range(2):
                tile = 2 * x + y
                for p, size in ((0, 8), (8, 8), (16, 3)):
                    row = s * SLOT + (p * PLANE + y * GROUP + x)
                    out[s, p : p + size, 128 * tile : 128 * tile + 128] = h_ref[
                        pl.ds(row, size, stride=PLANE), :
                    ]
        pltpu.make_async_copy(out.at[s], out_hbm.at[s], sems.at[s]).start()

    table_copy.wait()
    flags = (first_post, first_outer)
    stream_all((post_ref, first_outer), h_ref, flags, table, (0, 1), 3)
    collide_all(h_ref, flags, (post_ref, None), ((0, 1),))
    posts = (post_ref, next_outer)
    for _ in range(STEPS - 2):
        stream_all(posts, h_ref, flags, table, (0, 1, 2), 3)
        posts = (post_ref, outer_ref)
        collide_all(h_ref, flags, posts)
    stream_all(posts, h_ref, flags, table, (0, 1), 2, finish)
    for s in range(SLOTS):
        pltpu.make_async_copy(out.at[s], out_hbm.at[s], sems.at[s]).wait()


def swapped(value, axis, unit=1):
    count = lax.axis_size(axis)
    results = []
    for which in (0, 1):
        others = [i + (unit if i // unit % 2 == which else -unit) for i in range(count)]
        pairs = [(i, j if 0 <= j < count else i) for i, j in enumerate(others)]
        results.append(lax.ppermute(value[which], axis, pairs))
    return results


def rows128(count):
    return jax.ShapeDtypeStruct((count, 128), jnp.float32)


def call(kernel, in_spaces, out_spaces, outs, ins, scratch, limit=LIMIT, cost=None):
    spaces = {
        "S": pl.BlockSpec(memory_space=pltpu.SMEM),
        "V": pl.BlockSpec(memory_space=pltpu.VMEM),
        "H": pl.BlockSpec(memory_space=pltpu.HBM),
    }
    return pl.pallas_call(
        kernel,
        out_shape=outs,
        in_specs=[spaces[x] for x in in_spaces],
        out_specs=[spaces[x] for x in out_spaces],
        scratch_shapes=scratch,
        compiler_params=pltpu.CompilerParams(vmem_limit_bytes=limit),
        cost_estimate=cost,
    )(*ins)


def per_device(populations, site_flags, neighbours, migrations, counts):
    sizes = (lax.axis_size("curve"), lax.axis_size("cross"))
    moves = migrations.T
    floats = lambda rows: pltpu.VMEM((rows, 128), jnp.float32)
    messages = [
        OWN2 + 12 * GROUP,
        STRIPS + 2 * LAYERS,
        STRIPS + 2 * LAYERS,
        6 * GROUP,
        6 * GROUP,
        REST,
    ]
    cells, mate_msg, other_msg, mate2_msg, other2_msg, rest_msg = call(
        functools.partial(pack_kernel, *sizes),
        "HHHHH",
        "HHHHHH",
        [rows128(rows) for rows in messages],
        (moves, counts, populations, site_flags, neighbours),
        [
            pltpu.SMEM(moves.shape, jnp.int32),
            pltpu.SMEM(counts.shape, jnp.int32),
            pltpu.VMEM(populations.shape, jnp.float32),
            pltpu.VMEM(site_flags.shape, jnp.int32),
            pltpu.VMEM(neighbours.shape, jnp.int32),
            *[floats(rows) for rows in messages],
            pltpu.VMEM((8, 5888), jnp.float32),
            pltpu.VMEM((128, 384), jnp.bfloat16),
            floats(256),
            floats(8),
            pltpu.SemaphoreType.DMA((4 + SLOTS + 8,)),
        ],
        WIDE_LIMIT,
    )
    mate_msg, other_msg = swapped((mate_msg, other_msg), "curve")
    mate2_msg, other2_msg = swapped((mate2_msg, other2_msg), "curve", 2)
    assert sizes[0] % 2 == 0
    pairs = [(i, i ^ 1) for i in range(sizes[0])]
    mate_rest = lax.ppermute(rest_msg, "curve", pairs)
    last = sizes[0] - 1
    pairs = [(i, max(i - 2, 0) if i % 2 else min(i + 2, last)) for i in range(sizes[0])]
    passed_rest = lax.ppermute(mate_rest, "curve", pairs)
    (outer,) = call(spread_kernel, "V", "V", [rows128(PLANES * GROUP)], (cells,), [])
    strips = (cells, mate_msg, other_msg, mate2_msg, other2_msg)
    sorted_rows = [messages[1], messages[1], messages[3], messages[3]]
    near_msg, far_msg = call(
        edge_kernel,
        "VVVVVV",
        "VV",
        [rows128(NEAR_ROWS), rows128(FAR_ROWS)],
        (outer, *strips),
        [floats(rows) for rows in [PLANES * GROUP] + sorted_rows],
        cost=pl.CostEstimate(flops=10**10, bytes_accessed=0, transcendentals=0),
    )
    near_msg, far_msg = swapped((near_msg, far_msg), "cross")
    post, own_slots = call(
        join_kernel,
        "VVVVV",
        "VV",
        [rows128(ALL_PLANES * PAIR), jax.ShapeDtypeStruct((24, 128), jnp.int32)],
        strips,
        [floats(rows) for rows in sorted_rows],
    )
    slots, outer_post, next_outer = call(
        outer_kernel,
        "VVVV",
        "VVV",
        [
            jax.ShapeDtypeStruct((72, 128), jnp.int32),
            rows128(ALL_PLANES * GROUP),
            rows128(ALL_PLANES * GROUP),
        ],
        (own_slots, post, near_msg, far_msg),
        [floats(SLOTS * SLOT), pltpu.SMEM((72, 128), jnp.int32), pltpu.SemaphoreType.DMA],
    )
    arriving = (cells, mate_msg, other_msg, mate_rest, passed_rest)
    return call(
        steps_kernel,
        "VVVVVVVVV",
        "H",
        [jax.ShapeDtypeStruct(populations.shape, jnp.float32)],
        (slots, post, outer_post, next_outer, *arriving),
        [
            floats(SLOTS * SLOT),
            floats(ALL_PLANES * PAIR),
            floats(ALL_PLANES * GROUP),
            pltpu.VMEM(populations.shape, jnp.float32),
            pltpu.SMEM((72, 128), jnp.int32),
            pltpu.SemaphoreType.DMA((SLOTS + 1,)),
        ],
    )[0]


def solution(mesh):
    return jax.shard_map(
        per_device,
        mesh=mesh,
        in_specs=(
            P(("curve", "cross"), None, None),
            P(("curve", "cross"), None),
            P(("curve", "cross"), None),
            P(),
            P(("curve", "cross")),
        ),
        out_specs=P(("curve", "cross"), None, None),
        check_vma=False,
    )
```

```python
import functools
import itertools

import jax
import jax.numpy as jnp
import numpy as np
from jax import lax
from jax.experimental import pallas as pl
from jax.experimental.pallas import tpu as pltpu
from jax.sharding import PartitionSpec as P

EDGE = 16
STEPS = 3
SLOTS = 3
POPS = 19
PLANES = SLOTS * POPS + SLOTS
FLAG0 = SLOTS * POPS
GROUP = 24
PLANE = 3 * GROUP
SLOT = POPS * PLANE
CELLS = PLANES * 32
LANDINGS = CELLS + 8
OWN2 = LANDINGS + 8
OUTWARD = SLOTS * 5 + SLOTS
LAYERS = 2 * PLANES + OUTWARD
RIM = 11 * EDGE
REST = POPS * EDGE + 10 * EDGE
HALF = REST // 2
PAIR = 2 * GROUP
QUADS = PLANES // 4
TABLE = RIM
STRIPS = RIM + 8
FAR = QUADS * GROUP
EDGE_TABLE = FAR + 3 * GROUP
EDGE_ROWS = EDGE_TABLE + 24
NEAR_ROWS, FAR_ROWS = EDGE_ROWS + 16, EDGE_ROWS + 24
NOWHERE = PLANES * GROUP
ALL_PLANES = PLANES + POPS
LIMIT = 20 * 1024 * 1024
WIDE_LIMIT = 127 * 512 * 1024

VELOCITY = [
    (0, 0, 0),
    (1, 0, 0),
    (-1, 0, 0),
    (0, 1, 0),
    (0, -1, 0),
    (0, 0, 1),
    (0, 0, -1),
    (1, 1, 0),
    (-1, -1, 0),
    (1, -1, 0),
    (-1, 1, 0),
    (1, 0, 1),
    (-1, 0, -1),
    (1, 0, -1),
    (-1, 0, 1),
    (0, 1, 1),
    (0, -1, -1),
    (0, 1, -1),
    (0, -1, 1),
]
NORTHWARD, SOUTHWARD = (
    [s * POPS + p for s in range(SLOTS) for p in range(POPS) if VELOCITY[p][1] == side]
    + [FLAG0 + s for s in range(SLOTS)]
    for side in (1, -1)
)
THIRD = [
    (pop, source, *((32 + 16 * k, 9) if k < 4 else (16 * (k - 4), 10)))
    for k, (pop, source) in enumerate(
        [(p, 32) for p in (4, 8, 9, 16, 18)] + [(p, 80) for p in (3, 7, 10, 15, 17)]
    )
]
OPPOSITE = [0, 2, 1, 4, 3, 6, 5, 8, 7, 10, 9, 12, 11, 14, 13, 16, 15, 18, 17]


def lanes_iota():
    return lax.broadcasted_iota(jnp.int32, (8, 128), 1)


def is_even(axis, unit=1):
    return lax.rem(lax.axis_index(axis) // unit, 2) == 0


def rows_iota():
    return lax.broadcasted_iota(jnp.int32, (8, 128), 0)


def aligned(start, size=8):
    return pl.ds(pl.multiple_of(start, 8), size)


def move_slots(moves, curve_size, cross_size):
    curve, cross = lax.axis_index("curve"), lax.axis_index("cross")

    def landed(source, target):
        inside = (source >= 0) & (source < curve_size) & (target >= 0) & (target < curve_size)
        row = jnp.clip(source, 0, curve_size - 1) * cross_size + cross
        rank = target * cross_size + cross
        hit = inside & (moves[0, row] >= 0) & (moves[1, row] == rank)
        return jnp.where(hit, moves[2, row], -1)

    return (
        landed(curve - 1, curve),
        landed(curve + 1, curve),
        landed(curve - 2, curve - 1),
        landed(curve, curve - 1),
        landed(curve + 2, curve + 1),
        landed(curve, curve + 1),
    )


def pack_kernel(
    curve_size,
    cross_size,
    moves_hbm,
    counts_hbm,
    pops_hbm,
    flags_hbm,
    neighbours_hbm,
    cells_hbm,
    mate_hbm,
    other_hbm,
    mate2_hbm,
    other2_hbm,
    rest_hbm,
    rest2_hbm,
    moves,
    counts,
    pops,
    flags,
    neighbours,
    cells,
    up_msg,
    down_msg,
    up2_msg,
    down2_msg,
    rest_msg,
    wide_flags,
    plane_flags,
    site_flags,
    near,
    sems,
):
    started = []

    def copy(source, target):
        one = pltpu.make_async_copy(source, target, sems.at[len(started)])
        one.start()
        started.append(one)
        return one

    flags_copy = copy(flags_hbm, flags)
    copies = [copy(pops_hbm.at[s], pops.at[s]) for s in range(SLOTS)]
    small = [
        copy(neighbours_hbm, neighbours),
        copy(counts_hbm, counts),
        copy(moves_hbm, moves),
    ]
    for one in small:
        one.wait()

    near[...] = jnp.zeros_like(near)
    named = neighbours[...]
    slot = jnp.where(named >= 0, lax.rem(jnp.maximum(named, 0), SLOTS), SLOTS)
    near[0:SLOTS, 0 : named.shape[1]] = slot.astype(jnp.float32)
    for ref, row in ((cells, CELLS), (up_msg, TABLE), (down_msg, TABLE)):
        ref[row : row + 8, :] = near[...]

    wide_flags[...] = jnp.zeros_like(wide_flags)
    flags_copy.wait()
    wide_flags[0:SLOTS, 0 : flags.shape[1]] = flags[...].astype(jnp.float32)
    span = EDGE + 2
    for x in range(EDGE):
        start = (x + 1) * span * span
        base = start // 128 * 128
        window = wide_flags[:, base : base + 512]
        window = pltpu.roll(window, (512 - (start - base)) % 512, axis=1)
        plane_flags[8 * x : 8 * x + 8, :] = window[:, :384].astype(jnp.bfloat16)
    lane_in = lax.broadcasted_iota(jnp.int32, (384, 256), 0)
    site = lax.broadcasted_iota(jnp.int32, (384, 256), 1)
    chosen = lane_in == (site // EDGE + 1) * span + site % EDGE + 1
    product = jnp.dot(
        plane_flags[...],
        jnp.where(chosen, 1.0, 0.0).astype(jnp.bfloat16),
        preferred_element_type=jnp.float32,
    )
    site_flags[0:128, :] = product[:, :128]
    site_flags[128:256, :] = product[:, 128:]
    for s in range(SLOTS):
        live = s < counts[0]
        for y in range(2):
            piece = site_flags[pl.ds(128 * y + s, EDGE, stride=8), :]
            is_fluid = (piece == 1.0) & live
            row = (FLAG0 + s) * 32 + y * EDGE
            cells[row : row + EDGE, :] = jnp.where(is_fluid, 1.0, 0.0)

    for s in range(SLOTS):
        copies[s].wait()
        for x in range(EDGE):
            for y in range(2):
                tile = 2 * x + y
                for p, size in ((0, 8), (8, 8), (16, 3)):
                    row = (s * POPS + p) * 32 + y * EDGE + x
                    cells[pl.ds(row, size, stride=32), :] = pops[
                        s, p : p + size, 128 * tile : 128 * tile + 128
                    ]

    @pl.loop(0, SLOTS)
    def _(s):
        @pl.loop(0, 4, unroll=2)
        def _(c):
            base = s * (POPS * 32) + c * 8
            view = cells.at[aligned(base, (POPS - 1) * 32 + 8), :]
            h = [view[p * 32 : p * 32 + 8, :] for p in range(POPS)]
            for p, value in enumerate(collided(h)):
                view[p * 32 : p * 32 + 8, :] = value

    for i, slot in enumerate(move_slots(moves, curve_size, cross_size)):
        value = jnp.full((1, 128), slot, jnp.int32)
        cells[LANDINGS + i : LANDINGS + i + 1, :] = value.astype(jnp.float32)

    body_copy = copy(cells.at[:OWN2], cells_hbm.at[:OWN2])

    for y in range(2):
        for msg, x0, first in ((up_msg, 15, 1), (down_msg, 0, 2)):
            step = -1 if x0 else 1
            for k in range(2):
                out = STRIPS + y * LAYERS + k * PLANES
                msg[out : out + PLANES, :] = cells[
                    pl.ds(y * EDGE + x0 + step * k, PLANES, stride=32), :
                ]
            row = y * EDGE + x0 + 2 * step
            out = STRIPS + y * LAYERS + 2 * PLANES
            for s in range(SLOTS):
                base = s * POPS * 32 + row
                msg[out + 5 * s : out + 5 * s + 1, :] = cells[pl.ds(base + first * 32, 1), :]
                msg[out + 5 * s + 1 : out + 5 * s + 5, :] = cells[
                    pl.ds(base + (first + 6) * 32, 4, stride=64), :
                ]
            msg[out + 5 * SLOTS : out + OUTWARD, :] = cells[
                pl.ds(FLAG0 * 32 + row, SLOTS, stride=32), :
            ]

    here = lax.axis_index("curve") * cross_size + lax.axis_index("cross")
    leaving = jnp.maximum(moves[0, here], 0)
    lane = lanes_iota()
    for v in range(2):
        halves = [
            [cells[aligned(leaving * (POPS * 32) + p * 32 + y * EDGE + v * 8), :] for y in (0, 1)]
            for p in range(POPS)
        ]
        outer = [jnp.where(lane < 64, first, second) for first, second in halves]
        middle = (lane >= 32) & (lane < 96)
        sets = [
            jnp.where(middle, pltpu.roll(outer[p + 1], 64, axis=1), outer[p])
            for p in range(0, POPS - 1, 2)
        ]
        sets += [outer[POPS - 1], jnp.zeros_like(outer[0])]
        for pop, source, target, which in THIRD:
            moved = pltpu.roll(outer[pop], (target - source) % 128, axis=1)
            sets[which] = jnp.where(lane // 16 == target // 16, moved, sets[which])
        for k, value in enumerate(sets):
            row = k * EDGE + v * 8
            up_msg[row : row + 8, :] = value
            down_msg[row : row + 8, :] = value
        for p, (first, second) in enumerate(halves):
            row = p * EDGE + v * 8
            rest_msg[row : row + 8, :] = jnp.where(lane < 32, second, first)
        for p in range(0, POPS, 2):
            value = halves[p][1]
            if p + 1 < POPS:
                value = jnp.where(middle, value, pltpu.roll(halves[p + 1][1], 64, axis=1))
            row = (POPS + p // 2) * EDGE + v * 8
            rest_msg[row : row + 8, :] = value
    for s in range(SLOTS):

        @pl.when(leaving == s)
        def _():
            for y in range(2):
                for k in range(3):
                    out = (y * 3 + k) * GROUP
                    row = s * POPS * 32 + y * EDGE + k
                    up2_msg[out : out + POPS, :] = cells[pl.ds(row + 13, POPS, stride=32), :]
                    down2_msg[out : out + POPS, :] = cells[pl.ds(row, POPS, stride=32), :]

    cells[OWN2 : OWN2 + 6 * GROUP, :] = up2_msg[...]
    cells[OWN2 + 6 * GROUP :, :] = down2_msg[...]
    last = [copy(cells.at[OWN2:], cells_hbm.at[OWN2:]), copy(rest_msg, rest_hbm)]
    last.append(copy(rest_msg.at[HALF:], rest2_hbm))
    count = len(started)
    for i, (up, down, mate, other, unit) in enumerate(
        ((up_msg, down_msg, mate_hbm, other_hbm, 1), (up2_msg, down2_msg, mate2_hbm, other2_hbm, 2))
    ):
        first, second = sems.at[count + 2 * i], sems.at[count + 2 * i + 1]
        even = is_even("curve", unit)

        @pl.when(even)
        def _():
            pltpu.make_async_copy(up, mate, first).start()
            pltpu.make_async_copy(down, other, second).start()

        @pl.when(jnp.logical_not(even))
        def _():
            pltpu.make_async_copy(down, mate, first).start()
            pltpu.make_async_copy(up, other, second).start()

        last.append(pltpu.make_async_copy(up, mate, first))
        last.append(pltpu.make_async_copy(down, other, second))
    body_copy.wait()
    for one in last:
        one.wait()


def spread_kernel(cells, outer):
    low = lanes_iota() < 64
    for q in range(PLANES):
        for v in range(2):
            row = q * 32 + v * 8
            first, second = cells[row : row + 8, :], cells[row + EDGE : row + EDGE + 8, :]
            row = q * GROUP + v * 8
            outer[row : row + 8, :] = jnp.where(low, first, second)


def sort_messages(mate_msg, other_msg, mate2_msg, other2_msg, low_msg, high_msg, low2, high2):
    for mate, other, low, high, unit in (
        (mate_msg, other_msg, low_msg, high_msg, 1),
        (mate2_msg, other2_msg, low2, high2, 2),
    ):
        even = is_even("curve", unit)

        @pl.when(even)
        def _():
            low[...] = other[...]
            high[...] = mate[...]

        @pl.when(jnp.logical_not(even))
        def _():
            low[...] = mate[...]
            high[...] = other[...]


def landed_slots(cells):
    return [jnp.max(cells[LANDINGS + i : LANDINGS + i + 1, :]) for i in range(6)]


def rim_of(msg, p, v):
    row = p // 2 * EDGE + v * 8
    value = msg[row : row + 8, :]
    return pltpu.roll(value, 64, axis=1) if p % 2 else value


def sel4(parts, lane):
    first = jnp.where(lane < 32, parts[0], parts[1])
    second = jnp.where(lane < 96, parts[2], parts[3])
    return jnp.where(lane < 64, first, second)


def strip_rows(first, row0, step):
    pieces = []
    for k in range(2):
        pieces.append(
            (PLANES, lambda size, row: pl.ds(row, PLANES, stride=size), row0 + step * k, STRIPS + k * PLANES)
        )
    row, source = row0 + 2 * step, STRIPS + 2 * PLANES
    for s in range(SLOTS):
        plane = s * POPS + first
        pieces.append((1, lambda size, row, plane=plane: pl.ds(plane * size + row, 1), row, source))
        pieces.append(
            (
                4,
                lambda size, row, plane=plane: pl.ds(
                    (plane + 6) * size + row, 4, stride=2 * size
                ),
                row,
                source + 1,
            )
        )
        source += 5
    pieces.append(
        (SLOTS, lambda size, row: pl.ds(FLAG0 * size + row, SLOTS, stride=size), row, source)
    )
    return pieces


def edge_kernel(
    own_outer,
    cells,
    mate_msg,
    other_msg,
    mate2_msg,
    other2_msg,
    along_z,
    near_msg,
    far_msg,
    outer,
    low_msg,
    high_msg,
    low2_msg,
    high2_msg,
):
    sort_messages(
        mate_msg, other_msg, mate2_msg, other2_msg, low_msg, high_msg, low2_msg, high2_msg
    )
    from_low, from_high, low_low, low_me, high_high, high_me = landed_slots(cells)
    low = lanes_iota() < 64
    for q in range(PLANES):
        for v in range(2):
            row = q * GROUP + v * 8
            outer[row : row + 8, :] = own_outer[row : row + 8, :]

    def both(first, second):
        lane = lax.broadcasted_iota(jnp.int32, first.shape, 1)
        return jnp.where(lane < 64, first, second)

    for msg, row0, step, first in ((high_msg, 16, 1, 2), (low_msg, 23, -1, 1)):
        for count, planes, row, source in strip_rows(first, row0, step):
            outer[planes(GROUP, row), :] = both(
                msg[source : source + count, :],
                msg[LAYERS + source : LAYERS + source + count, :],
            )
    lane = lanes_iota()
    for s, (slot, msg) in itertools.product(
        range(SLOTS), ((from_low, low_msg), (from_high, high_msg))
    ):

        @pl.when(slot == s)
        def _():
            for v in range(2):
                values = [rim_of(msg, p, v) for p in range(POPS)]
                for pop, target, source, which in THIRD:
                    row = which * EDGE + v * 8
                    moved = pltpu.roll(msg[row : row + 8, :], (target - source) % 128, axis=1)
                    values[pop] = jnp.where(lane // 16 == target // 16, moved, values[pop])
                for p, value in enumerate(values):
                    row = (s * POPS + p) * GROUP + v * 8
                    outer[row : row + 8, :] = value

    for s in range(SLOTS):
        for slot, msg, row0 in (
            (low_low, low2_msg, 21),
            (low_me, cells.at[OWN2:], 21),
            (high_high, high2_msg, 16),
            (high_me, cells.at[OWN2 + 6 * GROUP :], 16),
        ):

            @pl.when(slot == s)
            def _():
                for k in range(3):
                    outer[pl.ds(s * POPS * GROUP + row0 + k, POPS, stride=GROUP), :] = both(
                        msg[k * GROUP : k * GROUP + POPS, :],
                        msg[(3 + k) * GROUP : (3 + k) * GROUP + POPS, :],
                    )

    even = is_even("cross")

    def send(row, north, south):
        near_msg[row : row + 8, :] = jnp.where(even, north, south)
        far_msg[row : row + 8, :] = jnp.where(even, south, north)

    for v in range(3):

        def plane(q):
            return outer[q * GROUP + v * 8 : q * GROUP + v * 8 + 8, :]

        for quad in range(QUADS):
            parts = [plane(4 * quad)]
            parts += [pltpu.roll(plane(4 * quad + k), 32 * k, axis=1) for k in (1, 2, 3)]
            send(quad * GROUP + v * 8, sel4(parts[1:] + parts[:1], lane), sel4(parts, lane))
        for part in range(3):
            values = []
            for planes, source in ((NORTHWARD, 80), (SOUTHWARD, 32)):
                value = None
                for k, q in enumerate(planes[8 * part : 8 * part + 8]):
                    moved = pltpu.roll(plane(q), (16 * k - source) % 128, axis=1)
                    value = moved if value is None else jnp.where(lane < 16 * k, value, moved)
                values.append(value)
            send(FAR + part * GROUP + v * 8, *values)
    tables = (low_msg, TABLE), (cells, CELLS), (high_msg, TABLE)
    for i, (ref, row) in enumerate(tables):
        value = ref[row : row + 8, :]
        send(EDGE_TABLE + 8 * i, value, value)


def collided(h):
    shear = 1.0 / 0.6
    rest = h[0]
    sx, dx = h[1] + h[2], h[1] - h[2]
    sy, dy = h[3] + h[4], h[3] - h[4]
    sz, dz = h[5] + h[6], h[5] - h[6]
    s7, d7 = h[7] + h[8], h[7] - h[8]
    s9, d9 = h[9] + h[10], h[9] - h[10]
    s11, d11 = h[11] + h[12], h[11] - h[12]
    s13, d13 = h[13] + h[14], h[13] - h[14]
    s15, d15 = h[15] + h[16], h[15] - h[16]
    s17, d17 = h[17] + h[18], h[17] - h[18]
    txy, txz, tyz = s7 + s9, s11 + s13, s15 + s17
    pxy, pxz, pyz = s7 - s9, s11 - s13, s15 - s17
    ax, bx = d7 + d9, d11 + d13
    ay, by = d7 - d9, d15 + d17
    az, bz = d11 - d13, d15 - d17
    axes = sx + sy + sz
    diags = txy + txz + tyz
    rho = rest * (1.0 / 3.0) + axes * (1.0 / 18.0) + diags * (1.0 / 36.0)
    fx, fy, fz = ax + bx, ay + by, az + bz
    jx = dx * (1.0 / 18.0) + fx * (1.0 / 36.0)
    jy = dy * (1.0 / 18.0) + fy * (1.0 / 36.0)
    jz = dz * (1.0 / 18.0) + fz * (1.0 / 36.0)
    inverse = 1.0 / rho
    ux, uy, uz = jx * inverse, jy * inverse, jz * inverse
    qxx, qyy, qzz = jx * ux, jy * uy, jz * uz
    total = qxx + qyy + qzz

    energy = -10.0 * rest - axes * (11.0 / 18.0) + diags * (8.0 / 36.0)
    energy = (energy + 11.0 * rho - 19.0 * total) * (1.19 / 2394.0)
    square = 4.0 * rest - axes * (4.0 / 18.0) + diags * (1.0 / 36.0)
    square = (square - 3.0 * rho + 5.5 * total) * (1.4 / 252.0)
    axis_x = (3.0 * sx - axes) * (1.0 / 18.0)
    diag_x = (diags - 3.0 * tyz) * (1.0 / 36.0)
    want_x = 3.0 * qxx - total
    stress_x = (axis_x + diag_x - want_x) * (shear / 36.0)
    third_x = (diag_x - 2.0 * axis_x + 0.5 * want_x) * (1.4 / 72.0)
    axis_w = (sy - sz) * (1.0 / 18.0)
    diag_w = (txy - txz) * (1.0 / 36.0)
    want_w = qyy - qzz
    stress_w = (axis_w + diag_w - want_w) * (shear / 12.0)
    third_w = (diag_w - 2.0 * axis_w + 0.5 * want_w) * (1.4 / 24.0)

    rest_out = rest - 3.0 * (12.0 * square - 30.0 * energy)
    common = -18.0 * (11.0 * energy + 4.0 * square)
    along_x = 18.0 * (stress_x - 2.0 * third_x)
    along_w = 18.0 * (stress_w - 2.0 * third_w)
    ex = common + 2.0 * along_x
    ey = common - along_x + along_w
    ez = common - along_x - along_w
    common = 36.0 * (8.0 * energy + square)
    across_x = 36.0 * (stress_x + third_x)
    across_w = 36.0 * (stress_w + third_w)
    exy = common + across_x + across_w
    exz = common + across_x - across_w
    eyz = common - 2.0 * across_x
    cxy = shear * (0.25 * pxy - 9.0 * jx * uy)
    cxz = shear * (0.25 * pxz - 9.0 * jx * uz)
    cyz = shear * (0.25 * pyz - 9.0 * jy * uz)

    def flux(d, f, j):
        return (f * (1.0 / 36.0) - d * (4.0 / 18.0) + j * (2.0 / 3.0)) * (1.2 / 40.0)

    hx, hy, hz = flux(dx, fx, jx), flux(dy, fy, jy), flux(dz, fz, jz)
    mx = (ax - bx) * (1.98 / 8.0)
    my = (by - ay) * (1.98 / 8.0)
    mz = (az - bz) * (1.98 / 8.0)
    hx36, hy36, hz36 = 36.0 * hx, 36.0 * hy, 36.0 * hz
    xy_x, xz_x = hx36 + mx, hx36 - mx
    yz_y, xy_y = hy36 + my, hy36 - my
    xz_z, yz_z = hz36 + mz, hz36 - mz
    ox, oy, oz = -2.0 * hx36, -2.0 * hy36, -2.0 * hz36

    out = [rest_out]

    def pair(i, even, odd):
        out.append(h[i] - (even + odd))
        out.append(h[i + 1] - (even - odd))

    pair(1, ex, ox)
    pair(3, ey, oy)
    pair(5, ez, oz)
    pair(7, exy + cxy, xy_x + xy_y)
    pair(9, exy - cxy, xy_x - xy_y)
    pair(11, exz + cxz, xz_x + xz_z)
    pair(13, exz - cxz, xz_x - xz_z)
    pair(15, eyz + cyz, yz_y + yz_z)
    pair(17, eyz - cyz, yz_y - yz_z)
    return out


def collide_all(h_ref, flags, posts, parts=((0, 1), (2,))):
    for groups in parts:
        ref = posts[groups[0] // 2]
        size = len(groups) * GROUP

        @pl.loop(0, SLOTS)
        def _(s):
            @pl.loop(0, size // 8, unroll=3)
            def _(c):
                is_fluid = flags[groups[0] // 2][aligned((FLAG0 + s) * size + c * 8), :] > 0.0
                start = s * SLOT + groups[0] * GROUP + c * 8
                h_view = h_ref.at[aligned(start, (POPS - 1) * PLANE + 8), :]
                start = s * (POPS * size) + c * 8
                view = ref.at[aligned(start, (POPS - 1) * size + 8), :]
                h = [h_view[p * PLANE : p * PLANE + 8, :] for p in range(POPS)]
                for p, value in enumerate(collided(h)):
                    view[p * size : p * size + 8, :] = jnp.where(is_fluid, value, jnp.nan)


def hide_walls(ref, size):
    @pl.loop(0, SLOTS)
    def _(s):
        @pl.loop(0, size // 8)
        def _(c):
            is_fluid = ref[aligned((FLAG0 + s) * size + c * 8), :] > 0.0
            start = s * (POPS * size) + c * 8
            view = ref.at[aligned(start, (POPS - 1) * size + 8), :]
            for p in range(POPS):
                row = p * size
                view[row : row + 8, :] = jnp.where(is_fluid, view[row : row + 8, :], jnp.nan)


def stream_all(posts, h_ref, flags, table, groups, vregs, finish=None):
    lane = lanes_iota()
    row = rows_iota()
    low = lane < 64

    def one_slot(s):
        views = {}

        def view(which, key):
            if (which, key) not in views:
                start = s * (POPS * GROUP) if key == "own" else table[key[0] * 8 + s, key[1]]
                start = start if which else 2 * start
                views[which, key] = posts[which].at[
                    aligned(start, POPS * (GROUP if which else PAIR)), :
                ]
            return views[which, key]

        def load(key, pop, group, v):
            if group == 2:
                row = pop * GROUP + v * 8
            else:
                row = pop * PAIR + group * GROUP + v * 8
            return view(group // 2, key)[row : row + 8, :]

        h_view = h_ref.at[aligned(s * SLOT, SLOT), :]

        def shifted(pop, group, j, dy, dz):
            cx = VELOCITY[pop][0]

            def rows(key, v):
                return load(key, pop, group, v)

            def look(i, j, dx, v):
                if (dx, dy, dz) == (0, 0, 0):
                    return rows("own", v)
                if j is None:
                    return jnp.where(low, look(i, 1, dx, v), look(i, -1, dx, v))
                region = (i + 1) * 3 + j + 1
                return rows((region, VELOCITY.index((dx, dy, dz)) - 1), v)

            need_last = vregs == 3
            values = [look(0, j, 0, 0), look(0, j, 0, 1)]
            if need_last:
                if dy == 0 and dz == 0:
                    values.append(rows("own", 2))
                else:
                    values.append(jnp.where(row < 4, look(1, j, 0, 2), look(-1, j, 0, 2)))
            if cx == 0:
                return values
            turn = 1 if cx > 0 else 7
            rolled = [pltpu.roll(value, turn, axis=0) for value in values]
            if cx > 0:
                before = pltpu.roll(look(0, j, -1, 2), 1, axis=0)
                result = [
                    jnp.where(row == 0, before, rolled[0]),
                    jnp.where(row == 0, rolled[0], rolled[1]),
                ]
                if need_last:
                    edge = pltpu.roll(look(1, j, -1, 1), 1, axis=0)
                    result.append(jnp.where(row == 0, edge, rolled[2]))
                return result
            after = pltpu.roll(look(0, j, 1, 2), 7, axis=0)
            result = [
                jnp.where(row == 7, rolled[1], rolled[0]),
                jnp.where(row == 7, after, rolled[1]),
            ]
            if need_last:
                edge = pltpu.roll(look(-1, j, 1, 0), 7, axis=0)
                result.append(jnp.where(row == 7, edge, rolled[2]))
            return result

        for pop in range(POPS):
            cx, cy, cz = VELOCITY[pop]
            kept = {}

            def source(*key):
                if key not in kept:
                    kept[key] = shifted(pop, *key)
                return kept[key]

            def along_y(group, dz):
                values = source(group, None if group == 2 else 0, 0, dz)
                if cy == 0:
                    return values
                other = (group - cy) % 3
                if group != 2 and other != 2:
                    carried = source(other, 0, 0, dz)
                else:
                    carried = source(other, cy if group == 2 else 0, -cy, dz)
                mask = lane >= 112 if cy > 0 else lane < 16
                return [jnp.where(mask, b, a) for a, b in zip(values, carried)]

            for group in groups:
                values = along_y(group, 0)
                turn = (16 * cy + cz) % 128
                if turn:
                    values = [pltpu.roll(value, turn, axis=1) for value in values]
                if cz:
                    turn = (16 * cy - 15 * cz) % 128
                    wrapped = [pltpu.roll(value, turn, axis=1) for value in along_y(group, -cz)]
                    mask = lane % 16 == (0 if cz > 0 else 15)
                    values = [jnp.where(mask, b, a) for a, b in zip(values, wrapped)]
                for v, value in enumerate(values[:vregs]):
                    if pop:
                        value = jnp.where(value != value, load("own", OPPOSITE[pop], group, v), value)
                    if finish is not None:
                        is_fluid = flags[group // 2][
                            aligned((FLAG0 + s) * PAIR + group * GROUP + v * 8), :
                        ]
                        value = jnp.where(is_fluid > 0.0, value, 0.0)
                    target = pop * PLANE + group * GROUP + v * 8
                    h_view[target : target + 8, :] = value

    @pl.loop(0, SLOTS)
    def _(s):
        one_slot(s)
        if finish is not None:
            finish(s)


def join_kernel(
    cells,
    mate_msg,
    other_msg,
    mate2_msg,
    other2_msg,
    post_ref,
    slots,
    low_msg,
    high_msg,
    low2_msg,
    high2_msg,
):
    sort_messages(
        mate_msg, other_msg, mate2_msg, other2_msg, low_msg, high_msg, low2_msg, high2_msg
    )
    for i, (ref, row) in enumerate(((low_msg, TABLE), (cells, CELLS), (high_msg, TABLE))):
        slots[8 * i : 8 * i + 8, :] = first_rows(ref[row : row + 8, :])

    from_low, from_high, low_low, low_me, high_high, high_me = landed_slots(cells)
    post_ref[PLANES * PAIR :, :] = jnp.full((POPS * PAIR, 128), jnp.nan, jnp.float32)
    for q in range(PLANES):
        for y in range(2):
            start = q * PAIR + y * GROUP
            post_ref[start : start + EDGE, :] = cells[
                q * 32 + y * EDGE : q * 32 + (y + 1) * EDGE, :
            ]
    for s, (slot, msg) in itertools.product(
        range(SLOTS), ((from_low, low_msg), (from_high, high_msg))
    ):

        @pl.when(slot == s)
        def _():
            for p in range(POPS):
                for v in range(2):
                    rim = rim_of(msg, p, v)
                    row = (s * POPS + p) * PAIR + v * 8
                    post_ref[row : row + 8, :] = rim
                    post_ref[row + GROUP : row + GROUP + 8, :] = rim

    for msg, row0, step, first in ((high_msg, 16, 1, 2), (low_msg, 23, -1, 1)):
        for y in range(2):
            for count, planes, row, source in strip_rows(first, row0, step):
                source += y * LAYERS
                post_ref[planes(PAIR, row + y * GROUP), :] = msg[source : source + count, :]
    for s in range(SLOTS):
        for slot, msg, row0 in (
            (low_low, low2_msg, 21),
            (low_me, cells.at[OWN2:], 21),
            (high_high, high2_msg, 16),
            (high_me, cells.at[OWN2 + 6 * GROUP :], 16),
        ):

            @pl.when(slot == s)
            def _():
                for y in range(2):
                    for k in range(3):
                        row = s * POPS * PAIR + y * GROUP + row0 + k
                        source = (y * 3 + k) * GROUP
                        post_ref[pl.ds(row, POPS, stride=PAIR), :] = msg[source : source + POPS, :]
    hide_walls(post_ref, PAIR)


def first_rows(slot):
    slot = slot.astype(jnp.int32)
    return jnp.where(slot == SLOTS, NOWHERE, slot * (POPS * GROUP))


def outer_kernel(
    own_slots, first_post, near_msg, far_msg, slots, outer_ref, next_ref, h_ref, table, sem
):
    even = is_even("cross")

    def received(row):
        near, far = near_msg[row : row + 8, :], far_msg[row : row + 8, :]
        return jnp.where(even, far, near), jnp.where(even, near, far)

    for i in range(3):
        south, north = received(EDGE_TABLE + 8 * i)
        slots[24 * i : 24 * i + 8, :] = first_rows(south)
        slots[24 * i + 8 : 24 * i + 16, :] = own_slots[8 * i : 8 * i + 8, :]
        slots[24 * i + 16 : 24 * i + 24, :] = first_rows(north)
    table_copy = pltpu.make_async_copy(slots, table, sem)
    table_copy.start()

    nothing = jnp.full((8, 128), jnp.nan, jnp.float32)
    for row in range(0, POPS * GROUP, 8):
        outer_ref[NOWHERE + row : NOWHERE + row + 8, :] = nothing
        next_ref[NOWHERE + row : NOWHERE + row + 8, :] = nothing
    lane = lanes_iota()
    for v in range(3):

        def rows(q):
            return slice(q * GROUP + v * 8, q * GROUP + v * 8 + 8)

        for quad in range(QUADS):
            south, north = received(quad * GROUP + v * 8)
            for k in range(4):
                value = jnp.where(lane // 32 == (k + 3) % 4, south, north)
                if k:
                    value = pltpu.roll(value, 128 - 32 * k, axis=1)
                outer_ref[rows(4 * quad + k), :] = value
        for part in range(3):
            values = received(FAR + part * GROUP + v * 8)
            for planes, target, value in zip((NORTHWARD, SOUTHWARD), (80, 32), values):
                for k, q in enumerate(planes[8 * part : 8 * part + 8]):
                    moved = pltpu.roll(value, (target - 16 * k) % 128, axis=1)
                    outer_ref[rows(q), :] = jnp.where(
                        lane // 16 == target // 16, moved, outer_ref[rows(q), :]
                    )
    for row in range(FLAG0 * GROUP, NOWHERE, 8):
        next_ref[row : row + 8, :] = outer_ref[row : row + 8, :]
    hide_walls(outer_ref, GROUP)
    table_copy.wait()
    flags = (first_post, outer_ref)
    stream_all(flags, h_ref, flags, table, (2,), 3)
    collide_all(h_ref, flags, (None, next_ref), ((2,),))


def steps_kernel(
    slots,
    first_post,
    first_outer,
    next_outer,
    cells,
    mate_msg,
    other_msg,
    mate_rest,
    passed_rest,
    passed2_rest,
    out_hbm,
    h_ref,
    post_ref,
    outer_ref,
    out,
    table,
    sems,
):
    table_copy = pltpu.make_async_copy(slots, table, sems.at[SLOTS])
    table_copy.start()
    post_ref[...] = first_post[...]
    nothing = jnp.full((8, 128), jnp.nan, jnp.float32)
    for row in range(0, POPS * GROUP, 8):
        outer_ref[NOWHERE + row : NOWHERE + row + 8, :] = nothing

    def rest(row, is_mate):
        if is_mate:
            return mate_rest[row : row + 8, :]
        if row < HALF:
            return passed_rest[row : row + 8, :]
        return passed2_rest[row - HALF : row - HALF + 8, :]

    from_low, from_high = landed_slots(cells)[:2]
    lane = lanes_iota()
    even = is_even("curve")
    odd = jnp.logical_not(even)
    for s, (slot, wanted, msg, is_mate) in itertools.product(
        range(SLOTS),
        (
            (from_low, odd, mate_msg, True),
            (from_low, even, other_msg, False),
            (from_high, even, mate_msg, True),
            (from_high, odd, other_msg, False),
        ),
    ):

        @pl.when((slot == s) & wanted)
        def _():
            for v in range(2):
                starts = [(FLAG0 + s) * PAIR + y * GROUP + v * 8 for y in range(2)]
                fluid = [first_post[row : row + 8, :] > 0.0 for row in starts]
                for p in range(POPS):
                    rim = rim_of(msg, p, v)
                    row = p * EDGE + v * 8
                    wide = rest(row, is_mate)
                    row = (POPS + p // 2) * EDGE + v * 8
                    middle = rest(row, is_mate)
                    if p % 2:
                        middle = pltpu.roll(middle, 64, axis=1)
                    first = jnp.where(lane < 32, rim, wide)
                    second = jnp.where(lane < 32, wide, jnp.where(lane < 96, middle, rim))
                    row = (s * POPS + p) * PAIR + v * 8
                    post_ref[row : row + 8, :] = jnp.where(fluid[0], first, jnp.nan)
                    row += GROUP
                    post_ref[row : row + 8, :] = jnp.where(fluid[1], second, jnp.nan)

    def finish(s):
        for x in range(EDGE):
            for y in range(2):
                tile = 2 * x + y
                for p, size in ((0, 8), (8, 8), (16, 3)):
                    row = s * SLOT + (p * PLANE + y * GROUP + x)
                    out[s, p : p + size, 128 * tile : 128 * tile + 128] = h_ref[
                        pl.ds(row, size, stride=PLANE), :
                    ]
        pltpu.make_async_copy(out.at[s], out_hbm.at[s], sems.at[s]).start()

    table_copy.wait()
    flags = (first_post, first_outer)
    stream_all((post_ref, first_outer), h_ref, flags, table, (0, 1), 3)
    collide_all(h_ref, flags, (post_ref, None), ((0, 1),))
    posts = (post_ref, next_outer)
    for _ in range(STEPS - 2):
        stream_all(posts, h_ref, flags, table, (0, 1, 2), 3)
        posts = (post_ref, outer_ref)
        collide_all(h_ref, flags, posts)
    stream_all(posts, h_ref, flags, table, (0, 1), 2, finish)
    for s in range(SLOTS):
        pltpu.make_async_copy(out.at[s], out_hbm.at[s], sems.at[s]).wait()


def swapped(value, axis, unit=1):
    count = lax.axis_size(axis)
    results = []
    for which in (0, 1):
        others = [i + (unit if i // unit % 2 == which else -unit) for i in range(count)]
        pairs = [(i, j if 0 <= j < count else i) for i, j in enumerate(others)]
        results.append(lax.ppermute(value[which], axis, pairs))
    return results


def rows128(count):
    return jax.ShapeDtypeStruct((count, 128), jnp.float32)


def call(kernel, in_spaces, out_spaces, outs, ins, scratch, limit=LIMIT, cost=None):
    spaces = {
        "S": pl.BlockSpec(memory_space=pltpu.SMEM),
        "V": pl.BlockSpec(memory_space=pltpu.VMEM),
        "H": pl.BlockSpec(memory_space=pltpu.HBM),
    }
    return pl.pallas_call(
        kernel,
        out_shape=outs,
        in_specs=[spaces[x] for x in in_spaces],
        out_specs=[spaces[x] for x in out_spaces],
        scratch_shapes=scratch,
        compiler_params=pltpu.CompilerParams(vmem_limit_bytes=limit),
        cost_estimate=cost,
    )(*ins)


def per_device(populations, site_flags, neighbours, migrations, counts):
    sizes = (lax.axis_size("curve"), lax.axis_size("cross"))
    moves = migrations.T
    floats = lambda rows: pltpu.VMEM((rows, 128), jnp.float32)
    messages = [
        OWN2 + 12 * GROUP,
        STRIPS + 2 * LAYERS,
        STRIPS + 2 * LAYERS,
        6 * GROUP,
        6 * GROUP,
        REST,
    ]
    cells, mate_msg, other_msg, mate2_msg, other2_msg, rest_msg, rest2_msg = call(
        functools.partial(pack_kernel, *sizes),
        "HHHHH",
        "HHHHHHH",
        [rows128(rows) for rows in (*messages, REST - HALF)],
        (moves, counts, populations, site_flags, neighbours),
        [
            pltpu.SMEM(moves.shape, jnp.int32),
            pltpu.SMEM(counts.shape, jnp.int32),
            pltpu.VMEM(populations.shape, jnp.float32),
            pltpu.VMEM(site_flags.shape, jnp.int32),
            pltpu.VMEM(neighbours.shape, jnp.int32),
            *[floats(rows) for rows in messages],
            pltpu.VMEM((8, 5888), jnp.float32),
            pltpu.VMEM((128, 384), jnp.bfloat16),
            floats(256),
            floats(8),
            pltpu.SemaphoreType.DMA((4 + SLOTS + 9,)),
        ],
        WIDE_LIMIT,
    )
    mate_msg, other_msg = swapped((mate_msg, other_msg), "curve")
    mate2_msg, other2_msg = swapped((mate2_msg, other2_msg), "curve", 2)
    assert sizes[0] % 2 == 0
    pairs = [(i, i ^ 1) for i in range(sizes[0])]
    mate_rest = lax.ppermute(rest_msg, "curve", pairs)
    last = sizes[0] - 1
    pairs = [(i, max(i - 2, 0) if i % 2 else min(i + 2, last)) for i in range(sizes[0])]
    passed_rest = lax.ppermute(mate_rest[:HALF], "curve", pairs)
    back = [(target, source) for source, target in pairs]
    along_z = lax.ppermute(rest2_msg, "curve", back)
    passed2_rest = lax.ppermute(along_z, "curve", [(i, i ^ 1) for i in range(last + 1)])
    (outer,) = call(spread_kernel, "V", "V", [rows128(PLANES * GROUP)], (cells,), [])
    strips = (cells, mate_msg, other_msg, mate2_msg, other2_msg)
    sorted_rows = [messages[1], messages[1], messages[3], messages[3]]
    near_msg, far_msg = call(
        edge_kernel,
        "VVVVVVV",
        "VV",
        [rows128(NEAR_ROWS), rows128(FAR_ROWS)],
        (outer, *strips, along_z),
        [floats(rows) for rows in [PLANES * GROUP] + sorted_rows],
        cost=pl.CostEstimate(flops=10**10, bytes_accessed=0, transcendentals=0),
    )
    near_msg, far_msg = swapped((near_msg, far_msg), "cross")
    post, own_slots = call(
        join_kernel,
        "VVVVV",
        "VV",
        [rows128(ALL_PLANES * PAIR), jax.ShapeDtypeStruct((24, 128), jnp.int32)],
        strips,
        [floats(rows) for rows in sorted_rows],
    )
    slots, outer_post, next_outer = call(
        outer_kernel,
        "VVVV",
        "VVV",
        [
            jax.ShapeDtypeStruct((72, 128), jnp.int32),
            rows128(ALL_PLANES * GROUP),
            rows128(ALL_PLANES * GROUP),
        ],
        (own_slots, post, near_msg, far_msg),
        [floats(SLOTS * SLOT), pltpu.SMEM((72, 128), jnp.int32), pltpu.SemaphoreType.DMA],
    )
    arriving = (cells, mate_msg, other_msg, mate_rest, passed_rest, passed2_rest)
    return call(
        steps_kernel,
        "VVVVVVVVVV",
        "H",
        [jax.ShapeDtypeStruct(populations.shape, jnp.float32)],
        (slots, post, outer_post, next_outer, *arriving),
        [
            floats(SLOTS * SLOT),
            floats(ALL_PLANES * PAIR),
            floats(ALL_PLANES * GROUP),
            pltpu.VMEM(populations.shape, jnp.float32),
            pltpu.SMEM((72, 128), jnp.int32),
            pltpu.SemaphoreType.DMA((SLOTS + 1,)),
        ],
    )[0]


def solution(mesh):
    return jax.shard_map(
        per_device,
        mesh=mesh,
        in_specs=(
            P(("curve", "cross"), None, None),
            P(("curve", "cross"), None),
            P(("curve", "cross"), None),
            P(),
            P(("curve", "cross")),
        ),
        out_specs=P(("curve", "cross"), None, None),
        check_vma=False,
    )
```

```python
import functools
import itertools

import jax
import jax.numpy as jnp
import numpy as np
from jax import lax
from jax.experimental import pallas as pl
from jax.experimental.pallas import tpu as pltpu
from jax.sharding import PartitionSpec as P

EDGE = 16
STEPS = 3
SLOTS = 3
POPS = 19
PLANES = SLOTS * POPS + SLOTS
FLAG0 = SLOTS * POPS
GROUP = 24
PLANE = 3 * GROUP
SLOT = POPS * PLANE
CELL = 40
CELLS = PLANES * CELL
LANDINGS = CELLS + 8
OWN2 = LANDINGS + 8
OUTWARD = SLOTS * 5 + SLOTS
LAYERS = 2 * PLANES + OUTWARD
RIM = 11 * EDGE
REST = POPS * EDGE + 10 * EDGE
HALF = REST - 136
PAIR = 2 * GROUP
QUADS = PLANES // 4
TABLE = RIM
STRIPS = RIM + 8
FAR = QUADS * GROUP
EDGE_TABLE = FAR + 3 * GROUP
EDGE_ROWS = EDGE_TABLE + 24
NEAR_ROWS, FAR_ROWS = EDGE_ROWS + 16, EDGE_ROWS + 24
NOWHERE = PLANES * GROUP
ALL_PLANES = PLANES + POPS
LIMIT = 20 * 1024 * 1024
WIDE_LIMIT = 127 * 512 * 1024

VELOCITY = [
    (0, 0, 0),
    (1, 0, 0),
    (-1, 0, 0),
    (0, 1, 0),
    (0, -1, 0),
    (0, 0, 1),
    (0, 0, -1),
    (1, 1, 0),
    (-1, -1, 0),
    (1, -1, 0),
    (-1, 1, 0),
    (1, 0, 1),
    (-1, 0, -1),
    (1, 0, -1),
    (-1, 0, 1),
    (0, 1, 1),
    (0, -1, -1),
    (0, 1, -1),
    (0, -1, 1),
]
NORTHWARD, SOUTHWARD = (
    [s * POPS + p for s in range(SLOTS) for p in range(POPS) if VELOCITY[p][1] == side]
    + [FLAG0 + s for s in range(SLOTS)]
    for side in (1, -1)
)
THIRD = [
    (pop, source, *((32 + 16 * k, 9) if k < 4 else (16 * (k - 4), 10)))
    for k, (pop, source) in enumerate(
        [(p, 32) for p in (4, 8, 9, 16, 18)] + [(p, 80) for p in (3, 7, 10, 15, 17)]
    )
]
OPPOSITE = [0, 2, 1, 4, 3, 6, 5, 8, 7, 10, 9, 12, 11, 14, 13, 16, 15, 18, 17]


def lanes_iota():
    return lax.broadcasted_iota(jnp.int32, (8, 128), 1)


def is_even(axis, unit=1):
    return lax.rem(lax.axis_index(axis) // unit, 2) == 0


def rows_iota():
    return lax.broadcasted_iota(jnp.int32, (8, 128), 0)


def aligned(start, size=8):
    return pl.ds(pl.multiple_of(start, 8), size)


def move_slots(moves, curve_size, cross_size):
    curve, cross = lax.axis_index("curve"), lax.axis_index("cross")

    def landed(source, target):
        inside = (source >= 0) & (source < curve_size) & (target >= 0) & (target < curve_size)
        row = jnp.clip(source, 0, curve_size - 1) * cross_size + cross
        rank = target * cross_size + cross
        hit = inside & (moves[0, row] >= 0) & (moves[1, row] == rank)
        return jnp.where(hit, moves[2, row], -1)

    return (
        landed(curve - 1, curve),
        landed(curve + 1, curve),
        landed(curve - 2, curve - 1),
        landed(curve, curve - 1),
        landed(curve + 2, curve + 1),
        landed(curve, curve + 1),
    )


def pack_kernel(
    curve_size,
    cross_size,
    moves_hbm,
    counts_hbm,
    pops_hbm,
    flags_hbm,
    neighbours_hbm,
    cells_hbm,
    mate_hbm,
    other_hbm,
    mate2_hbm,
    other2_hbm,
    rest_hbm,
    rest2_hbm,
    moves,
    counts,
    pops,
    flags,
    neighbours,
    cells,
    up_msg,
    down_msg,
    up2_msg,
    down2_msg,
    rest_msg,
    wide_flags,
    plane_flags,
    site_flags,
    near,
    sems,
):
    started = []

    def copy(source, target):
        one = pltpu.make_async_copy(source, target, sems.at[len(started)])
        one.start()
        started.append(one)
        return one

    flags_copy = copy(flags_hbm, flags)
    copies = [copy(pops_hbm.at[s], pops.at[s]) for s in range(SLOTS)]
    small = [
        copy(neighbours_hbm, neighbours),
        copy(counts_hbm, counts),
        copy(moves_hbm, moves),
    ]
    for one in small:
        one.wait()

    near[...] = jnp.zeros_like(near)
    named = neighbours[...]
    slot = jnp.where(named >= 0, lax.rem(jnp.maximum(named, 0), SLOTS), SLOTS)
    near[0:SLOTS, 0 : named.shape[1]] = slot.astype(jnp.float32)
    for ref, row in ((cells, CELLS), (up_msg, TABLE), (down_msg, TABLE)):
        ref[row : row + 8, :] = near[...]

    wide_flags[...] = jnp.zeros_like(wide_flags)
    flags_copy.wait()
    wide_flags[0:SLOTS, 0 : flags.shape[1]] = flags[...].astype(jnp.float32)
    span = EDGE + 2
    for x in range(EDGE):
        start = (x + 1) * span * span
        base = start // 128 * 128
        window = wide_flags[:, base : base + 512]
        window = pltpu.roll(window, (512 - (start - base)) % 512, axis=1)
        plane_flags[8 * x : 8 * x + 8, :] = window[:, :384].astype(jnp.bfloat16)
    lane_in = lax.broadcasted_iota(jnp.int32, (384, 256), 0)
    site = lax.broadcasted_iota(jnp.int32, (384, 256), 1)
    chosen = lane_in == (site // EDGE + 1) * span + site % EDGE + 1
    product = jnp.dot(
        plane_flags[...],
        jnp.where(chosen, 1.0, 0.0).astype(jnp.bfloat16),
        preferred_element_type=jnp.float32,
    )
    site_flags[0:128, :] = product[:, :128]
    site_flags[128:256, :] = product[:, 128:]
    for s in range(SLOTS):
        live = s < counts[0]
        for y in range(2):
            piece = site_flags[pl.ds(128 * y + s, EDGE, stride=8), :]
            is_fluid = (piece == 1.0) & live
            row = (FLAG0 + s) * CELL + y * EDGE
            cells[row : row + EDGE, :] = jnp.where(is_fluid, 1.0, 0.0)

    for s in range(SLOTS):
        copies[s].wait()
        for x in range(EDGE):
            for y in range(2):
                tile = 2 * x + y
                for p, size in ((0, 8), (8, 8), (16, 3)):
                    row = (s * POPS + p) * CELL + y * EDGE + x
                    cells[pl.ds(row, size, stride=CELL), :] = pops[
                        s, p : p + size, 128 * tile : 128 * tile + 128
                    ]

    @pl.loop(0, SLOTS)
    def _(s):
        @pl.loop(0, 4, unroll=2)
        def _(c):
            base = s * (POPS * CELL) + c * 8
            view = cells.at[aligned(base, (POPS - 1) * CELL + 8), :]
            h = [view[p * CELL : p * CELL + 8, :] for p in range(POPS)]
            for p, value in enumerate(collided(h)):
                view[p * CELL : p * CELL + 8, :] = value

    for i, slot in enumerate(move_slots(moves, curve_size, cross_size)):
        value = jnp.full((1, 128), slot, jnp.int32)
        cells[LANDINGS + i : LANDINGS + i + 1, :] = value.astype(jnp.float32)

    body_copy = copy(cells.at[:OWN2], cells_hbm.at[:OWN2])

    for y in range(2):
        for msg, x0, first in ((up_msg, 15, 1), (down_msg, 0, 2)):
            step = -1 if x0 else 1
            for k in range(2):
                out = STRIPS + y * LAYERS + k * PLANES
                msg[out : out + PLANES, :] = cells[
                    pl.ds(y * EDGE + x0 + step * k, PLANES, stride=CELL), :
                ]
            row = y * EDGE + x0 + 2 * step
            out = STRIPS + y * LAYERS + 2 * PLANES
            for s in range(SLOTS):
                base = s * POPS * CELL + row
                msg[out + 5 * s : out + 5 * s + 1, :] = cells[pl.ds(base + first * CELL, 1), :]
                msg[out + 5 * s + 1 : out + 5 * s + 5, :] = cells[
                    pl.ds(base + (first + 6) * CELL, 4, stride=2 * CELL), :
                ]
            msg[out + 5 * SLOTS : out + OUTWARD, :] = cells[
                pl.ds(FLAG0 * CELL + row, SLOTS, stride=CELL), :
            ]

    here = lax.axis_index("curve") * cross_size + lax.axis_index("cross")
    leaving = jnp.maximum(moves[0, here], 0)
    lane = lanes_iota()
    for v in range(2):
        halves = [
            [cells[aligned(leaving * (POPS * CELL) + p * CELL + y * EDGE + v * 8), :] for y in (0, 1)]
            for p in range(POPS)
        ]
        outer = [jnp.where(lane < 64, first, second) for first, second in halves]
        middle = (lane >= 32) & (lane < 96)
        sets = [
            jnp.where(middle, pltpu.roll(outer[p + 1], 64, axis=1), outer[p])
            for p in range(0, POPS - 1, 2)
        ]
        sets += [outer[POPS - 1], jnp.zeros_like(outer[0])]
        for pop, source, target, which in THIRD:
            moved = pltpu.roll(outer[pop], (target - source) % 128, axis=1)
            sets[which] = jnp.where(lane // 16 == target // 16, moved, sets[which])
        for k, value in enumerate(sets):
            row = k * EDGE + v * 8
            up_msg[row : row + 8, :] = value
            down_msg[row : row + 8, :] = value
        for p, (first, second) in enumerate(halves):
            row = p * EDGE + v * 8
            rest_msg[row : row + 8, :] = jnp.where(lane < 32, second, first)
        for p in range(0, POPS, 2):
            value = halves[p][1]
            if p + 1 < POPS:
                value = jnp.where(middle, value, pltpu.roll(halves[p + 1][1], 64, axis=1))
            row = (POPS + p // 2) * EDGE + v * 8
            rest_msg[row : row + 8, :] = value
    for s in range(SLOTS):

        @pl.when(leaving == s)
        def _():
            for y in range(2):
                for k in range(3):
                    out = (y * 3 + k) * GROUP
                    row = s * POPS * CELL + y * EDGE + k
                    up2_msg[out : out + POPS, :] = cells[pl.ds(row + 13, POPS, stride=CELL), :]
                    down2_msg[out : out + POPS, :] = cells[pl.ds(row, POPS, stride=CELL), :]

    cells[OWN2 : OWN2 + 6 * GROUP, :] = up2_msg[...]
    cells[OWN2 + 6 * GROUP :, :] = down2_msg[...]
    last = [copy(cells.at[OWN2:], cells_hbm.at[OWN2:]), copy(rest_msg, rest_hbm)]
    last.append(copy(rest_msg.at[HALF:], rest2_hbm))
    count = len(started)
    for i, (up, down, mate, other, unit) in enumerate(
        ((up_msg, down_msg, mate_hbm, other_hbm, 1), (up2_msg, down2_msg, mate2_hbm, other2_hbm, 2))
    ):
        first, second = sems.at[count + 2 * i], sems.at[count + 2 * i + 1]
        even = is_even("curve", unit)

        @pl.when(even)
        def _():
            pltpu.make_async_copy(up, mate, first).start()
            pltpu.make_async_copy(down, other, second).start()

        @pl.when(jnp.logical_not(even))
        def _():
            pltpu.make_async_copy(down, mate, first).start()
            pltpu.make_async_copy(up, other, second).start()

        last.append(pltpu.make_async_copy(up, mate, first))
        last.append(pltpu.make_async_copy(down, other, second))
    body_copy.wait()
    for one in last:
        one.wait()


def spread_kernel(cells, outer):
    low = lanes_iota() < 64
    for q in range(PLANES):
        for v in range(2):
            row = q * CELL + v * 8
            first, second = cells[row : row + 8, :], cells[row + EDGE : row + EDGE + 8, :]
            row = q * GROUP + v * 8
            outer[row : row + 8, :] = jnp.where(low, first, second)


def sort_messages(mate_msg, other_msg, mate2_msg, other2_msg, low_msg, high_msg, low2, high2):
    for mate, other, low, high, unit in (
        (mate_msg, other_msg, low_msg, high_msg, 1),
        (mate2_msg, other2_msg, low2, high2, 2),
    ):
        even = is_even("curve", unit)

        @pl.when(even)
        def _():
            low[...] = other[...]
            high[...] = mate[...]

        @pl.when(jnp.logical_not(even))
        def _():
            low[...] = mate[...]
            high[...] = other[...]


def landed_slots(cells):
    return [jnp.max(cells[LANDINGS + i : LANDINGS + i + 1, :]) for i in range(6)]


def rim_of(msg, p, v):
    row = p // 2 * EDGE + v * 8
    value = msg[row : row + 8, :]
    return pltpu.roll(value, 64, axis=1) if p % 2 else value


def sel4(parts, lane):
    first = jnp.where(lane < 32, parts[0], parts[1])
    second = jnp.where(lane < 96, parts[2], parts[3])
    return jnp.where(lane < 64, first, second)


def strip_rows(first, row0, step):
    pieces = []
    for k in range(2):
        pieces.append(
            (PLANES, lambda size, row: pl.ds(row, PLANES, stride=size), row0 + step * k, STRIPS + k * PLANES)
        )
    row, source = row0 + 2 * step, STRIPS + 2 * PLANES
    for s in range(SLOTS):
        plane = s * POPS + first
        pieces.append((1, lambda size, row, plane=plane: pl.ds(plane * size + row, 1), row, source))
        pieces.append(
            (
                4,
                lambda size, row, plane=plane: pl.ds(
                    (plane + 6) * size + row, 4, stride=2 * size
                ),
                row,
                source + 1,
            )
        )
        source += 5
    pieces.append(
        (SLOTS, lambda size, row: pl.ds(FLAG0 * size + row, SLOTS, stride=size), row, source)
    )
    return pieces


def edge_kernel(
    own_outer,
    cells,
    mate_msg,
    other_msg,
    mate2_msg,
    other2_msg,
    along_z,
    near_msg,
    far_msg,
    outer,
    low_msg,
    high_msg,
    low2_msg,
    high2_msg,
):
    sort_messages(
        mate_msg, other_msg, mate2_msg, other2_msg, low_msg, high_msg, low2_msg, high2_msg
    )
    from_low, from_high, low_low, low_me, high_high, high_me = landed_slots(cells)
    low = lanes_iota() < 64
    for q in range(PLANES):
        for v in range(2):
            row = q * GROUP + v * 8
            outer[row : row + 8, :] = own_outer[row : row + 8, :]

    def both(first, second):
        lane = lax.broadcasted_iota(jnp.int32, first.shape, 1)
        return jnp.where(lane < 64, first, second)

    for msg, row0, step, first in ((high_msg, 16, 1, 2), (low_msg, 23, -1, 1)):
        for count, planes, row, source in strip_rows(first, row0, step):
            outer[planes(GROUP, row), :] = both(
                msg[source : source + count, :],
                msg[LAYERS + source : LAYERS + source + count, :],
            )
    lane = lanes_iota()
    for s, (slot, msg) in itertools.product(
        range(SLOTS), ((from_low, low_msg), (from_high, high_msg))
    ):

        @pl.when(slot == s)
        def _():
            for v in range(2):
                values = [rim_of(msg, p, v) for p in range(POPS)]
                for pop, target, source, which in THIRD:
                    row = which * EDGE + v * 8
                    moved = pltpu.roll(msg[row : row + 8, :], (target - source) % 128, axis=1)
                    values[pop] = jnp.where(lane // 16 == target // 16, moved, values[pop])
                for p, value in enumerate(values):
                    row = (s * POPS + p) * GROUP + v * 8
                    outer[row : row + 8, :] = value

    for s in range(SLOTS):
        for slot, msg, row0 in (
            (low_low, low2_msg, 21),
            (low_me, cells.at[OWN2:], 21),
            (high_high, high2_msg, 16),
            (high_me, cells.at[OWN2 + 6 * GROUP :], 16),
        ):

            @pl.when(slot == s)
            def _():
                for k in range(3):
                    outer[pl.ds(s * POPS * GROUP + row0 + k, POPS, stride=GROUP), :] = both(
                        msg[k * GROUP : k * GROUP + POPS, :],
                        msg[(3 + k) * GROUP : (3 + k) * GROUP + POPS, :],
                    )

    even = is_even("cross")

    def send(row, north, south):
        near_msg[row : row + 8, :] = jnp.where(even, north, south)
        far_msg[row : row + 8, :] = jnp.where(even, south, north)

    for v in range(3):

        def plane(q):
            return outer[q * GROUP + v * 8 : q * GROUP + v * 8 + 8, :]

        for quad in range(QUADS):
            parts = [plane(4 * quad)]
            parts += [pltpu.roll(plane(4 * quad + k), 32 * k, axis=1) for k in (1, 2, 3)]
            send(quad * GROUP + v * 8, sel4(parts[1:] + parts[:1], lane), sel4(parts, lane))
        for part in range(3):
            values = []
            for planes, source in ((NORTHWARD, 80), (SOUTHWARD, 32)):
                value = None
                for k, q in enumerate(planes[8 * part : 8 * part + 8]):
                    moved = pltpu.roll(plane(q), (16 * k - source) % 128, axis=1)
                    value = moved if value is None else jnp.where(lane < 16 * k, value, moved)
                values.append(value)
            send(FAR + part * GROUP + v * 8, *values)
    tables = (low_msg, TABLE), (cells, CELLS), (high_msg, TABLE)
    for i, (ref, row) in enumerate(tables):
        value = ref[row : row + 8, :]
        send(EDGE_TABLE + 8 * i, value, value)


def collided(h):
    shear = 1.0 / 0.6
    rest = h[0]
    sx, dx = h[1] + h[2], h[1] - h[2]
    sy, dy = h[3] + h[4], h[3] - h[4]
    sz, dz = h[5] + h[6], h[5] - h[6]
    s7, d7 = h[7] + h[8], h[7] - h[8]
    s9, d9 = h[9] + h[10], h[9] - h[10]
    s11, d11 = h[11] + h[12], h[11] - h[12]
    s13, d13 = h[13] + h[14], h[13] - h[14]
    s15, d15 = h[15] + h[16], h[15] - h[16]
    s17, d17 = h[17] + h[18], h[17] - h[18]
    txy, txz, tyz = s7 + s9, s11 + s13, s15 + s17
    pxy, pxz, pyz = s7 - s9, s11 - s13, s15 - s17
    ax, bx = d7 + d9, d11 + d13
    ay, by = d7 - d9, d15 + d17
    az, bz = d11 - d13, d15 - d17
    axes = sx + sy + sz
    diags = txy + txz + tyz
    rho = rest * (1.0 / 3.0) + axes * (1.0 / 18.0) + diags * (1.0 / 36.0)
    fx, fy, fz = ax + bx, ay + by, az + bz
    jx = dx * (1.0 / 18.0) + fx * (1.0 / 36.0)
    jy = dy * (1.0 / 18.0) + fy * (1.0 / 36.0)
    jz = dz * (1.0 / 18.0) + fz * (1.0 / 36.0)
    inverse = 1.0 / rho
    ux, uy, uz = jx * inverse, jy * inverse, jz * inverse
    qxx, qyy, qzz = jx * ux, jy * uy, jz * uz
    total = qxx + qyy + qzz

    energy = -10.0 * rest - axes * (11.0 / 18.0) + diags * (8.0 / 36.0)
    energy = (energy + 11.0 * rho - 19.0 * total) * (1.19 / 2394.0)
    square = 4.0 * rest - axes * (4.0 / 18.0) + diags * (1.0 / 36.0)
    square = (square - 3.0 * rho + 5.5 * total) * (1.4 / 252.0)
    axis_x = (3.0 * sx - axes) * (1.0 / 18.0)
    diag_x = (diags - 3.0 * tyz) * (1.0 / 36.0)
    want_x = 3.0 * qxx - total
    stress_x = (axis_x + diag_x - want_x) * (shear / 36.0)
    third_x = (diag_x - 2.0 * axis_x + 0.5 * want_x) * (1.4 / 72.0)
    axis_w = (sy - sz) * (1.0 / 18.0)
    diag_w = (txy - txz) * (1.0 / 36.0)
    want_w = qyy - qzz
    stress_w = (axis_w + diag_w - want_w) * (shear / 12.0)
    third_w = (diag_w - 2.0 * axis_w + 0.5 * want_w) * (1.4 / 24.0)

    rest_out = rest - 3.0 * (12.0 * square - 30.0 * energy)
    common = -18.0 * (11.0 * energy + 4.0 * square)
    along_x = 18.0 * (stress_x - 2.0 * third_x)
    along_w = 18.0 * (stress_w - 2.0 * third_w)
    ex = common + 2.0 * along_x
    ey = common - along_x + along_w
    ez = common - along_x - along_w
    common = 36.0 * (8.0 * energy + square)
    across_x = 36.0 * (stress_x + third_x)
    across_w = 36.0 * (stress_w + third_w)
    exy = common + across_x + across_w
    exz = common + across_x - across_w
    eyz = common - 2.0 * across_x
    cxy = shear * (0.25 * pxy - 9.0 * jx * uy)
    cxz = shear * (0.25 * pxz - 9.0 * jx * uz)
    cyz = shear * (0.25 * pyz - 9.0 * jy * uz)

    def flux(d, f, j):
        return (f * (1.0 / 36.0) - d * (4.0 / 18.0) + j * (2.0 / 3.0)) * (1.2 / 40.0)

    hx, hy, hz = flux(dx, fx, jx), flux(dy, fy, jy), flux(dz, fz, jz)
    mx = (ax - bx) * (1.98 / 8.0)
    my = (by - ay) * (1.98 / 8.0)
    mz = (az - bz) * (1.98 / 8.0)
    hx36, hy36, hz36 = 36.0 * hx, 36.0 * hy, 36.0 * hz
    xy_x, xz_x = hx36 + mx, hx36 - mx
    yz_y, xy_y = hy36 + my, hy36 - my
    xz_z, yz_z = hz36 + mz, hz36 - mz
    ox, oy, oz = -2.0 * hx36, -2.0 * hy36, -2.0 * hz36

    out = [rest_out]

    def pair(i, even, odd):
        out.append(h[i] - (even + odd))
        out.append(h[i + 1] - (even - odd))

    pair(1, ex, ox)
    pair(3, ey, oy)
    pair(5, ez, oz)
    pair(7, exy + cxy, xy_x + xy_y)
    pair(9, exy - cxy, xy_x - xy_y)
    pair(11, exz + cxz, xz_x + xz_z)
    pair(13, exz - cxz, xz_x - xz_z)
    pair(15, eyz + cyz, yz_y + yz_z)
    pair(17, eyz - cyz, yz_y - yz_z)
    return out


def collide_all(h_ref, flags, posts, parts=((0, 1), (2,))):
    for groups in parts:
        ref = posts[groups[0] // 2]
        size = len(groups) * GROUP

        @pl.loop(0, SLOTS)
        def _(s):
            @pl.loop(0, size // 8, unroll=3)
            def _(c):
                is_fluid = flags[groups[0] // 2][aligned((FLAG0 + s) * size + c * 8), :] > 0.0
                start = s * SLOT + groups[0] * GROUP + c * 8
                h_view = h_ref.at[aligned(start, (POPS - 1) * PLANE + 8), :]
                start = s * (POPS * size) + c * 8
                view = ref.at[aligned(start, (POPS - 1) * size + 8), :]
                h = [h_view[p * PLANE : p * PLANE + 8, :] for p in range(POPS)]
                for p, value in enumerate(collided(h)):
                    view[p * size : p * size + 8, :] = jnp.where(is_fluid, value, jnp.nan)


def hide_walls(ref, size):
    @pl.loop(0, SLOTS)
    def _(s):
        @pl.loop(0, size // 8)
        def _(c):
            is_fluid = ref[aligned((FLAG0 + s) * size + c * 8), :] > 0.0
            start = s * (POPS * size) + c * 8
            view = ref.at[aligned(start, (POPS - 1) * size + 8), :]
            for p in range(POPS):
                row = p * size
                view[row : row + 8, :] = jnp.where(is_fluid, view[row : row + 8, :], jnp.nan)


def stream_all(posts, h_ref, flags, table, groups, vregs, finish=None):
    lane = lanes_iota()
    row = rows_iota()
    low = lane < 64

    def one_slot(s):
        views = {}

        def view(which, key):
            if (which, key) not in views:
                start = s * (POPS * GROUP) if key == "own" else table[key[0] * 8 + s, key[1]]
                start = start if which else 2 * start
                views[which, key] = posts[which].at[
                    aligned(start, POPS * (GROUP if which else PAIR)), :
                ]
            return views[which, key]

        def load(key, pop, group, v):
            if group == 2:
                row = pop * GROUP + v * 8
            else:
                row = pop * PAIR + group * GROUP + v * 8
            return view(group // 2, key)[row : row + 8, :]

        h_view = h_ref.at[aligned(s * SLOT, SLOT), :]

        def shifted(pop, group, j, dy, dz):
            cx = VELOCITY[pop][0]

            def rows(key, v):
                return load(key, pop, group, v)

            def look(i, j, dx, v):
                if (dx, dy, dz) == (0, 0, 0):
                    return rows("own", v)
                if j is None:
                    return jnp.where(low, look(i, 1, dx, v), look(i, -1, dx, v))
                region = (i + 1) * 3 + j + 1
                return rows((region, VELOCITY.index((dx, dy, dz)) - 1), v)

            need_last = vregs == 3
            values = [look(0, j, 0, 0), look(0, j, 0, 1)]
            if need_last:
                if dy == 0 and dz == 0:
                    values.append(rows("own", 2))
                else:
                    values.append(jnp.where(row < 4, look(1, j, 0, 2), look(-1, j, 0, 2)))
            if cx == 0:
                return values
            turn = 1 if cx > 0 else 7
            rolled = [pltpu.roll(value, turn, axis=0) for value in values]
            if cx > 0:
                before = pltpu.roll(look(0, j, -1, 2), 1, axis=0)
                result = [
                    jnp.where(row == 0, before, rolled[0]),
                    jnp.where(row == 0, rolled[0], rolled[1]),
                ]
                if need_last:
                    edge = pltpu.roll(look(1, j, -1, 1), 1, axis=0)
                    result.append(jnp.where(row == 0, edge, rolled[2]))
                return result
            after = pltpu.roll(look(0, j, 1, 2), 7, axis=0)
            result = [
                jnp.where(row == 7, rolled[1], rolled[0]),
                jnp.where(row == 7, after, rolled[1]),
            ]
            if need_last:
                edge = pltpu.roll(look(-1, j, 1, 0), 7, axis=0)
                result.append(jnp.where(row == 7, edge, rolled[2]))
            return result

        for pop in range(POPS):
            cx, cy, cz = VELOCITY[pop]
            kept = {}

            def source(*key):
                if key not in kept:
                    kept[key] = shifted(pop, *key)
                return kept[key]

            def along_y(group, dz):
                values = source(group, None if group == 2 else 0, 0, dz)
                if cy == 0:
                    return values
                other = (group - cy) % 3
                if group != 2 and other != 2:
                    carried = source(other, 0, 0, dz)
                else:
                    carried = source(other, cy if group == 2 else 0, -cy, dz)
                mask = lane >= 112 if cy > 0 else lane < 16
                return [jnp.where(mask, b, a) for a, b in zip(values, carried)]

            for group in groups:
                values = along_y(group, 0)
                turn = (16 * cy + cz) % 128
                if turn:
                    values = [pltpu.roll(value, turn, axis=1) for value in values]
                if cz:
                    turn = (16 * cy - 15 * cz) % 128
                    wrapped = [pltpu.roll(value, turn, axis=1) for value in along_y(group, -cz)]
                    mask = lane % 16 == (0 if cz > 0 else 15)
                    values = [jnp.where(mask, b, a) for a, b in zip(values, wrapped)]
                for v, value in enumerate(values[:vregs]):
                    if pop:
                        value = jnp.where(value != value, load("own", OPPOSITE[pop], group, v), value)
                    if finish is not None:
                        is_fluid = flags[group // 2][
                            aligned((FLAG0 + s) * PAIR + group * GROUP + v * 8), :
                        ]
                        value = jnp.where(is_fluid > 0.0, value, 0.0)
                    target = pop * PLANE + group * GROUP + v * 8
                    h_view[target : target + 8, :] = value

    @pl.loop(0, SLOTS)
    def _(s):
        one_slot(s)
        if finish is not None:
            finish(s)


def join_kernel(
    cells,
    mate_msg,
    other_msg,
    mate2_msg,
    other2_msg,
    post_ref,
    slots,
    low_msg,
    high_msg,
    low2_msg,
    high2_msg,
):
    sort_messages(
        mate_msg, other_msg, mate2_msg, other2_msg, low_msg, high_msg, low2_msg, high2_msg
    )
    for i, (ref, row) in enumerate(((low_msg, TABLE), (cells, CELLS), (high_msg, TABLE))):
        slots[8 * i : 8 * i + 8, :] = first_rows(ref[row : row + 8, :])

    from_low, from_high, low_low, low_me, high_high, high_me = landed_slots(cells)
    post_ref[PLANES * PAIR :, :] = jnp.full((POPS * PAIR, 128), jnp.nan, jnp.float32)
    for q in range(PLANES):
        for y in range(2):
            start = q * PAIR + y * GROUP
            post_ref[start : start + EDGE, :] = cells[
                q * CELL + y * EDGE : q * CELL + (y + 1) * EDGE, :
            ]
    for s, (slot, msg) in itertools.product(
        range(SLOTS), ((from_low, low_msg), (from_high, high_msg))
    ):

        @pl.when(slot == s)
        def _():
            for p in range(POPS):
                for v in range(2):
                    rim = rim_of(msg, p, v)
                    row = (s * POPS + p) * PAIR + v * 8
                    post_ref[row : row + 8, :] = rim
                    post_ref[row + GROUP : row + GROUP + 8, :] = rim

    for msg, row0, step, first in ((high_msg, 16, 1, 2), (low_msg, 23, -1, 1)):
        for y in range(2):
            for count, planes, row, source in strip_rows(first, row0, step):
                source += y * LAYERS
                post_ref[planes(PAIR, row + y * GROUP), :] = msg[source : source + count, :]
    for s in range(SLOTS):
        for slot, msg, row0 in (
            (low_low, low2_msg, 21),
            (low_me, cells.at[OWN2:], 21),
            (high_high, high2_msg, 16),
            (high_me, cells.at[OWN2 + 6 * GROUP :], 16),
        ):

            @pl.when(slot == s)
            def _():
                for y in range(2):
                    for k in range(3):
                        row = s * POPS * PAIR + y * GROUP + row0 + k
                        source = (y * 3 + k) * GROUP
                        post_ref[pl.ds(row, POPS, stride=PAIR), :] = msg[source : source + POPS, :]
    hide_walls(post_ref, PAIR)


def first_rows(slot):
    slot = slot.astype(jnp.int32)
    return jnp.where(slot == SLOTS, NOWHERE, slot * (POPS * GROUP))


def outer_kernel(
    own_slots, first_post, near_msg, far_msg, slots, outer_ref, next_ref, h_ref, table, sem
):
    even = is_even("cross")

    def received(row):
        near, far = near_msg[row : row + 8, :], far_msg[row : row + 8, :]
        return jnp.where(even, far, near), jnp.where(even, near, far)

    for i in range(3):
        south, north = received(EDGE_TABLE + 8 * i)
        slots[24 * i : 24 * i + 8, :] = first_rows(south)
        slots[24 * i + 8 : 24 * i + 16, :] = own_slots[8 * i : 8 * i + 8, :]
        slots[24 * i + 16 : 24 * i + 24, :] = first_rows(north)
    table_copy = pltpu.make_async_copy(slots, table, sem)
    table_copy.start()

    nothing = jnp.full((8, 128), jnp.nan, jnp.float32)
    for row in range(0, POPS * GROUP, 8):
        outer_ref[NOWHERE + row : NOWHERE + row + 8, :] = nothing
        next_ref[NOWHERE + row : NOWHERE + row + 8, :] = nothing
    lane = lanes_iota()
    for v in range(3):

        def rows(q):
            return slice(q * GROUP + v * 8, q * GROUP + v * 8 + 8)

        for quad in range(QUADS):
            south, north = received(quad * GROUP + v * 8)
            for k in range(4):
                value = jnp.where(lane // 32 == (k + 3) % 4, south, north)
                if k:
                    value = pltpu.roll(value, 128 - 32 * k, axis=1)
                outer_ref[rows(4 * quad + k), :] = value
        for part in range(3):
            values = received(FAR + part * GROUP + v * 8)
            for planes, target, value in zip((NORTHWARD, SOUTHWARD), (80, 32), values):
                for k, q in enumerate(planes[8 * part : 8 * part + 8]):
                    moved = pltpu.roll(value, (target - 16 * k) % 128, axis=1)
                    outer_ref[rows(q), :] = jnp.where(
                        lane // 16 == target // 16, moved, outer_ref[rows(q), :]
                    )
    for row in range(FLAG0 * GROUP, NOWHERE, 8):
        next_ref[row : row + 8, :] = outer_ref[row : row + 8, :]
    hide_walls(outer_ref, GROUP)
    table_copy.wait()
    flags = (first_post, outer_ref)
    stream_all(flags, h_ref, flags, table, (2,), 3)
    collide_all(h_ref, flags, (None, next_ref), ((2,),))


def steps_kernel(
    slots,
    first_post,
    first_outer,
    next_outer,
    cells,
    mate_msg,
    other_msg,
    mate_rest,
    passed_rest,
    passed2_rest,
    out_hbm,
    h_ref,
    post_ref,
    outer_ref,
    out,
    table,
    sems,
):
    table_copy = pltpu.make_async_copy(slots, table, sems.at[SLOTS])
    table_copy.start()
    post_ref[...] = first_post[...]
    nothing = jnp.full((8, 128), jnp.nan, jnp.float32)
    for row in range(0, POPS * GROUP, 8):
        outer_ref[NOWHERE + row : NOWHERE + row + 8, :] = nothing

    def rest(row, is_mate):
        if is_mate:
            return mate_rest[row : row + 8, :]
        if row < HALF:
            return passed_rest[row : row + 8, :]
        return passed2_rest[row - HALF : row - HALF + 8, :]

    from_low, from_high = landed_slots(cells)[:2]
    lane = lanes_iota()
    even = is_even("curve")
    odd = jnp.logical_not(even)
    for s, (slot, wanted, msg, is_mate) in itertools.product(
        range(SLOTS),
        (
            (from_low, odd, mate_msg, True),
            (from_low, even, other_msg, False),
            (from_high, even, mate_msg, True),
            (from_high, odd, other_msg, False),
        ),
    ):

        @pl.when((slot == s) & wanted)
        def _():
            for v in range(2):
                starts = [(FLAG0 + s) * PAIR + y * GROUP + v * 8 for y in range(2)]
                fluid = [first_post[row : row + 8, :] > 0.0 for row in starts]
                for p in range(POPS):
                    rim = rim_of(msg, p, v)
                    row = p * EDGE + v * 8
                    wide = rest(row, is_mate)
                    row = (POPS + p // 2) * EDGE + v * 8
                    middle = rest(row, is_mate)
                    if p % 2:
                        middle = pltpu.roll(middle, 64, axis=1)
                    first = jnp.where(lane < 32, rim, wide)
                    second = jnp.where(lane < 32, wide, jnp.where(lane < 96, middle, rim))
                    row = (s * POPS + p) * PAIR + v * 8
                    post_ref[row : row + 8, :] = jnp.where(fluid[0], first, jnp.nan)
                    row += GROUP
                    post_ref[row : row + 8, :] = jnp.where(fluid[1], second, jnp.nan)

    def finish(s):
        for x in range(EDGE):
            for y in range(2):
                tile = 2 * x + y
                for p, size in ((0, 8), (8, 8), (16, 3)):
                    row = s * SLOT + (p * PLANE + y * GROUP + x)
                    out[s, p : p + size, 128 * tile : 128 * tile + 128] = h_ref[
                        pl.ds(row, size, stride=PLANE), :
                    ]
        pltpu.make_async_copy(out.at[s], out_hbm.at[s], sems.at[s]).start()

    table_copy.wait()
    flags = (first_post, first_outer)
    stream_all((post_ref, first_outer), h_ref, flags, table, (0, 1), 3)
    collide_all(h_ref, flags, (post_ref, None), ((0, 1),))
    posts = (post_ref, next_outer)
    for _ in range(STEPS - 2):
        stream_all(posts, h_ref, flags, table, (0, 1, 2), 3)
        posts = (post_ref, outer_ref)
        collide_all(h_ref, flags, posts)
    stream_all(posts, h_ref, flags, table, (0, 1), 2, finish)
    for s in range(SLOTS):
        pltpu.make_async_copy(out.at[s], out_hbm.at[s], sems.at[s]).wait()


def swapped(value, axis, unit=1):
    count = lax.axis_size(axis)
    results = []
    for which in (0, 1):
        others = [i + (unit if i // unit % 2 == which else -unit) for i in range(count)]
        pairs = [(i, j if 0 <= j < count else i) for i, j in enumerate(others)]
        results.append(lax.ppermute(value[which], axis, pairs))
    return results


def rows128(count):
    return jax.ShapeDtypeStruct((count, 128), jnp.float32)


def call(kernel, in_spaces, out_spaces, outs, ins, scratch, limit=LIMIT, cost=None):
    spaces = {
        "S": pl.BlockSpec(memory_space=pltpu.SMEM),
        "V": pl.BlockSpec(memory_space=pltpu.VMEM),
        "H": pl.BlockSpec(memory_space=pltpu.HBM),
    }
    return pl.pallas_call(
        kernel,
        out_shape=outs,
        in_specs=[spaces[x] for x in in_spaces],
        out_specs=[spaces[x] for x in out_spaces],
        scratch_shapes=scratch,
        compiler_params=pltpu.CompilerParams(vmem_limit_bytes=limit),
        cost_estimate=cost,
    )(*ins)


def per_device(populations, site_flags, neighbours, migrations, counts):
    sizes = (lax.axis_size("curve"), lax.axis_size("cross"))
    moves = migrations.T
    floats = lambda rows: pltpu.VMEM((rows, 128), jnp.float32)
    messages = [
        OWN2 + 12 * GROUP,
        STRIPS + 2 * LAYERS,
        STRIPS + 2 * LAYERS,
        6 * GROUP,
        6 * GROUP,
        REST,
    ]
    cells, mate_msg, other_msg, mate2_msg, other2_msg, rest_msg, rest2_msg = call(
        functools.partial(pack_kernel, *sizes),
        "HHHHH",
        "HHHHHHH",
        [rows128(rows) for rows in (*messages, REST - HALF)],
        (moves, counts, populations, site_flags, neighbours),
        [
            pltpu.SMEM(moves.shape, jnp.int32),
            pltpu.SMEM(counts.shape, jnp.int32),
            pltpu.VMEM(populations.shape, jnp.float32),
            pltpu.VMEM(site_flags.shape, jnp.int32),
            pltpu.VMEM(neighbours.shape, jnp.int32),
            *[floats(rows) for rows in messages],
            pltpu.VMEM((8, 5888), jnp.float32),
            pltpu.VMEM((128, 384), jnp.bfloat16),
            floats(256),
            floats(8),
            pltpu.SemaphoreType.DMA((4 + SLOTS + 9,)),
        ],
        WIDE_LIMIT,
    )
    mate_msg, other_msg = swapped((mate_msg, other_msg), "curve")
    mate2_msg, other2_msg = swapped((mate2_msg, other2_msg), "curve", 2)
    assert sizes[0] % 2 == 0
    pairs = [(i, i ^ 1) for i in range(sizes[0])]
    mate_rest = lax.ppermute(rest_msg, "curve", pairs)
    last = sizes[0] - 1
    pairs = [(i, max(i - 2, 0) if i % 2 else min(i + 2, last)) for i in range(sizes[0])]
    passed_rest = lax.ppermute(mate_rest[:HALF], "curve", pairs)
    back = [(target, source) for source, target in pairs]
    along_z = lax.ppermute(rest2_msg, "curve", back)
    passed2_rest = lax.ppermute(along_z, "curve", [(i, i ^ 1) for i in range(last + 1)])
    (outer,) = call(spread_kernel, "V", "V", [rows128(PLANES * GROUP)], (cells,), [])
    strips = (cells, mate_msg, other_msg, mate2_msg, other2_msg)
    sorted_rows = [messages[1], messages[1], messages[3], messages[3]]
    near_msg, far_msg = call(
        edge_kernel,
        "VVVVVVV",
        "VV",
        [rows128(NEAR_ROWS), rows128(FAR_ROWS)],
        (outer, *strips, along_z),
        [floats(rows) for rows in [PLANES * GROUP] + sorted_rows],
        cost=pl.CostEstimate(flops=10**10, bytes_accessed=0, transcendentals=0),
    )
    near_msg, far_msg = swapped((near_msg, far_msg), "cross")
    post, own_slots = call(
        join_kernel,
        "VVVVV",
        "VV",
        [rows128(ALL_PLANES * PAIR), jax.ShapeDtypeStruct((24, 128), jnp.int32)],
        strips,
        [floats(rows) for rows in sorted_rows],
    )
    slots, outer_post, next_outer = call(
        outer_kernel,
        "VVVV",
        "VVV",
        [
            jax.ShapeDtypeStruct((72, 128), jnp.int32),
            rows128(ALL_PLANES * GROUP),
            rows128(ALL_PLANES * GROUP),
        ],
        (own_slots, post, near_msg, far_msg),
        [floats(SLOTS * SLOT), pltpu.SMEM((72, 128), jnp.int32), pltpu.SemaphoreType.DMA],
    )
    arriving = (cells, mate_msg, other_msg, mate_rest, passed_rest, passed2_rest)
    return call(
        steps_kernel,
        "VVVVVVVVVV",
        "H",
        [jax.ShapeDtypeStruct(populations.shape, jnp.float32)],
        (slots, post, outer_post, next_outer, *arriving),
        [
            floats(SLOTS * SLOT),
            floats(ALL_PLANES * PAIR),
            floats(ALL_PLANES * GROUP),
            pltpu.VMEM(populations.shape, jnp.float32),
            pltpu.SMEM((72, 128), jnp.int32),
            pltpu.SemaphoreType.DMA((SLOTS + 1,)),
        ],
    )[0]


def solution(mesh):
    return jax.shard_map(
        per_device,
        mesh=mesh,
        in_specs=(
            P(("curve", "cross"), None, None),
            P(("curve", "cross"), None),
            P(("curve", "cross"), None),
            P(),
            P(("curve", "cross")),
        ),
        out_specs=P(("curve", "cross"), None, None),
        check_vma=False,
    )
```

```python
import functools
import itertools

import jax
import jax.numpy as jnp
import numpy as np
from jax import lax
from jax.experimental import pallas as pl
from jax.experimental.pallas import tpu as pltpu
from jax.sharding import PartitionSpec as P

EDGE = 16
STEPS = 3
SLOTS = 3
POPS = 19
PLANES = SLOTS * POPS + SLOTS
FLAG0 = SLOTS * POPS
GROUP = 24
PLANE = 3 * GROUP
SLOT = POPS * PLANE
CELL = 40
CELLS = PLANES * CELL
LANDINGS = CELLS + 8
OWN2 = LANDINGS + 8
OUTWARD = SLOTS * 5 + SLOTS
LAYERS = 2 * PLANES + OUTWARD
RIM = 11 * EDGE
REST = POPS * EDGE + 10 * EDGE
PAIR = 2 * GROUP
QUADS = PLANES // 4
TABLE = RIM
STRIPS = RIM + 8
FAR = QUADS * GROUP
EDGE_TABLE = FAR + 3 * GROUP
EDGE_ROWS = EDGE_TABLE + 24
NEAR_ROWS, FAR_ROWS = EDGE_ROWS + 16, EDGE_ROWS + 24
NOWHERE = PLANES * GROUP
ALL_PLANES = PLANES + POPS
LIMIT = 20 * 1024 * 1024
WIDE_LIMIT = 127 * 512 * 1024

VELOCITY = [
    (0, 0, 0),
    (1, 0, 0),
    (-1, 0, 0),
    (0, 1, 0),
    (0, -1, 0),
    (0, 0, 1),
    (0, 0, -1),
    (1, 1, 0),
    (-1, -1, 0),
    (1, -1, 0),
    (-1, 1, 0),
    (1, 0, 1),
    (-1, 0, -1),
    (1, 0, -1),
    (-1, 0, 1),
    (0, 1, 1),
    (0, -1, -1),
    (0, 1, -1),
    (0, -1, 1),
]
NORTHWARD, SOUTHWARD = (
    [s * POPS + p for s in range(SLOTS) for p in range(POPS) if VELOCITY[p][1] == side]
    + [FLAG0 + s for s in range(SLOTS)]
    for side in (1, -1)
)
THIRD = [
    (pop, source, *((32 + 16 * k, 9) if k < 4 else (16 * (k - 4), 10)))
    for k, (pop, source) in enumerate(
        [(p, 32) for p in (4, 8, 9, 16, 18)] + [(p, 80) for p in (3, 7, 10, 15, 17)]
    )
]
OPPOSITE = [0, 2, 1, 4, 3, 6, 5, 8, 7, 10, 9, 12, 11, 14, 13, 16, 15, 18, 17]


def lanes_iota():
    return lax.broadcasted_iota(jnp.int32, (8, 128), 1)


def is_even(axis, unit=1):
    return lax.rem(lax.axis_index(axis) // unit, 2) == 0


def rows_iota():
    return lax.broadcasted_iota(jnp.int32, (8, 128), 0)


def aligned(start, size=8):
    return pl.ds(pl.multiple_of(start, 8), size)


def move_slots(moves, curve_size, cross_size):
    curve, cross = lax.axis_index("curve"), lax.axis_index("cross")

    def landed(source, target):
        inside = (source >= 0) & (source < curve_size) & (target >= 0) & (target < curve_size)
        row = jnp.clip(source, 0, curve_size - 1) * cross_size + cross
        rank = target * cross_size + cross
        hit = inside & (moves[0, row] >= 0) & (moves[1, row] == rank)
        return jnp.where(hit, moves[2, row], -1)

    return (
        landed(curve - 1, curve),
        landed(curve + 1, curve),
        landed(curve - 2, curve - 1),
        landed(curve, curve - 1),
        landed(curve + 2, curve + 1),
        landed(curve, curve + 1),
    )


def pack_kernel(
    curve_size,
    cross_size,
    moves_hbm,
    counts_hbm,
    pops_hbm,
    flags_hbm,
    neighbours_hbm,
    cells_hbm,
    mate_hbm,
    other_hbm,
    mate2_hbm,
    other2_hbm,
    rest_hbm,
    moves,
    counts,
    pops,
    flags,
    neighbours,
    cells,
    up_msg,
    down_msg,
    up2_msg,
    down2_msg,
    rest_msg,
    wide_flags,
    plane_flags,
    site_flags,
    near,
    sems,
):
    started = []

    def copy(source, target):
        one = pltpu.make_async_copy(source, target, sems.at[len(started)])
        one.start()
        started.append(one)
        return one

    flags_copy = copy(flags_hbm, flags)
    copies = [copy(pops_hbm.at[s], pops.at[s]) for s in range(SLOTS)]
    small = [
        copy(neighbours_hbm, neighbours),
        copy(counts_hbm, counts),
        copy(moves_hbm, moves),
    ]
    for one in small:
        one.wait()

    near[...] = jnp.zeros_like(near)
    named = neighbours[...]
    slot = jnp.where(named >= 0, lax.rem(jnp.maximum(named, 0), SLOTS), SLOTS)
    near[0:SLOTS, 0 : named.shape[1]] = slot.astype(jnp.float32)
    for ref, row in ((cells, CELLS), (up_msg, TABLE), (down_msg, TABLE)):
        ref[row : row + 8, :] = near[...]

    wide_flags[...] = jnp.zeros_like(wide_flags)
    flags_copy.wait()
    wide_flags[0:SLOTS, 0 : flags.shape[1]] = flags[...].astype(jnp.float32)
    span = EDGE + 2
    for x in range(EDGE):
        start = (x + 1) * span * span
        base = start // 128 * 128
        window = wide_flags[:, base : base + 512]
        window = pltpu.roll(window, (512 - (start - base)) % 512, axis=1)
        plane_flags[8 * x : 8 * x + 8, :] = window[:, :384].astype(jnp.bfloat16)
    lane_in = lax.broadcasted_iota(jnp.int32, (384, 256), 0)
    site = lax.broadcasted_iota(jnp.int32, (384, 256), 1)
    chosen = lane_in == (site // EDGE + 1) * span + site % EDGE + 1
    product = jnp.dot(
        plane_flags[...],
        jnp.where(chosen, 1.0, 0.0).astype(jnp.bfloat16),
        preferred_element_type=jnp.float32,
    )
    site_flags[0:128, :] = product[:, :128]
    site_flags[128:256, :] = product[:, 128:]
    for s in range(SLOTS):
        live = s < counts[0]
        for y in range(2):
            piece = site_flags[pl.ds(128 * y + s, EDGE, stride=8), :]
            is_fluid = (piece == 1.0) & live
            row = (FLAG0 + s) * CELL + y * EDGE
            cells[row : row + EDGE, :] = jnp.where(is_fluid, 1.0, 0.0)

    for s in range(SLOTS):
        copies[s].wait()
        for x in range(EDGE):
            for y in range(2):
                tile = 2 * x + y
                for p, size in ((0, 8), (8, 8), (16, 3)):
                    row = (s * POPS + p) * CELL + y * EDGE + x
                    cells[pl.ds(row, size, stride=CELL), :] = pops[
                        s, p : p + size, 128 * tile : 128 * tile + 128
                    ]

    @pl.loop(0, SLOTS)
    def _(s):
        @pl.loop(0, 4, unroll=2)
        def _(c):
            base = s * (POPS * CELL) + c * 8
            view = cells.at[aligned(base, (POPS - 1) * CELL + 8), :]
            h = [view[p * CELL : p * CELL + 8, :] for p in range(POPS)]
            for p, value in enumerate(collided(h)):
                view[p * CELL : p * CELL + 8, :] = value

    for i, slot in enumerate(move_slots(moves, curve_size, cross_size)):
        value = jnp.full((1, 128), slot, jnp.int32)
        cells[LANDINGS + i : LANDINGS + i + 1, :] = value.astype(jnp.float32)

    body_copy = copy(cells.at[:OWN2], cells_hbm.at[:OWN2])

    for y in range(2):
        for msg, x0, first in ((up_msg, 15, 1), (down_msg, 0, 2)):
            step = -1 if x0 else 1
            for k in range(2):
                out = STRIPS + y * LAYERS + k * PLANES
                msg[out : out + PLANES, :] = cells[
                    pl.ds(y * EDGE + x0 + step * k, PLANES, stride=CELL), :
                ]
            row = y * EDGE + x0 + 2 * step
            out = STRIPS + y * LAYERS + 2 * PLANES
            for s in range(SLOTS):
                base = s * POPS * CELL + row
                msg[out + 5 * s : out + 5 * s + 1, :] = cells[pl.ds(base + first * CELL, 1), :]
                msg[out + 5 * s + 1 : out + 5 * s + 5, :] = cells[
                    pl.ds(base + (first + 6) * CELL, 4, stride=2 * CELL), :
                ]
            msg[out + 5 * SLOTS : out + OUTWARD, :] = cells[
                pl.ds(FLAG0 * CELL + row, SLOTS, stride=CELL), :
            ]

    here = lax.axis_index("curve") * cross_size + lax.axis_index("cross")
    leaving = jnp.maximum(moves[0, here], 0)
    lane = lanes_iota()
    for v in range(2):
        halves = [
            [cells[aligned(leaving * (POPS * CELL) + p * CELL + y * EDGE + v * 8), :] for y in (0, 1)]
            for p in range(POPS)
        ]
        outer = [jnp.where(lane < 64, first, second) for first, second in halves]
        middle = (lane >= 32) & (lane < 96)
        sets = [
            jnp.where(middle, pltpu.roll(outer[p + 1], 64, axis=1), outer[p])
            for p in range(0, POPS - 1, 2)
        ]
        sets += [outer[POPS - 1], jnp.zeros_like(outer[0])]
        for pop, source, target, which in THIRD:
            moved = pltpu.roll(outer[pop], (target - source) % 128, axis=1)
            sets[which] = jnp.where(lane // 16 == target // 16, moved, sets[which])
        for k, value in enumerate(sets):
            row = k * EDGE + v * 8
            up_msg[row : row + 8, :] = value
            down_msg[row : row + 8, :] = value
        for p, (first, second) in enumerate(halves):
            row = p * EDGE + v * 8
            rest_msg[row : row + 8, :] = jnp.where(lane < 32, second, first)
        for p in range(0, POPS, 2):
            value = halves[p][1]
            if p + 1 < POPS:
                value = jnp.where(middle, value, pltpu.roll(halves[p + 1][1], 64, axis=1))
            row = (POPS + p // 2) * EDGE + v * 8
            rest_msg[row : row + 8, :] = value
    for s in range(SLOTS):

        @pl.when(leaving == s)
        def _():
            for y in range(2):
                for k in range(3):
                    out = (y * 3 + k) * GROUP
                    row = s * POPS * CELL + y * EDGE + k
                    up2_msg[out : out + POPS, :] = cells[pl.ds(row + 13, POPS, stride=CELL), :]
                    down2_msg[out : out + POPS, :] = cells[pl.ds(row, POPS, stride=CELL), :]

    cells[OWN2 : OWN2 + 6 * GROUP, :] = up2_msg[...]
    cells[OWN2 + 6 * GROUP :, :] = down2_msg[...]
    last = [copy(cells.at[OWN2:], cells_hbm.at[OWN2:]), copy(rest_msg, rest_hbm)]
    count = len(started)
    for i, (up, down, mate, other, unit) in enumerate(
        ((up_msg, down_msg, mate_hbm, other_hbm, 1), (up2_msg, down2_msg, mate2_hbm, other2_hbm, 2))
    ):
        first, second = sems.at[count + 2 * i], sems.at[count + 2 * i + 1]
        even = is_even("curve", unit)

        @pl.when(even)
        def _():
            pltpu.make_async_copy(up, mate, first).start()
            pltpu.make_async_copy(down, other, second).start()

        @pl.when(jnp.logical_not(even))
        def _():
            pltpu.make_async_copy(down, mate, first).start()
            pltpu.make_async_copy(up, other, second).start()

        last.append(pltpu.make_async_copy(up, mate, first))
        last.append(pltpu.make_async_copy(down, other, second))
    body_copy.wait()
    for one in last:
        one.wait()


def spread_kernel(cells, outer):
    low = lanes_iota() < 64
    for q in range(PLANES):
        for v in range(2):
            row = q * CELL + v * 8
            first, second = cells[row : row + 8, :], cells[row + EDGE : row + EDGE + 8, :]
            row = q * GROUP + v * 8
            outer[row : row + 8, :] = jnp.where(low, first, second)


def sort_messages(mate_msg, other_msg, mate2_msg, other2_msg, low_msg, high_msg, low2, high2):
    for mate, other, low, high, unit in (
        (mate_msg, other_msg, low_msg, high_msg, 1),
        (mate2_msg, other2_msg, low2, high2, 2),
    ):
        even = is_even("curve", unit)

        @pl.when(even)
        def _():
            low[...] = other[...]
            high[...] = mate[...]

        @pl.when(jnp.logical_not(even))
        def _():
            low[...] = mate[...]
            high[...] = other[...]


def landed_slots(cells):
    return [jnp.max(cells[LANDINGS + i : LANDINGS + i + 1, :]) for i in range(6)]


def rim_of(msg, p, v):
    row = p // 2 * EDGE + v * 8
    value = msg[row : row + 8, :]
    return pltpu.roll(value, 64, axis=1) if p % 2 else value


def sel4(parts, lane):
    first = jnp.where(lane < 32, parts[0], parts[1])
    second = jnp.where(lane < 96, parts[2], parts[3])
    return jnp.where(lane < 64, first, second)


def strip_rows(first, row0, step):
    pieces = []
    for k in range(2):
        pieces.append(
            (PLANES, lambda size, row: pl.ds(row, PLANES, stride=size), row0 + step * k, STRIPS + k * PLANES)
        )
    row, source = row0 + 2 * step, STRIPS + 2 * PLANES
    for s in range(SLOTS):
        plane = s * POPS + first
        pieces.append((1, lambda size, row, plane=plane: pl.ds(plane * size + row, 1), row, source))
        pieces.append(
            (
                4,
                lambda size, row, plane=plane: pl.ds(
                    (plane + 6) * size + row, 4, stride=2 * size
                ),
                row,
                source + 1,
            )
        )
        source += 5
    pieces.append(
        (SLOTS, lambda size, row: pl.ds(FLAG0 * size + row, SLOTS, stride=size), row, source)
    )
    return pieces


def edge_kernel(
    own_outer,
    cells,
    mate_msg,
    other_msg,
    mate2_msg,
    other2_msg,
    near_msg,
    far_msg,
    outer,
    low_msg,
    high_msg,
    low2_msg,
    high2_msg,
):
    sort_messages(
        mate_msg, other_msg, mate2_msg, other2_msg, low_msg, high_msg, low2_msg, high2_msg
    )
    from_low, from_high, low_low, low_me, high_high, high_me = landed_slots(cells)
    low = lanes_iota() < 64
    for q in range(PLANES):
        for v in range(2):
            row = q * GROUP + v * 8
            outer[row : row + 8, :] = own_outer[row : row + 8, :]

    def both(first, second):
        lane = lax.broadcasted_iota(jnp.int32, first.shape, 1)
        return jnp.where(lane < 64, first, second)

    for msg, row0, step, first in ((high_msg, 16, 1, 2), (low_msg, 23, -1, 1)):
        for count, planes, row, source in strip_rows(first, row0, step):
            outer[planes(GROUP, row), :] = both(
                msg[source : source + count, :],
                msg[LAYERS + source : LAYERS + source + count, :],
            )
    lane = lanes_iota()
    for s, (slot, msg) in itertools.product(
        range(SLOTS), ((from_low, low_msg), (from_high, high_msg))
    ):

        @pl.when(slot == s)
        def _():
            for v in range(2):
                values = [rim_of(msg, p, v) for p in range(POPS)]
                for pop, target, source, which in THIRD:
                    row = which * EDGE + v * 8
                    moved = pltpu.roll(msg[row : row + 8, :], (target - source) % 128, axis=1)
                    values[pop] = jnp.where(lane // 16 == target // 16, moved, values[pop])
                for p, value in enumerate(values):
                    row = (s * POPS + p) * GROUP + v * 8
                    outer[row : row + 8, :] = value

    for s in range(SLOTS):
        for slot, msg, row0 in (
            (low_low, low2_msg, 21),
            (low_me, cells.at[OWN2:], 21),
            (high_high, high2_msg, 16),
            (high_me, cells.at[OWN2 + 6 * GROUP :], 16),
        ):

            @pl.when(slot == s)
            def _():
                for k in range(3):
                    outer[pl.ds(s * POPS * GROUP + row0 + k, POPS, stride=GROUP), :] = both(
                        msg[k * GROUP : k * GROUP + POPS, :],
                        msg[(3 + k) * GROUP : (3 + k) * GROUP + POPS, :],
                    )

    even = is_even("cross")

    def send(row, north, south):
        near_msg[row : row + 8, :] = jnp.where(even, north, south)
        far_msg[row : row + 8, :] = jnp.where(even, south, north)

    for v in range(3):

        def plane(q):
            return outer[q * GROUP + v * 8 : q * GROUP + v * 8 + 8, :]

        for quad in range(QUADS):
            parts = [plane(4 * quad)]
            parts += [pltpu.roll(plane(4 * quad + k), 32 * k, axis=1) for k in (1, 2, 3)]
            send(quad * GROUP + v * 8, sel4(parts[1:] + parts[:1], lane), sel4(parts, lane))
        for part in range(3):
            values = []
            for planes, source in ((NORTHWARD, 80), (SOUTHWARD, 32)):
                value = None
                for k, q in enumerate(planes[8 * part : 8 * part + 8]):
                    moved = pltpu.roll(plane(q), (16 * k - source) % 128, axis=1)
                    value = moved if value is None else jnp.where(lane < 16 * k, value, moved)
                values.append(value)
            send(FAR + part * GROUP + v * 8, *values)
    tables = (low_msg, TABLE), (cells, CELLS), (high_msg, TABLE)
    for i, (ref, row) in enumerate(tables):
        value = ref[row : row + 8, :]
        send(EDGE_TABLE + 8 * i, value, value)


def collided(h):
    shear = 1.0 / 0.6
    rest = h[0]
    sx, dx = h[1] + h[2], h[1] - h[2]
    sy, dy = h[3] + h[4], h[3] - h[4]
    sz, dz = h[5] + h[6], h[5] - h[6]
    s7, d7 = h[7] + h[8], h[7] - h[8]
    s9, d9 = h[9] + h[10], h[9] - h[10]
    s11, d11 = h[11] + h[12], h[11] - h[12]
    s13, d13 = h[13] + h[14], h[13] - h[14]
    s15, d15 = h[15] + h[16], h[15] - h[16]
    s17, d17 = h[17] + h[18], h[17] - h[18]
    txy, txz, tyz = s7 + s9, s11 + s13, s15 + s17
    pxy, pxz, pyz = s7 - s9, s11 - s13, s15 - s17
    ax, bx = d7 + d9, d11 + d13
    ay, by = d7 - d9, d15 + d17
    az, bz = d11 - d13, d15 - d17
    axes = sx + sy + sz
    diags = txy + txz + tyz
    rho = rest * (1.0 / 3.0) + axes * (1.0 / 18.0) + diags * (1.0 / 36.0)
    fx, fy, fz = ax + bx, ay + by, az + bz
    jx = dx * (1.0 / 18.0) + fx * (1.0 / 36.0)
    jy = dy * (1.0 / 18.0) + fy * (1.0 / 36.0)
    jz = dz * (1.0 / 18.0) + fz * (1.0 / 36.0)
    inverse = 1.0 / rho
    ux, uy, uz = jx * inverse, jy * inverse, jz * inverse
    qxx, qyy, qzz = jx * ux, jy * uy, jz * uz
    total = qxx + qyy + qzz

    energy = -10.0 * rest - axes * (11.0 / 18.0) + diags * (8.0 / 36.0)
    energy = (energy + 11.0 * rho - 19.0 * total) * (1.19 / 2394.0)
    square = 4.0 * rest - axes * (4.0 / 18.0) + diags * (1.0 / 36.0)
    square = (square - 3.0 * rho + 5.5 * total) * (1.4 / 252.0)
    axis_x = (3.0 * sx - axes) * (1.0 / 18.0)
    diag_x = (diags - 3.0 * tyz) * (1.0 / 36.0)
    want_x = 3.0 * qxx - total
    stress_x = (axis_x + diag_x - want_x) * (shear / 36.0)
    third_x = (diag_x - 2.0 * axis_x + 0.5 * want_x) * (1.4 / 72.0)
    axis_w = (sy - sz) * (1.0 / 18.0)
    diag_w = (txy - txz) * (1.0 / 36.0)
    want_w = qyy - qzz
    stress_w = (axis_w + diag_w - want_w) * (shear / 12.0)
    third_w = (diag_w - 2.0 * axis_w + 0.5 * want_w) * (1.4 / 24.0)

    rest_out = rest - 3.0 * (12.0 * square - 30.0 * energy)
    common = -18.0 * (11.0 * energy + 4.0 * square)
    along_x = 18.0 * (stress_x - 2.0 * third_x)
    along_w = 18.0 * (stress_w - 2.0 * third_w)
    ex = common + 2.0 * along_x
    ey = common - along_x + along_w
    ez = common - along_x - along_w
    common = 36.0 * (8.0 * energy + square)
    across_x = 36.0 * (stress_x + third_x)
    across_w = 36.0 * (stress_w + third_w)
    exy = common + across_x + across_w
    exz = common + across_x - across_w
    eyz = common - 2.0 * across_x
    cxy = shear * (0.25 * pxy - 9.0 * jx * uy)
    cxz = shear * (0.25 * pxz - 9.0 * jx * uz)
    cyz = shear * (0.25 * pyz - 9.0 * jy * uz)

    def flux(d, f, j):
        return (f * (1.0 / 36.0) - d * (4.0 / 18.0) + j * (2.0 / 3.0)) * (1.2 / 40.0)

    hx, hy, hz = flux(dx, fx, jx), flux(dy, fy, jy), flux(dz, fz, jz)
    mx = (ax - bx) * (1.98 / 8.0)
    my = (by - ay) * (1.98 / 8.0)
    mz = (az - bz) * (1.98 / 8.0)
    hx36, hy36, hz36 = 36.0 * hx, 36.0 * hy, 36.0 * hz
    xy_x, xz_x = hx36 + mx, hx36 - mx
    yz_y, xy_y = hy36 + my, hy36 - my
    xz_z, yz_z = hz36 + mz, hz36 - mz
    ox, oy, oz = -2.0 * hx36, -2.0 * hy36, -2.0 * hz36

    out = [rest_out]

    def pair(i, even, odd):
        out.append(h[i] - (even + odd))
        out.append(h[i + 1] - (even - odd))

    pair(1, ex, ox)
    pair(3, ey, oy)
    pair(5, ez, oz)
    pair(7, exy + cxy, xy_x + xy_y)
    pair(9, exy - cxy, xy_x - xy_y)
    pair(11, exz + cxz, xz_x + xz_z)
    pair(13, exz - cxz, xz_x - xz_z)
    pair(15, eyz + cyz, yz_y + yz_z)
    pair(17, eyz - cyz, yz_y - yz_z)
    return out


def collide_all(h_ref, flags, posts, parts=((0, 1), (2,))):
    for groups in parts:
        ref = posts[groups[0] // 2]
        size = len(groups) * GROUP

        @pl.loop(0, SLOTS)
        def _(s):
            @pl.loop(0, size // 8, unroll=3)
            def _(c):
                is_fluid = flags[groups[0] // 2][aligned((FLAG0 + s) * size + c * 8), :] > 0.0
                start = s * SLOT + groups[0] * GROUP + c * 8
                h_view = h_ref.at[aligned(start, (POPS - 1) * PLANE + 8), :]
                start = s * (POPS * size) + c * 8
                view = ref.at[aligned(start, (POPS - 1) * size + 8), :]
                h = [h_view[p * PLANE : p * PLANE + 8, :] for p in range(POPS)]
                for p, value in enumerate(collided(h)):
                    view[p * size : p * size + 8, :] = jnp.where(is_fluid, value, jnp.nan)


def hide_walls(ref, size):
    @pl.loop(0, SLOTS)
    def _(s):
        @pl.loop(0, size // 8)
        def _(c):
            is_fluid = ref[aligned((FLAG0 + s) * size + c * 8), :] > 0.0
            start = s * (POPS * size) + c * 8
            view = ref.at[aligned(start, (POPS - 1) * size + 8), :]
            for p in range(POPS):
                row = p * size
                view[row : row + 8, :] = jnp.where(is_fluid, view[row : row + 8, :], jnp.nan)


def stream_all(posts, h_ref, flags, table, groups, vregs, finish=None):
    lane = lanes_iota()
    row = rows_iota()
    low = lane < 64

    def one_slot(s):
        views = {}

        def view(which, key):
            if (which, key) not in views:
                start = s * (POPS * GROUP) if key == "own" else table[key[0] * 8 + s, key[1]]
                start = start if which else 2 * start
                views[which, key] = posts[which].at[
                    aligned(start, POPS * (GROUP if which else PAIR)), :
                ]
            return views[which, key]

        def load(key, pop, group, v):
            if group == 2:
                row = pop * GROUP + v * 8
            else:
                row = pop * PAIR + group * GROUP + v * 8
            return view(group // 2, key)[row : row + 8, :]

        h_view = h_ref.at[aligned(s * SLOT, SLOT), :]

        def shifted(pop, group, j, dy, dz):
            cx = VELOCITY[pop][0]

            def rows(key, v):
                return load(key, pop, group, v)

            def look(i, j, dx, v):
                if (dx, dy, dz) == (0, 0, 0):
                    return rows("own", v)
                if j is None:
                    return jnp.where(low, look(i, 1, dx, v), look(i, -1, dx, v))
                region = (i + 1) * 3 + j + 1
                return rows((region, VELOCITY.index((dx, dy, dz)) - 1), v)

            need_last = vregs == 3
            values = [look(0, j, 0, 0), look(0, j, 0, 1)]
            if need_last:
                if dy == 0 and dz == 0:
                    values.append(rows("own", 2))
                else:
                    values.append(jnp.where(row < 4, look(1, j, 0, 2), look(-1, j, 0, 2)))
            if cx == 0:
                return values
            turn = 1 if cx > 0 else 7
            rolled = [pltpu.roll(value, turn, axis=0) for value in values]
            if cx > 0:
                before = pltpu.roll(look(0, j, -1, 2), 1, axis=0)
                result = [
                    jnp.where(row == 0, before, rolled[0]),
                    jnp.where(row == 0, rolled[0], rolled[1]),
                ]
                if need_last:
                    edge = pltpu.roll(look(1, j, -1, 1), 1, axis=0)
                    result.append(jnp.where(row == 0, edge, rolled[2]))
                return result
            after = pltpu.roll(look(0, j, 1, 2), 7, axis=0)
            result = [
                jnp.where(row == 7, rolled[1], rolled[0]),
                jnp.where(row == 7, after, rolled[1]),
            ]
            if need_last:
                edge = pltpu.roll(look(-1, j, 1, 0), 7, axis=0)
                result.append(jnp.where(row == 7, edge, rolled[2]))
            return result

        for pop in range(POPS):
            cx, cy, cz = VELOCITY[pop]
            kept = {}

            def source(*key):
                if key not in kept:
                    kept[key] = shifted(pop, *key)
                return kept[key]

            def along_y(group, dz):
                values = source(group, None if group == 2 else 0, 0, dz)
                if cy == 0:
                    return values
                other = (group - cy) % 3
                if group != 2 and other != 2:
                    carried = source(other, 0, 0, dz)
                else:
                    carried = source(other, cy if group == 2 else 0, -cy, dz)
                mask = lane >= 112 if cy > 0 else lane < 16
                return [jnp.where(mask, b, a) for a, b in zip(values, carried)]

            for group in groups:
                values = along_y(group, 0)
                turn = (16 * cy + cz) % 128
                if turn:
                    values = [pltpu.roll(value, turn, axis=1) for value in values]
                if cz:
                    turn = (16 * cy - 15 * cz) % 128
                    wrapped = [pltpu.roll(value, turn, axis=1) for value in along_y(group, -cz)]
                    mask = lane % 16 == (0 if cz > 0 else 15)
                    values = [jnp.where(mask, b, a) for a, b in zip(values, wrapped)]
                for v, value in enumerate(values[:vregs]):
                    if pop:
                        value = jnp.where(value != value, load("own", OPPOSITE[pop], group, v), value)
                    if finish is not None:
                        is_fluid = flags[group // 2][
                            aligned((FLAG0 + s) * PAIR + group * GROUP + v * 8), :
                        ]
                        value = jnp.where(is_fluid > 0.0, value, 0.0)
                    target = pop * PLANE + group * GROUP + v * 8
                    h_view[target : target + 8, :] = value

    @pl.loop(0, SLOTS)
    def _(s):
        one_slot(s)
        if finish is not None:
            finish(s)


def join_kernel(
    cells,
    mate_msg,
    other_msg,
    mate2_msg,
    other2_msg,
    post_ref,
    slots,
    low_msg,
    high_msg,
    low2_msg,
    high2_msg,
):
    sort_messages(
        mate_msg, other_msg, mate2_msg, other2_msg, low_msg, high_msg, low2_msg, high2_msg
    )
    for i, (ref, row) in enumerate(((low_msg, TABLE), (cells, CELLS), (high_msg, TABLE))):
        slots[8 * i : 8 * i + 8, :] = first_rows(ref[row : row + 8, :])

    from_low, from_high, low_low, low_me, high_high, high_me = landed_slots(cells)
    post_ref[PLANES * PAIR :, :] = jnp.full((POPS * PAIR, 128), jnp.nan, jnp.float32)
    for q in range(PLANES):
        for y in range(2):
            start = q * PAIR + y * GROUP
            post_ref[start : start + EDGE, :] = cells[
                q * CELL + y * EDGE : q * CELL + (y + 1) * EDGE, :
            ]
    for s, (slot, msg) in itertools.product(
        range(SLOTS), ((from_low, low_msg), (from_high, high_msg))
    ):

        @pl.when(slot == s)
        def _():
            for p in range(POPS):
                for v in range(2):
                    rim = rim_of(msg, p, v)
                    row = (s * POPS + p) * PAIR + v * 8
                    post_ref[row : row + 8, :] = rim
                    post_ref[row + GROUP : row + GROUP + 8, :] = rim

    for msg, row0, step, first in ((high_msg, 16, 1, 2), (low_msg, 23, -1, 1)):
        for y in range(2):
            for count, planes, row, source in strip_rows(first, row0, step):
                source += y * LAYERS
                post_ref[planes(PAIR, row + y * GROUP), :] = msg[source : source + count, :]
    for s in range(SLOTS):
        for slot, msg, row0 in (
            (low_low, low2_msg, 21),
            (low_me, cells.at[OWN2:], 21),
            (high_high, high2_msg, 16),
            (high_me, cells.at[OWN2 + 6 * GROUP :], 16),
        ):

            @pl.when(slot == s)
            def _():
                for y in range(2):
                    for k in range(3):
                        row = s * POPS * PAIR + y * GROUP + row0 + k
                        source = (y * 3 + k) * GROUP
                        post_ref[pl.ds(row, POPS, stride=PAIR), :] = msg[source : source + POPS, :]
    hide_walls(post_ref, PAIR)


def first_rows(slot):
    slot = slot.astype(jnp.int32)
    return jnp.where(slot == SLOTS, NOWHERE, slot * (POPS * GROUP))


def outer_kernel(
    own_slots, first_post, near_msg, far_msg, slots, outer_ref, next_ref, h_ref, table, sem
):
    even = is_even("cross")

    def received(row):
        near, far = near_msg[row : row + 8, :], far_msg[row : row + 8, :]
        return jnp.where(even, far, near), jnp.where(even, near, far)

    for i in range(3):
        south, north = received(EDGE_TABLE + 8 * i)
        slots[24 * i : 24 * i + 8, :] = first_rows(south)
        slots[24 * i + 8 : 24 * i + 16, :] = own_slots[8 * i : 8 * i + 8, :]
        slots[24 * i + 16 : 24 * i + 24, :] = first_rows(north)
    table_copy = pltpu.make_async_copy(slots, table, sem)
    table_copy.start()

    nothing = jnp.full((8, 128), jnp.nan, jnp.float32)
    for row in range(0, POPS * GROUP, 8):
        outer_ref[NOWHERE + row : NOWHERE + row + 8, :] = nothing
        next_ref[NOWHERE + row : NOWHERE + row + 8, :] = nothing
    lane = lanes_iota()
    for v in range(3):

        def rows(q):
            return slice(q * GROUP + v * 8, q * GROUP + v * 8 + 8)

        for quad in range(QUADS):
            south, north = received(quad * GROUP + v * 8)
            for k in range(4):
                value = jnp.where(lane // 32 == (k + 3) % 4, south, north)
                if k:
                    value = pltpu.roll(value, 128 - 32 * k, axis=1)
                outer_ref[rows(4 * quad + k), :] = value
        for part in range(3):
            values = received(FAR + part * GROUP + v * 8)
            for planes, target, value in zip((NORTHWARD, SOUTHWARD), (80, 32), values):
                for k, q in enumerate(planes[8 * part : 8 * part + 8]):
                    moved = pltpu.roll(value, (target - 16 * k) % 128, axis=1)
                    outer_ref[rows(q), :] = jnp.where(
                        lane // 16 == target // 16, moved, outer_ref[rows(q), :]
                    )
    for row in range(FLAG0 * GROUP, NOWHERE, 8):
        next_ref[row : row + 8, :] = outer_ref[row : row + 8, :]
    hide_walls(outer_ref, GROUP)
    table_copy.wait()
    flags = (first_post, outer_ref)
    stream_all(flags, h_ref, flags, table, (2,), 3)
    collide_all(h_ref, flags, (None, next_ref), ((2,),))


def steps_kernel(
    slots,
    first_post,
    first_outer,
    next_outer,
    cells,
    mate_msg,
    other_msg,
    mate_rest,
    passed_rest,
    out_hbm,
    h_ref,
    post_ref,
    outer_ref,
    out,
    table,
    sems,
):
    table_copy = pltpu.make_async_copy(slots, table, sems.at[SLOTS])
    table_copy.start()
    post_ref[...] = first_post[...]
    nothing = jnp.full((8, 128), jnp.nan, jnp.float32)
    for row in range(0, POPS * GROUP, 8):
        outer_ref[NOWHERE + row : NOWHERE + row + 8, :] = nothing

    from_low, from_high = landed_slots(cells)[:2]
    lane = lanes_iota()
    even = is_even("curve")
    odd = jnp.logical_not(even)
    for s, (slot, wanted, msg, rest) in itertools.product(
        range(SLOTS),
        (
            (from_low, odd, mate_msg, mate_rest),
            (from_low, even, other_msg, passed_rest),
            (from_high, even, mate_msg, mate_rest),
            (from_high, odd, other_msg, passed_rest),
        ),
    ):

        @pl.when((slot == s) & wanted)
        def _():
            for v in range(2):
                starts = [(FLAG0 + s) * PAIR + y * GROUP + v * 8 for y in range(2)]
                fluid = [first_post[row : row + 8, :] > 0.0 for row in starts]
                for p in range(POPS):
                    rim = rim_of(msg, p, v)
                    row = p * EDGE + v * 8
                    wide = rest[row : row + 8, :]
                    row = (POPS + p // 2) * EDGE + v * 8
                    middle = rest[row : row + 8, :]
                    if p % 2:
                        middle = pltpu.roll(middle, 64, axis=1)
                    first = jnp.where(lane < 32, rim, wide)
                    second = jnp.where(lane < 32, wide, jnp.where(lane < 96, middle, rim))
                    row = (s * POPS + p) * PAIR + v * 8
                    post_ref[row : row + 8, :] = jnp.where(fluid[0], first, jnp.nan)
                    row += GROUP
                    post_ref[row : row + 8, :] = jnp.where(fluid[1], second, jnp.nan)

    def finish(s):
        for x in range(EDGE):
            for y in range(2):
                tile = 2 * x + y
                for p, size in ((0, 8), (8, 8), (16, 3)):
                    row = s * SLOT + (p * PLANE + y * GROUP + x)
                    out[s, p : p + size, 128 * tile : 128 * tile + 128] = h_ref[
                        pl.ds(row, size, stride=PLANE), :
                    ]
        pltpu.make_async_copy(out.at[s], out_hbm.at[s], sems.at[s]).start()

    table_copy.wait()
    flags = (first_post, first_outer)
    stream_all((post_ref, first_outer), h_ref, flags, table, (0, 1), 3)
    collide_all(h_ref, flags, (post_ref, None), ((0, 1),))
    posts = (post_ref, next_outer)
    for _ in range(STEPS - 2):
        stream_all(posts, h_ref, flags, table, (0, 1, 2), 3)
        posts = (post_ref, outer_ref)
        collide_all(h_ref, flags, posts)
    stream_all(posts, h_ref, flags, table, (0, 1), 2, finish)
    for s in range(SLOTS):
        pltpu.make_async_copy(out.at[s], out_hbm.at[s], sems.at[s]).wait()


def swapped(value, axis, unit=1):
    count = lax.axis_size(axis)
    results = []
    for which in (0, 1):
        others = [i + (unit if i // unit % 2 == which else -unit) for i in range(count)]
        pairs = [(i, j if 0 <= j < count else i) for i, j in enumerate(others)]
        results.append(lax.ppermute(value[which], axis, pairs))
    return results


def rows128(count):
    return jax.ShapeDtypeStruct((count, 128), jnp.float32)


def call(kernel, in_spaces, out_spaces, outs, ins, scratch, limit=LIMIT, cost=None):
    spaces = {
        "S": pl.BlockSpec(memory_space=pltpu.SMEM),
        "V": pl.BlockSpec(memory_space=pltpu.VMEM),
        "H": pl.BlockSpec(memory_space=pltpu.HBM),
    }
    return pl.pallas_call(
        kernel,
        out_shape=outs,
        in_specs=[spaces[x] for x in in_spaces],
        out_specs=[spaces[x] for x in out_spaces],
        scratch_shapes=scratch,
        compiler_params=pltpu.CompilerParams(vmem_limit_bytes=limit),
        cost_estimate=cost,
    )(*ins)


def per_device(populations, site_flags, neighbours, migrations, counts):
    sizes = (lax.axis_size("curve"), lax.axis_size("cross"))
    moves = migrations.T
    floats = lambda rows: pltpu.VMEM((rows, 128), jnp.float32)
    messages = [
        OWN2 + 12 * GROUP,
        STRIPS + 2 * LAYERS,
        STRIPS + 2 * LAYERS,
        6 * GROUP,
        6 * GROUP,
        REST,
    ]
    cells, mate_msg, other_msg, mate2_msg, other2_msg, rest_msg = call(
        functools.partial(pack_kernel, *sizes),
        "HHHHH",
        "HHHHHH",
        [rows128(rows) for rows in messages],
        (moves, counts, populations, site_flags, neighbours),
        [
            pltpu.SMEM(moves.shape, jnp.int32),
            pltpu.SMEM(counts.shape, jnp.int32),
            pltpu.VMEM(populations.shape, jnp.float32),
            pltpu.VMEM(site_flags.shape, jnp.int32),
            pltpu.VMEM(neighbours.shape, jnp.int32),
            *[floats(rows) for rows in messages],
            pltpu.VMEM((8, 5888), jnp.float32),
            pltpu.VMEM((128, 384), jnp.bfloat16),
            floats(256),
            floats(8),
            pltpu.SemaphoreType.DMA((4 + SLOTS + 8,)),
        ],
        WIDE_LIMIT,
    )
    mate_msg, other_msg = swapped((mate_msg, other_msg), "curve")
    mate2_msg, other2_msg = swapped((mate2_msg, other2_msg), "curve", 2)
    assert sizes[0] % 2 == 0
    pairs = [(i, i ^ 1) for i in range(sizes[0])]
    mate_rest = lax.ppermute(rest_msg, "curve", pairs)
    last = sizes[0] - 1
    pairs = [(i, max(i - 2, 0) if i % 2 else min(i + 2, last)) for i in range(sizes[0])]
    passed_rest = lax.ppermute(mate_rest, "curve", pairs)
    (outer,) = call(spread_kernel, "V", "V", [rows128(PLANES * GROUP)], (cells,), [])
    strips = (cells, mate_msg, other_msg, mate2_msg, other2_msg)
    sorted_rows = [messages[1], messages[1], messages[3], messages[3]]
    near_msg, far_msg = call(
        edge_kernel,
        "VVVVVV",
        "VV",
        [rows128(NEAR_ROWS), rows128(FAR_ROWS)],
        (outer, *strips),
        [floats(rows) for rows in [PLANES * GROUP] + sorted_rows],
        cost=pl.CostEstimate(flops=10**10, bytes_accessed=0, transcendentals=0),
    )
    near_msg, far_msg = swapped((near_msg, far_msg), "cross")
    post, own_slots = call(
        join_kernel,
        "VVVVV",
        "VV",
        [rows128(ALL_PLANES * PAIR), jax.ShapeDtypeStruct((24, 128), jnp.int32)],
        strips,
        [floats(rows) for rows in sorted_rows],
    )
    slots, outer_post, next_outer = call(
        outer_kernel,
        "VVVV",
        "VVV",
        [
            jax.ShapeDtypeStruct((72, 128), jnp.int32),
            rows128(ALL_PLANES * GROUP),
            rows128(ALL_PLANES * GROUP),
        ],
        (own_slots, post, near_msg, far_msg),
        [floats(SLOTS * SLOT), pltpu.SMEM((72, 128), jnp.int32), pltpu.SemaphoreType.DMA],
    )
    arriving = (cells, mate_msg, other_msg, mate_rest, passed_rest)
    return call(
        steps_kernel,
        "VVVVVVVVV",
        "H",
        [jax.ShapeDtypeStruct(populations.shape, jnp.float32)],
        (slots, post, outer_post, next_outer, *arriving),
        [
            floats(SLOTS * SLOT),
            floats(ALL_PLANES * PAIR),
            floats(ALL_PLANES * GROUP),
            pltpu.VMEM(populations.shape, jnp.float32),
            pltpu.SMEM((72, 128), jnp.int32),
            pltpu.SemaphoreType.DMA((SLOTS + 1,)),
        ],
    )[0]


def solution(mesh):
    return jax.shard_map(
        per_device,
        mesh=mesh,
        in_specs=(
            P(("curve", "cross"), None, None),
            P(("curve", "cross"), None),
            P(("curve", "cross"), None),
            P(),
            P(("curve", "cross")),
        ),
        out_specs=P(("curve", "cross"), None, None),
        check_vma=False,
    )
```

```python
import functools
import itertools

import jax
import jax.numpy as jnp
import numpy as np
from jax import lax
from jax.experimental import pallas as pl
from jax.experimental.pallas import tpu as pltpu
from jax.sharding import PartitionSpec as P

EDGE = 16
STEPS = 3
SLOTS = 3
POPS = 19
PLANES = SLOTS * POPS + SLOTS
FLAG0 = SLOTS * POPS
GROUP = 24
PLANE = 3 * GROUP
SLOT = POPS * PLANE
CELL = 40
CELLS = PLANES * CELL
LANDINGS = CELLS + 8
OWN2 = LANDINGS + 8
OUTWARD = SLOTS * 5 + SLOTS
LAYERS = 2 * PLANES + OUTWARD
RIM = 11 * EDGE
REST = POPS * EDGE + 10 * EDGE
ALONG_Z = 128
HALF = REST - ALONG_Z
SECOND = 6 * GROUP + ALONG_Z
PAIR = 2 * GROUP
QUADS = PLANES // 4
TABLE = RIM
STRIPS = RIM + 8
FAR = QUADS * GROUP
EDGE_TABLE = FAR + 3 * GROUP
EDGE_ROWS = EDGE_TABLE + 24
NEAR_ROWS, FAR_ROWS = EDGE_ROWS + 16, EDGE_ROWS + 24
NOWHERE = PLANES * GROUP
ALL_PLANES = PLANES + POPS
LIMIT = 20 * 1024 * 1024
WIDE_LIMIT = 127 * 512 * 1024

VELOCITY = [
    (0, 0, 0),
    (1, 0, 0),
    (-1, 0, 0),
    (0, 1, 0),
    (0, -1, 0),
    (0, 0, 1),
    (0, 0, -1),
    (1, 1, 0),
    (-1, -1, 0),
    (1, -1, 0),
    (-1, 1, 0),
    (1, 0, 1),
    (-1, 0, -1),
    (1, 0, -1),
    (-1, 0, 1),
    (0, 1, 1),
    (0, -1, -1),
    (0, 1, -1),
    (0, -1, 1),
]
NORTHWARD, SOUTHWARD = (
    [s * POPS + p for s in range(SLOTS) for p in range(POPS) if VELOCITY[p][1] == side]
    + [FLAG0 + s for s in range(SLOTS)]
    for side in (1, -1)
)
THIRD = [
    (pop, source, *((32 + 16 * k, 9) if k < 4 else (16 * (k - 4), 10)))
    for k, (pop, source) in enumerate(
        [(p, 32) for p in (4, 8, 9, 16, 18)] + [(p, 80) for p in (3, 7, 10, 15, 17)]
    )
]
OPPOSITE = [0, 2, 1, 4, 3, 6, 5, 8, 7, 10, 9, 12, 11, 14, 13, 16, 15, 18, 17]


def lanes_iota():
    return lax.broadcasted_iota(jnp.int32, (8, 128), 1)


def is_even(axis, unit=1):
    return lax.rem(lax.axis_index(axis) // unit, 2) == 0


def rows_iota():
    return lax.broadcasted_iota(jnp.int32, (8, 128), 0)


def aligned(start, size=8):
    return pl.ds(pl.multiple_of(start, 8), size)


def move_slots(moves, curve_size, cross_size):
    curve, cross = lax.axis_index("curve"), lax.axis_index("cross")

    def landed(source, target):
        inside = (source >= 0) & (source < curve_size) & (target >= 0) & (target < curve_size)
        row = jnp.clip(source, 0, curve_size - 1) * cross_size + cross
        rank = target * cross_size + cross
        hit = inside & (moves[0, row] >= 0) & (moves[1, row] == rank)
        return jnp.where(hit, moves[2, row], -1)

    return (
        landed(curve - 1, curve),
        landed(curve + 1, curve),
        landed(curve - 2, curve - 1),
        landed(curve, curve - 1),
        landed(curve + 2, curve + 1),
        landed(curve, curve + 1),
    )


def pack_kernel(
    curve_size,
    cross_size,
    moves_hbm,
    counts_hbm,
    pops_hbm,
    flags_hbm,
    neighbours_hbm,
    cells_hbm,
    mate_hbm,
    other_hbm,
    mate2_hbm,
    other2_hbm,
    rest_hbm,
    moves,
    counts,
    pops,
    flags,
    neighbours,
    cells,
    up_msg,
    down_msg,
    up2_msg,
    down2_msg,
    rest_msg,
    wide_flags,
    plane_flags,
    site_flags,
    near,
    sems,
):
    started = []

    def copy(source, target):
        one = pltpu.make_async_copy(source, target, sems.at[len(started)])
        one.start()
        started.append(one)
        return one

    flags_copy = copy(flags_hbm, flags)
    copies = [copy(pops_hbm.at[s], pops.at[s]) for s in range(SLOTS)]
    small = [
        copy(neighbours_hbm, neighbours),
        copy(counts_hbm, counts),
        copy(moves_hbm, moves),
    ]
    for one in small:
        one.wait()

    near[...] = jnp.zeros_like(near)
    named = neighbours[...]
    slot = jnp.where(named >= 0, lax.rem(jnp.maximum(named, 0), SLOTS), SLOTS)
    near[0:SLOTS, 0 : named.shape[1]] = slot.astype(jnp.float32)
    for ref, row in ((cells, CELLS), (up_msg, TABLE), (down_msg, TABLE)):
        ref[row : row + 8, :] = near[...]

    wide_flags[...] = jnp.zeros_like(wide_flags)
    flags_copy.wait()
    wide_flags[0:SLOTS, 0 : flags.shape[1]] = flags[...].astype(jnp.float32)
    span = EDGE + 2
    for x in range(EDGE):
        start = (x + 1) * span * span
        base = start // 128 * 128
        window = wide_flags[:, base : base + 512]
        window = pltpu.roll(window, (512 - (start - base)) % 512, axis=1)
        plane_flags[8 * x : 8 * x + 8, :] = window[:, :384].astype(jnp.bfloat16)
    lane_in = lax.broadcasted_iota(jnp.int32, (384, 256), 0)
    site = lax.broadcasted_iota(jnp.int32, (384, 256), 1)
    chosen = lane_in == (site // EDGE + 1) * span + site % EDGE + 1
    product = jnp.dot(
        plane_flags[...],
        jnp.where(chosen, 1.0, 0.0).astype(jnp.bfloat16),
        preferred_element_type=jnp.float32,
    )
    site_flags[0:128, :] = product[:, :128]
    site_flags[128:256, :] = product[:, 128:]
    for s in range(SLOTS):
        live = s < counts[0]
        for y in range(2):
            piece = site_flags[pl.ds(128 * y + s, EDGE, stride=8), :]
            is_fluid = (piece == 1.0) & live
            row = (FLAG0 + s) * CELL + y * EDGE
            cells[row : row + EDGE, :] = jnp.where(is_fluid, 1.0, 0.0)

    for s in range(SLOTS):
        copies[s].wait()
        for x in range(EDGE):
            for y in range(2):
                tile = 2 * x + y
                for p, size in ((0, 8), (8, 8), (16, 3)):
                    row = (s * POPS + p) * CELL + y * EDGE + x
                    cells[pl.ds(row, size, stride=CELL), :] = pops[
                        s, p : p + size, 128 * tile : 128 * tile + 128
                    ]

    @pl.loop(0, SLOTS)
    def _(s):
        @pl.loop(0, 4, unroll=2)
        def _(c):
            base = s * (POPS * CELL) + c * 8
            view = cells.at[aligned(base, (POPS - 1) * CELL + 8), :]
            h = [view[p * CELL : p * CELL + 8, :] for p in range(POPS)]
            for p, value in enumerate(collided(h)):
                view[p * CELL : p * CELL + 8, :] = value

    for i, slot in enumerate(move_slots(moves, curve_size, cross_size)):
        value = jnp.full((1, 128), slot, jnp.int32)
        cells[LANDINGS + i : LANDINGS + i + 1, :] = value.astype(jnp.float32)

    body_copy = copy(cells.at[:OWN2], cells_hbm.at[:OWN2])

    for y in range(2):
        for msg, x0, first in ((up_msg, 15, 1), (down_msg, 0, 2)):
            step = -1 if x0 else 1
            for k in range(2):
                out = STRIPS + y * LAYERS + k * PLANES
                msg[out : out + PLANES, :] = cells[
                    pl.ds(y * EDGE + x0 + step * k, PLANES, stride=CELL), :
                ]
            row = y * EDGE + x0 + 2 * step
            out = STRIPS + y * LAYERS + 2 * PLANES
            for s in range(SLOTS):
                base = s * POPS * CELL + row
                msg[out + 5 * s : out + 5 * s + 1, :] = cells[pl.ds(base + first * CELL, 1), :]
                msg[out + 5 * s + 1 : out + 5 * s + 5, :] = cells[
                    pl.ds(base + (first + 6) * CELL, 4, stride=2 * CELL), :
                ]
            msg[out + 5 * SLOTS : out + OUTWARD, :] = cells[
                pl.ds(FLAG0 * CELL + row, SLOTS, stride=CELL), :
            ]

    here = lax.axis_index("curve") * cross_size + lax.axis_index("cross")
    leaving = jnp.maximum(moves[0, here], 0)
    lane = lanes_iota()
    for v in range(2):
        halves = [
            [cells[aligned(leaving * (POPS * CELL) + p * CELL + y * EDGE + v * 8), :] for y in (0, 1)]
            for p in range(POPS)
        ]
        outer = [jnp.where(lane < 64, first, second) for first, second in halves]
        middle = (lane >= 32) & (lane < 96)
        sets = [
            jnp.where(middle, pltpu.roll(outer[p + 1], 64, axis=1), outer[p])
            for p in range(0, POPS - 1, 2)
        ]
        sets += [outer[POPS - 1], jnp.zeros_like(outer[0])]
        for pop, source, target, which in THIRD:
            moved = pltpu.roll(outer[pop], (target - source) % 128, axis=1)
            sets[which] = jnp.where(lane // 16 == target // 16, moved, sets[which])
        for k, value in enumerate(sets):
            row = k * EDGE + v * 8
            up_msg[row : row + 8, :] = value
            down_msg[row : row + 8, :] = value
        for p, (first, second) in enumerate(halves):
            row = p * EDGE + v * 8
            rest_msg[row : row + 8, :] = jnp.where(lane < 32, second, first)
        for p in range(0, POPS, 2):
            value = halves[p][1]
            if p + 1 < POPS:
                value = jnp.where(middle, value, pltpu.roll(halves[p + 1][1], 64, axis=1))
            row = (POPS + p // 2) * EDGE + v * 8
            rest_msg[row : row + 8, :] = value
    for s in range(SLOTS):

        @pl.when(leaving == s)
        def _():
            for y in range(2):
                for k in range(3):
                    out = (y * 3 + k) * GROUP
                    row = s * POPS * CELL + y * EDGE + k
                    up2_msg[out : out + POPS, :] = cells[pl.ds(row + 13, POPS, stride=CELL), :]
                    down2_msg[out : out + POPS, :] = cells[pl.ds(row, POPS, stride=CELL), :]

    cells[OWN2 : OWN2 + 6 * GROUP, :] = up2_msg[: 6 * GROUP, :]
    cells[OWN2 + 6 * GROUP :, :] = down2_msg[: 6 * GROUP, :]
    for msg in (up2_msg, down2_msg):
        msg[6 * GROUP :, :] = rest_msg[HALF:, :]
    last = [copy(cells.at[OWN2:], cells_hbm.at[OWN2:]), copy(rest_msg, rest_hbm)]
    count = len(started)
    for i, (up, down, mate, other, unit) in enumerate(
        ((up_msg, down_msg, mate_hbm, other_hbm, 1), (up2_msg, down2_msg, mate2_hbm, other2_hbm, 2))
    ):
        first, second = sems.at[count + 2 * i], sems.at[count + 2 * i + 1]
        even = is_even("curve", unit)

        @pl.when(even)
        def _():
            pltpu.make_async_copy(up, mate, first).start()
            pltpu.make_async_copy(down, other, second).start()

        @pl.when(jnp.logical_not(even))
        def _():
            pltpu.make_async_copy(down, mate, first).start()
            pltpu.make_async_copy(up, other, second).start()

        last.append(pltpu.make_async_copy(up, mate, first))
        last.append(pltpu.make_async_copy(down, other, second))
    body_copy.wait()
    for one in last:
        one.wait()


def spread_kernel(cells, outer):
    low = lanes_iota() < 64
    for q in range(PLANES):
        for v in range(2):
            row = q * CELL + v * 8
            first, second = cells[row : row + 8, :], cells[row + EDGE : row + EDGE + 8, :]
            row = q * GROUP + v * 8
            outer[row : row + 8, :] = jnp.where(low, first, second)


def sort_messages(mate_msg, other_msg, mate2_msg, other2_msg, low_msg, high_msg, low2, high2):
    for mate, other, low, high, unit in (
        (mate_msg, other_msg, low_msg, high_msg, 1),
        (mate2_msg, other2_msg, low2, high2, 2),
    ):
        even = is_even("curve", unit)

        @pl.when(even)
        def _():
            low[...] = other[...]
            high[...] = mate[...]

        @pl.when(jnp.logical_not(even))
        def _():
            low[...] = mate[...]
            high[...] = other[...]


def landed_slots(cells):
    return [jnp.max(cells[LANDINGS + i : LANDINGS + i + 1, :]) for i in range(6)]


def rim_of(msg, p, v):
    row = p // 2 * EDGE + v * 8
    value = msg[row : row + 8, :]
    return pltpu.roll(value, 64, axis=1) if p % 2 else value


def sel4(parts, lane):
    first = jnp.where(lane < 32, parts[0], parts[1])
    second = jnp.where(lane < 96, parts[2], parts[3])
    return jnp.where(lane < 64, first, second)


def strip_rows(first, row0, step):
    pieces = []
    for k in range(2):
        pieces.append(
            (PLANES, lambda size, row: pl.ds(row, PLANES, stride=size), row0 + step * k, STRIPS + k * PLANES)
        )
    row, source = row0 + 2 * step, STRIPS + 2 * PLANES
    for s in range(SLOTS):
        plane = s * POPS + first
        pieces.append((1, lambda size, row, plane=plane: pl.ds(plane * size + row, 1), row, source))
        pieces.append(
            (
                4,
                lambda size, row, plane=plane: pl.ds(
                    (plane + 6) * size + row, 4, stride=2 * size
                ),
                row,
                source + 1,
            )
        )
        source += 5
    pieces.append(
        (SLOTS, lambda size, row: pl.ds(FLAG0 * size + row, SLOTS, stride=size), row, source)
    )
    return pieces


def edge_kernel(
    own_outer,
    cells,
    mate_msg,
    other_msg,
    mate2_msg,
    other2_msg,
    near_msg,
    far_msg,
    turn_msg,
    outer,
    low_msg,
    high_msg,
    low2_msg,
    high2_msg,
):
    sort_messages(
        mate_msg, other_msg, mate2_msg, other2_msg, low_msg, high_msg, low2_msg, high2_msg
    )
    from_low, from_high, low_low, low_me, high_high, high_me = landed_slots(cells)
    low = lanes_iota() < 64
    for q in range(PLANES):
        for v in range(2):
            row = q * GROUP + v * 8
            outer[row : row + 8, :] = own_outer[row : row + 8, :]

    def both(first, second):
        lane = lax.broadcasted_iota(jnp.int32, first.shape, 1)
        return jnp.where(lane < 64, first, second)

    for msg, row0, step, first in ((high_msg, 16, 1, 2), (low_msg, 23, -1, 1)):
        for count, planes, row, source in strip_rows(first, row0, step):
            outer[planes(GROUP, row), :] = both(
                msg[source : source + count, :],
                msg[LAYERS + source : LAYERS + source + count, :],
            )
    lane = lanes_iota()
    for s, (slot, msg) in itertools.product(
        range(SLOTS), ((from_low, low_msg), (from_high, high_msg))
    ):

        @pl.when(slot == s)
        def _():
            for v in range(2):
                values = [rim_of(msg, p, v) for p in range(POPS)]
                for pop, target, source, which in THIRD:
                    row = which * EDGE + v * 8
                    moved = pltpu.roll(msg[row : row + 8, :], (target - source) % 128, axis=1)
                    values[pop] = jnp.where(lane // 16 == target // 16, moved, values[pop])
                for p, value in enumerate(values):
                    row = (s * POPS + p) * GROUP + v * 8
                    outer[row : row + 8, :] = value

    for s in range(SLOTS):
        for slot, msg, row0 in (
            (low_low, low2_msg, 21),
            (low_me, cells.at[OWN2:], 21),
            (high_high, high2_msg, 16),
            (high_me, cells.at[OWN2 + 6 * GROUP :], 16),
        ):

            @pl.when(slot == s)
            def _():
                for k in range(3):
                    outer[pl.ds(s * POPS * GROUP + row0 + k, POPS, stride=GROUP), :] = both(
                        msg[k * GROUP : k * GROUP + POPS, :],
                        msg[(3 + k) * GROUP : (3 + k) * GROUP + POPS, :],
                    )

    from_above = is_even("curve")
    for row in range(0, ALONG_Z, 8):
        tail = slice(6 * GROUP + row, 6 * GROUP + row + 8)
        value = jnp.where(from_above, high2_msg[tail, :], low2_msg[tail, :])
        turn_msg[row : row + 8, :] = value

    even = is_even("cross")

    def send(row, north, south):
        near_msg[row : row + 8, :] = jnp.where(even, north, south)
        far_msg[row : row + 8, :] = jnp.where(even, south, north)

    for v in range(3):

        def plane(q):
            return outer[q * GROUP + v * 8 : q * GROUP + v * 8 + 8, :]

        for quad in range(QUADS):
            parts = [plane(4 * quad)]
            parts += [pltpu.roll(plane(4 * quad + k), 32 * k, axis=1) for k in (1, 2, 3)]
            send(quad * GROUP + v * 8, sel4(parts[1:] + parts[:1], lane), sel4(parts, lane))
        for part in range(3):
            values = []
            for planes, source in ((NORTHWARD, 80), (SOUTHWARD, 32)):
                value = None
                for k, q in enumerate(planes[8 * part : 8 * part + 8]):
                    moved = pltpu.roll(plane(q), (16 * k - source) % 128, axis=1)
                    value = moved if value is None else jnp.where(lane < 16 * k, value, moved)
                values.append(value)
            send(FAR + part * GROUP + v * 8, *values)
    tables = (low_msg, TABLE), (cells, CELLS), (high_msg, TABLE)
    for i, (ref, row) in enumerate(tables):
        value = ref[row : row + 8, :]
        send(EDGE_TABLE + 8 * i, value, value)


def collided(h):
    shear = 1.0 / 0.6
    rest = h[0]
    sx, dx = h[1] + h[2], h[1] - h[2]
    sy, dy = h[3] + h[4], h[3] - h[4]
    sz, dz = h[5] + h[6], h[5] - h[6]
    s7, d7 = h[7] + h[8], h[7] - h[8]
    s9, d9 = h[9] + h[10], h[9] - h[10]
    s11, d11 = h[11] + h[12], h[11] - h[12]
    s13, d13 = h[13] + h[14], h[13] - h[14]
    s15, d15 = h[15] + h[16], h[15] - h[16]
    s17, d17 = h[17] + h[18], h[17] - h[18]
    txy, txz, tyz = s7 + s9, s11 + s13, s15 + s17
    pxy, pxz, pyz = s7 - s9, s11 - s13, s15 - s17
    ax, bx = d7 + d9, d11 + d13
    ay, by = d7 - d9, d15 + d17
    az, bz = d11 - d13, d15 - d17
    axes = sx + sy + sz
    diags = txy + txz + tyz
    rho = rest * (1.0 / 3.0) + axes * (1.0 / 18.0) + diags * (1.0 / 36.0)
    fx, fy, fz = ax + bx, ay + by, az + bz
    jx = dx * (1.0 / 18.0) + fx * (1.0 / 36.0)
    jy = dy * (1.0 / 18.0) + fy * (1.0 / 36.0)
    jz = dz * (1.0 / 18.0) + fz * (1.0 / 36.0)
    inverse = 1.0 / rho
    ux, uy, uz = jx * inverse, jy * inverse, jz * inverse
    qxx, qyy, qzz = jx * ux, jy * uy, jz * uz
    total = qxx + qyy + qzz

    energy = -10.0 * rest - axes * (11.0 / 18.0) + diags * (8.0 / 36.0)
    energy = (energy + 11.0 * rho - 19.0 * total) * (1.19 / 2394.0)
    square = 4.0 * rest - axes * (4.0 / 18.0) + diags * (1.0 / 36.0)
    square = (square - 3.0 * rho + 5.5 * total) * (1.4 / 252.0)
    axis_x = (3.0 * sx - axes) * (1.0 / 18.0)
    diag_x = (diags - 3.0 * tyz) * (1.0 / 36.0)
    want_x = 3.0 * qxx - total
    stress_x = (axis_x + diag_x - want_x) * (shear / 36.0)
    third_x = (diag_x - 2.0 * axis_x + 0.5 * want_x) * (1.4 / 72.0)
    axis_w = (sy - sz) * (1.0 / 18.0)
    diag_w = (txy - txz) * (1.0 / 36.0)
    want_w = qyy - qzz
    stress_w = (axis_w + diag_w - want_w) * (shear / 12.0)
    third_w = (diag_w - 2.0 * axis_w + 0.5 * want_w) * (1.4 / 24.0)

    rest_out = rest - 3.0 * (12.0 * square - 30.0 * energy)
    common = -18.0 * (11.0 * energy + 4.0 * square)
    along_x = 18.0 * (stress_x - 2.0 * third_x)
    along_w = 18.0 * (stress_w - 2.0 * third_w)
    ex = common + 2.0 * along_x
    ey = common - along_x + along_w
    ez = common - along_x - along_w
    common = 36.0 * (8.0 * energy + square)
    across_x = 36.0 * (stress_x + third_x)
    across_w = 36.0 * (stress_w + third_w)
    exy = common + across_x + across_w
    exz = common + across_x - across_w
    eyz = common - 2.0 * across_x
    cxy = shear * (0.25 * pxy - 9.0 * jx * uy)
    cxz = shear * (0.25 * pxz - 9.0 * jx * uz)
    cyz = shear * (0.25 * pyz - 9.0 * jy * uz)

    def flux(d, f, j):
        return (f * (1.0 / 36.0) - d * (4.0 / 18.0) + j * (2.0 / 3.0)) * (1.2 / 40.0)

    hx, hy, hz = flux(dx, fx, jx), flux(dy, fy, jy), flux(dz, fz, jz)
    mx = (ax - bx) * (1.98 / 8.0)
    my = (by - ay) * (1.98 / 8.0)
    mz = (az - bz) * (1.98 / 8.0)
    hx36, hy36, hz36 = 36.0 * hx, 36.0 * hy, 36.0 * hz
    xy_x, xz_x = hx36 + mx, hx36 - mx
    yz_y, xy_y = hy36 + my, hy36 - my
    xz_z, yz_z = hz36 + mz, hz36 - mz
    ox, oy, oz = -2.0 * hx36, -2.0 * hy36, -2.0 * hz36

    out = [rest_out]

    def pair(i, even, odd):
        out.append(h[i] - (even + odd))
        out.append(h[i + 1] - (even - odd))

    pair(1, ex, ox)
    pair(3, ey, oy)
    pair(5, ez, oz)
    pair(7, exy + cxy, xy_x + xy_y)
    pair(9, exy - cxy, xy_x - xy_y)
    pair(11, exz + cxz, xz_x + xz_z)
    pair(13, exz - cxz, xz_x - xz_z)
    pair(15, eyz + cyz, yz_y + yz_z)
    pair(17, eyz - cyz, yz_y - yz_z)
    return out


def collide_all(h_ref, flags, posts, parts=((0, 1), (2,))):
    for groups in parts:
        ref = posts[groups[0] // 2]
        size = len(groups) * GROUP

        @pl.loop(0, SLOTS)
        def _(s):
            @pl.loop(0, size // 8, unroll=3)
            def _(c):
                is_fluid = flags[groups[0] // 2][aligned((FLAG0 + s) * size + c * 8), :] > 0.0
                start = s * SLOT + groups[0] * GROUP + c * 8
                h_view = h_ref.at[aligned(start, (POPS - 1) * PLANE + 8), :]
                start = s * (POPS * size) + c * 8
                view = ref.at[aligned(start, (POPS - 1) * size + 8), :]
                h = [h_view[p * PLANE : p * PLANE + 8, :] for p in range(POPS)]
                for p, value in enumerate(collided(h)):
                    view[p * size : p * size + 8, :] = jnp.where(is_fluid, value, jnp.nan)


def hide_walls(ref, size):
    @pl.loop(0, SLOTS)
    def _(s):
        @pl.loop(0, size // 8)
        def _(c):
            is_fluid = ref[aligned((FLAG0 + s) * size + c * 8), :] > 0.0
            start = s * (POPS * size) + c * 8
            view = ref.at[aligned(start, (POPS - 1) * size + 8), :]
            for p in range(POPS):
                row = p * size
                view[row : row + 8, :] = jnp.where(is_fluid, view[row : row + 8, :], jnp.nan)


def stream_all(posts, h_ref, flags, table, groups, vregs, finish=None):
    lane = lanes_iota()
    row = rows_iota()
    low = lane < 64

    def one_slot(s):
        views = {}

        def view(which, key):
            if (which, key) not in views:
                start = s * (POPS * GROUP) if key == "own" else table[key[0] * 8 + s, key[1]]
                start = start if which else 2 * start
                views[which, key] = posts[which].at[
                    aligned(start, POPS * (GROUP if which else PAIR)), :
                ]
            return views[which, key]

        def load(key, pop, group, v):
            if group == 2:
                row = pop * GROUP + v * 8
            else:
                row = pop * PAIR + group * GROUP + v * 8
            return view(group // 2, key)[row : row + 8, :]

        h_view = h_ref.at[aligned(s * SLOT, SLOT), :]

        def shifted(pop, group, j, dy, dz):
            cx = VELOCITY[pop][0]

            def rows(key, v):
                return load(key, pop, group, v)

            def look(i, j, dx, v):
                if (dx, dy, dz) == (0, 0, 0):
                    return rows("own", v)
                if j is None:
                    return jnp.where(low, look(i, 1, dx, v), look(i, -1, dx, v))
                region = (i + 1) * 3 + j + 1
                return rows((region, VELOCITY.index((dx, dy, dz)) - 1), v)

            need_last = vregs == 3
            values = [look(0, j, 0, 0), look(0, j, 0, 1)]
            if need_last:
                if dy == 0 and dz == 0:
                    values.append(rows("own", 2))
                else:
                    values.append(jnp.where(row < 4, look(1, j, 0, 2), look(-1, j, 0, 2)))
            if cx == 0:
                return values
            turn = 1 if cx > 0 else 7
            rolled = [pltpu.roll(value, turn, axis=0) for value in values]
            if cx > 0:
                before = pltpu.roll(look(0, j, -1, 2), 1, axis=0)
                result = [
                    jnp.where(row == 0, before, rolled[0]),
                    jnp.where(row == 0, rolled[0], rolled[1]),
                ]
                if need_last:
                    edge = pltpu.roll(look(1, j, -1, 1), 1, axis=0)
                    result.append(jnp.where(row == 0, edge, rolled[2]))
                return result
            after = pltpu.roll(look(0, j, 1, 2), 7, axis=0)
            result = [
                jnp.where(row == 7, rolled[1], rolled[0]),
                jnp.where(row == 7, after, rolled[1]),
            ]
            if need_last:
                edge = pltpu.roll(look(-1, j, 1, 0), 7, axis=0)
                result.append(jnp.where(row == 7, edge, rolled[2]))
            return result

        for pop in range(POPS):
            cx, cy, cz = VELOCITY[pop]
            kept = {}

            def source(*key):
                if key not in kept:
                    kept[key] = shifted(pop, *key)
                return kept[key]

            def along_y(group, dz):
                values = source(group, None if group == 2 else 0, 0, dz)
                if cy == 0:
                    return values
                other = (group - cy) % 3
                if group != 2 and other != 2:
                    carried = source(other, 0, 0, dz)
                else:
                    carried = source(other, cy if group == 2 else 0, -cy, dz)
                mask = lane >= 112 if cy > 0 else lane < 16
                return [jnp.where(mask, b, a) for a, b in zip(values, carried)]

            for group in groups:
                values = along_y(group, 0)
                turn = (16 * cy + cz) % 128
                if turn:
                    values = [pltpu.roll(value, turn, axis=1) for value in values]
                if cz:
                    turn = (16 * cy - 15 * cz) % 128
                    wrapped = [pltpu.roll(value, turn, axis=1) for value in along_y(group, -cz)]
                    mask = lane % 16 == (0 if cz > 0 else 15)
                    values = [jnp.where(mask, b, a) for a, b in zip(values, wrapped)]
                for v, value in enumerate(values[:vregs]):
                    if pop:
                        value = jnp.where(value != value, load("own", OPPOSITE[pop], group, v), value)
                    if finish is not None:
                        is_fluid = flags[group // 2][
                            aligned((FLAG0 + s) * PAIR + group * GROUP + v * 8), :
                        ]
                        value = jnp.where(is_fluid > 0.0, value, 0.0)
                    target = pop * PLANE + group * GROUP + v * 8
                    h_view[target : target + 8, :] = value

    @pl.loop(0, SLOTS)
    def _(s):
        one_slot(s)
        if finish is not None:
            finish(s)


def join_kernel(
    cells,
    mate_msg,
    other_msg,
    mate2_msg,
    other2_msg,
    post_ref,
    slots,
    low_msg,
    high_msg,
    low2_msg,
    high2_msg,
):
    sort_messages(
        mate_msg, other_msg, mate2_msg, other2_msg, low_msg, high_msg, low2_msg, high2_msg
    )
    for i, (ref, row) in enumerate(((low_msg, TABLE), (cells, CELLS), (high_msg, TABLE))):
        slots[8 * i : 8 * i + 8, :] = first_rows(ref[row : row + 8, :])

    from_low, from_high, low_low, low_me, high_high, high_me = landed_slots(cells)
    post_ref[PLANES * PAIR :, :] = jnp.full((POPS * PAIR, 128), jnp.nan, jnp.float32)
    for q in range(PLANES):
        for y in range(2):
            start = q * PAIR + y * GROUP
            post_ref[start : start + EDGE, :] = cells[
                q * CELL + y * EDGE : q * CELL + (y + 1) * EDGE, :
            ]
    for s, (slot, msg) in itertools.product(
        range(SLOTS), ((from_low, low_msg), (from_high, high_msg))
    ):

        @pl.when(slot == s)
        def _():
            for p in range(POPS):
                for v in range(2):
                    rim = rim_of(msg, p, v)
                    row = (s * POPS + p) * PAIR + v * 8
                    post_ref[row : row + 8, :] = rim
                    post_ref[row + GROUP : row + GROUP + 8, :] = rim

    for msg, row0, step, first in ((high_msg, 16, 1, 2), (low_msg, 23, -1, 1)):
        for y in range(2):
            for count, planes, row, source in strip_rows(first, row0, step):
                source += y * LAYERS
                post_ref[planes(PAIR, row + y * GROUP), :] = msg[source : source + count, :]
    for s in range(SLOTS):
        for slot, msg, row0 in (
            (low_low, low2_msg, 21),
            (low_me, cells.at[OWN2:], 21),
            (high_high, high2_msg, 16),
            (high_me, cells.at[OWN2 + 6 * GROUP :], 16),
        ):

            @pl.when(slot == s)
            def _():
                for y in range(2):
                    for k in range(3):
                        row = s * POPS * PAIR + y * GROUP + row0 + k
                        source = (y * 3 + k) * GROUP
                        post_ref[pl.ds(row, POPS, stride=PAIR), :] = msg[source : source + POPS, :]
    hide_walls(post_ref, PAIR)


def first_rows(slot):
    slot = slot.astype(jnp.int32)
    return jnp.where(slot == SLOTS, NOWHERE, slot * (POPS * GROUP))


def outer_kernel(
    own_slots, first_post, near_msg, far_msg, slots, outer_ref, next_ref, h_ref, table, sem
):
    even = is_even("cross")

    def received(row):
        near, far = near_msg[row : row + 8, :], far_msg[row : row + 8, :]
        return jnp.where(even, far, near), jnp.where(even, near, far)

    for i in range(3):
        south, north = received(EDGE_TABLE + 8 * i)
        slots[24 * i : 24 * i + 8, :] = first_rows(south)
        slots[24 * i + 8 : 24 * i + 16, :] = own_slots[8 * i : 8 * i + 8, :]
        slots[24 * i + 16 : 24 * i + 24, :] = first_rows(north)
    table_copy = pltpu.make_async_copy(slots, table, sem)
    table_copy.start()

    nothing = jnp.full((8, 128), jnp.nan, jnp.float32)
    for row in range(0, POPS * GROUP, 8):
        outer_ref[NOWHERE + row : NOWHERE + row + 8, :] = nothing
        next_ref[NOWHERE + row : NOWHERE + row + 8, :] = nothing
    lane = lanes_iota()
    for v in range(3):

        def rows(q):
            return slice(q * GROUP + v * 8, q * GROUP + v * 8 + 8)

        for quad in range(QUADS):
            south, north = received(quad * GROUP + v * 8)
            for k in range(4):
                value = jnp.where(lane // 32 == (k + 3) % 4, south, north)
                if k:
                    value = pltpu.roll(value, 128 - 32 * k, axis=1)
                outer_ref[rows(4 * quad + k), :] = value
        for part in range(3):
            values = received(FAR + part * GROUP + v * 8)
            for planes, target, value in zip((NORTHWARD, SOUTHWARD), (80, 32), values):
                for k, q in enumerate(planes[8 * part : 8 * part + 8]):
                    moved = pltpu.roll(value, (target - 16 * k) % 128, axis=1)
                    outer_ref[rows(q), :] = jnp.where(
                        lane // 16 == target // 16, moved, outer_ref[rows(q), :]
                    )
    for row in range(FLAG0 * GROUP, NOWHERE, 8):
        next_ref[row : row + 8, :] = outer_ref[row : row + 8, :]
    hide_walls(outer_ref, GROUP)
    table_copy.wait()
    flags = (first_post, outer_ref)
    stream_all(flags, h_ref, flags, table, (2,), 3)
    collide_all(h_ref, flags, (None, next_ref), ((2,),))


def steps_kernel(
    slots,
    first_post,
    first_outer,
    next_outer,
    cells,
    mate_msg,
    other_msg,
    mate_rest,
    passed_rest,
    passed2_rest,
    out_hbm,
    h_ref,
    post_ref,
    outer_ref,
    out,
    table,
    sems,
):
    table_copy = pltpu.make_async_copy(slots, table, sems.at[SLOTS])
    table_copy.start()
    post_ref[...] = first_post[...]
    nothing = jnp.full((8, 128), jnp.nan, jnp.float32)
    for row in range(0, POPS * GROUP, 8):
        outer_ref[NOWHERE + row : NOWHERE + row + 8, :] = nothing

    def rest(row, is_mate):
        if is_mate:
            return mate_rest[row : row + 8, :]
        if row < HALF:
            return passed_rest[row : row + 8, :]
        return passed2_rest[row - HALF : row - HALF + 8, :]

    from_low, from_high = landed_slots(cells)[:2]
    lane = lanes_iota()
    even = is_even("curve")
    odd = jnp.logical_not(even)
    for s, (slot, wanted, msg, is_mate) in itertools.product(
        range(SLOTS),
        (
            (from_low, odd, mate_msg, True),
            (from_low, even, other_msg, False),
            (from_high, even, mate_msg, True),
            (from_high, odd, other_msg, False),
        ),
    ):

        @pl.when((slot == s) & wanted)
        def _():
            for v in range(2):
                starts = [(FLAG0 + s) * PAIR + y * GROUP + v * 8 for y in range(2)]
                fluid = [first_post[row : row + 8, :] > 0.0 for row in starts]
                for p in range(POPS):
                    rim = rim_of(msg, p, v)
                    row = p * EDGE + v * 8
                    wide = rest(row, is_mate)
                    row = (POPS + p // 2) * EDGE + v * 8
                    middle = rest(row, is_mate)
                    if p % 2:
                        middle = pltpu.roll(middle, 64, axis=1)
                    first = jnp.where(lane < 32, rim, wide)
                    second = jnp.where(lane < 32, wide, jnp.where(lane < 96, middle, rim))
                    row = (s * POPS + p) * PAIR + v * 8
                    post_ref[row : row + 8, :] = jnp.where(fluid[0], first, jnp.nan)
                    row += GROUP
                    post_ref[row : row + 8, :] = jnp.where(fluid[1], second, jnp.nan)

    def finish(s):
        for x in range(EDGE):
            for y in range(2):
                tile = 2 * x + y
                for p, size in ((0, 8), (8, 8), (16, 3)):
                    row = s * SLOT + (p * PLANE + y * GROUP + x)
                    out[s, p : p + size, 128 * tile : 128 * tile + 128] = h_ref[
                        pl.ds(row, size, stride=PLANE), :
                    ]
        pltpu.make_async_copy(out.at[s], out_hbm.at[s], sems.at[s]).start()

    table_copy.wait()
    flags = (first_post, first_outer)
    stream_all((post_ref, first_outer), h_ref, flags, table, (0, 1), 3)
    collide_all(h_ref, flags, (post_ref, None), ((0, 1),))
    posts = (post_ref, next_outer)
    for _ in range(STEPS - 2):
        stream_all(posts, h_ref, flags, table, (0, 1, 2), 3)
        posts = (post_ref, outer_ref)
        collide_all(h_ref, flags, posts)
    stream_all(posts, h_ref, flags, table, (0, 1), 2, finish)
    for s in range(SLOTS):
        pltpu.make_async_copy(out.at[s], out_hbm.at[s], sems.at[s]).wait()


def swapped(value, axis, unit=1):
    count = lax.axis_size(axis)
    results = []
    for which in (0, 1):
        others = [i + (unit if i // unit % 2 == which else -unit) for i in range(count)]
        pairs = [(i, j if 0 <= j < count else i) for i, j in enumerate(others)]
        results.append(lax.ppermute(value[which], axis, pairs))
    return results


def rows128(count):
    return jax.ShapeDtypeStruct((count, 128), jnp.float32)


def call(kernel, in_spaces, out_spaces, outs, ins, scratch, limit=LIMIT, cost=None):
    spaces = {
        "S": pl.BlockSpec(memory_space=pltpu.SMEM),
        "V": pl.BlockSpec(memory_space=pltpu.VMEM),
        "H": pl.BlockSpec(memory_space=pltpu.HBM),
    }
    return pl.pallas_call(
        kernel,
        out_shape=outs,
        in_specs=[spaces[x] for x in in_spaces],
        out_specs=[spaces[x] for x in out_spaces],
        scratch_shapes=scratch,
        compiler_params=pltpu.CompilerParams(vmem_limit_bytes=limit),
        cost_estimate=cost,
    )(*ins)


def per_device(populations, site_flags, neighbours, migrations, counts):
    sizes = (lax.axis_size("curve"), lax.axis_size("cross"))
    moves = migrations.T
    floats = lambda rows: pltpu.VMEM((rows, 128), jnp.float32)
    messages = [
        OWN2 + 12 * GROUP,
        STRIPS + 2 * LAYERS,
        STRIPS + 2 * LAYERS,
        SECOND,
        SECOND,
        REST,
    ]
    cells, mate_msg, other_msg, mate2_msg, other2_msg, rest_msg = call(
        functools.partial(pack_kernel, *sizes),
        "HHHHH",
        "HHHHHH",
        [rows128(rows) for rows in messages],
        (moves, counts, populations, site_flags, neighbours),
        [
            pltpu.SMEM(moves.shape, jnp.int32),
            pltpu.SMEM(counts.shape, jnp.int32),
            pltpu.VMEM(populations.shape, jnp.float32),
            pltpu.VMEM(site_flags.shape, jnp.int32),
            pltpu.VMEM(neighbours.shape, jnp.int32),
            *[floats(rows) for rows in messages],
            pltpu.VMEM((8, 5888), jnp.float32),
            pltpu.VMEM((128, 384), jnp.bfloat16),
            floats(256),
            floats(8),
            pltpu.SemaphoreType.DMA((4 + SLOTS + 8,)),
        ],
        WIDE_LIMIT,
    )
    mate_msg, other_msg = swapped((mate_msg, other_msg), "curve")
    mate2_msg, other2_msg = swapped((mate2_msg, other2_msg), "curve", 2)
    assert sizes[0] % 2 == 0
    pairs = [(i, i ^ 1) for i in range(sizes[0])]
    mate_rest = lax.ppermute(rest_msg, "curve", pairs)
    last = sizes[0] - 1
    pairs = [(i, max(i - 2, 0) if i % 2 else min(i + 2, last)) for i in range(sizes[0])]
    passed_rest = lax.ppermute(mate_rest[:HALF], "curve", pairs)
    (outer,) = call(spread_kernel, "V", "V", [rows128(PLANES * GROUP)], (cells,), [])
    strips = (cells, mate_msg, other_msg, mate2_msg, other2_msg)
    sorted_rows = [messages[1], messages[1], messages[3], messages[3]]
    near_msg, far_msg, turn_msg = call(
        edge_kernel,
        "VVVVVV",
        "VVV",
        [rows128(NEAR_ROWS), rows128(FAR_ROWS), rows128(ALONG_Z)],
        (outer, *strips),
        [floats(rows) for rows in [PLANES * GROUP] + sorted_rows],
        cost=pl.CostEstimate(flops=10**10, bytes_accessed=0, transcendentals=0),
    )
    near_msg, far_msg = swapped((near_msg, far_msg), "cross")
    pairs = [(i, i ^ 1) for i in range(sizes[0])]
    passed2_rest = lax.ppermute(turn_msg, "curve", pairs)
    post, own_slots = call(
        join_kernel,
        "VVVVV",
        "VV",
        [rows128(ALL_PLANES * PAIR), jax.ShapeDtypeStruct((24, 128), jnp.int32)],
        strips,
        [floats(rows) for rows in sorted_rows],
    )
    slots, outer_post, next_outer = call(
        outer_kernel,
        "VVVV",
        "VVV",
        [
            jax.ShapeDtypeStruct((72, 128), jnp.int32),
            rows128(ALL_PLANES * GROUP),
            rows128(ALL_PLANES * GROUP),
        ],
        (own_slots, post, near_msg, far_msg),
        [floats(SLOTS * SLOT), pltpu.SMEM((72, 128), jnp.int32), pltpu.SemaphoreType.DMA],
    )
    arriving = (cells, mate_msg, other_msg, mate_rest, passed_rest, passed2_rest)
    return call(
        steps_kernel,
        "VVVVVVVVVV",
        "H",
        [jax.ShapeDtypeStruct(populations.shape, jnp.float32)],
        (slots, post, outer_post, next_outer, *arriving),
        [
            floats(SLOTS * SLOT),
            floats(ALL_PLANES * PAIR),
            floats(ALL_PLANES * GROUP),
            pltpu.VMEM(populations.shape, jnp.float32),
            pltpu.SMEM((72, 128), jnp.int32),
            pltpu.SemaphoreType.DMA((SLOTS + 1,)),
        ],
    )[0]


def solution(mesh):
    return jax.shard_map(
        per_device,
        mesh=mesh,
        in_specs=(
            P(("curve", "cross"), None, None),
            P(("curve", "cross"), None),
            P(("curve", "cross"), None),
            P(),
            P(("curve", "cross")),
        ),
        out_specs=P(("curve", "cross"), None, None),
        check_vma=False,
    )
```

```python
import functools
import itertools

import jax
import jax.numpy as jnp
import numpy as np
from jax import lax
from jax.experimental import pallas as pl
from jax.experimental.pallas import tpu as pltpu
from jax.sharding import PartitionSpec as P

EDGE = 16
STEPS = 3
SLOTS = 3
POPS = 19
PLANES = SLOTS * POPS + SLOTS
FLAG0 = SLOTS * POPS
GROUP = 24
PLANE = 3 * GROUP
SLOT = POPS * PLANE
CELL = 40
CELLS = PLANES * CELL
LANDINGS = CELLS + 8
OWN2 = LANDINGS + 8
OUTWARD = SLOTS * 5 + SLOTS
LAYERS = 2 * PLANES + OUTWARD
RIM = 11 * EDGE
REST = POPS * EDGE + 10 * EDGE
ALONG_Z = 128
HALF = REST - ALONG_Z
SECOND = 6 * GROUP + ALONG_Z
PAIR = 2 * GROUP
QUADS = PLANES // 4
TABLE = RIM
STRIPS = RIM + 8
FAR = QUADS * GROUP
EDGE_TABLE = FAR + 3 * GROUP
EDGE_ROWS = EDGE_TABLE + 24
NEAR_ROWS, FAR_ROWS = EDGE_ROWS + 16, EDGE_ROWS + 24
NOWHERE = PLANES * GROUP
ALL_PLANES = PLANES + POPS
LIMIT = 20 * 1024 * 1024
WIDE_LIMIT = 127 * 512 * 1024

VELOCITY = [
    (0, 0, 0),
    (1, 0, 0),
    (-1, 0, 0),
    (0, 1, 0),
    (0, -1, 0),
    (0, 0, 1),
    (0, 0, -1),
    (1, 1, 0),
    (-1, -1, 0),
    (1, -1, 0),
    (-1, 1, 0),
    (1, 0, 1),
    (-1, 0, -1),
    (1, 0, -1),
    (-1, 0, 1),
    (0, 1, 1),
    (0, -1, -1),
    (0, 1, -1),
    (0, -1, 1),
]
NORTHWARD, SOUTHWARD = (
    [s * POPS + p for s in range(SLOTS) for p in range(POPS) if VELOCITY[p][1] == side]
    + [FLAG0 + s for s in range(SLOTS)]
    for side in (1, -1)
)
THIRD = [
    (pop, source, *((32 + 16 * k, 9) if k < 4 else (16 * (k - 4), 10)))
    for k, (pop, source) in enumerate(
        [(p, 32) for p in (4, 8, 9, 16, 18)] + [(p, 80) for p in (3, 7, 10, 15, 17)]
    )
]
OPPOSITE = [0, 2, 1, 4, 3, 6, 5, 8, 7, 10, 9, 12, 11, 14, 13, 16, 15, 18, 17]


def lanes_iota():
    return lax.broadcasted_iota(jnp.int32, (8, 128), 1)


def is_even(axis, unit=1):
    return lax.rem(lax.axis_index(axis) // unit, 2) == 0


def rows_iota():
    return lax.broadcasted_iota(jnp.int32, (8, 128), 0)


def aligned(start, size=8):
    return pl.ds(pl.multiple_of(start, 8), size)


def move_slots(moves, curve_size, cross_size):
    curve, cross = lax.axis_index("curve"), lax.axis_index("cross")

    def landed(source, target):
        inside = (source >= 0) & (source < curve_size) & (target >= 0) & (target < curve_size)
        row = jnp.clip(source, 0, curve_size - 1) * cross_size + cross
        rank = target * cross_size + cross
        hit = inside & (moves[0, row] >= 0) & (moves[1, row] == rank)
        return jnp.where(hit, moves[2, row], -1)

    return (
        landed(curve - 1, curve),
        landed(curve + 1, curve),
        landed(curve - 2, curve - 1),
        landed(curve, curve - 1),
        landed(curve + 2, curve + 1),
        landed(curve, curve + 1),
    )


def pack_kernel(
    curve_size,
    cross_size,
    moves_hbm,
    counts_hbm,
    pops_hbm,
    flags_hbm,
    neighbours_hbm,
    cells_hbm,
    mate_hbm,
    other_hbm,
    mate2_hbm,
    other2_hbm,
    rest_hbm,
    moves,
    counts,
    pops,
    flags,
    neighbours,
    cells,
    up_msg,
    down_msg,
    up2_msg,
    down2_msg,
    rest_msg,
    wide_flags,
    plane_flags,
    site_flags,
    near,
    sems,
):
    started = []

    def copy(source, target):
        one = pltpu.make_async_copy(source, target, sems.at[len(started)])
        one.start()
        started.append(one)
        return one

    flags_copy = copy(flags_hbm, flags)
    copies = [copy(pops_hbm.at[s], pops.at[s]) for s in range(SLOTS)]
    small = [
        copy(neighbours_hbm, neighbours),
        copy(counts_hbm, counts),
        copy(moves_hbm, moves),
    ]
    for one in small:
        one.wait()

    near[...] = jnp.zeros_like(near)
    named = neighbours[...]
    slot = jnp.where(named >= 0, lax.rem(jnp.maximum(named, 0), SLOTS), SLOTS)
    near[0:SLOTS, 0 : named.shape[1]] = slot.astype(jnp.float32)
    for ref, row in ((cells, CELLS), (up_msg, TABLE), (down_msg, TABLE)):
        ref[row : row + 8, :] = near[...]

    wide_flags[...] = jnp.zeros_like(wide_flags)
    flags_copy.wait()
    wide_flags[0:SLOTS, 0 : flags.shape[1]] = flags[...].astype(jnp.float32)
    span = EDGE + 2
    for x in range(EDGE):
        start = (x + 1) * span * span
        base = start // 128 * 128
        window = wide_flags[:, base : base + 512]
        window = pltpu.roll(window, (512 - (start - base)) % 512, axis=1)
        plane_flags[8 * x : 8 * x + 8, :] = window[:, :384].astype(jnp.bfloat16)
    lane_in = lax.broadcasted_iota(jnp.int32, (384, 256), 0)
    site = lax.broadcasted_iota(jnp.int32, (384, 256), 1)
    chosen = lane_in == (site // EDGE + 1) * span + site % EDGE + 1
    product = jnp.dot(
        plane_flags[...],
        jnp.where(chosen, 1.0, 0.0).astype(jnp.bfloat16),
        preferred_element_type=jnp.float32,
    )
    site_flags[0:128, :] = product[:, :128]
    site_flags[128:256, :] = product[:, 128:]
    for s in range(SLOTS):
        live = s < counts[0]
        for y in range(2):
            piece = site_flags[pl.ds(128 * y + s, EDGE, stride=8), :]
            is_fluid = (piece == 1.0) & live
            row = (FLAG0 + s) * CELL + y * EDGE
            cells[row : row + EDGE, :] = jnp.where(is_fluid, 1.0, 0.0)

    for s in range(SLOTS):
        copies[s].wait()
        for x in range(EDGE):
            for y in range(2):
                tile = 2 * x + y
                for p, size in ((0, 8), (8, 8), (16, 3)):
                    row = (s * POPS + p) * CELL + y * EDGE + x
                    cells[pl.ds(row, size, stride=CELL), :] = pops[
                        s, p : p + size, 128 * tile : 128 * tile + 128
                    ]

    @pl.loop(0, SLOTS)
    def _(s):
        @pl.loop(0, 4, unroll=2)
        def _(c):
            base = s * (POPS * CELL) + c * 8
            view = cells.at[aligned(base, (POPS - 1) * CELL + 8), :]
            h = [view[p * CELL : p * CELL + 8, :] for p in range(POPS)]
            for p, value in enumerate(collided(h)):
                view[p * CELL : p * CELL + 8, :] = value

    for i, slot in enumerate(move_slots(moves, curve_size, cross_size)):
        value = jnp.full((1, 128), slot, jnp.int32)
        cells[LANDINGS + i : LANDINGS + i + 1, :] = value.astype(jnp.float32)

    body_copy = copy(cells.at[:OWN2], cells_hbm.at[:OWN2])

    for y in range(2):
        for msg, x0, first in ((up_msg, 15, 1), (down_msg, 0, 2)):
            step = -1 if x0 else 1
            for k in range(2):
                out = STRIPS + y * LAYERS + k * PLANES
                msg[out : out + PLANES, :] = cells[
                    pl.ds(y * EDGE + x0 + step * k, PLANES, stride=CELL), :
                ]
            row = y * EDGE + x0 + 2 * step
            out = STRIPS + y * LAYERS + 2 * PLANES
            for s in range(SLOTS):
                base = s * POPS * CELL + row
                msg[out + 5 * s : out + 5 * s + 1, :] = cells[pl.ds(base + first * CELL, 1), :]
                msg[out + 5 * s + 1 : out + 5 * s + 5, :] = cells[
                    pl.ds(base + (first + 6) * CELL, 4, stride=2 * CELL), :
                ]
            msg[out + 5 * SLOTS : out + OUTWARD, :] = cells[
                pl.ds(FLAG0 * CELL + row, SLOTS, stride=CELL), :
            ]

    here = lax.axis_index("curve") * cross_size + lax.axis_index("cross")
    leaving = jnp.maximum(moves[0, here], 0)
    lane = lanes_iota()
    for v in range(2):
        halves = [
            [cells[aligned(leaving * (POPS * CELL) + p * CELL + y * EDGE + v * 8), :] for y in (0, 1)]
            for p in range(POPS)
        ]
        outer = [jnp.where(lane < 64, first, second) for first, second in halves]
        middle = (lane >= 32) & (lane < 96)
        sets = [
            jnp.where(middle, pltpu.roll(outer[p + 1], 64, axis=1), outer[p])
            for p in range(0, POPS - 1, 2)
        ]
        sets += [outer[POPS - 1], jnp.zeros_like(outer[0])]
        for pop, source, target, which in THIRD:
            moved = pltpu.roll(outer[pop], (target - source) % 128, axis=1)
            sets[which] = jnp.where(lane // 16 == target // 16, moved, sets[which])
        for k, value in enumerate(sets):
            row = k * EDGE + v * 8
            up_msg[row : row + 8, :] = value
            down_msg[row : row + 8, :] = value
        for p, (first, second) in enumerate(halves):
            row = p * EDGE + v * 8
            rest_msg[row : row + 8, :] = jnp.where(lane < 32, second, first)
        for p in range(0, POPS, 2):
            value = halves[p][1]
            if p + 1 < POPS:
                value = jnp.where(middle, value, pltpu.roll(halves[p + 1][1], 64, axis=1))
            row = (POPS + p // 2) * EDGE + v * 8
            rest_msg[row : row + 8, :] = value
    for s in range(SLOTS):

        @pl.when(leaving == s)
        def _():
            for y in range(2):
                for k in range(3):
                    out = (y * 3 + k) * GROUP
                    row = s * POPS * CELL + y * EDGE + k
                    up2_msg[out : out + POPS, :] = cells[pl.ds(row + 13, POPS, stride=CELL), :]
                    down2_msg[out : out + POPS, :] = cells[pl.ds(row, POPS, stride=CELL), :]

    cells[OWN2 : OWN2 + 6 * GROUP, :] = up2_msg[: 6 * GROUP, :]
    cells[OWN2 + 6 * GROUP :, :] = down2_msg[: 6 * GROUP, :]
    for msg in (up2_msg, down2_msg):
        msg[6 * GROUP :, :] = rest_msg[HALF:, :]
    last = [copy(cells.at[OWN2:], cells_hbm.at[OWN2:]), copy(rest_msg, rest_hbm)]
    count = len(started)
    for i, (up, down, mate, other, unit) in enumerate(
        ((up_msg, down_msg, mate_hbm, other_hbm, 1), (up2_msg, down2_msg, mate2_hbm, other2_hbm, 2))
    ):
        first, second = sems.at[count + 2 * i], sems.at[count + 2 * i + 1]
        even = is_even("curve", unit)

        @pl.when(even)
        def _():
            pltpu.make_async_copy(up, mate, first).start()
            pltpu.make_async_copy(down, other, second).start()

        @pl.when(jnp.logical_not(even))
        def _():
            pltpu.make_async_copy(down, mate, first).start()
            pltpu.make_async_copy(up, other, second).start()

        last.append(pltpu.make_async_copy(up, mate, first))
        last.append(pltpu.make_async_copy(down, other, second))
    body_copy.wait()
    for one in last:
        one.wait()


def spread_kernel(cells, outer):
    low = lanes_iota() < 64
    for q in range(PLANES):
        for v in range(2):
            row = q * CELL + v * 8
            first, second = cells[row : row + 8, :], cells[row + EDGE : row + EDGE + 8, :]
            row = q * GROUP + v * 8
            outer[row : row + 8, :] = jnp.where(low, first, second)


def sort_messages(mate_msg, other_msg, mate2_msg, other2_msg, low_msg, high_msg, low2, high2):
    for mate, other, low, high, unit in (
        (mate_msg, other_msg, low_msg, high_msg, 1),
        (mate2_msg, other2_msg, low2, high2, 2),
    ):
        even = is_even("curve", unit)

        @pl.when(even)
        def _():
            low[...] = other[...]
            high[...] = mate[...]

        @pl.when(jnp.logical_not(even))
        def _():
            low[...] = mate[...]
            high[...] = other[...]


def landed_slots(cells):
    return [jnp.max(cells[LANDINGS + i : LANDINGS + i + 1, :]) for i in range(6)]


def rim_of(msg, p, v):
    row = p // 2 * EDGE + v * 8
    value = msg[row : row + 8, :]
    return pltpu.roll(value, 64, axis=1) if p % 2 else value


def sel4(parts, lane):
    first = jnp.where(lane < 32, parts[0], parts[1])
    second = jnp.where(lane < 96, parts[2], parts[3])
    return jnp.where(lane < 64, first, second)


def strip_rows(first, row0, step):
    pieces = []
    for k in range(2):
        pieces.append(
            (PLANES, lambda size, row: pl.ds(row, PLANES, stride=size), row0 + step * k, STRIPS + k * PLANES)
        )
    row, source = row0 + 2 * step, STRIPS + 2 * PLANES
    for s in range(SLOTS):
        plane = s * POPS + first
        pieces.append((1, lambda size, row, plane=plane: pl.ds(plane * size + row, 1), row, source))
        pieces.append(
            (
                4,
                lambda size, row, plane=plane: pl.ds(
                    (plane + 6) * size + row, 4, stride=2 * size
                ),
                row,
                source + 1,
            )
        )
        source += 5
    pieces.append(
        (SLOTS, lambda size, row: pl.ds(FLAG0 * size + row, SLOTS, stride=size), row, source)
    )
    return pieces


def edge_kernel(
    own_outer,
    cells,
    mate_msg,
    other_msg,
    mate2_msg,
    other2_msg,
    near_msg,
    far_msg,
    turn_msg,
    outer,
    low_msg,
    high_msg,
    low2_msg,
    high2_msg,
):
    sort_messages(
        mate_msg, other_msg, mate2_msg, other2_msg, low_msg, high_msg, low2_msg, high2_msg
    )
    from_low, from_high, low_low, low_me, high_high, high_me = landed_slots(cells)
    low = lanes_iota() < 64
    for q in range(PLANES):
        for v in range(2):
            row = q * GROUP + v * 8
            outer[row : row + 8, :] = own_outer[row : row + 8, :]

    def both(first, second):
        lane = lax.broadcasted_iota(jnp.int32, first.shape, 1)
        return jnp.where(lane < 64, first, second)

    for msg, row0, step, first in ((high_msg, 16, 1, 2), (low_msg, 23, -1, 1)):
        for count, planes, row, source in strip_rows(first, row0, step):
            outer[planes(GROUP, row), :] = both(
                msg[source : source + count, :],
                msg[LAYERS + source : LAYERS + source + count, :],
            )
    lane = lanes_iota()
    for s, (slot, msg) in itertools.product(
        range(SLOTS), ((from_low, low_msg), (from_high, high_msg))
    ):

        @pl.when(slot == s)
        def _():
            for v in range(2):
                values = [rim_of(msg, p, v) for p in range(POPS)]
                for pop, target, source, which in THIRD:
                    row = which * EDGE + v * 8
                    moved = pltpu.roll(msg[row : row + 8, :], (target - source) % 128, axis=1)
                    values[pop] = jnp.where(lane // 16 == target // 16, moved, values[pop])
                for p, value in enumerate(values):
                    row = (s * POPS + p) * GROUP + v * 8
                    outer[row : row + 8, :] = value

    for s in range(SLOTS):
        for slot, msg, row0 in (
            (low_low, low2_msg, 21),
            (low_me, cells.at[OWN2:], 21),
            (high_high, high2_msg, 16),
            (high_me, cells.at[OWN2 + 6 * GROUP :], 16),
        ):

            @pl.when(slot == s)
            def _():
                for k in range(3):
                    outer[pl.ds(s * POPS * GROUP + row0 + k, POPS, stride=GROUP), :] = both(
                        msg[k * GROUP : k * GROUP + POPS, :],
                        msg[(3 + k) * GROUP : (3 + k) * GROUP + POPS, :],
                    )

    from_above = is_even("curve")
    for row in range(0, ALONG_Z, 8):
        tail = slice(6 * GROUP + row, 6 * GROUP + row + 8)
        value = jnp.where(from_above, high2_msg[tail, :], low2_msg[tail, :])
        turn_msg[row : row + 8, :] = value

    even = is_even("cross")

    def send(row, north, south):
        near_msg[row : row + 8, :] = jnp.where(even, north, south)
        far_msg[row : row + 8, :] = jnp.where(even, south, north)

    for v in range(3):

        def plane(q):
            return outer[q * GROUP + v * 8 : q * GROUP + v * 8 + 8, :]

        for quad in range(QUADS):
            parts = [plane(4 * quad)]
            parts += [pltpu.roll(plane(4 * quad + k), 32 * k, axis=1) for k in (1, 2, 3)]
            send(quad * GROUP + v * 8, sel4(parts[1:] + parts[:1], lane), sel4(parts, lane))
        for part in range(3):
            values = []
            for planes, source in ((NORTHWARD, 80), (SOUTHWARD, 32)):
                value = None
                for k, q in enumerate(planes[8 * part : 8 * part + 8]):
                    moved = pltpu.roll(plane(q), (16 * k - source) % 128, axis=1)
                    value = moved if value is None else jnp.where(lane < 16 * k, value, moved)
                values.append(value)
            send(FAR + part * GROUP + v * 8, *values)
    tables = (low_msg, TABLE), (cells, CELLS), (high_msg, TABLE)
    for i, (ref, row) in enumerate(tables):
        value = ref[row : row + 8, :]
        send(EDGE_TABLE + 8 * i, value, value)


def collided(h):
    shear = 1.0 / 0.6
    rest = h[0]
    sx, dx = h[1] + h[2], h[1] - h[2]
    sy, dy = h[3] + h[4], h[3] - h[4]
    sz, dz = h[5] + h[6], h[5] - h[6]
    s7, d7 = h[7] + h[8], h[7] - h[8]
    s9, d9 = h[9] + h[10], h[9] - h[10]
    s11, d11 = h[11] + h[12], h[11] - h[12]
    s13, d13 = h[13] + h[14], h[13] - h[14]
    s15, d15 = h[15] + h[16], h[15] - h[16]
    s17, d17 = h[17] + h[18], h[17] - h[18]
    txy, txz, tyz = s7 + s9, s11 + s13, s15 + s17
    pxy, pxz, pyz = s7 - s9, s11 - s13, s15 - s17
    ax, bx = d7 + d9, d11 + d13
    ay, by = d7 - d9, d15 + d17
    az, bz = d11 - d13, d15 - d17
    axes = sx + sy + sz
    diags = txy + txz + tyz
    rho = rest * (1.0 / 3.0) + axes * (1.0 / 18.0) + diags * (1.0 / 36.0)
    fx, fy, fz = ax + bx, ay + by, az + bz
    jx = dx * (1.0 / 18.0) + fx * (1.0 / 36.0)
    jy = dy * (1.0 / 18.0) + fy * (1.0 / 36.0)
    jz = dz * (1.0 / 18.0) + fz * (1.0 / 36.0)
    inverse = 1.0 / rho
    ux, uy, uz = jx * inverse, jy * inverse, jz * inverse
    qxx, qyy, qzz = jx * ux, jy * uy, jz * uz
    total = qxx + qyy + qzz

    energy = -10.0 * rest - axes * (11.0 / 18.0) + diags * (8.0 / 36.0)
    energy = (energy + 11.0 * rho - 19.0 * total) * (1.19 / 2394.0)
    square = 4.0 * rest - axes * (4.0 / 18.0) + diags * (1.0 / 36.0)
    square = (square - 3.0 * rho + 5.5 * total) * (1.4 / 252.0)
    axis_x = (3.0 * sx - axes) * (1.0 / 18.0)
    diag_x = (diags - 3.0 * tyz) * (1.0 / 36.0)
    want_x = 3.0 * qxx - total
    stress_x = (axis_x + diag_x - want_x) * (shear / 36.0)
    third_x = (diag_x - 2.0 * axis_x + 0.5 * want_x) * (1.4 / 72.0)
    axis_w = (sy - sz) * (1.0 / 18.0)
    diag_w = (txy - txz) * (1.0 / 36.0)
    want_w = qyy - qzz
    stress_w = (axis_w + diag_w - want_w) * (shear / 12.0)
    third_w = (diag_w - 2.0 * axis_w + 0.5 * want_w) * (1.4 / 24.0)

    rest_out = rest - 3.0 * (12.0 * square - 30.0 * energy)
    common = -18.0 * (11.0 * energy + 4.0 * square)
    along_x = 18.0 * (stress_x - 2.0 * third_x)
    along_w = 18.0 * (stress_w - 2.0 * third_w)
    ex = common + 2.0 * along_x
    ey = common - along_x + along_w
    ez = common - along_x - along_w
    common = 36.0 * (8.0 * energy + square)
    across_x = 36.0 * (stress_x + third_x)
    across_w = 36.0 * (stress_w + third_w)
    exy = common + across_x + across_w
    exz = common + across_x - across_w
    eyz = common - 2.0 * across_x
    cxy = shear * (0.25 * pxy - 9.0 * jx * uy)
    cxz = shear * (0.25 * pxz - 9.0 * jx * uz)
    cyz = shear * (0.25 * pyz - 9.0 * jy * uz)

    def flux(d, f, j):
        return (f * (1.0 / 36.0) - d * (4.0 / 18.0) + j * (2.0 / 3.0)) * (1.2 / 40.0)

    hx, hy, hz = flux(dx, fx, jx), flux(dy, fy, jy), flux(dz, fz, jz)
    mx = (ax - bx) * (1.98 / 8.0)
    my = (by - ay) * (1.98 / 8.0)
    mz = (az - bz) * (1.98 / 8.0)
    hx36, hy36, hz36 = 36.0 * hx, 36.0 * hy, 36.0 * hz
    xy_x, xz_x = hx36 + mx, hx36 - mx
    yz_y, xy_y = hy36 + my, hy36 - my
    xz_z, yz_z = hz36 + mz, hz36 - mz
    ox, oy, oz = -2.0 * hx36, -2.0 * hy36, -2.0 * hz36

    out = [rest_out]

    def pair(i, even, odd):
        out.append(h[i] - (even + odd))
        out.append(h[i + 1] - (even - odd))

    pair(1, ex, ox)
    pair(3, ey, oy)
    pair(5, ez, oz)
    pair(7, exy + cxy, xy_x + xy_y)
    pair(9, exy - cxy, xy_x - xy_y)
    pair(11, exz + cxz, xz_x + xz_z)
    pair(13, exz - cxz, xz_x - xz_z)
    pair(15, eyz + cyz, yz_y + yz_z)
    pair(17, eyz - cyz, yz_y - yz_z)
    return out


def collide_all(h_ref, flags, posts, parts=((0, 1), (2,))):
    for groups in parts:
        ref = posts[groups[0] // 2]
        size = len(groups) * GROUP

        @pl.loop(0, SLOTS)
        def _(s):
            @pl.loop(0, size // 8, unroll=3)
            def _(c):
                is_fluid = flags[groups[0] // 2][aligned((FLAG0 + s) * size + c * 8), :] > 0.0
                start = s * SLOT + groups[0] * GROUP + c * 8
                h_view = h_ref.at[aligned(start, (POPS - 1) * PLANE + 8), :]
                start = s * (POPS * size) + c * 8
                view = ref.at[aligned(start, (POPS - 1) * size + 8), :]
                h = [h_view[p * PLANE : p * PLANE + 8, :] for p in range(POPS)]
                for p, value in enumerate(collided(h)):
                    view[p * size : p * size + 8, :] = jnp.where(is_fluid, value, jnp.nan)


def hide_walls(ref, size):
    @pl.loop(0, SLOTS)
    def _(s):
        @pl.loop(0, size // 8)
        def _(c):
            is_fluid = ref[aligned((FLAG0 + s) * size + c * 8), :] > 0.0
            start = s * (POPS * size) + c * 8
            view = ref.at[aligned(start, (POPS - 1) * size + 8), :]
            for p in range(POPS):
                row = p * size
                view[row : row + 8, :] = jnp.where(is_fluid, view[row : row + 8, :], jnp.nan)


def stream_all(posts, h_ref, flags, table, groups, vregs, finish=None):
    lane = lanes_iota()
    row = rows_iota()
    low = lane < 64

    def one_slot(s):
        views = {}

        def view(which, key):
            if (which, key) not in views:
                start = s * (POPS * GROUP) if key == "own" else table[key[0] * 8 + s, key[1]]
                start = start if which else 2 * start
                views[which, key] = posts[which].at[
                    aligned(start, POPS * (GROUP if which else PAIR)), :
                ]
            return views[which, key]

        def load(key, pop, group, v):
            if group == 2:
                row = pop * GROUP + v * 8
            else:
                row = pop * PAIR + group * GROUP + v * 8
            return view(group // 2, key)[row : row + 8, :]

        h_view = h_ref.at[aligned(s * SLOT, SLOT), :]

        def shifted(pop, group, j, dy, dz):
            cx = VELOCITY[pop][0]

            def rows(key, v):
                return load(key, pop, group, v)

            def look(i, j, dx, v):
                if (dx, dy, dz) == (0, 0, 0):
                    return rows("own", v)
                if j is None:
                    return jnp.where(low, look(i, 1, dx, v), look(i, -1, dx, v))
                region = (i + 1) * 3 + j + 1
                return rows((region, VELOCITY.index((dx, dy, dz)) - 1), v)

            need_last = vregs == 3
            values = [look(0, j, 0, 0), look(0, j, 0, 1)]
            if need_last:
                if dy == 0 and dz == 0:
                    values.append(rows("own", 2))
                else:
                    values.append(jnp.where(row < 4, look(1, j, 0, 2), look(-1, j, 0, 2)))
            if cx == 0:
                return values
            turn = 1 if cx > 0 else 7
            rolled = [pltpu.roll(value, turn, axis=0) for value in values]
            if cx > 0:
                before = pltpu.roll(look(0, j, -1, 2), 1, axis=0)
                result = [
                    jnp.where(row == 0, before, rolled[0]),
                    jnp.where(row == 0, rolled[0], rolled[1]),
                ]
                if need_last:
                    edge = pltpu.roll(look(1, j, -1, 1), 1, axis=0)
                    result.append(jnp.where(row == 0, edge, rolled[2]))
                return result
            after = pltpu.roll(look(0, j, 1, 2), 7, axis=0)
            result = [
                jnp.where(row == 7, rolled[1], rolled[0]),
                jnp.where(row == 7, after, rolled[1]),
            ]
            if need_last:
                edge = pltpu.roll(look(-1, j, 1, 0), 7, axis=0)
                result.append(jnp.where(row == 7, edge, rolled[2]))
            return result

        for pop in range(POPS):
            cx, cy, cz = VELOCITY[pop]
            kept = {}

            def source(*key):
                if key not in kept:
                    kept[key] = shifted(pop, *key)
                return kept[key]

            def along_y(group, dz):
                values = source(group, None if group == 2 else 0, 0, dz)
                if cy == 0:
                    return values
                other = (group - cy) % 3
                if group != 2 and other != 2:
                    carried = source(other, 0, 0, dz)
                else:
                    carried = source(other, cy if group == 2 else 0, -cy, dz)
                mask = lane >= 112 if cy > 0 else lane < 16
                return [jnp.where(mask, b, a) for a, b in zip(values, carried)]

            for group in groups:
                values = along_y(group, 0)
                turn = (16 * cy + cz) % 128
                if turn:
                    values = [pltpu.roll(value, turn, axis=1) for value in values]
                if cz:
                    turn = (16 * cy - 15 * cz) % 128
                    wrapped = [pltpu.roll(value, turn, axis=1) for value in along_y(group, -cz)]
                    mask = lane % 16 == (0 if cz > 0 else 15)
                    values = [jnp.where(mask, b, a) for a, b in zip(values, wrapped)]
                for v, value in enumerate(values[:vregs]):
                    if pop:
                        value = jnp.where(value != value, load("own", OPPOSITE[pop], group, v), value)
                    if finish is not None:
                        is_fluid = flags[group // 2][
                            aligned((FLAG0 + s) * PAIR + group * GROUP + v * 8), :
                        ]
                        value = jnp.where(is_fluid > 0.0, value, 0.0)
                    target = pop * PLANE + group * GROUP + v * 8
                    h_view[target : target + 8, :] = value

    @pl.loop(0, SLOTS)
    def _(s):
        one_slot(s)
        if finish is not None:
            finish(s)


def join_kernel(
    cells,
    mate_msg,
    other_msg,
    mate2_msg,
    other2_msg,
    post_ref,
    slots,
    low_msg,
    high_msg,
    low2_msg,
    high2_msg,
):
    sort_messages(
        mate_msg, other_msg, mate2_msg, other2_msg, low_msg, high_msg, low2_msg, high2_msg
    )
    for i, (ref, row) in enumerate(((low_msg, TABLE), (cells, CELLS), (high_msg, TABLE))):
        slots[8 * i : 8 * i + 8, :] = first_rows(ref[row : row + 8, :])

    from_low, from_high, low_low, low_me, high_high, high_me = landed_slots(cells)
    post_ref[PLANES * PAIR :, :] = jnp.full((POPS * PAIR, 128), jnp.nan, jnp.float32)
    for q in range(PLANES):
        for y in range(2):
            start = q * PAIR + y * GROUP
            post_ref[start : start + EDGE, :] = cells[
                q * CELL + y * EDGE : q * CELL + (y + 1) * EDGE, :
            ]
    for s, (slot, msg) in itertools.product(
        range(SLOTS), ((from_low, low_msg), (from_high, high_msg))
    ):

        @pl.when(slot == s)
        def _():
            for p in range(POPS):
                for v in range(2):
                    rim = rim_of(msg, p, v)
                    row = (s * POPS + p) * PAIR + v * 8
                    post_ref[row : row + 8, :] = rim
                    post_ref[row + GROUP : row + GROUP + 8, :] = rim

    for msg, row0, step, first in ((high_msg, 16, 1, 2), (low_msg, 23, -1, 1)):
        for y in range(2):
            for count, planes, row, source in strip_rows(first, row0, step):
                source += y * LAYERS
                post_ref[planes(PAIR, row + y * GROUP), :] = msg[source : source + count, :]
    for s in range(SLOTS):
        for slot, msg, row0 in (
            (low_low, low2_msg, 21),
            (low_me, cells.at[OWN2:], 21),
            (high_high, high2_msg, 16),
            (high_me, cells.at[OWN2 + 6 * GROUP :], 16),
        ):

            @pl.when(slot == s)
            def _():
                for y in range(2):
                    for k in range(3):
                        row = s * POPS * PAIR + y * GROUP + row0 + k
                        source = (y * 3 + k) * GROUP
                        post_ref[pl.ds(row, POPS, stride=PAIR), :] = msg[source : source + POPS, :]
    hide_walls(post_ref, PAIR)


def first_rows(slot):
    slot = slot.astype(jnp.int32)
    return jnp.where(slot == SLOTS, NOWHERE, slot * (POPS * GROUP))


def outer_kernel(
    own_slots, first_post, near_msg, far_msg, slots, outer_ref, next_ref, h_ref, table, sem
):
    even = is_even("cross")

    def received(row):
        near, far = near_msg[row : row + 8, :], far_msg[row : row + 8, :]
        return jnp.where(even, far, near), jnp.where(even, near, far)

    for i in range(3):
        south, north = received(EDGE_TABLE + 8 * i)
        slots[24 * i : 24 * i + 8, :] = first_rows(south)
        slots[24 * i + 8 : 24 * i + 16, :] = own_slots[8 * i : 8 * i + 8, :]
        slots[24 * i + 16 : 24 * i + 24, :] = first_rows(north)
    table_copy = pltpu.make_async_copy(slots, table, sem)
    table_copy.start()

    nothing = jnp.full((8, 128), jnp.nan, jnp.float32)
    for row in range(0, POPS * GROUP, 8):
        outer_ref[NOWHERE + row : NOWHERE + row + 8, :] = nothing
        next_ref[NOWHERE + row : NOWHERE + row + 8, :] = nothing
    lane = lanes_iota()
    for v in range(3):

        def rows(q):
            return slice(q * GROUP + v * 8, q * GROUP + v * 8 + 8)

        for quad in range(QUADS):
            south, north = received(quad * GROUP + v * 8)
            for k in range(4):
                value = jnp.where(lane // 32 == (k + 3) % 4, south, north)
                if k:
                    value = pltpu.roll(value, 128 - 32 * k, axis=1)
                outer_ref[rows(4 * quad + k), :] = value
        for part in range(3):
            values = received(FAR + part * GROUP + v * 8)
            for planes, target, value in zip((NORTHWARD, SOUTHWARD), (80, 32), values):
                for k, q in enumerate(planes[8 * part : 8 * part + 8]):
                    moved = pltpu.roll(value, (target - 16 * k) % 128, axis=1)
                    outer_ref[rows(q), :] = jnp.where(
                        lane // 16 == target // 16, moved, outer_ref[rows(q), :]
                    )
    for row in range(FLAG0 * GROUP, NOWHERE, 8):
        next_ref[row : row + 8, :] = outer_ref[row : row + 8, :]
    hide_walls(outer_ref, GROUP)
    table_copy.wait()
    flags = (first_post, outer_ref)
    stream_all(flags, h_ref, flags, table, (2,), 3)
    collide_all(h_ref, flags, (None, next_ref), ((2,),))


def steps_kernel(
    slots,
    first_post,
    first_outer,
    next_outer,
    cells,
    mate_msg,
    other_msg,
    mate_rest,
    passed_rest,
    passed2_rest,
    out_hbm,
    h_ref,
    post_ref,
    outer_ref,
    out,
    table,
    sems,
):
    table_copy = pltpu.make_async_copy(slots, table, sems.at[SLOTS])
    table_copy.start()
    post_ref[...] = first_post[...]
    nothing = jnp.full((8, 128), jnp.nan, jnp.float32)
    for row in range(0, POPS * GROUP, 8):
        outer_ref[NOWHERE + row : NOWHERE + row + 8, :] = nothing

    def rest(row, is_mate):
        if is_mate:
            return mate_rest[row : row + 8, :]
        if row < HALF:
            return passed_rest[row : row + 8, :]
        return passed2_rest[row - HALF : row - HALF + 8, :]

    from_low, from_high = landed_slots(cells)[:2]
    lane = lanes_iota()
    even = is_even("curve")
    odd = jnp.logical_not(even)
    for s, (slot, wanted, msg, is_mate) in itertools.product(
        range(SLOTS),
        (
            (from_low, odd, mate_msg, True),
            (from_low, even, other_msg, False),
            (from_high, even, mate_msg, True),
            (from_high, odd, other_msg, False),
        ),
    ):

        @pl.when((slot == s) & wanted)
        def _():
            for v in range(2):
                starts = [(FLAG0 + s) * PAIR + y * GROUP + v * 8 for y in range(2)]
                fluid = [first_post[row : row + 8, :] > 0.0 for row in starts]
                for p in range(POPS):
                    rim = rim_of(msg, p, v)
                    row = p * EDGE + v * 8
                    wide = rest(row, is_mate)
                    row = (POPS + p // 2) * EDGE + v * 8
                    middle = rest(row, is_mate)
                    if p % 2:
                        middle = pltpu.roll(middle, 64, axis=1)
                    first = jnp.where(lane < 32, rim, wide)
                    second = jnp.where(lane < 32, wide, jnp.where(lane < 96, middle, rim))
                    row = (s * POPS + p) * PAIR + v * 8
                    post_ref[row : row + 8, :] = jnp.where(fluid[0], first, jnp.nan)
                    row += GROUP
                    post_ref[row : row + 8, :] = jnp.where(fluid[1], second, jnp.nan)

    def finish(s):
        for x in range(EDGE):
            for y in range(2):
                tile = 2 * x + y
                for p, size in ((0, 8), (8, 8), (16, 3)):
                    row = s * SLOT + (p * PLANE + y * GROUP + x)
                    out[s, p : p + size, 128 * tile : 128 * tile + 128] = h_ref[
                        pl.ds(row, size, stride=PLANE), :
                    ]
        pltpu.make_async_copy(out.at[s], out_hbm.at[s], sems.at[s]).start()

    table_copy.wait()
    flags = (first_post, first_outer)
    stream_all((post_ref, first_outer), h_ref, flags, table, (0, 1), 3)
    collide_all(h_ref, flags, (post_ref, None), ((0, 1),))
    posts = (post_ref, next_outer)
    for _ in range(STEPS - 2):
        stream_all(posts, h_ref, flags, table, (0, 1, 2), 3)
        posts = (post_ref, outer_ref)
        collide_all(h_ref, flags, posts)
    stream_all(posts, h_ref, flags, table, (0, 1), 2, finish)
    for s in range(SLOTS):
        pltpu.make_async_copy(out.at[s], out_hbm.at[s], sems.at[s]).wait()


def swapped(value, axis, unit=1):
    count = lax.axis_size(axis)
    results = []
    for which in (0, 1):
        others = [i + (unit if i // unit % 2 == which else -unit) for i in range(count)]
        pairs = [(i, j if 0 <= j < count else i) for i, j in enumerate(others)]
        results.append(lax.ppermute(value[which], axis, pairs))
    return results


def rows128(count):
    return jax.ShapeDtypeStruct((count, 128), jnp.float32)


def call(kernel, in_spaces, out_spaces, outs, ins, scratch, limit=LIMIT, cost=None):
    spaces = {
        "S": pl.BlockSpec(memory_space=pltpu.SMEM),
        "V": pl.BlockSpec(memory_space=pltpu.VMEM),
        "H": pl.BlockSpec(memory_space=pltpu.HBM),
    }
    return pl.pallas_call(
        kernel,
        out_shape=outs,
        in_specs=[spaces[x] for x in in_spaces],
        out_specs=[spaces[x] for x in out_spaces],
        scratch_shapes=scratch,
        compiler_params=pltpu.CompilerParams(vmem_limit_bytes=limit),
        cost_estimate=cost,
    )(*ins)


def per_device(populations, site_flags, neighbours, migrations, counts):
    sizes = (lax.axis_size("curve"), lax.axis_size("cross"))
    moves = migrations.T
    floats = lambda rows: pltpu.VMEM((rows, 128), jnp.float32)
    messages = [
        OWN2 + 12 * GROUP,
        STRIPS + 2 * LAYERS,
        STRIPS + 2 * LAYERS,
        SECOND,
        SECOND,
        REST,
    ]
    cells, mate_msg, other_msg, mate2_msg, other2_msg, rest_msg = call(
        functools.partial(pack_kernel, *sizes),
        "HHHHH",
        "HHHHHH",
        [rows128(rows) for rows in messages],
        (moves, counts, populations, site_flags, neighbours),
        [
            pltpu.SMEM(moves.shape, jnp.int32),
            pltpu.SMEM(counts.shape, jnp.int32),
            pltpu.VMEM(populations.shape, jnp.float32),
            pltpu.VMEM(site_flags.shape, jnp.int32),
            pltpu.VMEM(neighbours.shape, jnp.int32),
            *[floats(rows) for rows in messages],
            pltpu.VMEM((8, 5888), jnp.float32),
            pltpu.VMEM((128, 384), jnp.bfloat16),
            floats(256),
            floats(8),
            pltpu.SemaphoreType.DMA((4 + SLOTS + 8,)),
        ],
        WIDE_LIMIT,
    )
    mate_msg, other_msg = swapped((mate_msg, other_msg), "curve")
    mate2_msg, other2_msg = swapped((mate2_msg, other2_msg), "curve", 2)
    assert sizes[0] % 2 == 0
    pairs = [(i, i ^ 1) for i in range(sizes[0])]
    mate_rest = lax.ppermute(rest_msg, "curve", pairs)
    pairs = [(i, i - 2 if i % 2 else i + 2) for i in range(sizes[0])]
    pairs = [pair for pair in pairs if 0 <= pair[1] < sizes[0]]
    passed_rest = lax.ppermute(mate_rest[:HALF], "curve", pairs)
    (outer,) = call(spread_kernel, "V", "V", [rows128(PLANES * GROUP)], (cells,), [])
    strips = (cells, mate_msg, other_msg, mate2_msg, other2_msg)
    sorted_rows = [messages[1], messages[1], messages[3], messages[3]]
    near_msg, far_msg, turn_msg = call(
        edge_kernel,
        "VVVVVV",
        "VVV",
        [rows128(NEAR_ROWS), rows128(FAR_ROWS), rows128(ALONG_Z)],
        (outer, *strips),
        [floats(rows) for rows in [PLANES * GROUP] + sorted_rows],
        cost=pl.CostEstimate(flops=10**10, bytes_accessed=0, transcendentals=0),
    )
    near_msg, far_msg = swapped((near_msg, far_msg), "cross")
    pairs = [(i, i ^ 1) for i in range(sizes[0])]
    passed2_rest = lax.ppermute(turn_msg, "curve", pairs)
    post, own_slots = call(
        join_kernel,
        "VVVVV",
        "VV",
        [rows128(ALL_PLANES * PAIR), jax.ShapeDtypeStruct((24, 128), jnp.int32)],
        strips,
        [floats(rows) for rows in sorted_rows],
    )
    slots, outer_post, next_outer = call(
        outer_kernel,
        "VVVV",
        "VVV",
        [
            jax.ShapeDtypeStruct((72, 128), jnp.int32),
            rows128(ALL_PLANES * GROUP),
            rows128(ALL_PLANES * GROUP),
        ],
        (own_slots, post, near_msg, far_msg),
        [floats(SLOTS * SLOT), pltpu.SMEM((72, 128), jnp.int32), pltpu.SemaphoreType.DMA],
    )
    arriving = (cells, mate_msg, other_msg, mate_rest, passed_rest, passed2_rest)
    return call(
        steps_kernel,
        "VVVVVVVVVV",
        "H",
        [jax.ShapeDtypeStruct(populations.shape, jnp.float32)],
        (slots, post, outer_post, next_outer, *arriving),
        [
            floats(SLOTS * SLOT),
            floats(ALL_PLANES * PAIR),
            floats(ALL_PLANES * GROUP),
            pltpu.VMEM(populations.shape, jnp.float32),
            pltpu.SMEM((72, 128), jnp.int32),
            pltpu.SemaphoreType.DMA((SLOTS + 1,)),
        ],
    )[0]


def solution(mesh):
    return jax.shard_map(
        per_device,
        mesh=mesh,
        in_specs=(
            P(("curve", "cross"), None, None),
            P(("curve", "cross"), None),
            P(("curve", "cross"), None),
            P(),
            P(("curve", "cross")),
        ),
        out_specs=P(("curve", "cross"), None, None),
        check_vma=False,
    )
```

```python
import functools
import itertools

import jax
import jax.numpy as jnp
import numpy as np
from jax import lax
from jax.experimental import pallas as pl
from jax.experimental.pallas import tpu as pltpu
from jax.sharding import PartitionSpec as P

EDGE = 16
STEPS = 3
SLOTS = 3
POPS = 19
PLANES = SLOTS * POPS + SLOTS
FLAG0 = SLOTS * POPS
GROUP = 24
PLANE = 3 * GROUP
SLOT = POPS * PLANE
CELL = 40
CELLS = PLANES * CELL
LANDINGS = CELLS + 8
OWN2 = LANDINGS + 8
OUTWARD = SLOTS * 5 + SLOTS
LAYERS = 2 * PLANES + OUTWARD
RIM = 11 * EDGE
REST = POPS * EDGE + 10 * EDGE
ALONG_Z = 128
HALF = REST - ALONG_Z
SECOND = 6 * GROUP + ALONG_Z
PAIR = 2 * GROUP
QUADS = PLANES // 4
TABLE = RIM
STRIPS = RIM + 8
FAR = QUADS * GROUP
EDGE_TABLE = FAR + 3 * GROUP
EDGE_ROWS = EDGE_TABLE + 24
NEAR_ROWS, FAR_ROWS = EDGE_ROWS + 16, EDGE_ROWS + 24
NOWHERE = PLANES * GROUP
ALL_PLANES = PLANES + POPS
LIMIT = 20 * 1024 * 1024
WIDE_LIMIT = 127 * 512 * 1024

VELOCITY = [
    (0, 0, 0),
    (1, 0, 0),
    (-1, 0, 0),
    (0, 1, 0),
    (0, -1, 0),
    (0, 0, 1),
    (0, 0, -1),
    (1, 1, 0),
    (-1, -1, 0),
    (1, -1, 0),
    (-1, 1, 0),
    (1, 0, 1),
    (-1, 0, -1),
    (1, 0, -1),
    (-1, 0, 1),
    (0, 1, 1),
    (0, -1, -1),
    (0, 1, -1),
    (0, -1, 1),
]
NORTHWARD, SOUTHWARD = (
    [s * POPS + p for s in range(SLOTS) for p in range(POPS) if VELOCITY[p][1] == side]
    + [FLAG0 + s for s in range(SLOTS)]
    for side in (1, -1)
)
THIRD = [
    (pop, source, *((32 + 16 * k, 9) if k < 4 else (16 * (k - 4), 10)))
    for k, (pop, source) in enumerate(
        [(p, 32) for p in (4, 8, 9, 16, 18)] + [(p, 80) for p in (3, 7, 10, 15, 17)]
    )
]
OPPOSITE = [0, 2, 1, 4, 3, 6, 5, 8, 7, 10, 9, 12, 11, 14, 13, 16, 15, 18, 17]


def lanes_iota():
    return lax.broadcasted_iota(jnp.int32, (8, 128), 1)


def is_even(axis, unit=1):
    return lax.rem(lax.axis_index(axis) // unit, 2) == 0


def rows_iota():
    return lax.broadcasted_iota(jnp.int32, (8, 128), 0)


def aligned(start, size=8):
    return pl.ds(pl.multiple_of(start, 8), size)


def move_slots(moves, curve_size, cross_size):
    curve, cross = lax.axis_index("curve"), lax.axis_index("cross")

    def landed(source, target):
        inside = (source >= 0) & (source < curve_size) & (target >= 0) & (target < curve_size)
        row = jnp.clip(source, 0, curve_size - 1) * cross_size + cross
        rank = target * cross_size + cross
        hit = inside & (moves[0, row] >= 0) & (moves[1, row] == rank)
        return jnp.where(hit, moves[2, row], -1)

    return (
        landed(curve - 1, curve),
        landed(curve + 1, curve),
        landed(curve - 2, curve - 1),
        landed(curve, curve - 1),
        landed(curve + 2, curve + 1),
        landed(curve, curve + 1),
    )


def pack_kernel(
    curve_size,
    cross_size,
    moves_hbm,
    counts_hbm,
    pops_hbm,
    flags_hbm,
    neighbours_hbm,
    cells_hbm,
    mate_hbm,
    other_hbm,
    mate2_hbm,
    other2_hbm,
    rest_hbm,
    moves,
    counts,
    pops,
    flags,
    neighbours,
    cells,
    up_msg,
    down_msg,
    up2_msg,
    down2_msg,
    rest_msg,
    wide_flags,
    plane_flags,
    site_flags,
    near,
    sems,
):
    started = []

    def copy(source, target):
        one = pltpu.make_async_copy(source, target, sems.at[len(started)])
        one.start()
        started.append(one)
        return one

    flags_copy = copy(flags_hbm, flags)
    copies = [copy(pops_hbm.at[s], pops.at[s]) for s in range(SLOTS)]
    small = [
        copy(neighbours_hbm, neighbours),
        copy(counts_hbm, counts),
        copy(moves_hbm, moves),
    ]
    for one in small:
        one.wait()

    near[...] = jnp.zeros_like(near)
    named = neighbours[...]
    slot = jnp.where(named >= 0, lax.rem(jnp.maximum(named, 0), SLOTS), SLOTS)
    near[0:SLOTS, 0 : named.shape[1]] = slot.astype(jnp.float32)
    for ref, row in ((cells, CELLS), (up_msg, TABLE), (down_msg, TABLE)):
        ref[row : row + 8, :] = near[...]

    wide_flags[...] = jnp.zeros_like(wide_flags)
    flags_copy.wait()
    wide_flags[0:SLOTS, 0 : flags.shape[1]] = flags[...].astype(jnp.float32)
    span = EDGE + 2
    for x in range(EDGE):
        start = (x + 1) * span * span
        base = start // 128 * 128
        window = wide_flags[:, base : base + 512]
        window = pltpu.roll(window, (512 - (start - base)) % 512, axis=1)
        plane_flags[8 * x : 8 * x + 8, :] = window[:, :384].astype(jnp.bfloat16)
    lane_in = lax.broadcasted_iota(jnp.int32, (384, 256), 0)
    site = lax.broadcasted_iota(jnp.int32, (384, 256), 1)
    chosen = lane_in == (site // EDGE + 1) * span + site % EDGE + 1
    product = jnp.dot(
        plane_flags[...],
        jnp.where(chosen, 1.0, 0.0).astype(jnp.bfloat16),
        preferred_element_type=jnp.float32,
    )
    site_flags[0:128, :] = product[:, :128]
    site_flags[128:256, :] = product[:, 128:]
    for s in range(SLOTS):
        live = s < counts[0]
        for y in range(2):
            piece = site_flags[pl.ds(128 * y + s, EDGE, stride=8), :]
            is_fluid = (piece == 1.0) & live
            row = (FLAG0 + s) * CELL + y * EDGE
            cells[row : row + EDGE, :] = jnp.where(is_fluid, 1.0, 0.0)

    for s in range(SLOTS):
        copies[s].wait()
        for x in range(EDGE):
            for y in range(2):
                tile = 2 * x + y
                for p, size in ((0, 8), (8, 8), (16, 3)):
                    row = (s * POPS + p) * CELL + y * EDGE + x
                    cells[pl.ds(row, size, stride=CELL), :] = pops[
                        s, p : p + size, 128 * tile : 128 * tile + 128
                    ]

    @pl.loop(0, SLOTS)
    def _(s):
        @pl.loop(0, 4, unroll=2)
        def _(c):
            base = s * (POPS * CELL) + c * 8
            view = cells.at[aligned(base, (POPS - 1) * CELL + 8), :]
            h = [view[p * CELL : p * CELL + 8, :] for p in range(POPS)]
            for p, value in enumerate(collided(h)):
                view[p * CELL : p * CELL + 8, :] = value

    for i, slot in enumerate(move_slots(moves, curve_size, cross_size)):
        value = jnp.full((1, 128), slot, jnp.int32)
        cells[LANDINGS + i : LANDINGS + i + 1, :] = value.astype(jnp.float32)

    body_copy = copy(cells.at[:OWN2], cells_hbm.at[:OWN2])

    for y in range(2):
        for msg, x0, first in ((up_msg, 15, 1), (down_msg, 0, 2)):
            step = -1 if x0 else 1
            for k in range(2):
                out = STRIPS + y * LAYERS + k * PLANES
                msg[out : out + PLANES, :] = cells[
                    pl.ds(y * EDGE + x0 + step * k, PLANES, stride=CELL), :
                ]
            row = y * EDGE + x0 + 2 * step
            out = STRIPS + y * LAYERS + 2 * PLANES
            for s in range(SLOTS):
                base = s * POPS * CELL + row
                msg[out + 5 * s : out + 5 * s + 1, :] = cells[pl.ds(base + first * CELL, 1), :]
                msg[out + 5 * s + 1 : out + 5 * s + 5, :] = cells[
                    pl.ds(base + (first + 6) * CELL, 4, stride=2 * CELL), :
                ]
            msg[out + 5 * SLOTS : out + OUTWARD, :] = cells[
                pl.ds(FLAG0 * CELL + row, SLOTS, stride=CELL), :
            ]

    here = lax.axis_index("curve") * cross_size + lax.axis_index("cross")
    leaving = jnp.maximum(moves[0, here], 0)
    lane = lanes_iota()
    for v in range(2):
        halves = [
            [cells[aligned(leaving * (POPS * CELL) + p * CELL + y * EDGE + v * 8), :] for y in (0, 1)]
            for p in range(POPS)
        ]
        outer = [jnp.where(lane < 64, first, second) for first, second in halves]
        middle = (lane >= 32) & (lane < 96)
        sets = [
            jnp.where(middle, pltpu.roll(outer[p + 1], 64, axis=1), outer[p])
            for p in range(0, POPS - 1, 2)
        ]
        sets += [outer[POPS - 1], jnp.zeros_like(outer[0])]
        for pop, source, target, which in THIRD:
            moved = pltpu.roll(outer[pop], (target - source) % 128, axis=1)
            sets[which] = jnp.where(lane // 16 == target // 16, moved, sets[which])
        for k, value in enumerate(sets):
            row = k * EDGE + v * 8
            up_msg[row : row + 8, :] = value
            down_msg[row : row + 8, :] = value
        for p, (first, second) in enumerate(halves):
            row = p * EDGE + v * 8
            rest_msg[row : row + 8, :] = jnp.where(lane < 32, second, first)
        for p in range(0, POPS, 2):
            value = halves[p][1]
            if p + 1 < POPS:
                value = jnp.where(middle, value, pltpu.roll(halves[p + 1][1], 64, axis=1))
            row = (POPS + p // 2) * EDGE + v * 8
            rest_msg[row : row + 8, :] = value
    for s in range(SLOTS):

        @pl.when(leaving == s)
        def _():
            for y in range(2):
                for k in range(3):
                    out = (y * 3 + k) * GROUP
                    row = s * POPS * CELL + y * EDGE + k
                    up2_msg[out : out + POPS, :] = cells[pl.ds(row + 13, POPS, stride=CELL), :]
                    down2_msg[out : out + POPS, :] = cells[pl.ds(row, POPS, stride=CELL), :]

    cells[OWN2 : OWN2 + 6 * GROUP, :] = up2_msg[: 6 * GROUP, :]
    cells[OWN2 + 6 * GROUP :, :] = down2_msg[: 6 * GROUP, :]
    for msg in (up2_msg, down2_msg):
        msg[6 * GROUP :, :] = rest_msg[HALF:, :]
    last = [copy(cells.at[OWN2:], cells_hbm.at[OWN2:]), copy(rest_msg, rest_hbm)]
    count = len(started)
    for i, (up, down, mate, other, unit) in enumerate(
        ((up_msg, down_msg, mate_hbm, other_hbm, 1), (up2_msg, down2_msg, mate2_hbm, other2_hbm, 2))
    ):
        first, second = sems.at[count + 2 * i], sems.at[count + 2 * i + 1]
        even = is_even("curve", unit)

        @pl.when(even)
        def _():
            pltpu.make_async_copy(up, mate, first).start()
            pltpu.make_async_copy(down, other, second).start()

        @pl.when(jnp.logical_not(even))
        def _():
            pltpu.make_async_copy(down, mate, first).start()
            pltpu.make_async_copy(up, other, second).start()

        last.append(pltpu.make_async_copy(up, mate, first))
        last.append(pltpu.make_async_copy(down, other, second))
    body_copy.wait()
    for one in last:
        one.wait()


def spread_kernel(cells, outer):
    low = lanes_iota() < 64
    for q in range(PLANES):
        for v in range(2):
            row = q * CELL + v * 8
            first, second = cells[row : row + 8, :], cells[row + EDGE : row + EDGE + 8, :]
            row = q * GROUP + v * 8
            outer[row : row + 8, :] = jnp.where(low, first, second)


def sort_messages(mate_msg, other_msg, mate2_msg, other2_msg, low_msg, high_msg, low2, high2):
    for mate, other, low, high, unit in (
        (mate_msg, other_msg, low_msg, high_msg, 1),
        (mate2_msg, other2_msg, low2, high2, 2),
    ):
        even = is_even("curve", unit)

        @pl.when(even)
        def _():
            low[...] = other[...]
            high[...] = mate[...]

        @pl.when(jnp.logical_not(even))
        def _():
            low[...] = mate[...]
            high[...] = other[...]


def landed_slots(cells):
    return [jnp.max(cells[LANDINGS + i : LANDINGS + i + 1, :]) for i in range(6)]


def rim_of(msg, p, v):
    row = p // 2 * EDGE + v * 8
    value = msg[row : row + 8, :]
    return pltpu.roll(value, 64, axis=1) if p % 2 else value


def sel4(parts, lane):
    first = jnp.where(lane < 32, parts[0], parts[1])
    second = jnp.where(lane < 96, parts[2], parts[3])
    return jnp.where(lane < 64, first, second)


def strip_rows(first, row0, step):
    pieces = []
    for k in range(2):
        pieces.append(
            (PLANES, lambda size, row: pl.ds(row, PLANES, stride=size), row0 + step * k, STRIPS + k * PLANES)
        )
    row, source = row0 + 2 * step, STRIPS + 2 * PLANES
    for s in range(SLOTS):
        plane = s * POPS + first
        pieces.append((1, lambda size, row, plane=plane: pl.ds(plane * size + row, 1), row, source))
        pieces.append(
            (
                4,
                lambda size, row, plane=plane: pl.ds(
                    (plane + 6) * size + row, 4, stride=2 * size
                ),
                row,
                source + 1,
            )
        )
        source += 5
    pieces.append(
        (SLOTS, lambda size, row: pl.ds(FLAG0 * size + row, SLOTS, stride=size), row, source)
    )
    return pieces


def edge_kernel(
    own_outer,
    cells,
    mate_msg,
    other_msg,
    mate2_msg,
    other2_msg,
    near_msg,
    far_msg,
    turn_msg,
    outer,
    low_msg,
    high_msg,
    low2_msg,
    high2_msg,
):
    sort_messages(
        mate_msg, other_msg, mate2_msg, other2_msg, low_msg, high_msg, low2_msg, high2_msg
    )
    from_low, from_high, low_low, low_me, high_high, high_me = landed_slots(cells)
    low = lanes_iota() < 64
    for q in range(PLANES):
        for v in range(2):
            row = q * GROUP + v * 8
            outer[row : row + 8, :] = own_outer[row : row + 8, :]

    def both(first, second):
        lane = lax.broadcasted_iota(jnp.int32, first.shape, 1)
        return jnp.where(lane < 64, first, second)

    for msg, row0, step, first in ((high_msg, 16, 1, 2), (low_msg, 23, -1, 1)):
        for count, planes, row, source in strip_rows(first, row0, step):
            outer[planes(GROUP, row), :] = both(
                msg[source : source + count, :],
                msg[LAYERS + source : LAYERS + source + count, :],
            )
    lane = lanes_iota()
    for s, (slot, msg) in itertools.product(
        range(SLOTS), ((from_low, low_msg), (from_high, high_msg))
    ):

        @pl.when(slot == s)
        def _():
            for v in range(2):
                values = [rim_of(msg, p, v) for p in range(POPS)]
                for pop, target, source, which in THIRD:
                    row = which * EDGE + v * 8
                    moved = pltpu.roll(msg[row : row + 8, :], (target - source) % 128, axis=1)
                    values[pop] = jnp.where(lane // 16 == target // 16, moved, values[pop])
                for p, value in enumerate(values):
                    row = (s * POPS + p) * GROUP + v * 8
                    outer[row : row + 8, :] = value

    for s in range(SLOTS):
        for slot, msg, row0 in (
            (low_low, low2_msg, 21),
            (low_me, cells.at[OWN2:], 21),
            (high_high, high2_msg, 16),
            (high_me, cells.at[OWN2 + 6 * GROUP :], 16),
        ):

            @pl.when(slot == s)
            def _():
                for k in range(3):
                    outer[pl.ds(s * POPS * GROUP + row0 + k, POPS, stride=GROUP), :] = both(
                        msg[k * GROUP : k * GROUP + POPS, :],
                        msg[(3 + k) * GROUP : (3 + k) * GROUP + POPS, :],
                    )

    from_above = is_even("curve")
    for row in range(0, ALONG_Z, 8):
        tail = slice(6 * GROUP + row, 6 * GROUP + row + 8)
        value = jnp.where(from_above, high2_msg[tail, :], low2_msg[tail, :])
        turn_msg[row : row + 8, :] = value

    even = is_even("cross")

    def send(row, north, south):
        near_msg[row : row + 8, :] = jnp.where(even, north, south)
        far_msg[row : row + 8, :] = jnp.where(even, south, north)

    for v in range(3):

        def plane(q):
            return outer[q * GROUP + v * 8 : q * GROUP + v * 8 + 8, :]

        for quad in range(QUADS):
            parts = [plane(4 * quad)]
            parts += [pltpu.roll(plane(4 * quad + k), 32 * k, axis=1) for k in (1, 2, 3)]
            send(quad * GROUP + v * 8, sel4(parts[1:] + parts[:1], lane), sel4(parts, lane))
        for part in range(3):
            values = []
            for planes, source in ((NORTHWARD, 80), (SOUTHWARD, 32)):
                value = None
                for k, q in enumerate(planes[8 * part : 8 * part + 8]):
                    moved = pltpu.roll(plane(q), (16 * k - source) % 128, axis=1)
                    value = moved if value is None else jnp.where(lane < 16 * k, value, moved)
                values.append(value)
            send(FAR + part * GROUP + v * 8, *values)
    tables = (low_msg, TABLE), (cells, CELLS), (high_msg, TABLE)
    for i, (ref, row) in enumerate(tables):
        value = ref[row : row + 8, :]
        send(EDGE_TABLE + 8 * i, value, value)


def collided(h):
    shear = 1.0 / 0.6
    rest = h[0]
    sx, dx = h[1] + h[2], h[1] - h[2]
    sy, dy = h[3] + h[4], h[3] - h[4]
    sz, dz = h[5] + h[6], h[5] - h[6]
    s7, d7 = h[7] + h[8], h[7] - h[8]
    s9, d9 = h[9] + h[10], h[9] - h[10]
    s11, d11 = h[11] + h[12], h[11] - h[12]
    s13, d13 = h[13] + h[14], h[13] - h[14]
    s15, d15 = h[15] + h[16], h[15] - h[16]
    s17, d17 = h[17] + h[18], h[17] - h[18]
    txy, txz, tyz = s7 + s9, s11 + s13, s15 + s17
    pxy, pxz, pyz = s7 - s9, s11 - s13, s15 - s17
    ax, bx = d7 + d9, d11 + d13
    ay, by = d7 - d9, d15 + d17
    az, bz = d11 - d13, d15 - d17
    axes = sx + sy + sz
    diags = txy + txz + tyz
    rho = rest * (1.0 / 3.0) + axes * (1.0 / 18.0) + diags * (1.0 / 36.0)
    fx, fy, fz = ax + bx, ay + by, az + bz
    jx = dx * (1.0 / 18.0) + fx * (1.0 / 36.0)
    jy = dy * (1.0 / 18.0) + fy * (1.0 / 36.0)
    jz = dz * (1.0 / 18.0) + fz * (1.0 / 36.0)
    inverse = 1.0 / rho
    ux, uy, uz = jx * inverse, jy * inverse, jz * inverse
    qxx, qyy, qzz = jx * ux, jy * uy, jz * uz
    total = qxx + qyy + qzz

    energy = -10.0 * rest - axes * (11.0 / 18.0) + diags * (8.0 / 36.0)
    energy = (energy + 11.0 * rho - 19.0 * total) * (1.19 / 2394.0)
    square = 4.0 * rest - axes * (4.0 / 18.0) + diags * (1.0 / 36.0)
    square = (square - 3.0 * rho + 5.5 * total) * (1.4 / 252.0)
    axis_x = (3.0 * sx - axes) * (1.0 / 18.0)
    diag_x = (diags - 3.0 * tyz) * (1.0 / 36.0)
    want_x = 3.0 * qxx - total
    stress_x = (axis_x + diag_x - want_x) * (shear / 36.0)
    third_x = (diag_x - 2.0 * axis_x + 0.5 * want_x) * (1.4 / 72.0)
    axis_w = (sy - sz) * (1.0 / 18.0)
    diag_w = (txy - txz) * (1.0 / 36.0)
    want_w = qyy - qzz
    stress_w = (axis_w + diag_w - want_w) * (shear / 12.0)
    third_w = (diag_w - 2.0 * axis_w + 0.5 * want_w) * (1.4 / 24.0)

    rest_out = rest - 3.0 * (12.0 * square - 30.0 * energy)
    common = -18.0 * (11.0 * energy + 4.0 * square)
    along_x = 18.0 * (stress_x - 2.0 * third_x)
    along_w = 18.0 * (stress_w - 2.0 * third_w)
    ex = common + 2.0 * along_x
    ey = common - along_x + along_w
    ez = common - along_x - along_w
    common = 36.0 * (8.0 * energy + square)
    across_x = 36.0 * (stress_x + third_x)
    across_w = 36.0 * (stress_w + third_w)
    exy = common + across_x + across_w
    exz = common + across_x - across_w
    eyz = common - 2.0 * across_x
    cxy = shear * (0.25 * pxy - 9.0 * jx * uy)
    cxz = shear * (0.25 * pxz - 9.0 * jx * uz)
    cyz = shear * (0.25 * pyz - 9.0 * jy * uz)

    def flux(d, f, j):
        return (f * (1.0 / 36.0) - d * (4.0 / 18.0) + j * (2.0 / 3.0)) * (1.2 / 40.0)

    hx, hy, hz = flux(dx, fx, jx), flux(dy, fy, jy), flux(dz, fz, jz)
    mx = (ax - bx) * (1.98 / 8.0)
    my = (by - ay) * (1.98 / 8.0)
    mz = (az - bz) * (1.98 / 8.0)
    hx36, hy36, hz36 = 36.0 * hx, 36.0 * hy, 36.0 * hz
    xy_x, xz_x = hx36 + mx, hx36 - mx
    yz_y, xy_y = hy36 + my, hy36 - my
    xz_z, yz_z = hz36 + mz, hz36 - mz
    ox, oy, oz = -2.0 * hx36, -2.0 * hy36, -2.0 * hz36

    out = [rest_out]

    def pair(i, even, odd):
        out.append(h[i] - (even + odd))
        out.append(h[i + 1] - (even - odd))

    pair(1, ex, ox)
    pair(3, ey, oy)
    pair(5, ez, oz)
    pair(7, exy + cxy, xy_x + xy_y)
    pair(9, exy - cxy, xy_x - xy_y)
    pair(11, exz + cxz, xz_x + xz_z)
    pair(13, exz - cxz, xz_x - xz_z)
    pair(15, eyz + cyz, yz_y + yz_z)
    pair(17, eyz - cyz, yz_y - yz_z)
    return out


def collide_all(h_ref, flags, posts, parts=((0, 1), (2,))):
    for groups in parts:
        ref = posts[groups[0] // 2]
        size = len(groups) * GROUP

        @pl.loop(0, SLOTS)
        def _(s):
            @pl.loop(0, size // 8, unroll=3)
            def _(c):
                is_fluid = flags[groups[0] // 2][aligned((FLAG0 + s) * size + c * 8), :] > 0.0
                start = s * SLOT + groups[0] * GROUP + c * 8
                h_view = h_ref.at[aligned(start, (POPS - 1) * PLANE + 8), :]
                start = s * (POPS * size) + c * 8
                view = ref.at[aligned(start, (POPS - 1) * size + 8), :]
                h = [h_view[p * PLANE : p * PLANE + 8, :] for p in range(POPS)]
                for p, value in enumerate(collided(h)):
                    view[p * size : p * size + 8, :] = jnp.where(is_fluid, value, jnp.nan)


def hide_walls(ref, size):
    @pl.loop(0, SLOTS)
    def _(s):
        @pl.loop(0, size // 8)
        def _(c):
            is_fluid = ref[aligned((FLAG0 + s) * size + c * 8), :] > 0.0
            start = s * (POPS * size) + c * 8
            view = ref.at[aligned(start, (POPS - 1) * size + 8), :]
            for p in range(POPS):
                row = p * size
                view[row : row + 8, :] = jnp.where(is_fluid, view[row : row + 8, :], jnp.nan)


def stream_all(posts, h_ref, flags, table, groups, vregs, finish=None):
    lane = lanes_iota()
    row = rows_iota()
    low = lane < 64

    def one_slot(s):
        views = {}

        def view(which, key):
            if (which, key) not in views:
                start = s * (POPS * GROUP) if key == "own" else table[key[0] * 8 + s, key[1]]
                start = start if which else 2 * start
                views[which, key] = posts[which].at[
                    aligned(start, POPS * (GROUP if which else PAIR)), :
                ]
            return views[which, key]

        def load(key, pop, group, v):
            if group == 2:
                row = pop * GROUP + v * 8
            else:
                row = pop * PAIR + group * GROUP + v * 8
            return view(group // 2, key)[row : row + 8, :]

        h_view = h_ref.at[aligned(s * SLOT, SLOT), :]

        def shifted(pop, group, j, dy, dz):
            cx = VELOCITY[pop][0]

            def rows(key, v):
                return load(key, pop, group, v)

            def look(i, j, dx, v):
                if (dx, dy, dz) == (0, 0, 0):
                    return rows("own", v)
                if j is None:
                    return jnp.where(low, look(i, 1, dx, v), look(i, -1, dx, v))
                region = (i + 1) * 3 + j + 1
                return rows((region, VELOCITY.index((dx, dy, dz)) - 1), v)

            need_last = vregs == 3
            values = [look(0, j, 0, 0), look(0, j, 0, 1)]
            if need_last:
                if dy == 0 and dz == 0:
                    values.append(rows("own", 2))
                else:
                    values.append(jnp.where(row < 4, look(1, j, 0, 2), look(-1, j, 0, 2)))
            if cx == 0:
                return values
            turn = 1 if cx > 0 else 7
            rolled = [pltpu.roll(value, turn, axis=0) for value in values]
            if cx > 0:
                before = pltpu.roll(look(0, j, -1, 2), 1, axis=0)
                result = [
                    jnp.where(row == 0, before, rolled[0]),
                    jnp.where(row == 0, rolled[0], rolled[1]),
                ]
                if need_last:
                    edge = pltpu.roll(look(1, j, -1, 1), 1, axis=0)
                    result.append(jnp.where(row == 0, edge, rolled[2]))
                return result
            after = pltpu.roll(look(0, j, 1, 2), 7, axis=0)
            result = [
                jnp.where(row == 7, rolled[1], rolled[0]),
                jnp.where(row == 7, after, rolled[1]),
            ]
            if need_last:
                edge = pltpu.roll(look(-1, j, 1, 0), 7, axis=0)
                result.append(jnp.where(row == 7, edge, rolled[2]))
            return result

        for pop in range(POPS):
            cx, cy, cz = VELOCITY[pop]
            kept = {}

            def source(*key):
                if key not in kept:
                    kept[key] = shifted(pop, *key)
                return kept[key]

            def along_y(group, dz):
                values = source(group, None if group == 2 else 0, 0, dz)
                if cy == 0:
                    return values
                other = (group - cy) % 3
                if group != 2 and other != 2:
                    carried = source(other, 0, 0, dz)
                else:
                    carried = source(other, cy if group == 2 else 0, -cy, dz)
                mask = lane >= 112 if cy > 0 else lane < 16
                return [jnp.where(mask, b, a) for a, b in zip(values, carried)]

            for group in groups:
                values = along_y(group, 0)
                turn = (16 * cy + cz) % 128
                if turn:
                    values = [pltpu.roll(value, turn, axis=1) for value in values]
                if cz:
                    turn = (16 * cy - 15 * cz) % 128
                    wrapped = [pltpu.roll(value, turn, axis=1) for value in along_y(group, -cz)]
                    mask = lane % 16 == (0 if cz > 0 else 15)
                    values = [jnp.where(mask, b, a) for a, b in zip(values, wrapped)]
                for v, value in enumerate(values[:vregs]):
                    if pop:
                        value = jnp.where(value != value, load("own", OPPOSITE[pop], group, v), value)
                    if finish is not None:
                        is_fluid = flags[group // 2][
                            aligned((FLAG0 + s) * PAIR + group * GROUP + v * 8), :
                        ]
                        value = jnp.where(is_fluid > 0.0, value, 0.0)
                    target = pop * PLANE + group * GROUP + v * 8
                    h_view[target : target + 8, :] = value

    @pl.loop(0, SLOTS)
    def _(s):
        one_slot(s)
        if finish is not None:
            finish(s)


def join_kernel(
    cells,
    mate_msg,
    other_msg,
    mate2_msg,
    other2_msg,
    post_ref,
    slots,
    low_msg,
    high_msg,
    low2_msg,
    high2_msg,
):
    sort_messages(
        mate_msg, other_msg, mate2_msg, other2_msg, low_msg, high_msg, low2_msg, high2_msg
    )
    for i, (ref, row) in enumerate(((low_msg, TABLE), (cells, CELLS), (high_msg, TABLE))):
        slots[8 * i : 8 * i + 8, :] = first_rows(ref[row : row + 8, :])

    from_low, from_high, low_low, low_me, high_high, high_me = landed_slots(cells)
    post_ref[PLANES * PAIR :, :] = jnp.full((POPS * PAIR, 128), jnp.nan, jnp.float32)
    for q in range(PLANES):
        for y in range(2):
            start = q * PAIR + y * GROUP
            post_ref[start : start + EDGE, :] = cells[
                q * CELL + y * EDGE : q * CELL + (y + 1) * EDGE, :
            ]
    for s, (slot, msg) in itertools.product(
        range(SLOTS), ((from_low, low_msg), (from_high, high_msg))
    ):

        @pl.when(slot == s)
        def _():
            for p in range(POPS):
                for v in range(2):
                    rim = rim_of(msg, p, v)
                    row = (s * POPS + p) * PAIR + v * 8
                    post_ref[row : row + 8, :] = rim
                    post_ref[row + GROUP : row + GROUP + 8, :] = rim

    for msg, row0, step, first in ((high_msg, 16, 1, 2), (low_msg, 23, -1, 1)):
        for y in range(2):
            for count, planes, row, source in strip_rows(first, row0, step):
                source += y * LAYERS
                post_ref[planes(PAIR, row + y * GROUP), :] = msg[source : source + count, :]
    for s in range(SLOTS):
        for slot, msg, row0 in (
            (low_low, low2_msg, 21),
            (low_me, cells.at[OWN2:], 21),
            (high_high, high2_msg, 16),
            (high_me, cells.at[OWN2 + 6 * GROUP :], 16),
        ):

            @pl.when(slot == s)
            def _():
                for y in range(2):
                    for k in range(3):
                        row = s * POPS * PAIR + y * GROUP + row0 + k
                        source = (y * 3 + k) * GROUP
                        post_ref[pl.ds(row, POPS, stride=PAIR), :] = msg[source : source + POPS, :]
    hide_walls(post_ref, PAIR)


def first_rows(slot):
    slot = slot.astype(jnp.int32)
    return jnp.where(slot == SLOTS, NOWHERE, slot * (POPS * GROUP))


def outer_kernel(
    own_slots, first_post, near_msg, far_msg, slots, outer_ref, next_ref, h_ref, table, sem
):
    even = is_even("cross")

    def received(row):
        near, far = near_msg[row : row + 8, :], far_msg[row : row + 8, :]
        return jnp.where(even, far, near), jnp.where(even, near, far)

    for i in range(3):
        south, north = received(EDGE_TABLE + 8 * i)
        slots[24 * i : 24 * i + 8, :] = first_rows(south)
        slots[24 * i + 8 : 24 * i + 16, :] = own_slots[8 * i : 8 * i + 8, :]
        slots[24 * i + 16 : 24 * i + 24, :] = first_rows(north)
    table_copy = pltpu.make_async_copy(slots, table, sem)
    table_copy.start()

    nothing = jnp.full((8, 128), jnp.nan, jnp.float32)
    for row in range(0, POPS * GROUP, 8):
        outer_ref[NOWHERE + row : NOWHERE + row + 8, :] = nothing
        next_ref[NOWHERE + row : NOWHERE + row + 8, :] = nothing
    lane = lanes_iota()
    for v in range(3):

        def rows(q):
            return slice(q * GROUP + v * 8, q * GROUP + v * 8 + 8)

        for quad in range(QUADS):
            south, north = received(quad * GROUP + v * 8)
            for k in range(4):
                value = jnp.where(lane // 32 == (k + 3) % 4, south, north)
                if k:
                    value = pltpu.roll(value, 128 - 32 * k, axis=1)
                outer_ref[rows(4 * quad + k), :] = value
        for part in range(3):
            values = received(FAR + part * GROUP + v * 8)
            for planes, target, value in zip((NORTHWARD, SOUTHWARD), (80, 32), values):
                for k, q in enumerate(planes[8 * part : 8 * part + 8]):
                    moved = pltpu.roll(value, (target - 16 * k) % 128, axis=1)
                    outer_ref[rows(q), :] = jnp.where(
                        lane // 16 == target // 16, moved, outer_ref[rows(q), :]
                    )
    for row in range(FLAG0 * GROUP, NOWHERE, 8):
        next_ref[row : row + 8, :] = outer_ref[row : row + 8, :]
    hide_walls(outer_ref, GROUP)
    table_copy.wait()
    flags = (first_post, outer_ref)
    stream_all(flags, h_ref, flags, table, (2,), 3)
    collide_all(h_ref, flags, (None, next_ref), ((2,),))


def steps_kernel(
    slots,
    first_post,
    first_outer,
    next_outer,
    cells,
    mate_msg,
    other_msg,
    mate_rest,
    passed_rest,
    passed2_rest,
    out_hbm,
    h_ref,
    post_ref,
    outer_ref,
    out,
    table,
    sems,
):
    table_copy = pltpu.make_async_copy(slots, table, sems.at[SLOTS])
    table_copy.start()
    post_ref[...] = first_post[...]
    nothing = jnp.full((8, 128), jnp.nan, jnp.float32)
    for row in range(0, POPS * GROUP, 8):
        outer_ref[NOWHERE + row : NOWHERE + row + 8, :] = nothing

    def rest(row, is_mate):
        if is_mate:
            return mate_rest[row : row + 8, :]
        if row < HALF:
            return passed_rest[row : row + 8, :]
        return passed2_rest[row - HALF : row - HALF + 8, :]

    from_low, from_high = landed_slots(cells)[:2]
    lane = lanes_iota()
    even = is_even("curve")
    odd = jnp.logical_not(even)
    for s, (slot, wanted, msg, is_mate) in itertools.product(
        range(SLOTS),
        (
            (from_low, odd, mate_msg, True),
            (from_low, even, other_msg, False),
            (from_high, even, mate_msg, True),
            (from_high, odd, other_msg, False),
        ),
    ):

        @pl.when((slot == s) & wanted)
        def _():
            for v in range(2):
                starts = [(FLAG0 + s) * PAIR + y * GROUP + v * 8 for y in range(2)]
                fluid = [first_post[row : row + 8, :] > 0.0 for row in starts]
                for p in range(POPS):
                    rim = rim_of(msg, p, v)
                    row = p * EDGE + v * 8
                    wide = rest(row, is_mate)
                    row = (POPS + p // 2) * EDGE + v * 8
                    middle = rest(row, is_mate)
                    if p % 2:
                        middle = pltpu.roll(middle, 64, axis=1)
                    first = jnp.where(lane < 32, rim, wide)
                    second = jnp.where(lane < 32, wide, jnp.where(lane < 96, middle, rim))
                    row = (s * POPS + p) * PAIR + v * 8
                    post_ref[row : row + 8, :] = jnp.where(fluid[0], first, jnp.nan)
                    row += GROUP
                    post_ref[row : row + 8, :] = jnp.where(fluid[1], second, jnp.nan)

    def finish(s):
        for x in range(EDGE):
            for y in range(2):
                tile = 2 * x + y
                for p, size in ((0, 8), (8, 8), (16, 3)):
                    row = s * SLOT + (p * PLANE + y * GROUP + x)
                    out[s, p : p + size, 128 * tile : 128 * tile + 128] = h_ref[
                        pl.ds(row, size, stride=PLANE), :
                    ]
        pltpu.make_async_copy(out.at[s], out_hbm.at[s], sems.at[s]).start()

    table_copy.wait()
    flags = (first_post, first_outer)
    stream_all((post_ref, first_outer), h_ref, flags, table, (0, 1), 3)
    collide_all(h_ref, flags, (post_ref, None), ((0, 1),))
    posts = (post_ref, next_outer)
    for _ in range(STEPS - 2):
        stream_all(posts, h_ref, flags, table, (0, 1, 2), 3)
        posts = (post_ref, outer_ref)
        collide_all(h_ref, flags, posts)
    stream_all(posts, h_ref, flags, table, (0, 1), 2, finish)
    for s in range(SLOTS):
        pltpu.make_async_copy(out.at[s], out_hbm.at[s], sems.at[s]).wait()


def swapped(value, axis, unit=1):
    count = lax.axis_size(axis)
    results = []
    for which in (0, 1):
        others = [i + (unit if i // unit % 2 == which else -unit) for i in range(count)]
        pairs = [(i, j if 0 <= j < count else i) for i, j in enumerate(others)]
        results.append(lax.ppermute(value[which], axis, pairs))
    return results


def rows128(count):
    return jax.ShapeDtypeStruct((count, 128), jnp.float32)


def call(kernel, in_spaces, out_spaces, outs, ins, scratch, limit=LIMIT, cost=None):
    spaces = {
        "S": pl.BlockSpec(memory_space=pltpu.SMEM),
        "V": pl.BlockSpec(memory_space=pltpu.VMEM),
        "H": pl.BlockSpec(memory_space=pltpu.HBM),
    }
    return pl.pallas_call(
        kernel,
        out_shape=outs,
        in_specs=[spaces[x] for x in in_spaces],
        out_specs=[spaces[x] for x in out_spaces],
        scratch_shapes=scratch,
        compiler_params=pltpu.CompilerParams(vmem_limit_bytes=limit),
        cost_estimate=cost,
    )(*ins)


def per_device(populations, site_flags, neighbours, migrations, counts):
    sizes = (lax.axis_size("curve"), lax.axis_size("cross"))
    moves = migrations.T
    floats = lambda rows: pltpu.VMEM((rows, 128), jnp.float32)
    messages = [
        OWN2 + 12 * GROUP,
        STRIPS + 2 * LAYERS,
        STRIPS + 2 * LAYERS,
        SECOND,
        SECOND,
        REST,
    ]
    cells, mate_msg, other_msg, mate2_msg, other2_msg, rest_msg = call(
        functools.partial(pack_kernel, *sizes),
        "HHHHH",
        "HHHHHH",
        [rows128(rows) for rows in messages],
        (moves, counts, populations, site_flags, neighbours),
        [
            pltpu.SMEM(moves.shape, jnp.int32),
            pltpu.SMEM(counts.shape, jnp.int32),
            pltpu.VMEM(populations.shape, jnp.float32),
            pltpu.VMEM(site_flags.shape, jnp.int32),
            pltpu.VMEM(neighbours.shape, jnp.int32),
            *[floats(rows) for rows in messages],
            pltpu.VMEM((8, 5888), jnp.float32),
            pltpu.VMEM((128, 384), jnp.bfloat16),
            floats(256),
            floats(8),
            pltpu.SemaphoreType.DMA((4 + SLOTS + 8,)),
        ],
        WIDE_LIMIT,
    )
    mate_msg, other_msg = swapped((mate_msg, other_msg), "curve")
    mate2_msg, other2_msg = swapped((mate2_msg, other2_msg), "curve", 2)
    assert sizes[0] % 2 == 0
    pairs = [(i, i ^ 1) for i in range(sizes[0])]
    mate_rest = lax.ppermute(rest_msg, "curve", pairs)
    last = sizes[0] - 1
    pairs = [(i, max(i - 2, 0) if i % 2 else min(i + 2, last)) for i in range(sizes[0])]
    passed_rest = lax.ppermute(mate_rest[:HALF], "curve", pairs)
    (outer,) = call(spread_kernel, "V", "V", [rows128(PLANES * GROUP)], (cells,), [])
    strips = (cells, mate_msg, other_msg, mate2_msg, other2_msg)
    sorted_rows = [messages[1], messages[1], messages[3], messages[3]]
    near_msg, far_msg, turn_msg = call(
        edge_kernel,
        "VVVVVV",
        "VVV",
        [rows128(NEAR_ROWS), rows128(FAR_ROWS), rows128(ALONG_Z)],
        (outer, *strips),
        [floats(rows) for rows in [(PLANES + 8) * GROUP] + sorted_rows],
        cost=pl.CostEstimate(flops=10**10, bytes_accessed=0, transcendentals=0),
    )
    near_msg, far_msg = swapped((near_msg, far_msg), "cross")
    pairs = [(i, i ^ 1) for i in range(sizes[0])]
    passed2_rest = lax.ppermute(turn_msg, "curve", pairs)
    post, own_slots = call(
        join_kernel,
        "VVVVV",
        "VV",
        [rows128(ALL_PLANES * PAIR), jax.ShapeDtypeStruct((24, 128), jnp.int32)],
        strips,
        [floats(rows) for rows in sorted_rows],
    )
    slots, outer_post, next_outer = call(
        outer_kernel,
        "VVVV",
        "VVV",
        [
            jax.ShapeDtypeStruct((72, 128), jnp.int32),
            rows128(ALL_PLANES * GROUP),
            rows128(ALL_PLANES * GROUP),
        ],
        (own_slots, post, near_msg, far_msg),
        [floats(SLOTS * SLOT), pltpu.SMEM((72, 128), jnp.int32), pltpu.SemaphoreType.DMA],
    )
    arriving = (cells, mate_msg, other_msg, mate_rest, passed_rest, passed2_rest)
    return call(
        steps_kernel,
        "VVVVVVVVVV",
        "H",
        [jax.ShapeDtypeStruct(populations.shape, jnp.float32)],
        (slots, post, outer_post, next_outer, *arriving),
        [
            floats(SLOTS * SLOT + 8 * PLANE),
            floats(ALL_PLANES * PAIR),
            floats(ALL_PLANES * GROUP),
            pltpu.VMEM(populations.shape, jnp.float32),
            pltpu.SMEM((72, 128), jnp.int32),
            pltpu.SemaphoreType.DMA((SLOTS + 1,)),
        ],
    )[0]


def solution(mesh):
    return jax.shard_map(
        per_device,
        mesh=mesh,
        in_specs=(
            P(("curve", "cross"), None, None),
            P(("curve", "cross"), None),
            P(("curve", "cross"), None),
            P(),
            P(("curve", "cross")),
        ),
        out_specs=P(("curve", "cross"), None, None),
        check_vma=False,
    )
```
